32 devices in a mesh: fsdp: 32 (over z, y, x, core).
Axes of the slice: x: 2, y: 2, z: 4, core: 2. Of those that a mesh axis runs over, the one named last changes fastest.
Arguments:
- inputs: bfloat16 [8192, 2048], P('fsdp'), may hold values from -6 to 6
- positions: int32 [8192], P('fsdp'), may hold values from 0 to 199, as said below
- norm1_gain: bfloat16 [2048], P('fsdp'), may hold values from 0.5 to 1.5
- norm1_bias: bfloat16 [2048], P('fsdp'), may hold values from -4 to 4
- qkv_weight: bfloat16 [2048, 6144], P('fsdp'), may hold values from -0.125 to 0.125
- qkv_bias: bfloat16 [6144], P('fsdp'), may hold values from -4 to 4
- out_weight: bfloat16 [2048, 2048], P('fsdp'), may hold values from -0.5 to 0.5
- norm2_gain: bfloat16 [2048], P('fsdp'), may hold values from 0.5 to 1.5
- norm2_bias: bfloat16 [2048], P('fsdp'), may hold values from -4 to 4
- gate_weight: bfloat16 [2048, 5632], P('fsdp'), may hold values from -0.125 to 0.125
- up_weight: bfloat16 [2048, 5632], P('fsdp'), may hold values from -0.125 to 0.125
- down_weight: bfloat16 [5632, 2048], P('fsdp'), may hold values from -0.078125 to 0.078125
- out_grad: bfloat16 [8192, 2048], P('fsdp'), may hold values from -6 to 6
Outputs:
- block_out: bfloat16 [8192, 2048], P('fsdp')
- input_grad: float32 [8192, 2048], P('fsdp')
- norm1_gain_grad: float32 [2048], P('fsdp')
- norm1_bias_grad: float32 [2048], P('fsdp')
- qkv_weight_grad: float32 [2048, 6144], P('fsdp')
- qkv_bias_grad: float32 [6144], P('fsdp')
- out_weight_grad: float32 [2048, 2048], P('fsdp')
- norm2_gain_grad: float32 [2048], P('fsdp')
- norm2_bias_grad: float32 [2048], P('fsdp')
- gate_weight_grad: float32 [2048, 5632], P('fsdp')
- up_weight_grad: float32 [2048, 5632], P('fsdp')
- down_weight_grad: float32 [5632, 2048], P('fsdp')
The draws below stay inside these ranges and needn't reach their ends.
Inputs may be any that keep to these rules, and one draw needn't show every extreme that they name: `positions`: positions count up by one from 0 inside each document; a document begins where the position is 0, every packed sequence of 256 tokens (tokens k * 256 onward) begins a document, and documents never cross sequences.
All inputs are finite; a program needn't handle non-finite values.
Results may differ from the reference program's by a relative error of at most 0.012.
Values may be sent and summed in bfloat16 or wider, within the bound.
A program may use at most 448 MiB of HBM per device.

```python
from functools import partial
import jax
import jax.numpy as jnp
from jax import lax

D = 2048
HEADS = 32
HEAD_DIM = 64
ROT = 16
FF = 5632
SEQ_LEN = 256
TOKENS = 8192


def draw_positions(key, part):
    key = jax.random.fold_in(key, 11)
    seq_count = TOKENS // SEQ_LEN
    long_doc = SEQ_LEN * 25 // 32
    start_key, cut_key = jax.random.split(key)
    starts = jax.random.randint(start_key, (seq_count, 1), 0, SEQ_LEN - long_doc + 1).astype(jnp.int32)
    indices = jnp.arange(SEQ_LEN, dtype=jnp.int32)[None, :]
    inside = (indices >= starts) & (indices < starts + long_doc)
    cuts = jax.random.randint(cut_key, (seq_count, SEQ_LEN), 0, max(2, SEQ_LEN // 16)) == 0
    begins = (indices == 0) | (indices == starts) | (indices == starts + long_doc) | cuts & ~inside
    doc_start = lax.cummax(jnp.where(begins, indices, 0), axis=1)
    return (indices - doc_start).reshape(-1).astype(jnp.int32)


def shard_levels(stream_key, extent, cuts, low, largest):
    gain = 1.0
    for dim, shards_of in cuts:
        draws = jax.random.uniform(jax.random.fold_in(jax.random.fold_in(stream_key, 6), dim), (shards_of,), jnp.float32, low / len(cuts), largest / len(cuts))
        gain = gain * jnp.repeat(jnp.exp(draws), extent[dim] // shards_of).reshape((-1,) + (1,) * (len(extent) - 1 - dim))
    return gain


def noise(key, shape, scale, bound, cuts=(), kind=jnp.bfloat16):
    loudness = shard_levels(key, shape, cuts, -0.22, 0.18) if cuts else 1.0
    drawn = jax.random.normal(key, shape, jnp.float32) * scale * loudness
    return jnp.minimum(jnp.maximum(drawn, -bound), bound).astype(kind)


def setup_inputs(seed: int = 0) -> dict:
    key_list = jax.random.split(jax.random.key(seed), 14)
    return {
        "inputs": noise(key_list[0], (TOKENS, D), 1.0, 6.0, ((0, 32),)),
        "positions": draw_positions(jax.random.fold_in(key_list[13], 71), 0),
        "norm1_gain": jnp.clip(1.0 + 0.1 * jax.random.normal(key_list[2], (D,), jnp.float32), 0.5, 1.5).astype(jnp.bfloat16),
        "norm1_bias": noise(key_list[3], (D,), 0.3, 4.0, ((0, 32),)),
        "qkv_weight": noise(key_list[4], (D, 3 * D), D ** -0.5, 0.125, ((0, 32),)),
        "qkv_bias": noise(key_list[5], (3 * D,), 0.3, 4.0, ((0, 32),)),
        "out_weight": noise(key_list[6], (D, D), (D // 16) ** -0.5, 0.5, ((0, 32),)),
        "norm2_gain": jnp.clip(1.0 + 0.1 * jax.random.normal(key_list[7], (D,), jnp.float32), 0.5, 1.5).astype(jnp.bfloat16),
        "norm2_bias": noise(key_list[8], (D,), 0.3, 4.0, ((0, 32),)),
        "gate_weight": noise(key_list[9], (D, FF), D ** -0.5, 0.125, ((0, 32),)),
        "up_weight": noise(key_list[10], (D, FF), D ** -0.5, 0.125, ((0, 32),)),
        "down_weight": noise(key_list[11], (FF, D), FF ** -0.5, 0.078125, ((0, 32),)),
        "out_grad": noise(key_list[12], (TOKENS, D), 1.0, 6.0, ((0, 32),)),
    }


EPS = 1e-05
HIGHEST = lax.Precision.HIGHEST

@jax.custom_vjp
def low(v):
    return lax.optimization_barrier(v.astype(jnp.bfloat16)).astype(jnp.float32)

@jax.custom_vjp
def low_back(v):
    return v

def low_keep(v):
    return (low(v), None)

def low_pass(kept, grad):
    return (grad,)

def back_keep(v):
    return (v, None)

def back_low(kept, grad):
    return (low(grad),)
low.defvjp(low_keep, low_pass)
low_back.defvjp(back_keep, back_low)

def layer_norm(stream, gain_vec, bias_vec):
    average = lax.optimization_barrier(jnp.mean(stream, axis=-1, keepdims=True))
    centered = stream - average
    variance = lax.optimization_barrier(jnp.mean(centered * centered, axis=-1, keepdims=True))
    return centered * lax.rsqrt(variance + EPS) * gain_vec + bias_vec

def rotate_pairs(heads, places, sign):
    half_rot = ROT // 2
    frequency = 10000.0 ** (-jnp.arange(half_rot, dtype=jnp.float32) / half_rot)
    angles = places.astype(jnp.float32)[:, None] * frequency[None, :]
    cosine = jnp.cos(angles)[:, None, :]
    sine_part = sign * jnp.sin(angles)[:, None, :]
    front_part = heads[..., :half_rot]
    back_part = heads[..., half_rot:ROT]
    return jnp.concatenate([front_part * cosine - back_part * sine_part, back_part * cosine + front_part * sine_part, heads[..., ROT:]], axis=-1)

def attend_one(block_items):
    query_part, key_part, value_part, places = block_items
    scores = low_back(jnp.einsum('qhd,khd->hqk', query_part, key_part, precision=HIGHEST) * 0.125)
    indices = jnp.arange(SEQ_LEN, dtype=jnp.int32)
    allowed = (indices[None, :] <= indices[:, None]) & (indices[None, :] >= (indices - places)[:, None])
    masked = jnp.where(allowed[None], scores, -1e+30)
    row_max = lax.optimization_barrier(jnp.max(masked, axis=-1, keepdims=True))
    exponent = jnp.exp(masked - row_max)
    soft_probs = exponent / lax.optimization_barrier(jnp.sum(exponent, axis=-1, keepdims=True))
    return jnp.einsum('hqk,khd->qhd', low(soft_probs), value_part, precision=HIGHEST)

def forward(places, stream, gain_one, bias_one, w_qkv, b_qkv, w_out, gain_two, bias_two, w_gate, w_up, w_down):
    h_one = low(layer_norm(stream, gain_one, bias_one))
    qkv_pre = low_back(jnp.dot(h_one, w_qkv, precision=HIGHEST) + b_qkv)
    qkv_heads = qkv_pre.reshape(-1, 3, HEADS, HEAD_DIM)
    query_rot = low(rotate_pairs(qkv_heads[:, 0], places, 1.0))
    key_rot = low(rotate_pairs(qkv_heads[:, 1], places, 1.0))
    value_low = low(qkv_heads[:, 2])
    seq_count = TOKENS // SEQ_LEN
    shaped = (seq_count, SEQ_LEN, HEADS, HEAD_DIM)
    attended = lax.map(jax.checkpoint(attend_one), (query_rot.reshape(shaped), key_rot.reshape(shaped), value_low.reshape(shaped), places.reshape(seq_count, SEQ_LEN)))
    attn_low = low(attended.reshape(-1, D))
    resid = stream + low_back(jnp.dot(attn_low, w_out, precision=HIGHEST))
    h_two = low(layer_norm(resid, gain_two, bias_two))
    gate_pre = low_back(jnp.dot(h_two, w_gate, precision=HIGHEST))
    up_pre = low_back(jnp.dot(h_two, w_up, precision=HIGHEST))
    hidden = low(jax.nn.silu(gate_pre) * up_pre)
    return resid + low_back(jnp.dot(hidden, w_down, precision=HIGHEST))

def reference(inputs, positions, norm1_gain, norm1_bias, qkv_weight, qkv_bias, out_weight, norm2_gain, norm2_bias, gate_weight, up_weight, down_weight, out_grad):
    floats = [arr.astype(jnp.float32) for arr in (inputs, norm1_gain, norm1_bias, qkv_weight, qkv_bias, out_weight, norm2_gain, norm2_bias, gate_weight, up_weight, down_weight)]
    output, pullback = jax.vjp(partial(forward, positions), *floats)
    grads = pullback(out_grad.astype(jnp.float32))
    return (output.astype(jnp.bfloat16), grads[0], grads[1], grads[2], grads[3], grads[4], grads[5], grads[6], grads[7], grads[8], grads[9], grads[10])
```

```python
import functools

import jax
import jax.numpy as jnp
from jax import lax
from jax.experimental import pallas as pl
from jax.experimental.pallas import tpu as pltpu
from jax.sharding import PartitionSpec as P

D = 2048
HEADS = 32
HEAD_DIM = 64
ROT = 16
EPS = 1e-05
TEAM = 8
LOCAL = HEADS // TEAM
MESH = pl.DeviceIdType.MESH
BF16 = jnp.bfloat16
F32 = jnp.float32
ANY = pl.BlockSpec(memory_space=pl.ANY)
VMEM = pl.BlockSpec(memory_space=pltpu.VMEM)


def params(cid=None, limit=56):
    extra = {} if cid is None else {"collective_id": cid, "has_side_effects": True}
    return pltpu.CompilerParams(vmem_limit_bytes=limit * 1024 * 1024, **extra)


def place():
    me = lax.axis_index("fsdp")
    mine = lax.rem(me, TEAM)
    return mine, me - mine, mine // 2, lax.rem(mine, 2)


def chip_at(chip, step):
    along_x, along_y = lax.rem(chip, 2), chip // 2
    if step & 1:
        along_x = 1 - along_x
    if step & 2:
        along_y = 1 - along_y
    return along_y * 2 + along_x


def greet(devices):
    barrier = pltpu.get_barrier_semaphore()
    for device in devices:
        pl.semaphore_signal(barrier, inc=1, device_id=(device,), device_id_type=MESH)
    pl.semaphore_wait(barrier, len(devices))


def remote(src, dst, send, recv, device):
    return pltpu.make_async_remote_copy(
        src_ref=src, dst_ref=dst, send_sem=send, recv_sem=recv, device_id=(device,), device_id_type=MESH
    )


def swap_kernel(x_ref, o_ref, own_sem, send_sem, recv_sem):
    mine, base, _, _ = place()
    greet([base + lax.rem(mine + k, TEAM) for k in range(1, TEAM)])
    copies = []
    for k in range(1, TEAM):
        other = lax.rem(mine + k, TEAM)
        copy = remote(x_ref.at[other], o_ref.at[mine], send_sem.at[k], recv_sem.at[k], base + other)
        copy.start()
        copies.append(copy)
    own = pltpu.make_async_copy(x_ref.at[mine], o_ref.at[mine], own_sem)
    own.start()
    for copy in copies:
        copy.wait()
    own.wait()


def team_swap(blocks, cid):
    return pl.pallas_call(
        swap_kernel,
        out_shape=jax.ShapeDtypeStruct(blocks.shape, blocks.dtype),
        in_specs=[ANY],
        out_specs=ANY,
        scratch_shapes=[pltpu.SemaphoreType.DMA] + [pltpu.SemaphoreType.DMA((TEAM,))] * 2,
        compiler_params=params(cid),
    )(blocks)


def gather_kernel(x_ref, o_ref, own_sem, send_sem, recv_sem, pass_sem, passed_sem):
    mine, base, chip, core = place()
    sibling = base + chip * 2 + 1 - core
    peers = {k: chip_at(chip, k) * 2 + core for k in (3, 1, 2)}
    greet([base + peer for peer in peers.values()] + [sibling])
    copies = {}
    for k, peer in peers.items():
        copies[k] = remote(x_ref, o_ref.at[mine], send_sem.at[k], recv_sem.at[k], base + peer)
        copies[k].start()
    copies[0] = remote(x_ref, o_ref.at[mine], send_sem.at[0], recv_sem.at[0], sibling)
    copies[0].start()
    own = pltpu.make_async_copy(x_ref, o_ref.at[mine], own_sem)
    own.start()
    passed = []
    for k in (1, 2, 3):
        copies[k].wait_recv()
        block = o_ref.at[peers[k]]
        copy = remote(block, block, pass_sem.at[k], passed_sem.at[k], sibling)
        copy.start()
        passed.append(copy)
    for k in (1, 2, 3):
        copies[k].wait_send()
    copies[0].wait()
    own.wait()
    for copy in passed:
        copy.wait()


def team_gather(block, cid):
    return pl.pallas_call(
        gather_kernel,
        out_shape=jax.ShapeDtypeStruct((TEAM,) + block.shape, block.dtype),
        in_specs=[ANY],
        out_specs=ANY,
        scratch_shapes=[pltpu.SemaphoreType.DMA] + [pltpu.SemaphoreType.DMA((4,))] * 4,
        compiler_params=params(cid),
    )(block)


def sum_kernel(x_ref, o_ref, own, near, far, own_sem, near_send, near_recv, far_send, far_recv):
    mine, base, chip, core = place()
    sibling = base + chip * 2 + 1 - core
    chips = {k: chip_at(chip, k) for k in (3, 1, 2, 0)}
    rows = own.shape[1]
    loads = {}
    for k, at in chips.items():
        loads[k] = pltpu.make_async_copy(x_ref.at[at * 2 + core], own.at[k], own_sem.at[k])
        loads[k].start()
    greet([base + chips[k] * 2 + core for k in (3, 1, 2)] + [sibling])
    nears = {}
    for k, at in chips.items():
        nears[k] = remote(x_ref.at[at * 2 + 1 - core], near.at[k], near_send.at[k], near_recv.at[k], sibling)
        nears[k].start()
    fars = {}
    for k in (3, 1, 2):
        loads[k].wait()
        nears[k].wait_recv()

        @pl.loop(0, rows // 16)
        def _(i, k=k):
            part = pl.ds(pl.multiple_of(i * 16, 16), 16)
            own[k, part, :] = (own[k, part, :].astype(F32) + near[k, part, :].astype(F32)).astype(BF16)

        fars[k] = remote(own.at[k], far.at[k - 1], far_send.at[k - 1], far_recv.at[k - 1], base + chips[k] * 2 + core)
        fars[k].start()
    loads[0].wait()
    nears[0].wait_recv()
    for k in (1, 2, 3):
        fars[k].wait_recv()

    @pl.loop(0, rows // 16)
    def _(i):
        part = pl.ds(pl.multiple_of(i * 16, 16), 16)
        total = own[0, part, :].astype(F32) + near[0, part, :].astype(F32)
        for k in range(3):
            total = total + far[k, part, :].astype(F32)
        o_ref[part, :] = total

    for k in (3, 1, 2, 0):
        nears[k].wait_send()
    for k in (3, 1, 2):
        fars[k].wait_send()


def team_sum(blocks, cid):
    _, rows, width = blocks.shape
    return pl.pallas_call(
        sum_kernel,
        out_shape=jax.ShapeDtypeStruct((rows, width), F32),
        in_specs=[ANY],
        out_specs=VMEM,
        scratch_shapes=[
            pltpu.VMEM((4, rows, width), BF16),
            pltpu.VMEM((4, rows, width), BF16),
            pltpu.VMEM((3, rows, width), BF16),
            pltpu.SemaphoreType.DMA((4,)),
            pltpu.SemaphoreType.DMA((4,)),
            pltpu.SemaphoreType.DMA((4,)),
            pltpu.SemaphoreType.DMA((3,)),
            pltpu.SemaphoreType.DMA((3,)),
        ],
        compiler_params=params(cid),
    )(blocks)


def dot(a, b, dims=((1,), (0,))):
    return lax.dot_general(a, b, (dims, ((), ())), preferred_element_type=F32)


NT = ((1,), (1,))
TN = ((0,), (0,))


def normalize(stream):
    average = jnp.mean(stream, axis=-1, keepdims=True)
    centered = stream - average
    variance = jnp.mean(centered * centered, axis=-1, keepdims=True)
    inverse = lax.rsqrt(variance + EPS)
    return centered * inverse, inverse


def norm_back(grad_norm, normed, inverse):
    return inverse * (
        grad_norm
        - jnp.mean(grad_norm, axis=-1, keepdims=True)
        - normed * jnp.mean(grad_norm * normed, axis=-1, keepdims=True)
    )


def turn(heads, cosine, front, back, sign):
    half, width = ROT // 2, heads.shape[-1]
    moved = pltpu.roll(heads, width - half, 1) * front + pltpu.roll(heads, half, 1) * back
    return heads * cosine + sign * moved


def visible(start):
    rows = lax.broadcasted_iota(jnp.int32, (start.shape[0],) * 2, 0)
    columns = lax.broadcasted_iota(jnp.int32, (start.shape[0],) * 2, 1)
    return (columns <= rows) & (columns >= start)


def head_of(x, h):
    lanes = lax.broadcasted_iota(jnp.int32, x.shape, 1)
    return jnp.where((lanes >= h * HEAD_DIM) & (lanes < (h + 1) * HEAD_DIM), x, jnp.zeros_like(x))


def soft(query, key, allowed):
    scores = dot(query, key, NT) * 0.125
    masked = jnp.where(allowed, scores, -1e30)
    exponent = jnp.exp(masked - jnp.max(masked, axis=-1, keepdims=True))
    return exponent / jnp.sum(exponent, axis=-1, keepdims=True)


def attend_kernel(x_ref, gain_ref, bias_ref, w_ref, b_ref, wo_ref, tab_ref, start_ref, h_ref, qkv_ref, attn_ref, part_ref):
    stream = x_ref[0].astype(F32)
    normed, _ = normalize(stream)
    h_one = (normed * gain_ref[...] + bias_ref[...]).astype(BF16)
    h_ref[0] = h_one
    qkv = dot(h_one, w_ref[...]) + b_ref[...]
    width = LOCAL * HEAD_DIM
    cosine, front, back = (jnp.concatenate([tab_ref[0, i]] * (width // 128), axis=1) for i in range(3))
    query = turn(qkv[:, :width], cosine, front, back, 1.0).astype(BF16)
    key = turn(qkv[:, width : 2 * width], cosine, front, back, 1.0).astype(BF16)
    value = qkv[:, 2 * width :].astype(BF16)
    qkv_ref[0, :, :width] = query
    qkv_ref[0, :, width : 2 * width] = key
    qkv_ref[0, :, 2 * width :] = value
    allowed = visible(start_ref[0])
    mixed = jnp.zeros((query.shape[0], width), F32)
    for h in range(LOCAL):
        probs = soft(head_of(query, h), key, allowed).astype(BF16)
        mixed = mixed + dot(probs, head_of(value, h))
    attn_low = mixed.astype(BF16)
    attn_ref[0] = attn_low
    part_ref[0] = dot(attn_low, wo_ref[...]).astype(BF16)


def per_seq(*shape):
    return pl.BlockSpec((1,) + shape, lambda s: (s,) + (0,) * len(shape))


def whole(*shape):
    return pl.BlockSpec(shape, lambda s: (0,) * len(shape))


def attend(x_all, gain, bias, w_qkv, b_qkv, w_out, tables, start):
    seqs, rows, _ = x_all.shape
    width = LOCAL * HEAD_DIM
    return pl.pallas_call(
        attend_kernel,
        grid=(seqs,),
        in_specs=[
            per_seq(rows, D),
            whole(1, D),
            whole(1, D),
            whole(D, 3 * width),
            whole(1, 3 * width),
            whole(width, D),
            per_seq(3, rows, 128),
            per_seq(rows, 1),
        ],
        out_specs=[per_seq(rows, D), per_seq(rows, 3 * width), per_seq(rows, width), per_seq(rows, D)],
        out_shape=[
            jax.ShapeDtypeStruct((seqs, rows, D), BF16),
            jax.ShapeDtypeStruct((seqs, rows, 3 * width), BF16),
            jax.ShapeDtypeStruct((seqs, rows, width), BF16),
            jax.ShapeDtypeStruct((seqs, rows, D), BF16),
        ],
        compiler_params=params(),
    )(x_all, gain, bias, w_qkv, b_qkv, w_out, tables, start)


def attend_back_kernel(g_ref, wo_ref, w_ref, qkv_ref, tab_ref, start_ref, gqkv_ref, part_ref, gb_ref):
    width = LOCAL * HEAD_DIM
    grad_att = dot(g_ref[0], wo_ref[...], NT).astype(BF16)
    query, key, value = (qkv_ref[0, :, i * width : (i + 1) * width] for i in range(3))
    allowed = visible(start_ref[0])
    zero = jnp.zeros((query.shape[0], width), F32)
    grad_query, grad_key, grad_value = zero, zero, zero
    for h in range(LOCAL):
        query_h, key_h, grad_h = head_of(query, h), head_of(key, h), head_of(grad_att, h)
        probs = soft(query_h, key, allowed)
        low = probs.astype(BF16)
        grad_probs = dot(grad_h, value, NT)
        delta = jnp.sum(low.astype(F32) * grad_probs, axis=-1, keepdims=True)
        grad_scores = (probs * (grad_probs - delta)).astype(BF16)
        grad_value = grad_value + dot(low, grad_h, TN)
        grad_query = grad_query + dot(grad_scores, key_h)
        grad_key = grad_key + dot(grad_scores, query_h, TN)
    cosine, front, back = (jnp.concatenate([tab_ref[0, i]] * (width // 128), axis=1) for i in range(3))
    grad_query = turn(grad_query * 0.125, cosine, front, back, -1.0)
    grad_key = turn(grad_key * 0.125, cosine, front, back, -1.0)
    grad_qkv = jnp.concatenate([grad_query, grad_key, grad_value], axis=1).astype(BF16)
    gqkv_ref[0] = grad_qkv
    gb_ref[0] = jnp.sum(grad_qkv.astype(F32), axis=0, keepdims=True)
    part_ref[0] = dot(grad_qkv, w_ref[...], NT).astype(BF16)


def attend_back(g_all, w_out, w_qkv, qkv, tables, start):
    seqs, rows, _ = g_all.shape
    width = LOCAL * HEAD_DIM
    return pl.pallas_call(
        attend_back_kernel,
        grid=(seqs,),
        in_specs=[
            per_seq(rows, D),
            whole(width, D),
            whole(D, 3 * width),
            per_seq(rows, 3 * width),
            per_seq(3, rows, 128),
            per_seq(rows, 1),
        ],
        out_specs=[per_seq(rows, 3 * width), per_seq(rows, D), per_seq(1, 3 * width)],
        out_shape=[
            jax.ShapeDtypeStruct((seqs, rows, 3 * width), BF16),
            jax.ShapeDtypeStruct((seqs, rows, D), BF16),
            jax.ShapeDtypeStruct((seqs, 1, 3 * width), F32),
        ],
        compiler_params=params(),
    )(g_all, w_out, w_qkv, qkv, tables, start)


def team_shards(
    inputs, positions, norm1_gain, norm1_bias, qkv_weight, qkv_bias, out_weight, norm2_gain, norm2_bias,
    gate_weight, up_weight, down_weight, out_grad,
):
    n = lax.axis_size("fsdp")
    planes = n // TEAM
    rows = inputs.shape[0]
    tokens = TEAM * rows
    depth = qkv_weight.shape[0]
    ff = down_weight.shape[0]
    width = LOCAL * HEAD_DIM
    lines = [[z * TEAM + i for z in range(planes)] for i in range(TEAM)]
    mine = lax.rem(lax.axis_index("fsdp"), TEAM)

    def line_gather(x):
        return lax.all_gather(x, "fsdp", axis=0, tiled=True, axis_index_groups=lines)

    def line_sum(x):
        return lax.psum_scatter(x, "fsdp", scatter_dimension=0, tiled=True, axis_index_groups=lines)

    w_out = line_gather(out_weight)
    vectors = jnp.concatenate([norm1_gain, norm1_bias, norm2_gain, norm2_bias, qkv_bias])
    extra = jnp.zeros((16, 3 * width), BF16)
    extra = extra.at[0, : vectors.shape[0]].set(vectors).at[1, :rows].set(positions.astype(BF16))
    pieces = qkv_weight.reshape(depth, 3, planes, TEAM, HEAD_DIM).transpose(3, 0, 1, 2, 4).reshape(TEAM, depth, 3 * width)
    pieces = jnp.concatenate([pieces, jnp.broadcast_to(extra, (TEAM,) + extra.shape)], axis=1)
    pieces = team_swap(pieces, 0)
    places = pieces[:, depth + 1, :rows].astype(F32)
    gathered = line_gather(pieces).reshape(n, depth + 16, 3 * width)
    w_qkv = gathered[:, :depth].reshape(D, 3 * width)
    vectors = gathered[:, depth, : vectors.shape[0]].astype(F32)
    gain_one, bias_one, gain_two, bias_two = (vectors[:, i * depth : (i + 1) * depth].reshape(1, D) for i in range(4))
    b_qkv = vectors[:, 4 * depth :].reshape(3, planes, TEAM, HEAD_DIM)
    b_qkv = lax.dynamic_index_in_dim(b_qkv, mine, 2, keepdims=False).reshape(1, 3 * width)

    both = jnp.stack([w.reshape(depth, planes, TEAM, ff) for w in (gate_weight, up_weight)], axis=1)
    both = both.transpose(3, 0, 1, 2, 4).reshape(TEAM, depth, 2 * planes * ff)
    both = team_swap(both, 1)
    w_both = line_gather(both.reshape(TEAM * depth, 2 * planes * ff))
    w_down = line_gather(down_weight)
    x_all = team_gather(inputs, 2)
    g_all = team_gather(out_grad, 3)

    half = ROT // 2
    frequency = 10000.0 ** (-jnp.arange(half, dtype=F32) / half)
    angles = places[:, :, None] * frequency
    cosine, sine = jnp.cos(angles), jnp.sin(angles)
    ones, zeros = (jnp.full(angles.shape[:2] + (HEAD_DIM - ROT,), v, F32) for v in (1.0, 0.0))
    none = jnp.zeros_like(sine)
    tables = jnp.stack(
        [
            jnp.concatenate([a, b, c] * (128 // HEAD_DIM), axis=-1)
            for a, b, c in ((cosine, cosine, ones), (-sine, none, zeros), (none, sine, zeros))
        ],
        axis=1,
    )
    start = (jnp.arange(rows, dtype=jnp.int32)[None] - places.astype(jnp.int32))[:, :, None]

    h_one, qkv, attn_low, part = attend(x_all, gain_one, bias_one, w_qkv, b_qkv, w_out, tables, start)
    stream = inputs.astype(F32)
    resid = stream + team_sum(part, 4)
    normed_two, inverse_two = normalize(resid)
    h_two = team_gather((normed_two * gain_two + bias_two).astype(BF16), 5).reshape(tokens, D)
    g_rows = g_all.reshape(tokens, D)
    pre = dot(h_two, w_both)
    gate_pre, up_pre = pre[:, : planes * ff], pre[:, planes * ff :]
    sigmoid = jax.nn.sigmoid(gate_pre)
    silu = gate_pre * sigmoid
    hidden = (silu * up_pre).astype(BF16)
    grad_down = line_sum(dot(hidden, g_rows, TN).astype(BF16))
    grad_hidden = dot(g_rows, w_down, NT)
    grad_gate = (grad_hidden * up_pre * sigmoid * (1.0 + gate_pre * (1.0 - sigmoid))).astype(BF16)
    grad_up = (grad_hidden * silu).astype(BF16)
    grad_both = jnp.concatenate([grad_gate, grad_up], axis=1)
    grad_w_both = line_sum(dot(h_two, grad_both, TN).astype(BF16))
    part = dot(grad_both, w_both, NT).astype(BF16).reshape(TEAM, rows, D)
    grad_htwo = team_sum(part, 6)
    grad_resid = out_grad.astype(F32) + norm_back(grad_htwo * gain_two, normed_two, inverse_two)
    branch = team_gather(grad_resid.astype(BF16), 7)
    grad_qkv, part, grad_bias = attend_back(branch, w_out, w_qkv, qkv, tables, start)
    grad_qkv = grad_qkv.reshape(tokens, 3 * width)
    grad_w_qkv = line_sum(dot(h_one.reshape(tokens, D), grad_qkv, TN).astype(BF16))
    grad_out = line_sum(dot(attn_low.reshape(tokens, width), branch.reshape(tokens, D), TN).astype(BF16))
    grad_hone = team_sum(part, 8)
    normed_one, inverse_one = normalize(stream)
    input_grad = grad_resid + norm_back(grad_hone * gain_one, normed_one, inverse_one)

    hidden, _ = lax.optimization_barrier((hidden, grad_hone))
    part = dot(hidden, w_down).astype(BF16).reshape(TEAM, rows, D)
    block_out = (resid + team_sum(part, 9)).astype(BF16)

    bias = jnp.zeros((3, planes, TEAM, HEAD_DIM), F32)
    bias = lax.dynamic_update_slice(
        bias, jnp.sum(grad_bias, axis=0).reshape(3, planes, 1, HEAD_DIM), (0, 0, mine, 0)
    ).reshape(n, -1)
    sums = [jnp.sum(v, axis=0).reshape(n, depth) for v in (grad_hone * normed_one, grad_hone, grad_htwo * normed_two, grad_htwo)]
    sums = lax.psum_scatter(jnp.concatenate(sums + [bias], axis=1), "fsdp", scatter_dimension=0, tiled=True)[0]
    sums = [sums[i * depth : (i + 1) * depth] for i in range(4)] + [sums[4 * depth :]]

    grad_w_both = team_swap(grad_w_both.reshape(TEAM, depth, 2 * planes * ff), 10)
    grad_w_both = grad_w_both.reshape(TEAM, depth, 2, planes, ff).transpose(2, 1, 3, 0, 4).reshape(2, depth, -1).astype(F32)
    grad_w_qkv = team_swap(grad_w_qkv.reshape(TEAM, depth, 3 * width), 11)
    grad_w_qkv = grad_w_qkv.reshape(TEAM, depth, 3, planes, HEAD_DIM).transpose(1, 2, 3, 0, 4).reshape(depth, -1).astype(F32)
    return (
        block_out,
        input_grad,
        sums[0],
        sums[1],
        grad_w_qkv,
        sums[4],
        grad_out.astype(F32),
        sums[2],
        sums[3],
        grad_w_both[0],
        grad_w_both[1],
        grad_down.astype(F32),
    )


def rotate_pairs(heads, places, sign):
    half_rot = ROT // 2
    frequency = 10000.0 ** (-jnp.arange(half_rot, dtype=jnp.float32) / half_rot)
    angles = places.astype(jnp.float32)[:, None] * frequency[None, :]
    cosine = jnp.cos(angles)[:, None, :]
    sine_part = sign * jnp.sin(angles)[:, None, :]
    front_part = heads[..., :half_rot]
    back_part = heads[..., half_rot:ROT]
    return jnp.concatenate(
        [
            front_part * cosine - back_part * sine_part,
            back_part * cosine + front_part * sine_part,
            heads[..., ROT:],
        ],
        axis=-1,
    )


def by_groups(heads):
    group_heads = min(8, HEADS)
    shaped = heads.reshape(heads.shape[0], HEADS // group_heads, group_heads, HEAD_DIM)
    return jnp.moveaxis(shaped, 1, 0)


def from_groups(grouped):
    return jnp.moveaxis(grouped, 0, 1).reshape(grouped.shape[1], HEADS, HEAD_DIM)


def plain_group(block_items, allowed):
    query_part, key_part, value_part = block_items
    scores = (
        jnp.einsum("qhd,khd->hqk", query_part, key_part, preferred_element_type=jnp.float32) * 0.125
    )
    masked = jnp.where(allowed[None], scores, -1e30)
    row_max = jnp.max(masked, axis=-1, keepdims=True)
    exponent = jnp.exp(masked - row_max)
    row_total = jnp.sum(exponent, axis=-1, keepdims=True)
    soft_probs = (exponent / row_total).astype(jnp.bfloat16)
    mixed_part = jnp.einsum(
        "hqk,khd->qhd", soft_probs, value_part, preferred_element_type=jnp.float32
    )
    return (mixed_part, (row_max + jnp.log(row_total))[..., 0])


def plain_back(block_items, allowed):
    query_part, key_part, value_part, grad_part, row_delta, log_total = block_items
    scores = (
        jnp.einsum("qhd,khd->hqk", query_part, key_part, preferred_element_type=jnp.float32) * 0.125
    )
    soft_probs = jnp.where(allowed[None], jnp.exp(scores - log_total[..., None]), 0.0)
    grad_probs = jnp.einsum(
        "qhd,khd->hqk", grad_part, value_part.astype(jnp.float32), precision=lax.Precision.HIGHEST
    )
    rounded_probs = soft_probs.astype(jnp.bfloat16).astype(jnp.float32)
    grad_value = jnp.einsum("hqk,qhd->khd", rounded_probs, grad_part, precision=lax.Precision.HIGHEST)
    grad_scores = (soft_probs * (grad_probs - row_delta[..., None])).astype(jnp.bfloat16)
    grad_query = 0.125 * jnp.einsum(
        "hqk,khd->qhd", grad_scores, key_part, preferred_element_type=jnp.float32
    )
    grad_key = 0.125 * jnp.einsum(
        "hqk,qhd->khd", grad_scores, query_part, preferred_element_type=jnp.float32
    )
    return (grad_query, grad_key, grad_value)


def shards(
    inputs,
    positions,
    norm1_gain,
    norm1_bias,
    qkv_weight,
    qkv_bias,
    out_weight,
    norm2_gain,
    norm2_bias,
    gate_weight,
    up_weight,
    down_weight,
    out_grad,
):
    tok_rows = inputs.shape[0]
    gain_one, bias_one, w_qkv, b_qkv, w_out = (
        lax.all_gather(norm1_gain, "fsdp", axis=0, tiled=True),
        lax.all_gather(norm1_bias, "fsdp", axis=0, tiled=True),
        lax.all_gather(qkv_weight, "fsdp", axis=0, tiled=True),
        lax.all_gather(qkv_bias, "fsdp", axis=0, tiled=True),
        lax.all_gather(out_weight, "fsdp", axis=0, tiled=True),
    )
    stream = inputs.astype(jnp.float32)
    normed_one, inverse_one = normalize(stream)
    h_one = (normed_one * gain_one.astype(jnp.float32) + bias_one.astype(jnp.float32)).astype(
        jnp.bfloat16
    )
    qkv_pre = jnp.dot(h_one, w_qkv, preferred_element_type=jnp.float32) + b_qkv.astype(jnp.float32)
    qkv_heads = qkv_pre.reshape(tok_rows, 3, HEADS, HEAD_DIM)
    query_low = rotate_pairs(qkv_heads[:, 0], positions, 1.0).astype(jnp.bfloat16)
    key_all = rotate_pairs(qkv_heads[:, 1], positions, 1.0).astype(jnp.bfloat16)
    value_all = qkv_heads[:, 2].astype(jnp.bfloat16)
    token_index = jnp.arange(tok_rows, dtype=jnp.int32)
    allowed = (token_index[None, :] <= token_index[:, None]) & (
        token_index[None, :] >= (token_index - positions)[:, None]
    )
    mixed_grouped, log_grouped = lax.map(
        lambda block_items: plain_group(block_items, allowed),
        (by_groups(query_low), by_groups(key_all), by_groups(value_all)),
    )
    mixed_heads = from_groups(mixed_grouped)
    attn_low = mixed_heads.reshape(tok_rows, D).astype(jnp.bfloat16)
    resid = stream + jnp.dot(attn_low, w_out, preferred_element_type=jnp.float32)
    gain_two, bias_two, w_gate, w_up, w_down = (
        lax.all_gather(norm2_gain, "fsdp", axis=0, tiled=True),
        lax.all_gather(norm2_bias, "fsdp", axis=0, tiled=True),
        lax.all_gather(gate_weight, "fsdp", axis=0, tiled=True),
        lax.all_gather(up_weight, "fsdp", axis=0, tiled=True),
        lax.all_gather(down_weight, "fsdp", axis=0, tiled=True),
    )
    normed_two, inverse_two = normalize(resid)
    h_two = (normed_two * gain_two.astype(jnp.float32) + bias_two.astype(jnp.float32)).astype(
        jnp.bfloat16
    )
    gate_pre = jnp.dot(h_two, w_gate, preferred_element_type=jnp.float32)
    up_pre = jnp.dot(h_two, w_up, preferred_element_type=jnp.float32)
    sigmoid_gate = jax.nn.sigmoid(gate_pre)
    silu_gate = gate_pre * sigmoid_gate
    hidden = (silu_gate * up_pre).astype(jnp.bfloat16)
    block_out = (resid + jnp.dot(hidden, w_down, preferred_element_type=jnp.float32)).astype(
        jnp.bfloat16
    )
    gain_two, w_gate, w_up, w_down = (
        lax.all_gather(norm2_gain, "fsdp", axis=0, tiled=True),
        lax.all_gather(gate_weight, "fsdp", axis=0, tiled=True),
        lax.all_gather(up_weight, "fsdp", axis=0, tiled=True),
        lax.all_gather(down_weight, "fsdp", axis=0, tiled=True),
    )
    grad_down_w = jnp.einsum("tf,td->fd", hidden, out_grad, preferred_element_type=jnp.float32)
    grad_hidden = jnp.einsum("td,fd->tf", out_grad, w_down, preferred_element_type=jnp.float32)
    grad_gate = (
        grad_hidden * up_pre * sigmoid_gate * (1.0 + gate_pre * (1.0 - sigmoid_gate))
    ).astype(jnp.bfloat16)
    grad_up = (grad_hidden * silu_gate).astype(jnp.bfloat16)
    grad_gate_w = jnp.einsum("td,tf->df", h_two, grad_gate, preferred_element_type=jnp.float32)
    grad_up_w = jnp.einsum("td,tf->df", h_two, grad_up, preferred_element_type=jnp.float32)
    grad_htwo = jnp.einsum(
        "tf,df->td", grad_gate, w_gate, preferred_element_type=jnp.float32
    ) + jnp.einsum("tf,df->td", grad_up, w_up, preferred_element_type=jnp.float32)
    grad_gain_two = jnp.sum(grad_htwo * normed_two, axis=0)
    grad_bias_two = jnp.sum(grad_htwo, axis=0)
    grad_resid = out_grad.astype(jnp.float32) + norm_back(
        grad_htwo * gain_two.astype(jnp.float32), normed_two, inverse_two
    )
    mlp_sums = (
        lax.psum_scatter(grad_gain_two, "fsdp", scatter_dimension=0, tiled=True),
        lax.psum_scatter(grad_bias_two, "fsdp", scatter_dimension=0, tiled=True),
        lax.psum_scatter(grad_gate_w, "fsdp", scatter_dimension=0, tiled=True),
        lax.psum_scatter(grad_up_w, "fsdp", scatter_dimension=0, tiled=True),
        lax.psum_scatter(grad_down_w, "fsdp", scatter_dimension=0, tiled=True),
    )
    gain_one, w_qkv, w_out = (
        lax.all_gather(norm1_gain, "fsdp", axis=0, tiled=True),
        lax.all_gather(qkv_weight, "fsdp", axis=0, tiled=True),
        lax.all_gather(out_weight, "fsdp", axis=0, tiled=True),
    )
    grad_branch = grad_resid.astype(jnp.bfloat16)
    grad_out_w = jnp.einsum("ti,td->id", attn_low, grad_branch, preferred_element_type=jnp.float32)
    grad_att = jnp.einsum(
        "td,id->ti", grad_branch, w_out, preferred_element_type=jnp.float32
    ).reshape(tok_rows, HEADS, HEAD_DIM)
    group_heads = min(8, HEADS)
    row_delta = jnp.sum(grad_att * mixed_heads, axis=-1)
    delta_grouped = row_delta.reshape(tok_rows, HEADS // group_heads, group_heads).transpose(
        1, 2, 0
    )
    query_grouped, key_grouped, value_grouped = lax.map(
        lambda block_items: plain_back(block_items, allowed),
        (
            by_groups(query_low),
            by_groups(key_all),
            by_groups(value_all),
            by_groups(grad_att),
            delta_grouped,
            log_grouped,
        ),
    )
    grad_query = from_groups(query_grouped)
    grad_key = from_groups(key_grouped)
    grad_value = from_groups(value_grouped)
    grad_qkv = (
        jnp.stack(
            [
                rotate_pairs(grad_query, positions, -1.0),
                rotate_pairs(grad_key, positions, -1.0),
                grad_value,
            ],
            axis=1,
        )
        .reshape(tok_rows, 3 * D)
        .astype(jnp.bfloat16)
    )
    grad_qkv_w = jnp.einsum("td,tk->dk", h_one, grad_qkv, preferred_element_type=jnp.float32)
    grad_qkv_b = jnp.sum(grad_qkv.astype(jnp.float32), axis=0)
    grad_hone = jnp.einsum("tk,dk->td", grad_qkv, w_qkv, preferred_element_type=jnp.float32)
    grad_gain_one = jnp.sum(grad_hone * normed_one, axis=0)
    grad_bias_one = jnp.sum(grad_hone, axis=0)
    input_grad = grad_resid + norm_back(
        grad_hone * gain_one.astype(jnp.float32), normed_one, inverse_one
    )
    attn_sums = (
        lax.psum_scatter(grad_gain_one, "fsdp", scatter_dimension=0, tiled=True),
        lax.psum_scatter(grad_bias_one, "fsdp", scatter_dimension=0, tiled=True),
        lax.psum_scatter(grad_qkv_w, "fsdp", scatter_dimension=0, tiled=True),
        lax.psum_scatter(grad_qkv_b, "fsdp", scatter_dimension=0, tiled=True),
        lax.psum_scatter(grad_out_w, "fsdp", scatter_dimension=0, tiled=True),
    )
    return (
        block_out,
        input_grad,
        attn_sums[0],
        attn_sums[1],
        attn_sums[2],
        attn_sums[3],
        attn_sums[4],
        mlp_sums[0],
        mlp_sums[1],
        mlp_sums[2],
        mlp_sums[3],
        mlp_sums[4],
    )


def solution(mesh):
    devices = mesh.shape["fsdp"]
    rows, columns = P("fsdp", None), P("fsdp")
    body = team_shards if devices % TEAM == 0 and D == devices * HEAD_DIM else shards
    return jax.shard_map(
        body,
        mesh=mesh,
        in_specs=(rows, columns, columns, columns, rows, columns, rows, columns, columns, rows, rows, rows, rows),
        out_specs=(rows, rows, columns, columns, rows, columns, rows, columns, columns, rows, rows, rows),
        check_vma=False,
    )
```

```python
import functools

import jax
import jax.numpy as jnp
from jax import lax
from jax.experimental import pallas as pl
from jax.experimental.pallas import tpu as pltpu
from jax.sharding import PartitionSpec as P

D = 2048
HEADS = 32
HEAD_DIM = 64
ROT = 16
EPS = 1e-05
TEAM = 8
LOCAL = HEADS // TEAM
MESH = pl.DeviceIdType.MESH
BF16 = jnp.bfloat16
F32 = jnp.float32
ANY = pl.BlockSpec(memory_space=pl.ANY)
VMEM = pl.BlockSpec(memory_space=pltpu.VMEM)


def lasting(us):
    return pl.CostEstimate(flops=0, bytes_accessed=int(us * 3.6e6), transcendentals=0)


def params(cid=None, limit=56):
    extra = {} if cid is None else {"collective_id": cid, "has_side_effects": True}
    return pltpu.CompilerParams(vmem_limit_bytes=limit * 1024 * 1024, **extra)


def place():
    me = lax.axis_index("fsdp")
    mine = lax.rem(me, TEAM)
    return mine, me - mine, mine // 2, lax.rem(mine, 2)


def chip_at(chip, step):
    along_x, along_y = lax.rem(chip, 2), chip // 2
    if step & 1:
        along_x = 1 - along_x
    if step & 2:
        along_y = 1 - along_y
    return along_y * 2 + along_x


def greet(devices):
    barrier = pltpu.get_barrier_semaphore()
    for device in devices:
        pl.semaphore_signal(barrier, inc=1, device_id=(device,), device_id_type=MESH)
    pl.semaphore_wait(barrier, len(devices))


def remote(src, dst, send, recv, device):
    return pltpu.make_async_remote_copy(
        src_ref=src, dst_ref=dst, send_sem=send, recv_sem=recv, device_id=(device,), device_id_type=MESH
    )


class Swap:
    sems = [pltpu.SemaphoreType.DMA, pltpu.SemaphoreType.DMA((TEAM,)), pltpu.SemaphoreType.DMA((TEAM,))]

    def __init__(self, src, out, sems, same=False):
        own_sem, send, recv = sems
        mine, base, _, _ = place()
        others = [lax.rem(mine + k, TEAM) for k in range(1, TEAM)]
        self.near = [base + other for other in others]
        self.copies = [
            remote(src if same else src.at[other], out.at[mine], send.at[k], recv.at[k], base + other)
            for k, other in enumerate(others)
        ]
        self.copies.append(pltpu.make_async_copy(src if same else src.at[mine], out.at[mine], own_sem))

    def start(self):
        for copy in self.copies:
            copy.start()

    def finish(self):
        for copy in self.copies:
            copy.wait()


def slices(ref, pieces, size):
    return jnp.concatenate([ref[:, i * size : (i + 1) * size] for i in pieces], axis=1)


def open_kernel(planes, w_ref, small_ref, pieces_ref, all_ref, made, *sems):
    swap, gather = Swap(made, pieces_ref, sems[:3]), Swap(small_ref, all_ref, sems[3:], same=True)
    for i in range(TEAM):
        made[i] = slices(w_ref, [s * HEADS + z * TEAM + i for s in range(3) for z in range(planes)], HEAD_DIM)
    greet(swap.near)
    swap.start()
    gather.start()
    swap.finish()
    gather.finish()


def opening(weight, small, planes, cid):
    shape = (TEAM, weight.shape[0], weight.shape[1] // TEAM)
    return pl.pallas_call(
        functools.partial(open_kernel, planes),
        out_shape=[jax.ShapeDtypeStruct(shape, BF16), jax.ShapeDtypeStruct((TEAM,) + small.shape, BF16)],
        in_specs=[VMEM, ANY],
        out_specs=[ANY, ANY],
        scratch_shapes=[pltpu.VMEM(shape, BF16)] + Swap.sems * 2,
        cost_estimate=lasting(15),
        compiler_params=params(cid),
    )(weight, small)


def second_kernel(planes, gate_ref, up_ref, x_ref, _, pieces_ref, x_all_ref, made, *sems):
    swap, gather = Swap(made, pieces_ref, sems[:3]), Gather(x_ref, x_all_ref, sems[3:])
    greet(swap.near)
    gather.start()
    size = gate_ref.shape[1] // (planes * TEAM)
    for i in range(TEAM):
        units = [z * TEAM + i for z in range(planes)]
        made[i] = jnp.concatenate([slices(gate_ref, units, size), slices(up_ref, units, size)], axis=1)
    swap.start()
    gather.middle()
    gather.finish()
    swap.finish()


def second(gate, up, inputs, after, planes, cid):
    shape = (TEAM, gate.shape[0], 2 * gate.shape[1] // TEAM)
    return pl.pallas_call(
        functools.partial(second_kernel, planes),
        out_shape=[jax.ShapeDtypeStruct(shape, BF16), jax.ShapeDtypeStruct((TEAM,) + inputs.shape, BF16)],
        in_specs=[VMEM, VMEM, ANY, ANY],
        out_specs=[ANY, ANY],
        scratch_shapes=[pltpu.VMEM(shape, BF16)] + Swap.sems + Gather.sems,
        cost_estimate=lasting(55),
        compiler_params=params(cid),
    )(gate, up, inputs, after)


def close_kernel(parts, planes, x_ref, _, *refs):
    outs, held, sems = refs[:-4], refs[-4], refs[-3:]
    swap = Swap(x_ref, held, sems)
    greet(swap.near)
    swap.start()
    swap.finish()
    size = held.shape[2] // (parts * planes)
    for part in range(parts):
        for z in range(planes):
            at = part * planes + z
            row = jnp.concatenate([held[i, :, at * size : (at + 1) * size] for i in range(TEAM)], axis=1)
            out, first = (outs[part], z) if len(outs) > 1 else (outs[0], at)
            out[:, first * TEAM * size : (first + 1) * TEAM * size] = row.astype(F32)


def closing(blocks, after, parts, outs, planes, cid):
    _, depth, width = blocks.shape
    return pl.pallas_call(
        functools.partial(close_kernel, parts, planes),
        out_shape=[jax.ShapeDtypeStruct((depth, TEAM * width // outs), F32)] * outs,
        in_specs=[ANY, ANY],
        out_specs=[VMEM] * outs,
        scratch_shapes=[pltpu.VMEM(blocks.shape, BF16)] + Swap.sems,
        cost_estimate=lasting(18),
        compiler_params=params(cid),
    )(blocks, after)


def vectors_kernel(planes, x_ref, _, o_ref, held, block, far, *sems):
    own_sem, send, recv = sems[3:]
    mine, base, _, _ = place()
    plane = base // TEAM
    swap = Swap(x_ref, held, sems[:3])
    others = [lax.rem(plane + k, planes) for k in range(1, planes)]
    greet(swap.near + [other * TEAM + mine for other in others])
    swap.start()
    swap.finish()
    total = held[0]
    for i in range(1, TEAM):
        total = total + held[i]
    block[...] = total
    copies = [
        remote(block.at[other], far.at[plane], send.at[k], recv.at[k], other * TEAM + mine)
        for k, other in enumerate(others)
    ]
    copies.append(pltpu.make_async_copy(block.at[plane], far.at[plane], own_sem))
    for copy in copies:
        copy.start()
    for copy in copies:
        copy.wait()
    total = far[0]
    for i in range(1, planes):
        total = total + far[i]
    o_ref[...] = total


def vector_sums(x, after, cid):
    planes = x.shape[1]
    many = pltpu.SemaphoreType.DMA((planes,))
    return pl.pallas_call(
        functools.partial(vectors_kernel, planes),
        out_shape=jax.ShapeDtypeStruct(x.shape[2:], F32),
        in_specs=[VMEM, ANY],
        out_specs=VMEM,
        scratch_shapes=[pltpu.VMEM(x.shape, F32), pltpu.VMEM(x.shape[1:], F32), pltpu.VMEM(x.shape[1:], F32)]
        + Swap.sems
        + [pltpu.SemaphoreType.DMA, many, many],
        cost_estimate=lasting(10),
        compiler_params=params(cid),
    )(x, after)


class Gather:
    sems = [pltpu.SemaphoreType.DMA((5,)), pltpu.SemaphoreType.DMA((5,)), pltpu.SemaphoreType.DMA((2,)),
            pltpu.SemaphoreType.DMA((2,)), pltpu.SemaphoreType.DMA((6,)), pltpu.SemaphoreType.DMA((6,)),
            pltpu.SemaphoreType.DMA]

    def __init__(self, src, out, sems):
        send, recv, hop_send, hop_recv, pass_send, pass_recv, own_sem = sems
        mine, base, chip, core = place()
        side, over, across = (chip_at(chip, k) * 2 + core for k in (1, 2, 3))
        self.sibling = base + chip * 2 + 1 - core
        self.near = [base + side, base + over, self.sibling]
        half = src.shape[0] // 2
        top, low = pl.ds(0, half), pl.ds(half, half)
        self.first = [
            remote(src.at[part], out.at[mine, part], send.at[i], recv.at[i], base + to)
            for i, (part, to) in enumerate(((top, side), (low, over), (low, side), (top, over)))
        ]
        self.first.append(remote(src, out.at[mine], send.at[4], recv.at[4], self.sibling))
        self.own = pltpu.make_async_copy(src, out.at[mine], own_sem)
        self.hops = [
            remote(out.at[at, part], out.at[at, part], hop_send.at[i], hop_recv.at[i], base + to)
            for i, (at, part, to) in enumerate(((side, top, over), (over, low, side)))
        ]
        self.passed = [
            remote(out.at[at, part], out.at[at, part], pass_send.at[i], pass_recv.at[i], self.sibling)
            for i, (at, part) in enumerate(
                ((side, top), (over, low), (side, low), (over, top), (across, top), (across, low))
            )
        ]

    def start(self):
        for copy in self.first:
            copy.start()
        self.own.start()

    def middle(self):
        for i in (0, 1):
            self.first[i].wait_recv()
            self.hops[i].start()
            self.passed[i].start()

    def finish(self):
        for i in (2, 3):
            self.first[i].wait_recv()
            self.passed[i].start()
        for i in (0, 1):
            self.hops[i].wait_recv()
            self.passed[4 + i].start()
        for copy in self.first[:4] + self.hops:
            copy.wait_send()
        self.first[4].wait()
        self.own.wait()
        for copy in self.passed:
            copy.wait()


class Sum:
    def scratch(rows, width):
        return [pltpu.VMEM((4, rows, width), BF16), pltpu.VMEM((4, rows, width), BF16),
                pltpu.VMEM((2, rows // 2, width), BF16), pltpu.VMEM((2, rows, width), BF16)]

    sems = [pltpu.SemaphoreType.DMA((4,))] * 3 + [pltpu.SemaphoreType.DMA((2,))] * 2 + [pltpu.SemaphoreType.DMA((4,))] * 2

    def __init__(self, blocks, scratch, sems, away=None):
        self.own, self.beside, self.via, self.far = scratch
        load_sem, near_send, near_recv, via_send, via_recv, far_send, far_recv = sems
        _, base, chip, core = place()
        chips = [chip_at(chip, k) for k in range(4)]
        sibling = base + chip * 2 + 1 - core
        side, over = (base + chips[k] * 2 + core for k in (1, 2))
        self.near = [side, over, sibling]
        self.half = self.own.shape[1] // 2
        top, low = pl.ds(0, self.half), pl.ds(self.half, self.half)
        self.loads = [
            pltpu.make_async_copy(blocks.at[chips[k] * 2 + core], self.own.at[k], load_sem.at[k])
            for k in range(4)
            if away is None
        ]

        def near_copy(k):
            src = blocks.at[chips[k] * 2 + 1 - core] if away is None else away.at[k]
            return remote(src, self.beside.at[k], near_send.at[k], near_recv.at[k], sibling)

        self.near_copy = near_copy
        self.nears = [near_copy(k) for k in range(4)]
        self.vias = [
            remote(self.own.at[3, part], self.via.at[i], via_send.at[i], via_recv.at[i], to)
            for i, (part, to) in enumerate(((top, side), (low, over)))
        ]
        self.fars = [
            remote(self.own.at[k, part], self.far.at[k - 1, part], far_send.at[i], far_recv.at[i], to)
            for i, (k, part, to) in enumerate(((2, low, over), (1, top, side), (2, top, over), (1, low, side)))
        ]

    def start(self):
        for k in (3, 2, 1, 0):
            self.loads[k].start()
            self.nears[k].start()

    def pair(self, k):
        if self.loads:
            self.loads[k].wait()
        self.nears[k].wait_recv()

        @pl.loop(0, self.own.shape[1] // 16)
        def _(i):
            part = pl.ds(pl.multiple_of(i * 16, 16), 16)
            self.own[k, part, :] = (self.own[k, part, :].astype(F32) + self.beside[k, part, :].astype(F32)).astype(BF16)

    def middle_a(self):
        self.pair(3)
        for copy in self.vias:
            copy.start()

    def middle_b(self):
        self.pair(2)
        self.fars[0].start()

    def middle_c(self):
        self.pair(1)
        self.fars[1].start()

    def middle(self):
        self.middle_a()
        self.middle_b()
        self.middle_c()

    def middle_two(self):
        for i, k in ((0, 2), (1, 1)):
            self.vias[i].wait_recv()

            @pl.loop(0, self.half // 16)
            def _(j, i=i, k=k):
                part = pl.ds(pl.multiple_of(j * 16, 16), 16)
                at = pl.ds(pl.multiple_of(j * 16 + i * self.half, 16), 16)
                self.own[k, at, :] = (self.own[k, at, :].astype(F32) + self.via[i, part, :].astype(F32)).astype(BF16)

            self.fars[2 + i].start()

    def finish(self, use):
        if self.loads:
            self.loads[0].wait()
        self.nears[0].wait_recv()
        for copy in self.fars:
            copy.wait_recv()

        @pl.loop(0, self.own.shape[1] // 16)
        def _(i):
            part = pl.ds(pl.multiple_of(i * 16, 16), 16)
            total = self.own[0, part, :].astype(F32) + self.beside[0, part, :].astype(F32)
            use(part, total + self.far[0, part, :].astype(F32) + self.far[1, part, :].astype(F32))

        for copy in self.nears + self.vias + self.fars:
            copy.wait_send()


def fold(x):
    return x[:8] + x[8:]


def mid_kernel(part_ref, x_ref, gain_ref, bias_ref, resid_ref, o_ref, block, *scratch):
    total = Sum(part_ref, scratch[:4], scratch[4:11])
    gather = Gather(block, o_ref, scratch[11:])
    greet(total.near)
    total.start()
    total.middle()
    total.middle_two()

    def use(rows, value):
        resid = x_ref[rows, :].astype(F32) + value
        resid_ref[rows, :] = resid
        normed, _ = normalize(resid)
        block[rows, :] = (normed * gain_ref[...] + bias_ref[...]).astype(BF16)

    total.finish(use)
    gather.start()
    gather.middle()
    gather.finish()


def mid(part, inputs, gain, bias, cid):
    rows, width = inputs.shape
    return pl.pallas_call(
        mid_kernel,
        out_shape=[jax.ShapeDtypeStruct((rows, width), F32), jax.ShapeDtypeStruct((TEAM, rows, width), BF16)],
        in_specs=[ANY, VMEM, VMEM, VMEM],
        out_specs=[VMEM, ANY],
        scratch_shapes=[pltpu.VMEM((rows, width), BF16)] + Sum.scratch(rows, width) + Sum.sems + Gather.sems,
        cost_estimate=lasting(85),
        compiler_params=params(cid),
    )(part, inputs, gain, bias)


def mid_back_kernel(grads_ref, w_ref, resid_ref, g_ref, gain_ref, _, __, out_ref, sums_ref, o_ref, block, away, *scratch):
    total = Sum(None, scratch[:4], scratch[4:11], away)
    gather = Gather(block, o_ref, scratch[11:])
    greet(total.near)
    _, _, chip, core = place()
    tile = 512

    @pl.loop(0, 8)
    def _(i):
        k = 3 - i // 2
        at = lax.rem(chip // 2 + k // 2, 2) * 2 + lax.rem(chip + k, 2)

        def make(to, at):
            @pl.loop(0, w_ref.shape[0] // tile)
            def _(j):
                columns = pl.ds(pl.multiple_of(j * tile, tile), tile)
                to[k, :, columns] = dot(grads_ref[at], w_ref[columns, :], NT).astype(BF16)

        @pl.when(lax.rem(i, 2) == 0)
        def _():
            make(away, at * 2 + 1 - core)
            total.near_copy(k).start()

        @pl.when(lax.rem(i, 2) == 1)
        def _():
            make(total.own, at * 2 + core)

        for step, advance in ((3, total.middle_a), (5, total.middle_b), (7, total.middle_c)):
            pl.when(i == step)(advance)

    total.middle_two()
    sums_ref[...] = jnp.zeros_like(sums_ref)

    def use(rows, value):
        normed, inverse = normalize(resid_ref[rows, :])
        sums_ref[:8, :] += fold(value * normed)
        sums_ref[8:, :] += fold(value)
        grad = g_ref[rows, :].astype(F32) + norm_back(value * gain_ref[...], normed, inverse)
        out_ref[rows, :] = grad
        block[rows, :] = grad.astype(BF16)

    total.finish(use)
    gather.start()
    gather.middle()
    gather.finish()


def mid_back(grads, w_both, resid, out_grad, gain, after, then, cid):
    rows, width = resid.shape
    return pl.pallas_call(
        mid_back_kernel,
        out_shape=[
            jax.ShapeDtypeStruct((rows, width), F32),
            jax.ShapeDtypeStruct((16, width), F32),
            jax.ShapeDtypeStruct((TEAM, rows, width), BF16),
        ],
        in_specs=[VMEM, VMEM, VMEM, VMEM, VMEM, ANY, ANY],
        out_specs=[VMEM, VMEM, ANY],
        scratch_shapes=[pltpu.VMEM((rows, width), BF16), pltpu.VMEM((4, rows, width), BF16)] + Sum.scratch(rows, width) + Sum.sems + Gather.sems,
        cost_estimate=lasting(87),
        compiler_params=params(cid),
    )(grads, w_both, resid, out_grad, gain, after, then)


def last_kernel(part_ref, x_ref, grad_ref, gain_ref, _, out_ref, sums_ref, *scratch):
    total = Sum(part_ref, scratch[:4], scratch[4:])
    greet(total.near)
    total.start()
    total.middle()
    total.middle_two()
    sums_ref[...] = jnp.zeros_like(sums_ref)

    def use(rows, value):
        normed, inverse = normalize(x_ref[rows, :].astype(F32))
        sums_ref[:8, :] += fold(value * normed)
        sums_ref[8:, :] += fold(value)
        out_ref[rows, :] = grad_ref[rows, :] + norm_back(value * gain_ref[...], normed, inverse)

    total.finish(use)


def last(part, inputs, grad_resid, gain, after, cid):
    rows, width = inputs.shape
    return pl.pallas_call(
        last_kernel,
        out_shape=[jax.ShapeDtypeStruct((rows, width), F32), jax.ShapeDtypeStruct((16, width), F32)],
        in_specs=[ANY, VMEM, VMEM, VMEM, ANY],
        out_specs=[VMEM, VMEM],
        scratch_shapes=Sum.scratch(rows, width) + Sum.sems,
        cost_estimate=lasting(47),
        compiler_params=params(cid),
    )(part, inputs, grad_resid, gain, after)


def dot(a, b, dims=((1,), (0,))):
    return lax.dot_general(a, b, (dims, ((), ())), preferred_element_type=F32)


NT = ((1,), (1,))
TN = ((0,), (0,))


def normalize(stream):
    average = jnp.mean(stream, axis=-1, keepdims=True)
    centered = stream - average
    variance = jnp.mean(centered * centered, axis=-1, keepdims=True)
    inverse = lax.rsqrt(variance + EPS)
    return centered * inverse, inverse


def norm_back(grad_norm, normed, inverse):
    return inverse * (
        grad_norm
        - jnp.mean(grad_norm, axis=-1, keepdims=True)
        - normed * jnp.mean(grad_norm * normed, axis=-1, keepdims=True)
    )


def turn(heads, cosine, sine):
    half, width = ROT // 2, heads.shape[-1]
    lanes = lax.broadcasted_iota(jnp.int32, heads.shape, 1) % HEAD_DIM
    moved = jnp.where(lanes < half, -pltpu.roll(heads, width - half, 1), pltpu.roll(heads, half, 1))
    return heads * cosine + moved * sine


def wide(table):
    return jnp.concatenate([table] * (LOCAL * HEAD_DIM // 128), axis=1)


def visible(start):
    size = start.shape[0]
    rows = lax.broadcasted_iota(jnp.int32, (size, size), 0)
    columns = lax.broadcasted_iota(jnp.int32, (size, size), 1)
    start = jnp.concatenate([start] * (size // start.shape[1]), axis=1)
    return (columns <= rows) & (columns.astype(F32) >= start)


def head_of(x, h):
    lanes = lax.broadcasted_iota(jnp.int32, x.shape, 1)
    return jnp.where((lanes >= h * HEAD_DIM) & (lanes < (h + 1) * HEAD_DIM), x, jnp.zeros_like(x))


def soft(query, key, allowed):
    scores = dot(query, key, NT) * 0.125
    masked = jnp.where(allowed, scores, -1e30)
    exponent = jnp.exp(masked - jnp.max(masked, axis=-1, keepdims=True))
    return exponent / jnp.sum(exponent, axis=-1, keepdims=True)


def attend_kernel(
    x_ref, gain_ref, bias_ref, w_ref, b_ref, wo_ref, tab_ref, g_ref, h_ref, qkv_ref, attn_ref, part_ref, g_all_ref, *sems
):
    gather = Gather(g_ref, g_all_ref, sems)
    step = pl.program_id(0)

    @pl.when(step == 0)
    def _():
        greet(gather.near)
        gather.start()

    pl.when(step == TEAM // 2)(gather.middle)
    stream = x_ref[0].astype(F32)
    normed, _ = normalize(stream)
    h_one = (normed * gain_ref[...] + bias_ref[...]).astype(BF16)
    h_ref[0] = h_one
    qkv = dot(h_one, w_ref[...]) + b_ref[...]
    width = LOCAL * HEAD_DIM
    cosine, sine = wide(tab_ref[0, 0]), wide(tab_ref[0, 1])
    query = turn(qkv[:, :width], cosine, sine).astype(BF16)
    key = turn(qkv[:, width : 2 * width], cosine, sine).astype(BF16)
    value = qkv[:, 2 * width :].astype(BF16)
    qkv_ref[0, :, :width] = query
    qkv_ref[0, :, width : 2 * width] = key
    qkv_ref[0, :, 2 * width :] = value
    allowed = visible(tab_ref[0, 2])
    mixed = jnp.zeros((query.shape[0], width), F32)
    for h in range(LOCAL):
        probs = soft(head_of(query, h), key, allowed).astype(BF16)
        mixed = mixed + dot(probs, head_of(value, h))
    attn_low = mixed.astype(BF16)
    attn_ref[0] = attn_low
    part_ref[0] = dot(attn_low, wo_ref[...]).astype(BF16)
    pl.when(step == TEAM - 1)(gather.finish)


def per_seq(*shape):
    return pl.BlockSpec((1,) + shape, lambda s: (s,) + (0,) * len(shape))


def whole(*shape):
    return pl.BlockSpec(shape, lambda s: (0,) * len(shape))


def attend(x_all, gain, bias, w_qkv, b_qkv, w_out, tables, out_grad, cid):
    seqs, rows, _ = x_all.shape
    width = LOCAL * HEAD_DIM
    return pl.pallas_call(
        attend_kernel,
        grid=(seqs,),
        in_specs=[
            per_seq(rows, D),
            whole(1, D),
            whole(1, D),
            whole(D, 3 * width),
            whole(1, 3 * width),
            whole(width, D),
            per_seq(3, rows, 128),
            ANY,
        ],
        out_specs=[per_seq(rows, D), per_seq(rows, 3 * width), per_seq(rows, width), per_seq(rows, D), ANY],
        out_shape=[
            jax.ShapeDtypeStruct((seqs, rows, D), BF16),
            jax.ShapeDtypeStruct((seqs, rows, 3 * width), BF16),
            jax.ShapeDtypeStruct((seqs, rows, width), BF16),
            jax.ShapeDtypeStruct((seqs, rows, D), BF16),
            jax.ShapeDtypeStruct((seqs, rows, D), BF16),
        ],
        scratch_shapes=Gather.sems,
        cost_estimate=lasting(44),
        compiler_params=params(cid),
    )(x_all, gain, bias, w_qkv, b_qkv, w_out, tables, out_grad)


def attend_back_kernel(
    g_ref, wo_ref, w_ref, qkv_ref, tab_ref, block_ref, resid_ref, _, gqkv_ref, part_ref, gb_ref, out_ref, *scratch
):
    total = Sum(block_ref, scratch[:4], scratch[4:])
    step = pl.program_id(0)

    @pl.when(step == 0)
    def _():
        greet(total.near)
        total.start()

    pl.when(step == 1)(total.middle)
    pl.when(step == TEAM - 3)(total.middle_two)
    width = LOCAL * HEAD_DIM
    grad_att = dot(g_ref[0], wo_ref[...], NT).astype(BF16)
    query, key, value = (qkv_ref[0, :, i * width : (i + 1) * width] for i in range(3))
    allowed = visible(tab_ref[0, 2])
    zero = jnp.zeros((query.shape[0], width), F32)
    grad_query, grad_key, grad_value = zero, zero, zero
    for h in range(LOCAL):
        query_h, key_h, grad_h = head_of(query, h), head_of(key, h), head_of(grad_att, h)
        probs = soft(query_h, key, allowed)
        low = probs.astype(BF16)
        grad_probs = dot(grad_h, value, NT)
        delta = jnp.sum(low.astype(F32) * grad_probs, axis=-1, keepdims=True)
        grad_scores = (probs * (grad_probs - delta)).astype(BF16)
        grad_value = grad_value + dot(low, grad_h, TN)
        grad_query = grad_query + dot(grad_scores, key_h)
        grad_key = grad_key + dot(grad_scores, query_h, TN)
    cosine, sine = wide(tab_ref[0, 0]), -wide(tab_ref[0, 1])
    grad_query = turn(grad_query * 0.125, cosine, sine)
    grad_key = turn(grad_key * 0.125, cosine, sine)
    grad_qkv = jnp.concatenate([grad_query, grad_key, grad_value], axis=1).astype(BF16)
    gqkv_ref[0] = grad_qkv
    gb_ref[0] = jnp.sum(grad_qkv.astype(F32), axis=0, keepdims=True)
    part_ref[0] = dot(grad_qkv, w_ref[...], NT).astype(BF16)

    def use(rows, value):
        out_ref[rows, :] = (resid_ref[rows, :] + value).astype(BF16)

    @pl.when(step == TEAM - 1)
    def _():
        total.finish(use)


def attend_back(g_all, w_out, w_qkv, qkv, tables, blocks, resid, after, cid):
    seqs, rows, _ = g_all.shape
    width = LOCAL * HEAD_DIM
    return pl.pallas_call(
        attend_back_kernel,
        grid=(seqs,),
        in_specs=[
            per_seq(rows, D),
            whole(width, D),
            whole(D, 3 * width),
            per_seq(rows, 3 * width),
            per_seq(3, rows, 128),
            ANY,
            whole(rows, D),
            ANY,
        ],
        out_specs=[per_seq(rows, 3 * width), per_seq(rows, D), per_seq(1, 3 * width), whole(rows, D)],
        out_shape=[
            jax.ShapeDtypeStruct((seqs, rows, 3 * width), BF16),
            jax.ShapeDtypeStruct((seqs, rows, D), BF16),
            jax.ShapeDtypeStruct((seqs, 1, 3 * width), F32),
            jax.ShapeDtypeStruct((rows, D), BF16),
        ],
        scratch_shapes=Sum.scratch(rows, D) + Sum.sems,
        cost_estimate=lasting(47),
        compiler_params=params(cid),
    )(g_all, w_out, w_qkv, qkv, tables, blocks, resid, after)


def team_shards(
    inputs, positions, norm1_gain, norm1_bias, qkv_weight, qkv_bias, out_weight, norm2_gain, norm2_bias,
    gate_weight, up_weight, down_weight, out_grad,
):
    n = lax.axis_size("fsdp")
    planes = n // TEAM
    rows = inputs.shape[0]
    tokens = TEAM * rows
    depth = qkv_weight.shape[0]
    ff = down_weight.shape[0]
    width = LOCAL * HEAD_DIM
    lines = [[z * TEAM + i for z in range(planes)] for i in range(TEAM)]
    mine = lax.rem(lax.axis_index("fsdp"), TEAM)

    def line_gather(x):
        return lax.all_gather(x, "fsdp", axis=0, tiled=True, axis_index_groups=lines)

    def line_sum(x):
        return lax.psum_scatter(x, "fsdp", scatter_dimension=0, tiled=True, axis_index_groups=lines)

    w_out = line_gather(out_weight)
    small = jnp.concatenate([norm1_gain, norm1_bias, norm2_gain, norm2_bias, qkv_bias])
    small = jnp.zeros((16, 2 * rows), BF16).at[0, : small.shape[0]].set(small).at[1, :rows].set(positions.astype(BF16))
    pieces, small = opening(qkv_weight, small, planes, 0)
    places = small[:, 1, :rows].astype(F32)
    vectors = jnp.zeros((16 * 3 * width,), BF16).at[: TEAM * 2 * rows].set(small[:, 0].reshape(-1))
    pieces = jnp.concatenate([pieces.reshape(TEAM * depth, 3 * width), vectors.reshape(16, 3 * width)])
    gathered = line_gather(pieces).reshape(planes, TEAM * depth + 16, 3 * width)
    w_qkv = gathered[:, : TEAM * depth].reshape(D, 3 * width)
    vectors = gathered[:, TEAM * depth :].reshape(planes, -1)[:, : TEAM * 2 * rows].reshape(n, 2 * rows).astype(F32)
    gain_one, bias_one, gain_two, bias_two = (vectors[:, i * depth : (i + 1) * depth].reshape(1, D) for i in range(4))
    b_qkv = vectors[:, 4 * depth : 4 * depth + qkv_bias.shape[0]].reshape(3, planes, TEAM, HEAD_DIM)
    b_qkv = lax.dynamic_index_in_dim(b_qkv, mine, 2, keepdims=False).reshape(1, 3 * width)

    both, x_all = second(gate_weight, up_weight, inputs, w_out, planes, 1)
    w_both = line_gather(both.reshape(TEAM * depth, 2 * planes * ff))
    w_down = line_gather(down_weight)

    half = ROT // 2
    frequency = 10000.0 ** (-jnp.arange(half, dtype=F32) / half)
    frequency = jnp.concatenate([frequency, frequency, jnp.zeros((HEAD_DIM - ROT,), F32)] * (128 // HEAD_DIM))
    angles = places[:, :, None] * frequency
    start = jnp.arange(rows, dtype=F32)[None] - places
    tables = jnp.stack([jnp.cos(angles), jnp.sin(angles), jnp.broadcast_to(start[:, :, None], angles.shape)], axis=1)

    h_one, qkv, attn_low, part, g_all = attend(x_all, gain_one, bias_one, w_qkv, b_qkv, w_out, tables, out_grad, 3)
    resid, h_two = mid(part, inputs, gain_two, bias_two, 4)
    h_two = h_two.reshape(tokens, D)
    g_rows = g_all.reshape(tokens, D)
    pre = dot(h_two, w_both)
    gate_pre, up_pre = pre[:, : planes * ff], pre[:, planes * ff :]
    sigmoid = jax.nn.sigmoid(gate_pre)
    silu = gate_pre * sigmoid
    hidden = (silu * up_pre).astype(BF16)
    grad_down = dot(hidden, g_rows, TN).astype(BF16)
    g_rows, grad_down = lax.optimization_barrier((g_rows, grad_down))
    grad_down = line_sum(grad_down)
    grad_hidden = dot(g_rows, w_down, NT)
    grad_gate = (grad_hidden * up_pre * sigmoid * (1.0 + gate_pre * (1.0 - sigmoid))).astype(BF16)
    grad_up = (grad_hidden * silu).astype(BF16)
    grad_both = jnp.concatenate([grad_gate, grad_up], axis=1)
    grad_w_both = dot(h_two, grad_both, TN).astype(BF16)
    grads = grad_both.reshape(TEAM, rows, 2 * planes * ff)
    grad_resid, sums_two, branch = mid_back(grads, w_both, resid, out_grad, gain_two, grad_w_both, grad_down, 5)
    grad_w_both = line_sum(grad_w_both)
    grad_out = dot(attn_low.reshape(tokens, width), branch.reshape(tokens, D), TN).astype(BF16)
    part = dot(hidden, w_down).astype(BF16).reshape(TEAM, rows, D)
    grad_qkv, part, grad_bias, block_out = attend_back(branch, w_out, w_qkv, qkv, tables, part, resid, grad_out, 6)
    grad_out = line_sum(grad_out).astype(F32)
    grad_qkv = grad_qkv.reshape(tokens, 3 * width)
    grad_qkv, grad_w_both = lax.optimization_barrier((grad_qkv, grad_w_both))
    grad_w_qkv = dot(h_one.reshape(tokens, D), grad_qkv, TN).astype(BF16)
    input_grad, sums_one = last(part, inputs, grad_resid, gain_one, grad_w_qkv, 7)
    grad_w_qkv = line_sum(grad_w_qkv)

    bias = jnp.zeros((3, planes, TEAM, HEAD_DIM), F32)
    bias = lax.dynamic_update_slice(
        bias, jnp.sum(grad_bias, axis=0).reshape(3, planes, 1, HEAD_DIM), (0, 0, mine, 0)
    ).reshape(n, -1)
    sums = [jnp.sum(v[i : i + 8], axis=0).reshape(n, depth) for v in (sums_one, sums_two) for i in (0, 8)]
    sums = jnp.pad(jnp.concatenate(sums + [bias], axis=1), ((0, 0), (0, 1024 - 4 * depth - bias.shape[1])))
    sums = sums.reshape(planes, TEAM, 8, 128).transpose(1, 0, 2, 3)
    sums = vector_sums(sums, input_grad, 8).reshape(-1)
    sums = [sums[i * depth : (i + 1) * depth] for i in range(4)] + [sums[4 * depth : 4 * depth + bias.shape[1]]]

    blocks = grad_w_both.reshape(TEAM, depth, 2 * planes * ff)
    grad_gate_w, grad_up_w = closing(blocks, sums[0], 2, 2, planes, 9)
    blocks = grad_w_qkv.reshape(TEAM, depth, 3 * width)
    (grad_w_qkv,) = closing(blocks, grad_up_w, 3, 1, planes, 10)
    return (
        block_out,
        input_grad,
        sums[0],
        sums[1],
        grad_w_qkv,
        sums[4],
        grad_out,
        sums[2],
        sums[3],
        grad_gate_w,
        grad_up_w,
        grad_down.astype(F32),
    )


def rotate_pairs(heads, places, sign):
    half_rot = ROT // 2
    frequency = 10000.0 ** (-jnp.arange(half_rot, dtype=jnp.float32) / half_rot)
    angles = places.astype(jnp.float32)[:, None] * frequency[None, :]
    cosine = jnp.cos(angles)[:, None, :]
    sine_part = sign * jnp.sin(angles)[:, None, :]
    front_part = heads[..., :half_rot]
    back_part = heads[..., half_rot:ROT]
    return jnp.concatenate(
        [
            front_part * cosine - back_part * sine_part,
            back_part * cosine + front_part * sine_part,
            heads[..., ROT:],
        ],
        axis=-1,
    )


def by_groups(heads):
    group_heads = min(8, HEADS)
    shaped = heads.reshape(heads.shape[0], HEADS // group_heads, group_heads, HEAD_DIM)
    return jnp.moveaxis(shaped, 1, 0)


def from_groups(grouped):
    return jnp.moveaxis(grouped, 0, 1).reshape(grouped.shape[1], HEADS, HEAD_DIM)


def plain_group(block_items, allowed):
    query_part, key_part, value_part = block_items
    scores = (
        jnp.einsum("qhd,khd->hqk", query_part, key_part, preferred_element_type=jnp.float32) * 0.125
    )
    masked = jnp.where(allowed[None], scores, -1e30)
    row_max = jnp.max(masked, axis=-1, keepdims=True)
    exponent = jnp.exp(masked - row_max)
    row_total = jnp.sum(exponent, axis=-1, keepdims=True)
    soft_probs = (exponent / row_total).astype(jnp.bfloat16)
    mixed_part = jnp.einsum(
        "hqk,khd->qhd", soft_probs, value_part, preferred_element_type=jnp.float32
    )
    return (mixed_part, (row_max + jnp.log(row_total))[..., 0])


def plain_back(block_items, allowed):
    query_part, key_part, value_part, grad_part, row_delta, log_total = block_items
    scores = (
        jnp.einsum("qhd,khd->hqk", query_part, key_part, preferred_element_type=jnp.float32) * 0.125
    )
    soft_probs = jnp.where(allowed[None], jnp.exp(scores - log_total[..., None]), 0.0)
    grad_probs = jnp.einsum(
        "qhd,khd->hqk", grad_part, value_part.astype(jnp.float32), precision=lax.Precision.HIGHEST
    )
    rounded_probs = soft_probs.astype(jnp.bfloat16).astype(jnp.float32)
    grad_value = jnp.einsum("hqk,qhd->khd", rounded_probs, grad_part, precision=lax.Precision.HIGHEST)
    grad_scores = (soft_probs * (grad_probs - row_delta[..., None])).astype(jnp.bfloat16)
    grad_query = 0.125 * jnp.einsum(
        "hqk,khd->qhd", grad_scores, key_part, preferred_element_type=jnp.float32
    )
    grad_key = 0.125 * jnp.einsum(
        "hqk,qhd->khd", grad_scores, query_part, preferred_element_type=jnp.float32
    )
    return (grad_query, grad_key, grad_value)


def shards(
    inputs,
    positions,
    norm1_gain,
    norm1_bias,
    qkv_weight,
    qkv_bias,
    out_weight,
    norm2_gain,
    norm2_bias,
    gate_weight,
    up_weight,
    down_weight,
    out_grad,
):
    tok_rows = inputs.shape[0]
    gain_one, bias_one, w_qkv, b_qkv, w_out = (
        lax.all_gather(norm1_gain, "fsdp", axis=0, tiled=True),
        lax.all_gather(norm1_bias, "fsdp", axis=0, tiled=True),
        lax.all_gather(qkv_weight, "fsdp", axis=0, tiled=True),
        lax.all_gather(qkv_bias, "fsdp", axis=0, tiled=True),
        lax.all_gather(out_weight, "fsdp", axis=0, tiled=True),
    )
    stream = inputs.astype(jnp.float32)
    normed_one, inverse_one = normalize(stream)
    h_one = (normed_one * gain_one.astype(jnp.float32) + bias_one.astype(jnp.float32)).astype(
        jnp.bfloat16
    )
    qkv_pre = jnp.dot(h_one, w_qkv, preferred_element_type=jnp.float32) + b_qkv.astype(jnp.float32)
    qkv_heads = qkv_pre.reshape(tok_rows, 3, HEADS, HEAD_DIM)
    query_low = rotate_pairs(qkv_heads[:, 0], positions, 1.0).astype(jnp.bfloat16)
    key_all = rotate_pairs(qkv_heads[:, 1], positions, 1.0).astype(jnp.bfloat16)
    value_all = qkv_heads[:, 2].astype(jnp.bfloat16)
    token_index = jnp.arange(tok_rows, dtype=jnp.int32)
    allowed = (token_index[None, :] <= token_index[:, None]) & (
        token_index[None, :] >= (token_index - positions)[:, None]
    )
    mixed_grouped, log_grouped = lax.map(
        lambda block_items: plain_group(block_items, allowed),
        (by_groups(query_low), by_groups(key_all), by_groups(value_all)),
    )
    mixed_heads = from_groups(mixed_grouped)
    attn_low = mixed_heads.reshape(tok_rows, D).astype(jnp.bfloat16)
    resid = stream + jnp.dot(attn_low, w_out, preferred_element_type=jnp.float32)
    gain_two, bias_two, w_gate, w_up, w_down = (
        lax.all_gather(norm2_gain, "fsdp", axis=0, tiled=True),
        lax.all_gather(norm2_bias, "fsdp", axis=0, tiled=True),
        lax.all_gather(gate_weight, "fsdp", axis=0, tiled=True),
        lax.all_gather(up_weight, "fsdp", axis=0, tiled=True),
        lax.all_gather(down_weight, "fsdp", axis=0, tiled=True),
    )
    normed_two, inverse_two = normalize(resid)
    h_two = (normed_two * gain_two.astype(jnp.float32) + bias_two.astype(jnp.float32)).astype(
        jnp.bfloat16
    )
    gate_pre = jnp.dot(h_two, w_gate, preferred_element_type=jnp.float32)
    up_pre = jnp.dot(h_two, w_up, preferred_element_type=jnp.float32)
    sigmoid_gate = jax.nn.sigmoid(gate_pre)
    silu_gate = gate_pre * sigmoid_gate
    hidden = (silu_gate * up_pre).astype(jnp.bfloat16)
    block_out = (resid + jnp.dot(hidden, w_down, preferred_element_type=jnp.float32)).astype(
        jnp.bfloat16
    )
    gain_two, w_gate, w_up, w_down = (
        lax.all_gather(norm2_gain, "fsdp", axis=0, tiled=True),
        lax.all_gather(gate_weight, "fsdp", axis=0, tiled=True),
        lax.all_gather(up_weight, "fsdp", axis=0, tiled=True),
        lax.all_gather(down_weight, "fsdp", axis=0, tiled=True),
    )
    grad_down_w = jnp.einsum("tf,td->fd", hidden, out_grad, preferred_element_type=jnp.float32)
    grad_hidden = jnp.einsum("td,fd->tf", out_grad, w_down, preferred_element_type=jnp.float32)
    grad_gate = (
        grad_hidden * up_pre * sigmoid_gate * (1.0 + gate_pre * (1.0 - sigmoid_gate))
    ).astype(jnp.bfloat16)
    grad_up = (grad_hidden * silu_gate).astype(jnp.bfloat16)
    grad_gate_w = jnp.einsum("td,tf->df", h_two, grad_gate, preferred_element_type=jnp.float32)
    grad_up_w = jnp.einsum("td,tf->df", h_two, grad_up, preferred_element_type=jnp.float32)
    grad_htwo = jnp.einsum(
        "tf,df->td", grad_gate, w_gate, preferred_element_type=jnp.float32
    ) + jnp.einsum("tf,df->td", grad_up, w_up, preferred_element_type=jnp.float32)
    grad_gain_two = jnp.sum(grad_htwo * normed_two, axis=0)
    grad_bias_two = jnp.sum(grad_htwo, axis=0)
    grad_resid = out_grad.astype(jnp.float32) + norm_back(
        grad_htwo * gain_two.astype(jnp.float32), normed_two, inverse_two
    )
    mlp_sums = (
        lax.psum_scatter(grad_gain_two, "fsdp", scatter_dimension=0, tiled=True),
        lax.psum_scatter(grad_bias_two, "fsdp", scatter_dimension=0, tiled=True),
        lax.psum_scatter(grad_gate_w, "fsdp", scatter_dimension=0, tiled=True),
        lax.psum_scatter(grad_up_w, "fsdp", scatter_dimension=0, tiled=True),
        lax.psum_scatter(grad_down_w, "fsdp", scatter_dimension=0, tiled=True),
    )
    gain_one, w_qkv, w_out = (
        lax.all_gather(norm1_gain, "fsdp", axis=0, tiled=True),
        lax.all_gather(qkv_weight, "fsdp", axis=0, tiled=True),
        lax.all_gather(out_weight, "fsdp", axis=0, tiled=True),
    )
    grad_branch = grad_resid.astype(jnp.bfloat16)
    grad_out_w = jnp.einsum("ti,td->id", attn_low, grad_branch, preferred_element_type=jnp.float32)
    grad_att = jnp.einsum(
        "td,id->ti", grad_branch, w_out, preferred_element_type=jnp.float32
    ).reshape(tok_rows, HEADS, HEAD_DIM)
    group_heads = min(8, HEADS)
    row_delta = jnp.sum(grad_att * mixed_heads, axis=-1)
    delta_grouped = row_delta.reshape(tok_rows, HEADS // group_heads, group_heads).transpose(
        1, 2, 0
    )
    query_grouped, key_grouped, value_grouped = lax.map(
        lambda block_items: plain_back(block_items, allowed),
        (
            by_groups(query_low),
            by_groups(key_all),
            by_groups(value_all),
            by_groups(grad_att),
            delta_grouped,
            log_grouped,
        ),
    )
    grad_query = from_groups(query_grouped)
    grad_key = from_groups(key_grouped)
    grad_value = from_groups(value_grouped)
    grad_qkv = (
        jnp.stack(
            [
                rotate_pairs(grad_query, positions, -1.0),
                rotate_pairs(grad_key, positions, -1.0),
                grad_value,
            ],
            axis=1,
        )
        .reshape(tok_rows, 3 * D)
        .astype(jnp.bfloat16)
    )
    grad_qkv_w = jnp.einsum("td,tk->dk", h_one, grad_qkv, preferred_element_type=jnp.float32)
    grad_qkv_b = jnp.sum(grad_qkv.astype(jnp.float32), axis=0)
    grad_hone = jnp.einsum("tk,dk->td", grad_qkv, w_qkv, preferred_element_type=jnp.float32)
    grad_gain_one = jnp.sum(grad_hone * normed_one, axis=0)
    grad_bias_one = jnp.sum(grad_hone, axis=0)
    input_grad = grad_resid + norm_back(
        grad_hone * gain_one.astype(jnp.float32), normed_one, inverse_one
    )
    attn_sums = (
        lax.psum_scatter(grad_gain_one, "fsdp", scatter_dimension=0, tiled=True),
        lax.psum_scatter(grad_bias_one, "fsdp", scatter_dimension=0, tiled=True),
        lax.psum_scatter(grad_qkv_w, "fsdp", scatter_dimension=0, tiled=True),
        lax.psum_scatter(grad_qkv_b, "fsdp", scatter_dimension=0, tiled=True),
        lax.psum_scatter(grad_out_w, "fsdp", scatter_dimension=0, tiled=True),
    )
    return (
        block_out,
        input_grad,
        attn_sums[0],
        attn_sums[1],
        attn_sums[2],
        attn_sums[3],
        attn_sums[4],
        mlp_sums[0],
        mlp_sums[1],
        mlp_sums[2],
        mlp_sums[3],
        mlp_sums[4],
    )


def solution(mesh):
    devices = mesh.shape["fsdp"]
    rows, columns = P("fsdp", None), P("fsdp")
    body = team_shards if devices % TEAM == 0 and D == devices * HEAD_DIM else shards
    return jax.shard_map(
        body,
        mesh=mesh,
        in_specs=(rows, columns, columns, columns, rows, columns, rows, columns, columns, rows, rows, rows, rows),
        out_specs=(rows, rows, columns, columns, rows, columns, rows, columns, columns, rows, rows, rows),
        check_vma=False,
    )
```

```python
import functools

import jax
import jax.numpy as jnp
from jax import lax
from jax.experimental import pallas as pl
from jax.experimental.pallas import tpu as pltpu
from jax.sharding import PartitionSpec as P

D = 2048
HEADS = 32
HEAD_DIM = 64
ROT = 16
EPS = 1e-05
TEAM = 8
LOCAL = HEADS // TEAM
MESH = pl.DeviceIdType.MESH
BF16 = jnp.bfloat16
F32 = jnp.float32
ANY = pl.BlockSpec(memory_space=pl.ANY)
VMEM = pl.BlockSpec(memory_space=pltpu.VMEM)


def lasting(us):
    return pl.CostEstimate(flops=0, bytes_accessed=int(us * 3.6e6), transcendentals=0)


def params(cid=None, limit=56):
    extra = {} if cid is None else {"collective_id": cid, "has_side_effects": True}
    return pltpu.CompilerParams(vmem_limit_bytes=limit * 1024 * 1024, **extra)


def place():
    me = lax.axis_index("fsdp")
    mine = lax.rem(me, TEAM)
    return mine, me - mine, mine // 2, lax.rem(mine, 2)


def chip_at(chip, step):
    along_x, along_y = lax.rem(chip, 2), chip // 2
    if step & 1:
        along_x = 1 - along_x
    if step & 2:
        along_y = 1 - along_y
    return along_y * 2 + along_x


def relation(chip, core, r):
    return chip_at(chip, r // 2) * 2 + lax.rem(core + r, 2)


def greet(devices):
    barrier = pltpu.get_barrier_semaphore()
    for device in devices:
        pl.semaphore_signal(barrier, inc=1, device_id=(device,), device_id_type=MESH)
    pl.semaphore_wait(barrier, len(devices))


def remote(src, dst, send, recv, device):
    return pltpu.make_async_remote_copy(
        src_ref=src, dst_ref=dst, send_sem=send, recv_sem=recv, device_id=(device,), device_id_type=MESH
    )


class Swap:
    sems = [pltpu.SemaphoreType.DMA, pltpu.SemaphoreType.DMA((TEAM,)), pltpu.SemaphoreType.DMA((TEAM,))]

    def __init__(self, src, out, sems, same=False, near_first=False):
        own_sem, send, recv = sems
        mine, base, chip, core = place()
        others = [relation(chip, core, r) for r in range(1, TEAM)]
        self.near = [base + other for other in others]
        self.copies = [
            remote(
                src if same else src.at[other], out.at[r if near_first else mine], send.at[r], recv.at[r], base + other
            )
            for r, other in enumerate(others, 1)
        ]
        own = src if same else src.at[mine]
        self.copies.append(pltpu.make_async_copy(own, out.at[0 if near_first else mine], own_sem))

    def start(self):
        for copy in self.copies:
            copy.start()

    def finish(self):
        for copy in self.copies:
            copy.wait()


class Line:
    def sems(planes):
        return [pltpu.SemaphoreType.DMA, pltpu.SemaphoreType.DMA((planes,)), pltpu.SemaphoreType.DMA((planes,))]

    def __init__(self, planes, src, out, sems, same=False, within=False):
        own_sem, send, recv = sems
        mine, base, _, _ = place()
        plane = base // TEAM
        others = [lax.rem(plane + k, planes) for k in range(1, planes)]
        self.near = [other * TEAM + mine for other in others]
        self.copies = [
            remote(src if same else src.at[other], out.at[plane], send.at[k], recv.at[k], other * TEAM + mine)
            for k, other in enumerate(others)
        ]
        own = src if same else src.at[plane]
        self.own = None if within else pltpu.make_async_copy(own, out.at[plane], own_sem)

    def start(self):
        for copy in self.copies:
            copy.start()
        if self.own is not None:
            self.own.start()

    def finish(self):
        for copy in self.copies:
            copy.wait()
        if self.own is not None:
            self.own.wait()


def slices(ref, pieces, size):
    return jnp.concatenate([ref[:, i * size : (i + 1) * size] for i in pieces], axis=1)


def open_kernel(planes, w_ref, out_weight_ref, pieces_ref, w_out_ref, made, *sems):
    swap, line = Swap(made, pieces_ref, sems[:3]), Line(planes, out_weight_ref, w_out_ref, sems[3:], same=True)
    greet(swap.near + line.near)
    line.start()
    for i in range(TEAM):
        made[i] = slices(w_ref, [s * HEADS + z * TEAM + i for s in range(3) for z in range(planes)], HEAD_DIM)
    swap.start()
    swap.finish()
    line.finish()


def opening(weight, out_weight, planes, cid):
    shape = (TEAM, weight.shape[0], weight.shape[1] // TEAM)
    return pl.pallas_call(
        functools.partial(open_kernel, planes),
        out_shape=[
            jax.ShapeDtypeStruct(shape, BF16),
            jax.ShapeDtypeStruct((planes,) + out_weight.shape, BF16),
        ],
        in_specs=[VMEM, ANY],
        out_specs=[ANY, ANY],
        scratch_shapes=[pltpu.VMEM(shape, BF16)] + Swap.sems + Line.sems(planes),
        cost_estimate=lasting(22),
        compiler_params=params(cid),
    )(weight, out_weight)


def second_kernel(
    planes, gate_ref, up_ref, x_ref, small_ref, place_ref, _, pieces_ref, x_all_ref, all_ref, places_ref, made, *sems
):
    plane = place()[1] // TEAM
    swap, gather = Swap(made, pieces_ref, sems[:3]), Gather(x_ref, x_all_ref, sems[3:10])
    vectors = Swap(small_ref, all_ref.at[plane], sems[10:13], same=True)
    places = Swap(place_ref, places_ref, sems[13:16], same=True, near_first=True)
    line = Line(planes, all_ref.at[plane], all_ref, sems[16:], same=True, within=True)
    greet(swap.near + line.near)
    vectors.start()
    places.start()
    gather.start()
    size = gate_ref.shape[1] // (planes * TEAM)
    for i in range(TEAM):
        units = [z * TEAM + i for z in range(planes)]
        made[i] = jnp.concatenate([slices(gate_ref, units, size), slices(up_ref, units, size)], axis=1)
    swap.start()
    vectors.finish()
    line.start()
    gather.middle()
    gather.finish()
    swap.finish()
    places.finish()
    line.finish()


def second(gate, up, inputs, small, positions, after, planes, cid):
    shape = (TEAM, gate.shape[0], 2 * gate.shape[1] // TEAM)
    return pl.pallas_call(
        functools.partial(second_kernel, planes),
        out_shape=[
            jax.ShapeDtypeStruct(shape, BF16),
            jax.ShapeDtypeStruct((TEAM,) + inputs.shape, BF16),
            jax.ShapeDtypeStruct((planes, TEAM) + small.shape, BF16),
            jax.ShapeDtypeStruct((TEAM,) + positions.shape, BF16),
        ],
        in_specs=[VMEM, VMEM] + [ANY] * 4,
        out_specs=[ANY] * 4,
        scratch_shapes=[pltpu.VMEM(shape, BF16)]
        + Swap.sems
        + Gather.sems
        + Swap.sems * 2
        + Line.sems(planes),
        cost_estimate=lasting(60),
        compiler_params=params(cid),
    )(gate, up, inputs, small, positions, after)


def unslice(held, parts, planes, outs):
    size = held.shape[2] // (parts * planes)
    for at in range(parts * planes):
        row = jnp.concatenate([held[i, :, at * size : (at + 1) * size] for i in range(TEAM)], axis=1)
        out, first = (outs[at // planes], at % planes) if len(outs) > 1 else (outs[0], at)
        out[:, first * TEAM * size : (first + 1) * TEAM * size] = row.astype(F32)


def added(ref):
    total = ref[0].astype(F32)
    for i in range(1, ref.shape[0]):
        total = total + ref[i].astype(F32)
    return total


def vectors_kernel(planes, x_ref, o_ref, held, block, far, *sems):
    swap, line = Swap(x_ref, held, sems[:3]), Line(planes, block, far, sems[3:])
    greet(swap.near + line.near)
    swap.start()
    swap.finish()
    block[...] = added(held)
    line.start()
    line.finish()
    o_ref[...] = added(far)


def vector_sums(x, cid):
    planes = x.shape[1]
    return pl.pallas_call(
        functools.partial(vectors_kernel, planes),
        out_shape=jax.ShapeDtypeStruct(x.shape[2:], F32),
        in_specs=[VMEM],
        out_specs=VMEM,
        scratch_shapes=[pltpu.VMEM(x.shape, F32), pltpu.VMEM(x.shape[1:], F32), pltpu.VMEM(x.shape[1:], F32)]
        + Swap.sems
        + Line.sems(planes),
        cost_estimate=lasting(10),
        compiler_params=params(cid),
    )(x)


def close_kernel(planes, w_ref, _, out_ref, pieces, *sems):
    swap = Swap(w_ref, pieces, sems)
    greet(swap.near)
    swap.start()
    swap.finish()
    unslice(pieces, 3, planes, [out_ref])


def closing(blocks, after, planes, cid):
    _, depth, width = blocks.shape
    return pl.pallas_call(
        functools.partial(close_kernel, planes),
        out_shape=jax.ShapeDtypeStruct((depth, TEAM * width), F32),
        in_specs=[ANY, ANY],
        out_specs=VMEM,
        scratch_shapes=[pltpu.VMEM(blocks.shape, BF16)] + Swap.sems,
        cost_estimate=lasting(14),
        compiler_params=params(cid),
    )(blocks, after)


class Gather:
    sems = [pltpu.SemaphoreType.DMA((5,)), pltpu.SemaphoreType.DMA((5,)), pltpu.SemaphoreType.DMA((2,)),
            pltpu.SemaphoreType.DMA((2,)), pltpu.SemaphoreType.DMA((6,)), pltpu.SemaphoreType.DMA((6,)),
            pltpu.SemaphoreType.DMA]

    def __init__(self, src, out, sems):
        send, recv, hop_send, hop_recv, pass_send, pass_recv, own_sem = sems
        _, base, chip, core = place()
        side, over = (chip_at(chip, k) * 2 + core for k in (1, 2))
        self.sibling = base + chip * 2 + 1 - core
        self.near = [base + side, base + over, self.sibling]
        half = src.shape[0] // 2
        top, low = pl.ds(0, half), pl.ds(half, half)
        self.first = [
            remote(src.at[part], out.at[at, part], send.at[i], recv.at[i], base + to)
            for i, (part, at, to) in enumerate(((top, 2, side), (low, 4, over), (low, 2, side), (top, 4, over)))
        ]
        self.first.append(remote(src, out.at[1], send.at[4], recv.at[4], self.sibling))
        self.own = pltpu.make_async_copy(src, out.at[0], own_sem)
        self.hops = [
            remote(out.at[at, part], out.at[6, part], hop_send.at[i], hop_recv.at[i], base + to)
            for i, (at, part, to) in enumerate(((2, top, over), (4, low, side)))
        ]
        self.passed = [
            remote(out.at[at, part], out.at[at + 1, part], pass_send.at[i], pass_recv.at[i], self.sibling)
            for i, (at, part) in enumerate(((2, top), (4, low), (2, low), (4, top), (6, top), (6, low)))
        ]

    def start(self):
        for copy in self.first:
            copy.start()
        self.own.start()

    def middle(self):
        for i in (0, 1):
            self.first[i].wait_recv()
            self.hops[i].start()
            self.passed[i].start()

    def finish(self):
        for i in range(2, TEAM):
            self.ready(i)
        self.first[4].wait_recv()
        self.own.wait()
        self.sent()

    def ready(self, i):
        if i == 0:
            self.own.wait()
        elif i == 1:
            self.first[4].wait_recv()
        elif i == 6:
            for j in (0, 1):
                self.hops[j].wait_recv()
                self.passed[4 + j].start()
        elif i % 2 == 0:
            self.first[1 + i // 2].wait_recv()
            self.passed[1 + i // 2].start()
        else:
            for j in {3: (0, 2), 5: (1, 3), 7: (4, 5)}[i]:
                self.passed[j].wait_recv()

    def sent(self):
        for copy in self.first + self.hops + self.passed:
            copy.wait_send()


class Sum:
    def scratch(rows, width):
        return [pltpu.VMEM((4, rows, width), BF16), pltpu.VMEM((4, rows, width), BF16),
                pltpu.VMEM((2, rows // 2, width), BF16), pltpu.VMEM((2, rows, width), BF16)]

    sems = [pltpu.SemaphoreType.DMA((4,))] * 3 + [pltpu.SemaphoreType.DMA((2,))] * 2 + [pltpu.SemaphoreType.DMA((4,))] * 2

    def __init__(self, blocks, scratch, sems, away=None):
        self.own, self.beside, self.via, self.far = scratch
        load_sem, near_send, near_recv, via_send, via_recv, far_send, far_recv = sems
        _, base, chip, core = place()
        sibling = base + chip * 2 + 1 - core
        side, over = (base + chip_at(chip, k) * 2 + core for k in (1, 2))
        self.near = [side, over, sibling]
        self.half = self.own.shape[1] // 2
        top, low = pl.ds(0, self.half), pl.ds(self.half, self.half)
        self.loads = [
            pltpu.make_async_copy(blocks.at[2 * k], self.own.at[k], load_sem.at[k])
            for k in range(4)
            if away is None
        ]

        def near_copy(k):
            src = blocks.at[2 * k + 1] if away is None else away.at[k]
            return remote(src, self.beside.at[k], near_send.at[k], near_recv.at[k], sibling)

        self.near_copy = near_copy
        self.nears = [near_copy(k) for k in range(4)]
        self.vias = [
            remote(self.own.at[3, part], self.via.at[i], via_send.at[i], via_recv.at[i], to)
            for i, (part, to) in enumerate(((top, side), (low, over)))
        ]
        self.fars = [
            remote(self.own.at[k, part], self.far.at[k - 1, part], far_send.at[i], far_recv.at[i], to)
            for i, (k, part, to) in enumerate(((2, low, over), (1, top, side), (2, top, over), (1, low, side)))
        ]

    def start(self):
        for k in (3, 2, 1, 0):
            self.loads[k].start()
            self.nears[k].start()

    def pair(self, k):
        if self.loads:
            self.loads[k].wait()
        self.nears[k].wait_recv()

        @pl.loop(0, self.own.shape[1] // 16)
        def _(i):
            part = pl.ds(pl.multiple_of(i * 16, 16), 16)
            self.own[k, part, :] = (self.own[k, part, :].astype(F32) + self.beside[k, part, :].astype(F32)).astype(BF16)

    def middle_a(self):
        self.pair(3)
        for copy in self.vias:
            copy.start()

    def middle_b(self):
        self.pair(2)
        self.fars[0].start()

    def middle_c(self):
        self.pair(1)
        self.fars[1].start()

    def middle(self):
        self.middle_a()
        self.middle_b()
        self.middle_c()

    def middle_two(self):
        for i, k in ((0, 2), (1, 1)):
            self.vias[i].wait_recv()

            @pl.loop(0, self.half // 16)
            def _(j, i=i, k=k):
                part = pl.ds(pl.multiple_of(j * 16, 16), 16)
                at = pl.ds(pl.multiple_of(j * 16 + i * self.half, 16), 16)
                self.own[k, at, :] = (self.own[k, at, :].astype(F32) + self.via[i, part, :].astype(F32)).astype(BF16)

            self.fars[2 + i].start()

    def finish(self, use):
        if self.loads:
            self.loads[0].wait()
        self.nears[0].wait_recv()
        for copy in self.fars:
            copy.wait_recv()

        @pl.loop(0, self.own.shape[1] // 16)
        def _(i):
            part = pl.ds(pl.multiple_of(i * 16, 16), 16)
            total = self.own[0, part, :].astype(F32) + self.beside[0, part, :].astype(F32)
            use(part, total + self.far[0, part, :].astype(F32) + self.far[1, part, :].astype(F32))

        for copy in self.nears + self.vias + self.fars:
            copy.wait_send()


def fold(x):
    return x[:8] + x[8:]


def mid_kernel(part_ref, x_ref, gain_ref, bias_ref, resid_ref, o_ref, block, *scratch):
    total = Sum(part_ref, scratch[:4], scratch[4:11])
    gather = Gather(block, o_ref, scratch[11:])
    greet(total.near)
    total.start()
    total.middle()
    total.middle_two()

    def use(rows, value):
        resid = x_ref[rows, :].astype(F32) + value
        resid_ref[rows, :] = resid
        normed, _ = normalize(resid)
        block[rows, :] = (normed * gain_ref[...] + bias_ref[...]).astype(BF16)

    total.finish(use)
    gather.start()
    gather.middle()
    gather.finish()


def mid(part, inputs, gain, bias, cid):
    rows, width = inputs.shape
    return pl.pallas_call(
        mid_kernel,
        out_shape=[jax.ShapeDtypeStruct((rows, width), F32), jax.ShapeDtypeStruct((TEAM, rows, width), BF16)],
        in_specs=[ANY, VMEM, VMEM, VMEM],
        out_specs=[VMEM, ANY],
        scratch_shapes=[pltpu.VMEM((rows, width), BF16)] + Sum.scratch(rows, width) + Sum.sems + Gather.sems,
        cost_estimate=lasting(85),
        compiler_params=params(cid),
    )(part, inputs, gain, bias)


def expand_kernel(h_ref, w_ref, pre_ref, hidden_ref):
    pre = dot(h_ref[0], w_ref[...])
    pre_ref[0] = pre
    ff = hidden_ref.shape[2]
    gate_pre, up_pre = pre[:, :ff], pre[:, ff:]
    hidden_ref[0] = (gate_pre * jax.nn.sigmoid(gate_pre) * up_pre).astype(BF16)


def expand(h_two, w_both):
    seqs, rows, _ = h_two.shape
    width = w_both.shape[1]
    return pl.pallas_call(
        expand_kernel,
        grid=(seqs,),
        in_specs=[per_seq(rows, D), whole(D, width)],
        out_specs=[per_seq(rows, width), per_seq(rows, width // 2)],
        out_shape=[
            jax.ShapeDtypeStruct((seqs, rows, width), F32),
            jax.ShapeDtypeStruct((seqs, rows, width // 2), BF16),
        ],
        cost_estimate=lasting(18),
        compiler_params=params(),
    )(h_two, w_both)


def mlp_back_kernel(
    pre_ref, g_all_ref, h_ref, wd_ref, w_ref, resid_ref, g_ref, gain_ref, _,
    out_ref, sums_ref, block_ref, grad_w_ref,
    pre, g_all, turned, made, grads, away, w, resid, own_grad, *scratch,
):
    pre_sem, g_sem, turned_sem, made_sem, late_sem = scratch[11:]
    total = Sum(None, scratch[:4], scratch[4:11], away)
    rows, ff = pre_ref.shape[1], wd_ref.shape[0]
    chunk = turned.shape[2]

    def loads(i):
        slot, at = lax.rem(i, 2), TEAM - 1 - i
        return (
            pltpu.make_async_copy(pre_ref.at[at], pre.at[slot], pre_sem.at[slot]),
            pltpu.make_async_copy(g_all_ref.at[at], g_all.at[slot], g_sem.at[slot]),
        )

    def load_chunk(i):
        slot = lax.rem(i, 2)
        columns = pl.ds(pl.multiple_of(i * chunk, chunk), chunk)
        return pltpu.make_async_copy(h_ref.at[:, columns], turned.at[slot], turned_sem.at[slot])

    def store_chunk(i):
        slot = lax.rem(i, 2)
        part = pl.ds(pl.multiple_of(i * chunk, chunk), chunk)
        return pltpu.make_async_copy(made.at[slot], grad_w_ref.at[part, :], made_sem.at[slot])

    for copy in loads(0):
        copy.start()
    late = [
        pltpu.make_async_copy(src, dst, late_sem.at[i])
        for i, (src, dst) in enumerate(((w_ref, w), (resid_ref, resid), (g_ref, own_grad)))
    ]
    for copy in late:
        copy.start()
    greet(total.near)

    @pl.loop(0, TEAM)
    def _(i):
        slot = lax.rem(i, 2)
        k, at = 3 - i // 2, TEAM - 1 - i

        @pl.when(i < TEAM - 1)
        def _():
            for copy in loads(i + 1):
                copy.start()

        for copy in loads(i):
            copy.wait()
        grad_hidden = dot(g_all[slot], wd_ref[...], NT)
        gate_pre, up_pre = pre[slot, :, :ff], pre[slot, :, ff:]
        sigmoid = jax.nn.sigmoid(gate_pre)
        grad_gate = grad_hidden * up_pre * sigmoid * (1.0 + gate_pre * (1.0 - sigmoid))
        grad_up = grad_hidden * (gate_pre * sigmoid)
        part = pl.ds(pl.multiple_of(at * rows, rows), rows)
        grads[part, :] = jnp.concatenate([grad_gate, grad_up], axis=1).astype(BF16)

        def make(to):
            to[k] = dot(grads[part, :], w[...], NT).astype(BF16)

        pl.when(i == 0)(late[0].wait)

        @pl.when(lax.rem(i, 2) == 0)
        def _():
            make(away)
            total.near_copy(k).start()

        @pl.when(lax.rem(i, 2) == 1)
        def _():
            make(total.own)

        for step, advance in ((1, total.middle_a), (3, total.middle_b), (5, total.middle_c)):
            pl.when(i == step)(advance)

    load_chunk(0).start()
    total.middle_two()
    chunks = h_ref.shape[1] // chunk

    @pl.loop(0, chunks)
    def _(i):
        slot = lax.rem(i, 2)

        @pl.when(i < chunks - 1)
        def _():
            load_chunk(i + 1).start()

        load_chunk(i).wait()

        @pl.when(i >= 2)
        def _():
            store_chunk(i - 2).wait()

        made[slot] = dot(turned[slot], grads[...], TN).astype(BF16)
        store_chunk(i).start()

    sums_ref[...] = jnp.zeros_like(sums_ref)
    for copy in late[1:]:
        copy.wait()

    def use(rows, value):
        normed, inverse = normalize(resid[rows, :])
        sums_ref[:8, :] += fold(value * normed)
        sums_ref[8:, :] += fold(value)
        grad = own_grad[rows, :].astype(F32) + norm_back(value * gain_ref[...], normed, inverse)
        out_ref[rows, :] = grad
        block_ref[rows, :] = grad.astype(BF16)

    total.finish(use)
    store_chunk(chunks - 2).wait()
    store_chunk(chunks - 1).wait()


def mlp_back(pre, g_all, h_two, w_down, w_both, resid, out_grad, gain, after, cid):
    seqs, rows, both = pre.shape
    width = resid.shape[1]
    chunk = 256
    two = pltpu.SemaphoreType.DMA((2,))
    return pl.pallas_call(
        mlp_back_kernel,
        out_shape=[
            jax.ShapeDtypeStruct((rows, width), F32),
            jax.ShapeDtypeStruct((16, width), F32),
            jax.ShapeDtypeStruct((rows, width), BF16),
            jax.ShapeDtypeStruct((width, both), BF16),
        ],
        in_specs=[ANY, ANY, ANY, VMEM, ANY, ANY, ANY, VMEM, ANY],
        out_specs=[VMEM, VMEM, VMEM, ANY],
        scratch_shapes=[
            pltpu.VMEM((2, rows, both), F32),
            pltpu.VMEM((2, rows, width), BF16),
            pltpu.VMEM((2, seqs * rows, chunk), BF16),
            pltpu.VMEM((2, chunk, both), BF16),
            pltpu.VMEM((seqs * rows, both), BF16),
            pltpu.VMEM((4, rows, width), BF16),
            pltpu.VMEM((width, both), BF16),
            pltpu.VMEM((rows, width), F32),
            pltpu.VMEM((rows, width), BF16),
        ]
        + Sum.scratch(rows, width)
        + Sum.sems
        + [two] * 4
        + [pltpu.SemaphoreType.DMA((3,))],
        cost_estimate=lasting(60),
        compiler_params=params(cid),
    )(pre, g_all, h_two, w_down, w_both, resid, out_grad, gain, after)


def last_kernel(
    planes, part_ref, x_ref, grad_ref, gain_ref, both_ref, branch_ref,
    out_ref, sums_ref, gate_ref, up_ref, wo_ref, held, far, *scratch,
):
    total = Sum(part_ref, scratch[:4], scratch[4:11])
    swap, line = Swap(both_ref, held, scratch[11:14]), Line(planes, branch_ref, far, scratch[14:])
    greet(swap.near + line.near)
    total.start()
    line.start()
    total.middle()
    swap.start()
    total.middle_two()
    sums_ref[...] = jnp.zeros_like(sums_ref)

    def use(rows, value):
        normed, inverse = normalize(x_ref[rows, :].astype(F32))
        sums_ref[:8, :] += fold(value * normed)
        sums_ref[8:, :] += fold(value)
        out_ref[rows, :] = grad_ref[rows, :] + norm_back(value * gain_ref[...], normed, inverse)

    total.finish(use)
    line.finish()
    wo_ref[...] = added(far)
    swap.finish()
    unslice(held, 2, planes, [gate_ref, up_ref])


def last(part, inputs, grad_resid, gain, both, branch, cid):
    rows, width = inputs.shape
    planes, depth, _ = branch.shape
    return pl.pallas_call(
        functools.partial(last_kernel, planes),
        out_shape=[
            jax.ShapeDtypeStruct((rows, width), F32),
            jax.ShapeDtypeStruct((16, width), F32),
        ]
        + [jax.ShapeDtypeStruct((depth, both.shape[2] * TEAM // 2), F32)] * 2
        + [jax.ShapeDtypeStruct((depth, width), F32)],
        in_specs=[ANY, VMEM, VMEM, VMEM, ANY, ANY],
        out_specs=[VMEM] * 5,
        scratch_shapes=[pltpu.VMEM(both.shape, BF16), pltpu.VMEM(branch.shape, BF16)]
        + Sum.scratch(rows, width)
        + Sum.sems
        + Swap.sems
        + Line.sems(planes),
        cost_estimate=lasting(60),
        compiler_params=params(cid),
    )(part, inputs, grad_resid, gain, both, branch)


def dot(a, b, dims=((1,), (0,))):
    return lax.dot_general(a, b, (dims, ((), ())), preferred_element_type=F32)


NT = ((1,), (1,))
TN = ((0,), (0,))


def normalize(stream):
    average = jnp.mean(stream, axis=-1, keepdims=True)
    centered = stream - average
    variance = jnp.mean(centered * centered, axis=-1, keepdims=True)
    inverse = lax.rsqrt(variance + EPS)
    return centered * inverse, inverse


def norm_back(grad_norm, normed, inverse):
    return inverse * (
        grad_norm
        - jnp.mean(grad_norm, axis=-1, keepdims=True)
        - normed * jnp.mean(grad_norm * normed, axis=-1, keepdims=True)
    )


def turn(heads, cosine, sine):
    half, width = ROT // 2, heads.shape[-1]
    lanes = lax.broadcasted_iota(jnp.int32, heads.shape, 1) % HEAD_DIM
    moved = jnp.where(lanes < half, -pltpu.roll(heads, width - half, 1), pltpu.roll(heads, half, 1))
    return heads * cosine + moved * sine


def wide(table):
    return jnp.concatenate([table] * (LOCAL * HEAD_DIM // 128), axis=1)


def visible(start):
    size = start.shape[0]
    rows = lax.broadcasted_iota(jnp.int32, (size, size), 0)
    columns = lax.broadcasted_iota(jnp.int32, (size, size), 1)
    start = jnp.concatenate([start] * (size // start.shape[1]), axis=1)
    return (columns <= rows) & (columns.astype(F32) >= start)


def head_of(x, h):
    lanes = lax.broadcasted_iota(jnp.int32, x.shape, 1)
    return jnp.where((lanes >= h * HEAD_DIM) & (lanes < (h + 1) * HEAD_DIM), x, jnp.zeros_like(x))


def soft(query, key, allowed):
    scores = dot(query, key, NT) * 0.125
    masked = jnp.where(allowed, scores, -1e30)
    exponent = jnp.exp(masked - jnp.max(masked, axis=-1, keepdims=True))
    return exponent / jnp.sum(exponent, axis=-1, keepdims=True)


def attend_kernel(
    x_ref, gain_ref, bias_ref, w_ref, b_ref, wo_ref, tab_ref, g_ref, h_ref, qkv_ref, attn_ref, part_ref, g_all_ref, *sems
):
    gather = Gather(g_ref, g_all_ref, sems)
    step = pl.program_id(0)

    @pl.when(step == 0)
    def _():
        greet(gather.near)
        gather.start()

    pl.when(step == TEAM // 2)(gather.middle)
    stream = x_ref[0].astype(F32)
    normed, _ = normalize(stream)
    h_one = (normed * gain_ref[...] + bias_ref[...]).astype(BF16)
    h_ref[0] = h_one
    qkv = dot(h_one, w_ref[...]) + b_ref[...]
    width = LOCAL * HEAD_DIM
    cosine, sine = wide(tab_ref[0, 0]), wide(tab_ref[0, 1])
    query = turn(qkv[:, :width], cosine, sine).astype(BF16)
    key = turn(qkv[:, width : 2 * width], cosine, sine).astype(BF16)
    value = qkv[:, 2 * width :].astype(BF16)
    qkv_ref[0, :, :width] = query
    qkv_ref[0, :, width : 2 * width] = key
    qkv_ref[0, :, 2 * width :] = value
    allowed = visible(tab_ref[0, 2])
    mixed = jnp.zeros((query.shape[0], width), F32)
    for h in range(LOCAL):
        probs = soft(head_of(query, h), key, allowed).astype(BF16)
        mixed = mixed + dot(probs, head_of(value, h))
    attn_low = mixed.astype(BF16)
    attn_ref[0] = attn_low
    part_ref[0] = dot(attn_low, wo_ref[...]).astype(BF16)
    pl.when(step == TEAM - 1)(gather.finish)


def per_seq(*shape):
    return pl.BlockSpec((1,) + shape, lambda s: (s,) + (0,) * len(shape))


def whole(*shape):
    return pl.BlockSpec(shape, lambda s: (0,) * len(shape))


def attend(x_all, gain, bias, w_qkv, b_qkv, w_out, tables, out_grad, cid):
    seqs, rows, _ = x_all.shape
    width = LOCAL * HEAD_DIM
    return pl.pallas_call(
        attend_kernel,
        grid=(seqs,),
        in_specs=[
            per_seq(rows, D),
            whole(1, D),
            whole(1, D),
            whole(D, 3 * width),
            whole(1, 3 * width),
            whole(width, D),
            per_seq(3, rows, 128),
            ANY,
        ],
        out_specs=[per_seq(rows, D), per_seq(rows, 3 * width), per_seq(rows, width), per_seq(rows, D), ANY],
        out_shape=[
            jax.ShapeDtypeStruct((seqs, rows, D), BF16),
            jax.ShapeDtypeStruct((seqs, rows, 3 * width), BF16),
            jax.ShapeDtypeStruct((seqs, rows, width), BF16),
            jax.ShapeDtypeStruct((seqs, rows, D), BF16),
            jax.ShapeDtypeStruct((seqs, rows, D), BF16),
        ],
        scratch_shapes=Gather.sems,
        cost_estimate=lasting(44),
        compiler_params=params(cid),
    )(x_all, gain, bias, w_qkv, b_qkv, w_out, tables, out_grad)


def attend_back_kernel(
    block_ref, wo_ref, w_ref, qkv_ref, tab_ref, attn_ref, down_ref, resid_ref, _,
    gqkv_ref, part_ref, gb_ref, wo_grad_ref, out_ref, held, wo_grad, *scratch,
):
    gather, block = Gather(block_ref, held, scratch[:7]), Sum(down_ref, scratch[7:11], scratch[11:])
    step = pl.program_id(0)

    @pl.when(step == 0)
    def _():
        greet(gather.near)
        gather.start()
        block.start()
        wo_grad[...] = jnp.zeros_like(wo_grad)

    for i in range(TEAM):
        pl.when(step == i)(functools.partial(gather.ready, i))
    grad = held[step]
    width = LOCAL * HEAD_DIM
    wo_grad[...] += dot(attn_ref[0], grad, TN)
    grad_att = dot(grad, wo_ref[...], NT).astype(BF16)
    query, key, value = (qkv_ref[0, :, i * width : (i + 1) * width] for i in range(3))
    allowed = visible(tab_ref[0, 2])
    zero = jnp.zeros((query.shape[0], width), F32)
    grad_query, grad_key, grad_value = zero, zero, zero
    for h in range(LOCAL):
        query_h, key_h, grad_h = head_of(query, h), head_of(key, h), head_of(grad_att, h)
        probs = soft(query_h, key, allowed)
        low = probs.astype(BF16)
        grad_probs = dot(grad_h, value, NT)
        delta = jnp.sum(low.astype(F32) * grad_probs, axis=-1, keepdims=True)
        grad_scores = (probs * (grad_probs - delta)).astype(BF16)
        grad_value = grad_value + dot(low, grad_h, TN)
        grad_query = grad_query + dot(grad_scores, key_h)
        grad_key = grad_key + dot(grad_scores, query_h, TN)
    cosine, sine = wide(tab_ref[0, 0]), -wide(tab_ref[0, 1])
    grad_query = turn(grad_query * 0.125, cosine, sine)
    grad_key = turn(grad_key * 0.125, cosine, sine)
    grad_qkv = jnp.concatenate([grad_query, grad_key, grad_value], axis=1).astype(BF16)
    gqkv_ref[0] = grad_qkv
    gb_ref[0] = jnp.sum(grad_qkv.astype(F32), axis=0, keepdims=True)
    part_ref[0] = dot(grad_qkv, w_ref[...], NT).astype(BF16)

    def use(rows, value):
        out_ref[rows, :] = (resid_ref[rows, :] + value).astype(BF16)

    pl.when(step == 1)(gather.middle)
    pl.when(step == 3)(block.middle)
    pl.when(step == 6)(block.middle_two)

    @pl.when(step == TEAM - 1)
    def _():
        wo_grad_ref[...] = wo_grad[...].astype(BF16)
        block.finish(use)
        gather.sent()


def attend_back(block, w_out, w_qkv, qkv, tables, attn, down, resid, after, cid):
    seqs, rows, _ = qkv.shape
    width = LOCAL * HEAD_DIM
    return pl.pallas_call(
        attend_back_kernel,
        grid=(seqs,),
        in_specs=[
            ANY,
            whole(width, D),
            whole(D, 3 * width),
            per_seq(rows, 3 * width),
            per_seq(3, rows, 128),
            per_seq(rows, width),
            ANY,
            whole(rows, D),
            ANY,
        ],
        out_specs=[per_seq(rows, 3 * width), per_seq(rows, D), per_seq(1, 3 * width), whole(width, D), whole(rows, D)],
        out_shape=[
            jax.ShapeDtypeStruct((seqs, rows, 3 * width), BF16),
            jax.ShapeDtypeStruct((seqs, rows, D), BF16),
            jax.ShapeDtypeStruct((seqs, 1, 3 * width), F32),
            jax.ShapeDtypeStruct((width, D), BF16),
            jax.ShapeDtypeStruct((rows, D), BF16),
        ],
        scratch_shapes=[pltpu.VMEM((seqs, rows, D), BF16), pltpu.VMEM((width, D), F32)]
        + Gather.sems
        + Sum.scratch(rows, D)
        + Sum.sems,
        cost_estimate=lasting(65),
        compiler_params=params(cid),
    )(block, w_out, w_qkv, qkv, tables, attn, down, resid, after)


def team_shards(
    inputs, positions, norm1_gain, norm1_bias, qkv_weight, qkv_bias, out_weight, norm2_gain, norm2_bias,
    gate_weight, up_weight, down_weight, out_grad,
):
    n = lax.axis_size("fsdp")
    planes = n // TEAM
    rows = inputs.shape[0]
    tokens = TEAM * rows
    depth = qkv_weight.shape[0]
    ff = down_weight.shape[0]
    width = LOCAL * HEAD_DIM
    lines = [[z * TEAM + i for z in range(planes)] for i in range(TEAM)]
    mine = lax.rem(lax.axis_index("fsdp"), TEAM)

    def line_gather(x):
        return lax.all_gather(x, "fsdp", axis=0, tiled=True, axis_index_groups=lines)

    def line_sum(x):
        return lax.psum_scatter(x, "fsdp", scatter_dimension=0, tiled=True, axis_index_groups=lines)

    pieces, w_out = opening(qkv_weight, out_weight, planes, 0)
    w_out = w_out.reshape(width, D)
    w_qkv = line_gather(pieces.reshape(TEAM * depth, 3 * width))
    small = jnp.stack([norm1_gain, norm1_bias, norm2_gain, norm2_bias])
    small = jnp.concatenate([small, qkv_bias.reshape(-1, depth)])
    small = jnp.pad(small, ((0, 16 - small.shape[0]), (0, 128 - depth)))
    places = jnp.pad(positions.reshape(-1, 128).astype(BF16), ((0, 16 - rows // 128), (0, 0)))
    both, x_all, small, places = second(gate_weight, up_weight, inputs, small, places, pieces, planes, 1)
    w_both = line_gather(both.reshape(TEAM * depth, 2 * planes * ff))
    w_down = line_gather(down_weight)
    vectors = small.reshape(n, 16, 128)[:, :, :depth].astype(F32)
    gain_one, bias_one, gain_two, bias_two = (vectors[:, i].reshape(1, D) for i in range(4))
    b_qkv = vectors[:, 4 : 4 + 3 * planes * TEAM * HEAD_DIM // (n * depth)].reshape(3, planes, TEAM, HEAD_DIM)
    b_qkv = lax.dynamic_index_in_dim(b_qkv, mine, 2, keepdims=False).reshape(1, 3 * width)
    places = places.reshape(TEAM, -1)[:, :rows].astype(F32)

    half = ROT // 2
    frequency = 10000.0 ** (-jnp.arange(half, dtype=F32) / half)
    frequency = jnp.concatenate([frequency, frequency, jnp.zeros((HEAD_DIM - ROT,), F32)] * (128 // HEAD_DIM))
    angles = places[:, :, None] * frequency
    start = jnp.arange(rows, dtype=F32)[None] - places
    tables = jnp.stack([jnp.cos(angles), jnp.sin(angles), jnp.broadcast_to(start[:, :, None], angles.shape)], axis=1)

    h_one, qkv, attn_low, part, g_all = attend(x_all, gain_one, bias_one, w_qkv, b_qkv, w_out, tables, out_grad, 3)
    resid, h_two = mid(part, inputs, gain_two, bias_two, 4)
    pre, hidden = expand(h_two, w_both)
    hidden = hidden.reshape(tokens, planes * ff)
    grad_down = dot(hidden, g_all.reshape(tokens, D), TN).astype(BF16)
    grad_resid, sums_two, block, grad_w_both = mlp_back(
        pre, g_all, h_two.reshape(tokens, D), w_down, w_both, resid, out_grad, gain_two, grad_down, 5
    )
    grad_down = line_sum(grad_down)
    grad_w_both = line_sum(grad_w_both)
    down = dot(hidden, w_down).astype(BF16).reshape(TEAM, rows, D)
    grad_qkv, part, grad_bias, grad_out, block_out = attend_back(
        block, w_out, w_qkv, qkv, tables, attn_low, down, resid, grad_down, 6
    )
    grad_qkv = grad_qkv.reshape(tokens, 3 * width)
    grad_w_qkv = dot(h_one.reshape(tokens, D), grad_qkv, TN).astype(BF16)
    part, grad_w_qkv, grad_w_both = lax.optimization_barrier((part, grad_w_qkv, grad_w_both))
    input_grad, sums_one, grad_gate_w, grad_up_w, grad_out = last(
        part, inputs, grad_resid, gain_one,
        grad_w_both.reshape(TEAM, depth, 2 * planes * ff), grad_out.reshape(planes, depth, D), 7,
    )
    grad_w_qkv = line_sum(grad_w_qkv)

    bias = jnp.zeros((3, planes, TEAM, HEAD_DIM), F32)
    bias = lax.dynamic_update_slice(
        bias, jnp.sum(grad_bias, axis=0).reshape(3, planes, 1, HEAD_DIM), (0, 0, mine, 0)
    ).reshape(n, -1)
    sums = [jnp.sum(v[i : i + 8], axis=0).reshape(n, depth) for v in (sums_one, sums_two) for i in (0, 8)]
    sums = jnp.pad(jnp.concatenate(sums + [bias], axis=1), ((0, 0), (0, 1024 - 4 * depth - bias.shape[1])))
    sums = sums.reshape(planes, TEAM, 8, 128).transpose(1, 0, 2, 3)
    sums = vector_sums(sums, 8)
    grad_w_qkv = closing(grad_w_qkv.reshape(TEAM, depth, 3 * width), sums, planes, 9)
    sums = sums.reshape(-1)
    sums = [sums[i * depth : (i + 1) * depth] for i in range(4)] + [sums[4 * depth : 4 * depth + bias.shape[1]]]
    return (
        block_out,
        input_grad,
        sums[0],
        sums[1],
        grad_w_qkv,
        sums[4],
        grad_out,
        sums[2],
        sums[3],
        grad_gate_w,
        grad_up_w,
        grad_down.astype(F32),
    )


def rotate_pairs(heads, places, sign):
    half_rot = ROT // 2
    frequency = 10000.0 ** (-jnp.arange(half_rot, dtype=jnp.float32) / half_rot)
    angles = places.astype(jnp.float32)[:, None] * frequency[None, :]
    cosine = jnp.cos(angles)[:, None, :]
    sine_part = sign * jnp.sin(angles)[:, None, :]
    front_part = heads[..., :half_rot]
    back_part = heads[..., half_rot:ROT]
    return jnp.concatenate(
        [
            front_part * cosine - back_part * sine_part,
            back_part * cosine + front_part * sine_part,
            heads[..., ROT:],
        ],
        axis=-1,
    )


def by_groups(heads):
    group_heads = min(8, HEADS)
    shaped = heads.reshape(heads.shape[0], HEADS // group_heads, group_heads, HEAD_DIM)
    return jnp.moveaxis(shaped, 1, 0)


def from_groups(grouped):
    return jnp.moveaxis(grouped, 0, 1).reshape(grouped.shape[1], HEADS, HEAD_DIM)


def plain_group(block_items, allowed):
    query_part, key_part, value_part = block_items
    scores = (
        jnp.einsum("qhd,khd->hqk", query_part, key_part, preferred_element_type=jnp.float32) * 0.125
    )
    masked = jnp.where(allowed[None], scores, -1e30)
    row_max = jnp.max(masked, axis=-1, keepdims=True)
    exponent = jnp.exp(masked - row_max)
    row_total = jnp.sum(exponent, axis=-1, keepdims=True)
    soft_probs = (exponent / row_total).astype(jnp.bfloat16)
    mixed_part = jnp.einsum(
        "hqk,khd->qhd", soft_probs, value_part, preferred_element_type=jnp.float32
    )
    return (mixed_part, (row_max + jnp.log(row_total))[..., 0])


def plain_back(block_items, allowed):
    query_part, key_part, value_part, grad_part, row_delta, log_total = block_items
    scores = (
        jnp.einsum("qhd,khd->hqk", query_part, key_part, preferred_element_type=jnp.float32) * 0.125
    )
    soft_probs = jnp.where(allowed[None], jnp.exp(scores - log_total[..., None]), 0.0)
    grad_probs = jnp.einsum(
        "qhd,khd->hqk", grad_part, value_part.astype(jnp.float32), precision=lax.Precision.HIGHEST
    )
    rounded_probs = soft_probs.astype(jnp.bfloat16).astype(jnp.float32)
    grad_value = jnp.einsum("hqk,qhd->khd", rounded_probs, grad_part, precision=lax.Precision.HIGHEST)
    grad_scores = (soft_probs * (grad_probs - row_delta[..., None])).astype(jnp.bfloat16)
    grad_query = 0.125 * jnp.einsum(
        "hqk,khd->qhd", grad_scores, key_part, preferred_element_type=jnp.float32
    )
    grad_key = 0.125 * jnp.einsum(
        "hqk,qhd->khd", grad_scores, query_part, preferred_element_type=jnp.float32
    )
    return (grad_query, grad_key, grad_value)


def shards(
    inputs,
    positions,
    norm1_gain,
    norm1_bias,
    qkv_weight,
    qkv_bias,
    out_weight,
    norm2_gain,
    norm2_bias,
    gate_weight,
    up_weight,
    down_weight,
    out_grad,
):
    tok_rows = inputs.shape[0]
    gain_one, bias_one, w_qkv, b_qkv, w_out = (
        lax.all_gather(norm1_gain, "fsdp", axis=0, tiled=True),
        lax.all_gather(norm1_bias, "fsdp", axis=0, tiled=True),
        lax.all_gather(qkv_weight, "fsdp", axis=0, tiled=True),
        lax.all_gather(qkv_bias, "fsdp", axis=0, tiled=True),
        lax.all_gather(out_weight, "fsdp", axis=0, tiled=True),
    )
    stream = inputs.astype(jnp.float32)
    normed_one, inverse_one = normalize(stream)
    h_one = (normed_one * gain_one.astype(jnp.float32) + bias_one.astype(jnp.float32)).astype(
        jnp.bfloat16
    )
    qkv_pre = jnp.dot(h_one, w_qkv, preferred_element_type=jnp.float32) + b_qkv.astype(jnp.float32)
    qkv_heads = qkv_pre.reshape(tok_rows, 3, HEADS, HEAD_DIM)
    query_low = rotate_pairs(qkv_heads[:, 0], positions, 1.0).astype(jnp.bfloat16)
    key_all = rotate_pairs(qkv_heads[:, 1], positions, 1.0).astype(jnp.bfloat16)
    value_all = qkv_heads[:, 2].astype(jnp.bfloat16)
    token_index = jnp.arange(tok_rows, dtype=jnp.int32)
    allowed = (token_index[None, :] <= token_index[:, None]) & (
        token_index[None, :] >= (token_index - positions)[:, None]
    )
    mixed_grouped, log_grouped = lax.map(
        lambda block_items: plain_group(block_items, allowed),
        (by_groups(query_low), by_groups(key_all), by_groups(value_all)),
    )
    mixed_heads = from_groups(mixed_grouped)
    attn_low = mixed_heads.reshape(tok_rows, D).astype(jnp.bfloat16)
    resid = stream + jnp.dot(attn_low, w_out, preferred_element_type=jnp.float32)
    gain_two, bias_two, w_gate, w_up, w_down = (
        lax.all_gather(norm2_gain, "fsdp", axis=0, tiled=True),
        lax.all_gather(norm2_bias, "fsdp", axis=0, tiled=True),
        lax.all_gather(gate_weight, "fsdp", axis=0, tiled=True),
        lax.all_gather(up_weight, "fsdp", axis=0, tiled=True),
        lax.all_gather(down_weight, "fsdp", axis=0, tiled=True),
    )
    normed_two, inverse_two = normalize(resid)
    h_two = (normed_two * gain_two.astype(jnp.float32) + bias_two.astype(jnp.float32)).astype(
        jnp.bfloat16
    )
    gate_pre = jnp.dot(h_two, w_gate, preferred_element_type=jnp.float32)
    up_pre = jnp.dot(h_two, w_up, preferred_element_type=jnp.float32)
    sigmoid_gate = jax.nn.sigmoid(gate_pre)
    silu_gate = gate_pre * sigmoid_gate
    hidden = (silu_gate * up_pre).astype(jnp.bfloat16)
    block_out = (resid + jnp.dot(hidden, w_down, preferred_element_type=jnp.float32)).astype(
        jnp.bfloat16
    )
    gain_two, w_gate, w_up, w_down = (
        lax.all_gather(norm2_gain, "fsdp", axis=0, tiled=True),
        lax.all_gather(gate_weight, "fsdp", axis=0, tiled=True),
        lax.all_gather(up_weight, "fsdp", axis=0, tiled=True),
        lax.all_gather(down_weight, "fsdp", axis=0, tiled=True),
    )
    grad_down_w = jnp.einsum("tf,td->fd", hidden, out_grad, preferred_element_type=jnp.float32)
    grad_hidden = jnp.einsum("td,fd->tf", out_grad, w_down, preferred_element_type=jnp.float32)
    grad_gate = (
        grad_hidden * up_pre * sigmoid_gate * (1.0 + gate_pre * (1.0 - sigmoid_gate))
    ).astype(jnp.bfloat16)
    grad_up = (grad_hidden * silu_gate).astype(jnp.bfloat16)
    grad_gate_w = jnp.einsum("td,tf->df", h_two, grad_gate, preferred_element_type=jnp.float32)
    grad_up_w = jnp.einsum("td,tf->df", h_two, grad_up, preferred_element_type=jnp.float32)
    grad_htwo = jnp.einsum(
        "tf,df->td", grad_gate, w_gate, preferred_element_type=jnp.float32
    ) + jnp.einsum("tf,df->td", grad_up, w_up, preferred_element_type=jnp.float32)
    grad_gain_two = jnp.sum(grad_htwo * normed_two, axis=0)
    grad_bias_two = jnp.sum(grad_htwo, axis=0)
    grad_resid = out_grad.astype(jnp.float32) + norm_back(
        grad_htwo * gain_two.astype(jnp.float32), normed_two, inverse_two
    )
    mlp_sums = (
        lax.psum_scatter(grad_gain_two, "fsdp", scatter_dimension=0, tiled=True),
        lax.psum_scatter(grad_bias_two, "fsdp", scatter_dimension=0, tiled=True),
        lax.psum_scatter(grad_gate_w, "fsdp", scatter_dimension=0, tiled=True),
        lax.psum_scatter(grad_up_w, "fsdp", scatter_dimension=0, tiled=True),
        lax.psum_scatter(grad_down_w, "fsdp", scatter_dimension=0, tiled=True),
    )
    gain_one, w_qkv, w_out = (
        lax.all_gather(norm1_gain, "fsdp", axis=0, tiled=True),
        lax.all_gather(qkv_weight, "fsdp", axis=0, tiled=True),
        lax.all_gather(out_weight, "fsdp", axis=0, tiled=True),
    )
    grad_branch = grad_resid.astype(jnp.bfloat16)
    grad_out_w = jnp.einsum("ti,td->id", attn_low, grad_branch, preferred_element_type=jnp.float32)
    grad_att = jnp.einsum(
        "td,id->ti", grad_branch, w_out, preferred_element_type=jnp.float32
    ).reshape(tok_rows, HEADS, HEAD_DIM)
    group_heads = min(8, HEADS)
    row_delta = jnp.sum(grad_att * mixed_heads, axis=-1)
    delta_grouped = row_delta.reshape(tok_rows, HEADS // group_heads, group_heads).transpose(
        1, 2, 0
    )
    query_grouped, key_grouped, value_grouped = lax.map(
        lambda block_items: plain_back(block_items, allowed),
        (
            by_groups(query_low),
            by_groups(key_all),
            by_groups(value_all),
            by_groups(grad_att),
            delta_grouped,
            log_grouped,
        ),
    )
    grad_query = from_groups(query_grouped)
    grad_key = from_groups(key_grouped)
    grad_value = from_groups(value_grouped)
    grad_qkv = (
        jnp.stack(
            [
                rotate_pairs(grad_query, positions, -1.0),
                rotate_pairs(grad_key, positions, -1.0),
                grad_value,
            ],
            axis=1,
        )
        .reshape(tok_rows, 3 * D)
        .astype(jnp.bfloat16)
    )
    grad_qkv_w = jnp.einsum("td,tk->dk", h_one, grad_qkv, preferred_element_type=jnp.float32)
    grad_qkv_b = jnp.sum(grad_qkv.astype(jnp.float32), axis=0)
    grad_hone = jnp.einsum("tk,dk->td", grad_qkv, w_qkv, preferred_element_type=jnp.float32)
    grad_gain_one = jnp.sum(grad_hone * normed_one, axis=0)
    grad_bias_one = jnp.sum(grad_hone, axis=0)
    input_grad = grad_resid + norm_back(
        grad_hone * gain_one.astype(jnp.float32), normed_one, inverse_one
    )
    attn_sums = (
        lax.psum_scatter(grad_gain_one, "fsdp", scatter_dimension=0, tiled=True),
        lax.psum_scatter(grad_bias_one, "fsdp", scatter_dimension=0, tiled=True),
        lax.psum_scatter(grad_qkv_w, "fsdp", scatter_dimension=0, tiled=True),
        lax.psum_scatter(grad_qkv_b, "fsdp", scatter_dimension=0, tiled=True),
        lax.psum_scatter(grad_out_w, "fsdp", scatter_dimension=0, tiled=True),
    )
    return (
        block_out,
        input_grad,
        attn_sums[0],
        attn_sums[1],
        attn_sums[2],
        attn_sums[3],
        attn_sums[4],
        mlp_sums[0],
        mlp_sums[1],
        mlp_sums[2],
        mlp_sums[3],
        mlp_sums[4],
    )


def solution(mesh):
    devices = mesh.shape["fsdp"]
    rows, columns = P("fsdp", None), P("fsdp")
    body = team_shards if devices % TEAM == 0 and D == devices * HEAD_DIM else shards
    return jax.shard_map(
        body,
        mesh=mesh,
        in_specs=(rows, columns, columns, columns, rows, columns, rows, columns, columns, rows, rows, rows, rows),
        out_specs=(rows, rows, columns, columns, rows, columns, rows, columns, columns, rows, rows, rows),
        check_vma=False,
    )
```

```python
import functools

import jax
import jax.numpy as jnp
import numpy as np
from jax import lax
from jax.experimental import pallas as pl
from jax.experimental.pallas import tpu as pltpu
from jax.sharding import PartitionSpec as P

D = 2048
HEADS = 32
HEAD_DIM = 64
ROT = 16
EPS = 1e-05
TEAM = 8
LOCAL = HEADS // TEAM
MESH = pl.DeviceIdType.MESH
BF16 = jnp.bfloat16
F32 = jnp.float32
ANY = pl.BlockSpec(memory_space=pl.ANY)
VMEM = pl.BlockSpec(memory_space=pltpu.VMEM)


def lasting(us):
    return pl.CostEstimate(flops=0, bytes_accessed=int(us * 3.6e6), transcendentals=0)


def params(cid=None, limit=56):
    extra = {} if cid is None else {"collective_id": cid, "has_side_effects": True}
    return pltpu.CompilerParams(vmem_limit_bytes=limit * 1024 * 1024, **extra)


def place():
    me = lax.axis_index("fsdp")
    mine = lax.rem(me, TEAM)
    return mine, me - mine, mine // 2, lax.rem(mine, 2)


def chip_at(chip, step):
    along_x, along_y = lax.rem(chip, 2), chip // 2
    if step & 1:
        along_x = 1 - along_x
    if step & 2:
        along_y = 1 - along_y
    return along_y * 2 + along_x


def relation(chip, core, r):
    return chip_at(chip, r // 2) * 2 + lax.rem(core + r, 2)


def greet(devices):
    barrier = pltpu.get_barrier_semaphore()
    for device in devices:
        pl.semaphore_signal(barrier, inc=1, device_id=(device,), device_id_type=MESH)
    pl.semaphore_wait(barrier, len(devices))


def remote(src, dst, send, recv, device):
    return pltpu.make_async_remote_copy(
        src_ref=src, dst_ref=dst, send_sem=send, recv_sem=recv, device_id=(device,), device_id_type=MESH
    )


class Swap:
    sems = [pltpu.SemaphoreType.DMA, pltpu.SemaphoreType.DMA((TEAM,)), pltpu.SemaphoreType.DMA((TEAM,))]

    def __init__(self, src, out, sems, same=False, near_first=False):
        own_sem, send, recv = sems
        mine, base, chip, core = place()
        others = [relation(chip, core, r) for r in range(1, TEAM)]
        self.near = [base + other for other in others]
        self.copies = [
            remote(
                src if same else src.at[other], out.at[r if near_first else mine], send.at[r], recv.at[r], base + other
            )
            for r, other in enumerate(others, 1)
        ]
        own = src if same else src.at[mine]
        self.copies.append(pltpu.make_async_copy(own, out.at[0 if near_first else mine], own_sem))

    def start(self):
        for copy in self.copies:
            copy.start()

    def finish(self):
        for copy in self.copies:
            copy.wait()


class Line:
    def sems(planes):
        return [pltpu.SemaphoreType.DMA, pltpu.SemaphoreType.DMA((planes,)), pltpu.SemaphoreType.DMA((planes,))]

    def __init__(self, planes, src, out, sems, same=False, within=False):
        own_sem, send, recv = sems
        mine, base, _, _ = place()
        plane = base // TEAM
        others = [lax.rem(plane + k, planes) for k in range(1, planes)]
        self.near = [other * TEAM + mine for other in others]
        self.copies = [
            remote(src if same else src.at[other], out.at[plane], send.at[k], recv.at[k], other * TEAM + mine)
            for k, other in enumerate(others)
        ]
        own = src if same else src.at[plane]
        self.own = None if within else pltpu.make_async_copy(own, out.at[plane], own_sem)

    def start(self):
        for copy in self.copies:
            copy.start()
        if self.own is not None:
            self.own.start()

    def finish(self):
        for copy in self.copies:
            copy.wait()
        if self.own is not None:
            self.own.wait()


class LineGather:
    def sems(planes):
        return [pltpu.SemaphoreType.DMA, pltpu.SemaphoreType.DMA((2, planes)), pltpu.SemaphoreType.DMA((2, planes))]

    def __init__(self, planes, src, out, sems):
        own_sem, self.send, self.recv = sems
        mine, base, _, _ = place()
        self.plane, self.planes, self.src, self.out = base // TEAM, planes, src, out
        self.me = base + mine
        self.near = [lax.rem(self.plane + k, planes) * TEAM + mine for k in (1, planes - 1)]
        self.own = pltpu.make_async_copy(src, out.at[self.plane], own_sem)

    def copy(self, way, stage):
        step = 1 - 2 * way
        block, to = self.plane - step * (stage - 1), self.plane + step
        is_there = (block >= 0) & (block < self.planes) & (to >= 0) & (to < self.planes)
        src = self.src if stage == 1 else self.out.at[block]
        sems = self.send.at[way, stage], self.recv.at[way, stage]
        return is_there, remote(src, self.out.at[block], *sems, self.me + step * TEAM)

    def arrived(self, way, stage):
        block = self.plane - (1 - 2 * way) * stage

        @pl.when((block >= 0) & (block < self.planes))
        def _():
            dst = self.out.at[block]
            remote(dst, dst, self.send.at[way, stage], self.recv.at[way, stage], self.me).wait_recv()

    def start(self):
        self.own.start()
        self.stage(1)

    def stage(self, stage):
        for way in (0, 1):
            if stage > 1:
                self.arrived(way, stage - 1)
            is_there, copy = self.copy(way, stage)
            pl.when(is_there)(copy.start)

    def finish(self):
        self.own.wait()
        for way in (0, 1):
            self.arrived(way, self.planes - 1)
            for stage in range(1, self.planes):
                is_there, copy = self.copy(way, stage)
                pl.when(is_there)(copy.wait_send)


def slices(ref, pieces, size):
    return jnp.concatenate([ref[:, i * size : (i + 1) * size] for i in pieces], axis=1)


def open_kernel(planes, w_ref, pieces_ref, made, *sems):
    swap = Swap(made, pieces_ref, sems)
    for i in range(TEAM):
        made[i] = slices(w_ref, [s * HEADS + z * TEAM + i for s in range(3) for z in range(planes)], HEAD_DIM)
    greet(swap.near)
    swap.start()
    swap.finish()


def opening(weight, planes, cid):
    shape = (TEAM, weight.shape[0], weight.shape[1] // TEAM)
    return pl.pallas_call(
        functools.partial(open_kernel, planes),
        out_shape=jax.ShapeDtypeStruct(shape, BF16),
        in_specs=[VMEM],
        out_specs=ANY,
        scratch_shapes=[pltpu.VMEM(shape, BF16)] + Swap.sems,
        cost_estimate=lasting(17),
        compiler_params=params(cid),
    )(weight)


def second_kernel(
    planes, gate_ref, up_ref, x_ref, small_ref, place_ref, qkv_ref, rate_ref,
    pieces_ref, x_all_ref, w_qkv_ref, tab_ref, norm_ref, b_ref, made, all_ref, places_ref, tables, *sems,
):
    mine, base, _, _ = place()
    plane = base // TEAM
    swap, gather = Swap(made, pieces_ref, sems[:3]), Gather(x_ref, x_all_ref, sems[3:10])
    vectors = Swap(small_ref, all_ref.at[plane], sems[10:13], same=True)
    places = Swap(place_ref, places_ref, sems[13:16], same=True, near_first=True)
    line = Line(planes, all_ref.at[plane], all_ref, sems[16:19], same=True, within=True)
    rows = LineGather(planes, qkv_ref, w_qkv_ref, sems[19:22])
    greet(swap.near + line.near)
    rows.start()
    vectors.start()
    places.start()
    gather.start()
    size = gate_ref.shape[1] // (planes * TEAM)
    for i in range(TEAM):
        units = [z * TEAM + i for z in range(planes)]
        made[i] = jnp.concatenate([slices(gate_ref, units, size), slices(up_ref, units, size)], axis=1)
    swap.start()
    vectors.finish()
    line.start()
    rows.stage(2)
    places.finish()
    square = (128, 128)

    @pl.loop(0, TEAM)
    def _(i):
        known = places_ref[i].astype(F32)
        for part in range(tables.shape[2] // 128):
            at = jnp.transpose(jnp.broadcast_to(known[part : part + 1, :], square))
            here = pl.ds(part * 128, 128)
            angle = at * rate_ref[...]
            tables[i, 0, here, :] = jnp.cos(angle)
            tables[i, 1, here, :] = jnp.sin(angle)
            token = lax.broadcasted_iota(jnp.int32, square, 0) + part * 128
            tables[i, 2, here, :] = token.astype(F32) - at

    store = pltpu.make_async_copy(tables, tab_ref, sems[22])
    store.start()
    gather.middle()
    for stage in range(3, planes):
        rows.stage(stage)
    line.finish()
    depth = gate_ref.shape[0]
    each = [all_ref[z, i].astype(F32) for z in range(planes) for i in range(TEAM)]
    for i in range(4):
        norm_ref[i : i + 1, :] = jnp.concatenate([known[i : i + 1, :depth] for known in each], axis=1)
    per = qkv_ref.shape[1] * TEAM // (planes * TEAM * depth)
    bias = []
    for part in range(3):
        for z in range(planes):
            head = part * HEADS + z * TEAM + mine
            known = all_ref[head // per // TEAM, lax.rem(head // per, TEAM)].astype(F32)
            row = lax.broadcasted_iota(jnp.int32, known.shape, 0) == 4 + lax.rem(head, per)
            bias.append(jnp.sum(jnp.where(row, known, 0.0), axis=0, keepdims=True)[:, :depth])
    b_ref[...] = jnp.concatenate(bias, axis=1)
    gather.finish()
    swap.finish()
    rows.finish()
    store.wait()


def second(gate, up, inputs, small, positions, qkv, rate, planes, cid):
    shape = (TEAM, gate.shape[0], 2 * gate.shape[1] // TEAM)
    tables = (TEAM, 3, inputs.shape[0], 128)
    return pl.pallas_call(
        functools.partial(second_kernel, planes),
        out_shape=[
            jax.ShapeDtypeStruct(shape, BF16),
            jax.ShapeDtypeStruct((TEAM,) + inputs.shape, BF16),
            jax.ShapeDtypeStruct((planes,) + qkv.shape, BF16),
            jax.ShapeDtypeStruct(tables, F32),
            jax.ShapeDtypeStruct((4, inputs.shape[1]), F32),
            jax.ShapeDtypeStruct((1, qkv.shape[1]), F32),
        ],
        in_specs=[VMEM] * 7,
        out_specs=[ANY] * 4 + [VMEM] * 2,
        scratch_shapes=[
            pltpu.VMEM(shape, BF16),
            pltpu.VMEM((planes, TEAM) + small.shape, BF16),
            pltpu.VMEM((TEAM,) + positions.shape, BF16),
            pltpu.VMEM(tables, F32),
        ]
        + Swap.sems
        + Gather.sems
        + Swap.sems * 2
        + Line.sems(planes)
        + LineGather.sems(planes)
        + [pltpu.SemaphoreType.DMA],
        cost_estimate=lasting(65),
        compiler_params=params(cid),
    )(gate, up, inputs, small, positions, qkv, rate)


def unslice(held, parts, planes, outs):
    size = held.shape[2] // (parts * planes)
    for at in range(parts * planes):
        row = jnp.concatenate([held[i, :, at * size : (at + 1) * size] for i in range(TEAM)], axis=1)
        out, first = (outs[at // planes], at % planes) if len(outs) > 1 else (outs[0], at)
        out[:, first * TEAM * size : (first + 1) * TEAM * size] = row.astype(F32)


def both_kernel(planes, held_ref, gate_ref, up_ref):
    unslice(held_ref, 2, planes, [gate_ref, up_ref])


def both_grads(held, planes):
    _, depth, width = held.shape
    return pl.pallas_call(
        functools.partial(both_kernel, planes),
        out_shape=[jax.ShapeDtypeStruct((depth, width * TEAM // 2), F32)] * 2,
        in_specs=[VMEM],
        out_specs=[VMEM] * 2,
        cost_estimate=lasting(4),
        compiler_params=params(),
    )(held)


def rest_kernel(planes, held_ref, far_ref, w_ref, wo_ref):
    unslice(held_ref, 3, planes, [w_ref])
    wo_ref[...] = added(far_ref)


def rest_grads(held, far):
    _, depth, width = held.shape
    return pl.pallas_call(
        functools.partial(rest_kernel, far.shape[0]),
        out_shape=[
            jax.ShapeDtypeStruct((depth, width * TEAM), F32),
            jax.ShapeDtypeStruct(far.shape[1:], F32),
        ],
        in_specs=[VMEM] * 2,
        out_specs=[VMEM] * 2,
        cost_estimate=lasting(4),
        compiler_params=params(),
    )(held, far)


def added(ref):
    total = ref[0].astype(F32)
    for i in range(1, ref.shape[0]):
        total = total + ref[i].astype(F32)
    return total


def close_kernel(planes, w_ref, block_ref, _, __, held_ref, vector_ref, beyond, *sems):
    swap, outer = Swap(w_ref, held_ref, sems[:3]), Line(planes, block_ref, beyond, sems[3:])
    greet(swap.near + outer.near)
    outer.start()
    swap.start()
    outer.finish()
    swap.finish()
    vector_ref[...] = added(beyond)


def closing(blocks, sums, after, cid):
    planes = sums.shape[0]
    return pl.pallas_call(
        functools.partial(close_kernel, planes),
        out_shape=[
            jax.ShapeDtypeStruct(blocks.shape, BF16),
            jax.ShapeDtypeStruct(sums.shape[1:], F32),
        ],
        in_specs=[VMEM, VMEM, ANY, ANY],
        out_specs=[ANY, VMEM],
        scratch_shapes=[pltpu.VMEM(sums.shape, F32)] + Swap.sems + Line.sems(planes),
        cost_estimate=lasting(16),
        compiler_params=params(cid),
    )(blocks, sums, *after)


class Gather:
    sems = [pltpu.SemaphoreType.DMA((5,)), pltpu.SemaphoreType.DMA((5,)), pltpu.SemaphoreType.DMA((2,)),
            pltpu.SemaphoreType.DMA((2,)), pltpu.SemaphoreType.DMA((6,)), pltpu.SemaphoreType.DMA((6,)),
            pltpu.SemaphoreType.DMA]

    def __init__(self, src, out, sems):
        send, recv, hop_send, hop_recv, pass_send, pass_recv, own_sem = sems
        _, base, chip, core = place()
        side, over = (chip_at(chip, k) * 2 + core for k in (1, 2))
        self.sibling = base + chip * 2 + 1 - core
        self.near = [base + side, base + over, self.sibling]
        half = src.shape[0] // 2
        top, low = pl.ds(0, half), pl.ds(half, half)
        self.first = [
            remote(src.at[part], out.at[at, part], send.at[i], recv.at[i], base + to)
            for i, (part, at, to) in enumerate(((top, 2, side), (low, 4, over), (low, 2, side), (top, 4, over)))
        ]
        self.first.append(remote(src, out.at[1], send.at[4], recv.at[4], self.sibling))
        self.own = pltpu.make_async_copy(src, out.at[0], own_sem)
        self.hops = [
            remote(out.at[at, part], out.at[6, part], hop_send.at[i], hop_recv.at[i], base + to)
            for i, (at, part, to) in enumerate(((2, top, over), (4, low, side)))
        ]
        self.passed = [
            remote(out.at[at, part], out.at[at + 1, part], pass_send.at[i], pass_recv.at[i], self.sibling)
            for i, (at, part) in enumerate(((2, top), (4, low), (2, low), (4, top), (6, top), (6, low)))
        ]

    def start(self):
        for copy in self.first:
            copy.start()
        self.own.start()

    def middle(self):
        for i in (0, 1):
            self.first[i].wait_recv()
            self.hops[i].start()
            self.passed[i].start()

    def finish(self):
        for i in range(2, TEAM):
            self.ready(i)
        self.first[4].wait_recv()
        self.own.wait()
        self.sent()

    def ready(self, i):
        if i == 0:
            self.own.wait()
        elif i == 1:
            self.first[4].wait_recv()
        elif i == 6:
            for j in (0, 1):
                self.hops[j].wait_recv()
                self.passed[4 + j].start()
        elif i % 2 == 0:
            self.first[1 + i // 2].wait_recv()
            self.passed[1 + i // 2].start()
        else:
            for j in {3: (0, 2), 5: (1, 3), 7: (4, 5)}[i]:
                self.passed[j].wait_recv()

    def sent(self):
        for copy in self.first + self.hops + self.passed:
            copy.wait_send()


class Sum:
    def scratch(rows, width):
        return [pltpu.VMEM((4, rows, width), BF16), pltpu.VMEM((4, rows, width), BF16),
                pltpu.VMEM((2, rows // 2, width), BF16), pltpu.VMEM((2, rows, width), BF16)]

    sems = [pltpu.SemaphoreType.DMA((4,))] * 3 + [pltpu.SemaphoreType.DMA((2,))] * 2 + [pltpu.SemaphoreType.DMA((4,))] * 2

    def __init__(self, blocks, scratch, sems, away=None):
        self.own, self.beside, self.via, self.far = scratch
        load_sem, near_send, near_recv, via_send, via_recv, far_send, far_recv = sems
        _, base, chip, core = place()
        sibling = base + chip * 2 + 1 - core
        side, over = (base + chip_at(chip, k) * 2 + core for k in (1, 2))
        self.near = [side, over, sibling]
        self.half = self.own.shape[1] // 2
        top, low = pl.ds(0, self.half), pl.ds(self.half, self.half)
        self.loads = [
            pltpu.make_async_copy(blocks.at[2 * k], self.own.at[k], load_sem.at[k])
            for k in range(4)
            if away is None
        ]

        def near_copy(k):
            src = blocks.at[2 * k + 1] if away is None else away.at[k]
            return remote(src, self.beside.at[k], near_send.at[k], near_recv.at[k], sibling)

        self.near_copy = near_copy
        self.nears = [near_copy(k) for k in range(4)]
        self.vias = [
            remote(self.own.at[3, part], self.via.at[i], via_send.at[i], via_recv.at[i], to)
            for i, (part, to) in enumerate(((top, side), (low, over)))
        ]
        self.fars = [
            remote(self.own.at[k, part], self.far.at[k - 1, part], far_send.at[i], far_recv.at[i], to)
            for i, (k, part, to) in enumerate(((2, low, over), (1, top, side), (2, top, over), (1, low, side)))
        ]

    def start(self):
        for k in (3, 2, 1, 0):
            self.loads[k].start()
            self.nears[k].start()

    def pair(self, k):
        if self.loads:
            self.loads[k].wait()
        self.nears[k].wait_recv()

        @pl.loop(0, self.own.shape[1] // 16)
        def _(i):
            part = pl.ds(pl.multiple_of(i * 16, 16), 16)
            self.own[k, part, :] = (self.own[k, part, :].astype(F32) + self.beside[k, part, :].astype(F32)).astype(BF16)

    def middle_a(self):
        self.pair(3)
        for copy in self.vias:
            copy.start()

    def middle_b(self):
        self.pair(2)
        self.fars[0].start()

    def middle_c(self):
        self.pair(1)
        self.fars[1].start()

    def middle(self):
        self.middle_a()
        self.middle_b()
        self.middle_c()

    def middle_two(self):
        for i, k in ((0, 2), (1, 1)):
            self.vias[i].wait_recv()

            @pl.loop(0, self.half // 16)
            def _(j, i=i, k=k):
                part = pl.ds(pl.multiple_of(j * 16, 16), 16)
                at = pl.ds(pl.multiple_of(j * 16 + i * self.half, 16), 16)
                self.own[k, at, :] = (self.own[k, at, :].astype(F32) + self.via[i, part, :].astype(F32)).astype(BF16)

            self.fars[2 + i].start()

    def finish(self, use):
        if self.loads:
            self.loads[0].wait()
        self.nears[0].wait_recv()
        for copy in self.fars:
            copy.wait_recv()

        @pl.loop(0, self.own.shape[1] // 16)
        def _(i):
            part = pl.ds(pl.multiple_of(i * 16, 16), 16)
            total = self.own[0, part, :].astype(F32) + self.beside[0, part, :].astype(F32)
            use(part, total + self.far[0, part, :].astype(F32) + self.far[1, part, :].astype(F32))

        for copy in self.nears + self.vias + self.fars:
            copy.wait_send()


def fold(x):
    return x[:8] + x[8:]


def expand_kernel(
    planes, h_ref, w_ref, g_ref, down_ref, pre_ref, hidden_ref, grad_ref, g_all_ref, wd_ref, held, g, total, w, *sems
):
    gather, line = Gather(g_ref, g_all_ref, sems[:7]), LineGather(planes, down_ref, wd_ref, sems[7:10])
    step = pl.program_id(0)

    @pl.when(step == 0)
    def _():
        greet(gather.near + line.near)
        line.start()
        gather.start()
        weights = pltpu.make_async_copy(w_ref, w, sems[11])
        weights.start()
        weights.wait()

    pre = dot(h_ref[0], w[...])
    pre_ref[0] = pre
    ff = hidden_ref.shape[2]
    gate_pre, up_pre = pre[:, :ff], pre[:, ff:]
    hidden = (gate_pre * jax.nn.sigmoid(gate_pre) * up_pre).astype(BF16)
    hidden_ref[0] = hidden
    held[step] = hidden
    pl.when(step == TEAM - 2)(functools.partial(line.stage, 2))

    @pl.when(step == TEAM - 1)
    def _():
        def load(i):
            return pltpu.make_async_copy(g_all_ref.at[i], g.at[i % 2], sems[10].at[i % 2])

        gather.middle()
        gather.ready(0)
        load(0).start()
        for i in range(TEAM):
            if i < TEAM - 1:
                gather.ready(i + 1)
                load(i + 1).start()
            load(i).wait()
            product = dot(held[i], g[i % 2], TN)
            total[...] = product if i == 0 else total[...] + product
            if i == 4:
                for stage in range(3, planes):
                    line.stage(stage)
        grad_ref[...] = total[...].astype(BF16)
        gather.sent()
        line.finish()


def expand(h_two, w_both, out_grad, down, planes, cid):
    seqs, rows, _ = h_two.shape
    width = w_both.shape[1]
    return pl.pallas_call(
        functools.partial(expand_kernel, planes),
        grid=(seqs,),
        in_specs=[per_seq(rows, D), ANY, VMEM, VMEM],
        out_specs=[per_seq(rows, width), per_seq(rows, width // 2), whole(width // 2, D), ANY, ANY],
        out_shape=[
            jax.ShapeDtypeStruct((seqs, rows, width), F32),
            jax.ShapeDtypeStruct((seqs, rows, width // 2), BF16),
            jax.ShapeDtypeStruct((width // 2, D), BF16),
            jax.ShapeDtypeStruct((seqs, rows, D), BF16),
            jax.ShapeDtypeStruct((planes,) + down.shape, BF16),
        ],
        scratch_shapes=[
            pltpu.VMEM((seqs, rows, width // 2), BF16),
            pltpu.VMEM((2, rows, D), BF16),
            pltpu.VMEM((width // 2, D), F32),
            pltpu.VMEM((D, width), BF16),
        ]
        + Gather.sems
        + LineGather.sems(planes)
        + [pltpu.SemaphoreType.DMA((2,)), pltpu.SemaphoreType.DMA],
        cost_estimate=lasting(55),
        compiler_params=params(cid),
    )(h_two, w_both, out_grad, down)


def mlp_back_kernel(
    pre_ref, g_all_ref, h_ref, wd_ref, w_ref, resid_ref, g_ref, gain_ref, _,
    out_ref, sums_ref, block_ref, grad_w_ref,
    pre, g_all, turned, made, grads, away, w, resid, own_grad, *scratch,
):
    pre_sem, g_sem, turned_sem, made_sem, late_sem = scratch[11:]
    total = Sum(None, scratch[:4], scratch[4:11], away)
    rows, ff = pre_ref.shape[1], wd_ref.shape[0]
    chunk = turned.shape[2]

    def loads(i):
        slot, at = lax.rem(i, 2), TEAM - 1 - i
        return (
            pltpu.make_async_copy(pre_ref.at[at], pre.at[slot], pre_sem.at[slot]),
            pltpu.make_async_copy(g_all_ref.at[at], g_all.at[slot], g_sem.at[slot]),
        )

    def load_chunk(i):
        slot = lax.rem(i, 2)
        columns = pl.ds(pl.multiple_of(i * chunk, chunk), chunk)
        return pltpu.make_async_copy(h_ref.at[:, columns], turned.at[slot], turned_sem.at[slot])

    def store_chunk(i):
        slot = lax.rem(i, 2)
        part = pl.ds(pl.multiple_of(i * chunk, chunk), chunk)
        return pltpu.make_async_copy(made.at[slot], grad_w_ref.at[part, :], made_sem.at[slot])

    for copy in loads(0):
        copy.start()
    late = [
        pltpu.make_async_copy(src, dst, late_sem.at[i])
        for i, (src, dst) in enumerate(((w_ref, w), (resid_ref, resid), (g_ref, own_grad)))
    ]
    for copy in late:
        copy.start()
    greet(total.near)

    @pl.loop(0, TEAM)
    def _(i):
        slot = lax.rem(i, 2)
        k, at = 3 - i // 2, TEAM - 1 - i

        @pl.when(i < TEAM - 1)
        def _():
            for copy in loads(i + 1):
                copy.start()

        for copy in loads(i):
            copy.wait()
        grad_hidden = dot(g_all[slot], wd_ref[...], NT)
        gate_pre, up_pre = pre[slot, :, :ff], pre[slot, :, ff:]
        sigmoid = jax.nn.sigmoid(gate_pre)
        grad_gate = grad_hidden * up_pre * sigmoid * (1.0 + gate_pre * (1.0 - sigmoid))
        grad_up = grad_hidden * (gate_pre * sigmoid)
        part = pl.ds(pl.multiple_of(at * rows, rows), rows)
        grads[part, :] = jnp.concatenate([grad_gate, grad_up], axis=1).astype(BF16)

        def make(to):
            to[k] = dot(grads[part, :], w[...], NT).astype(BF16)

        pl.when(i == 0)(late[0].wait)

        @pl.when(lax.rem(i, 2) == 0)
        def _():
            make(away)
            total.near_copy(k).start()

        @pl.when(lax.rem(i, 2) == 1)
        def _():
            make(total.own)

        for step, advance in ((1, total.middle_a), (3, total.middle_b), (5, total.middle_c)):
            pl.when(i == step)(advance)

    load_chunk(0).start()
    total.middle_two()
    chunks = h_ref.shape[1] // chunk

    @pl.loop(0, chunks)
    def _(i):
        slot = lax.rem(i, 2)

        @pl.when(i < chunks - 1)
        def _():
            load_chunk(i + 1).start()

        load_chunk(i).wait()

        @pl.when(i >= 2)
        def _():
            store_chunk(i - 2).wait()

        made[slot] = dot(turned[slot], grads[...], TN).astype(BF16)
        store_chunk(i).start()

    sums_ref[...] = jnp.zeros_like(sums_ref)
    for copy in late[1:]:
        copy.wait()

    def use(rows, value):
        normed, inverse = normalize(resid[rows, :])
        sums_ref[:8, :] += fold(value * normed)
        sums_ref[8:, :] += fold(value)
        grad = own_grad[rows, :].astype(F32) + norm_back(value * gain_ref[...], normed, inverse)
        out_ref[rows, :] = grad
        block_ref[rows, :] = grad.astype(BF16)

    total.finish(use)
    store_chunk(chunks - 2).wait()
    store_chunk(chunks - 1).wait()


def mlp_back(pre, g_all, h_two, w_down, w_both, resid, out_grad, gain, after, cid):
    seqs, rows, both = pre.shape
    width = resid.shape[1]
    chunk = 256
    two = pltpu.SemaphoreType.DMA((2,))
    return pl.pallas_call(
        mlp_back_kernel,
        out_shape=[
            jax.ShapeDtypeStruct((rows, width), F32),
            jax.ShapeDtypeStruct((16, width), F32),
            jax.ShapeDtypeStruct((rows, width), BF16),
            jax.ShapeDtypeStruct((width, both), BF16),
        ],
        in_specs=[ANY, ANY, ANY, VMEM, ANY, ANY, ANY, VMEM, ANY],
        out_specs=[VMEM, VMEM, VMEM, ANY],
        scratch_shapes=[
            pltpu.VMEM((2, rows, both), F32),
            pltpu.VMEM((2, rows, width), BF16),
            pltpu.VMEM((2, seqs * rows, chunk), BF16),
            pltpu.VMEM((2, chunk, both), BF16),
            pltpu.VMEM((seqs * rows, both), BF16),
            pltpu.VMEM((4, rows, width), BF16),
            pltpu.VMEM((width, both), BF16),
            pltpu.VMEM((rows, width), F32),
            pltpu.VMEM((rows, width), BF16),
        ]
        + Sum.scratch(rows, width)
        + Sum.sems
        + [two] * 4
        + [pltpu.SemaphoreType.DMA((3,))],
        cost_estimate=lasting(60),
        compiler_params=params(cid, 50),
    )(pre, g_all, h_two, w_down, w_both, resid, out_grad, gain, after)


def share(x, sums, bias, planes, per, depth):
    mine = place()[0]
    x[...] = jnp.zeros_like(x)
    sums = [jnp.sum(v, axis=0, keepdims=True) for v in sums]
    for z in range(planes):
        for i in range(TEAM):
            at = (z * TEAM + i) * depth
            for row, v in enumerate(sums):
                x[i, z, row : row + 1, :depth] = v[:, at : at + depth]
    for part in range(3):
        for z in range(planes):
            head = part * HEADS + z * TEAM + mine
            owner = head // per
            at = (part * planes + z) * HEAD_DIM
            x[lax.rem(owner, TEAM), owner // TEAM, pl.ds(4 + lax.rem(head, per), 1), :depth] = bias[:, at : at + HEAD_DIM]


def last_kernel(
    planes, part_ref, x_ref, gain_ref, both_ref, branch_ref, sums_two_ref, bias_ref, _,
    out_ref, held_ref, far_ref, vector_ref, sums, shared, got, *scratch,
):
    total, swap = Sum(part_ref, scratch[:4], scratch[4:11]), Swap(both_ref, held_ref, scratch[11:14])
    line, inner = Line(planes, branch_ref, far_ref, scratch[14:17]), Swap(shared, got, scratch[17:])
    greet(swap.near + line.near)
    total.start()
    line.start()
    total.middle()
    swap.start()
    total.middle_two()
    sums[...] = jnp.zeros_like(sums)

    def use(rows, value):
        normed, inverse = normalize(x_ref[rows, :].astype(F32))
        sums[:8, :] += fold(value * normed)
        sums[8:, :] += fold(value)
        out_ref[rows, :] = norm_back(value * gain_ref[...], normed, inverse)

    total.finish(use)
    vectors = [sums[:8, :], sums[8:, :], sums_two_ref[:8, :], sums_two_ref[8:, :]]
    depth = part_ref.shape[2] // (planes * TEAM)
    share(shared, vectors, added(bias_ref), planes, bias_ref.shape[2] // (planes * depth), depth)
    inner.start()
    inner.finish()
    vector_ref[...] = added(got)
    swap.finish()
    line.finish()


def last(part, inputs, gain, both, branch, sums_two, bias, after, cid):
    rows, width = inputs.shape
    planes = branch.shape[0]
    vectors = (TEAM, planes, 8, 128)
    return pl.pallas_call(
        functools.partial(last_kernel, planes),
        out_shape=[
            jax.ShapeDtypeStruct((rows, width), F32),
            jax.ShapeDtypeStruct(both.shape, BF16),
            jax.ShapeDtypeStruct(branch.shape, BF16),
            jax.ShapeDtypeStruct(vectors[1:], F32),
        ],
        in_specs=[ANY, VMEM, VMEM, VMEM, VMEM, VMEM, VMEM, ANY],
        out_specs=[VMEM, ANY, ANY, VMEM],
        scratch_shapes=[pltpu.VMEM((16, width), F32)]
        + [pltpu.VMEM(vectors, F32)] * 2
        + Sum.scratch(rows, width)
        + Sum.sems
        + Swap.sems
        + Line.sems(planes)
        + Swap.sems,
        cost_estimate=lasting(58),
        compiler_params=params(cid),
    )(part, inputs, gain, both, branch, sums_two, bias, after)


def dot(a, b, dims=((1,), (0,))):
    return lax.dot_general(a, b, (dims, ((), ())), preferred_element_type=F32)


NT = ((1,), (1,))
TN = ((0,), (0,))


def normalize(stream):
    average = jnp.mean(stream, axis=-1, keepdims=True)
    centered = stream - average
    variance = jnp.mean(centered * centered, axis=-1, keepdims=True)
    inverse = lax.rsqrt(variance + EPS)
    return centered * inverse, inverse


def norm_back(grad_norm, normed, inverse):
    return inverse * (
        grad_norm
        - jnp.mean(grad_norm, axis=-1, keepdims=True)
        - normed * jnp.mean(grad_norm * normed, axis=-1, keepdims=True)
    )


def turn(heads, cosine, sine):
    half, width = ROT // 2, heads.shape[-1]
    lanes = lax.broadcasted_iota(jnp.int32, heads.shape, 1) % HEAD_DIM
    moved = jnp.where(lanes < half, -pltpu.roll(heads, width - half, 1), pltpu.roll(heads, half, 1))
    return heads * cosine + moved * sine


def wide(table):
    return jnp.concatenate([table] * (LOCAL * HEAD_DIM // 128), axis=1)


def visible(start):
    size = start.shape[0]
    rows = lax.broadcasted_iota(jnp.int32, (size, size), 0)
    columns = lax.broadcasted_iota(jnp.int32, (size, size), 1)
    start = jnp.concatenate([start] * (size // start.shape[1]), axis=1)
    return (columns <= rows) & (columns.astype(F32) >= start)


def head_of(x, h):
    lanes = lax.broadcasted_iota(jnp.int32, x.shape, 1)
    return jnp.where((lanes >= h * HEAD_DIM) & (lanes < (h + 1) * HEAD_DIM), x, jnp.zeros_like(x))


def soft(query, key, allowed):
    scores = dot(query, key, NT) * 0.125
    masked = jnp.where(allowed, scores, -1e30)
    exponent = jnp.exp(masked - jnp.max(masked, axis=-1, keepdims=True))
    return exponent / jnp.sum(exponent, axis=-1, keepdims=True)


def attend_kernel(
    planes, x_ref, gain_ref, bias_ref, w_ref, b_ref, wo_ref, tab_ref, gain_two_ref, bias_two_ref, both_ref,
    h_ref, qkv_ref, attn_ref, resid_ref, h_two_ref, w_both_ref, block, away, *scratch,
):
    total, gather = Sum(None, scratch[:4], scratch[4:11], away), Gather(block, h_two_ref, scratch[11:18])
    line = LineGather(planes, both_ref, w_both_ref, scratch[18:])
    step = pl.program_id(0)

    @pl.when(step == 0)
    def _():
        greet(total.near + line.near)
        line.start()

    pl.when(step == TEAM - 2)(functools.partial(line.stage, 2))
    stream = x_ref[0].astype(F32)
    normed, _ = normalize(stream)
    h_one = (normed * gain_ref[...] + bias_ref[...]).astype(BF16)
    h_ref[0] = h_one
    qkv = dot(h_one, w_ref[...]) + b_ref[...]
    width = LOCAL * HEAD_DIM
    cosine, sine = wide(tab_ref[0, 0]), wide(tab_ref[0, 1])
    query = turn(qkv[:, :width], cosine, sine).astype(BF16)
    key = turn(qkv[:, width : 2 * width], cosine, sine).astype(BF16)
    value = qkv[:, 2 * width :].astype(BF16)
    qkv_ref[0, :, :width] = query
    qkv_ref[0, :, width : 2 * width] = key
    qkv_ref[0, :, 2 * width :] = value
    allowed = visible(tab_ref[0, 2])
    mixed = jnp.zeros((query.shape[0], width), F32)
    for h in range(LOCAL):
        probs = soft(head_of(query, h), key, allowed).astype(BF16)
        mixed = mixed + dot(probs, head_of(value, h))
    attn_low = mixed.astype(BF16)
    attn_ref[0] = attn_low
    part = dot(attn_low, wo_ref[...]).astype(BF16)
    k = 3 - step // 2

    @pl.when(lax.rem(step, 2) == 0)
    def _():
        away[k] = part
        total.near_copy(k).start()

    @pl.when(lax.rem(step, 2) == 1)
    def _():
        total.own[k] = part

    for at, advance in ((1, total.middle_a), (3, total.middle_b), (5, total.middle_c), (6, total.middle_two)):
        pl.when(step == at)(advance)

    def use(rows, value):
        resid = x_ref[0, rows, :].astype(F32) + value
        resid_ref[rows, :] = resid
        normed, _ = normalize(resid)
        block[rows, :] = (normed * gain_two_ref[...] + bias_two_ref[...]).astype(BF16)

    @pl.when(step == TEAM - 1)
    def _():
        total.finish(use)
        gather.start()
        for stage in range(3, planes):
            line.stage(stage)
        gather.middle()
        gather.finish()
        line.finish()


def per_seq(*shape):
    return pl.BlockSpec((1,) + shape, lambda s: (s,) + (0,) * len(shape))


def whole(*shape):
    return pl.BlockSpec(shape, lambda s: (0,) * len(shape))


def attend(x_all, gain, bias, w_qkv, b_qkv, w_out, tables, gain_two, bias_two, both, planes, cid):
    seqs, rows, _ = x_all.shape
    width = LOCAL * HEAD_DIM

    def far_first(*shape):
        return pl.BlockSpec((1,) + shape, lambda s: (seqs - 1 - s,) + (0,) * len(shape))

    return pl.pallas_call(
        functools.partial(attend_kernel, planes),
        grid=(seqs,),
        in_specs=[
            far_first(rows, D),
            whole(1, D),
            whole(1, D),
            whole(D, 3 * width),
            whole(1, 3 * width),
            whole(width, D),
            far_first(3, rows, 128),
            whole(1, D),
            whole(1, D),
            VMEM,
        ],
        out_specs=[far_first(rows, D), far_first(rows, 3 * width), far_first(rows, width), whole(rows, D), ANY, ANY],
        out_shape=[
            jax.ShapeDtypeStruct((seqs, rows, D), BF16),
            jax.ShapeDtypeStruct((seqs, rows, 3 * width), BF16),
            jax.ShapeDtypeStruct((seqs, rows, width), BF16),
            jax.ShapeDtypeStruct((rows, D), F32),
            jax.ShapeDtypeStruct((seqs, rows, D), BF16),
            jax.ShapeDtypeStruct((planes,) + both.shape, BF16),
        ],
        scratch_shapes=[pltpu.VMEM((rows, D), BF16), pltpu.VMEM((4, rows, D), BF16)]
        + Sum.scratch(rows, D)
        + Sum.sems
        + Gather.sems
        + LineGather.sems(planes),
        cost_estimate=lasting(100),
        compiler_params=params(cid),
    )(x_all, gain, bias, w_qkv, b_qkv, w_out, tables, gain_two, bias_two, both)


def attend_back_kernel(
    block_ref, wo_ref, w_ref, qkv_ref, tab_ref, attn_ref, down_ref, resid_ref, _,
    gqkv_ref, part_ref, gb_ref, wo_grad_ref, out_ref, held, wo_grad, *scratch,
):
    gather, block = Gather(block_ref, held, scratch[:7]), Sum(down_ref, scratch[7:11], scratch[11:])
    step = pl.program_id(0)

    @pl.when(step == 0)
    def _():
        greet(gather.near)
        gather.start()
        block.start()
        wo_grad[...] = jnp.zeros_like(wo_grad)

    for i in range(TEAM):
        pl.when(step == i)(functools.partial(gather.ready, i))
    grad = held[step]
    width = LOCAL * HEAD_DIM
    wo_grad[...] += dot(attn_ref[0], grad, TN)
    grad_att = dot(grad, wo_ref[...], NT).astype(BF16)
    query, key, value = (qkv_ref[0, :, i * width : (i + 1) * width] for i in range(3))
    allowed = visible(tab_ref[0, 2])
    zero = jnp.zeros((query.shape[0], width), F32)
    grad_query, grad_key, grad_value = zero, zero, zero
    for h in range(LOCAL):
        query_h, key_h, grad_h = head_of(query, h), head_of(key, h), head_of(grad_att, h)
        probs = soft(query_h, key, allowed)
        low = probs.astype(BF16)
        grad_probs = dot(grad_h, value, NT)
        delta = jnp.sum(low.astype(F32) * grad_probs, axis=-1, keepdims=True)
        grad_scores = (probs * (grad_probs - delta)).astype(BF16)
        grad_value = grad_value + dot(low, grad_h, TN)
        grad_query = grad_query + dot(grad_scores, key_h)
        grad_key = grad_key + dot(grad_scores, query_h, TN)
    cosine, sine = wide(tab_ref[0, 0]), -wide(tab_ref[0, 1])
    grad_query = turn(grad_query * 0.125, cosine, sine)
    grad_key = turn(grad_key * 0.125, cosine, sine)
    grad_qkv = jnp.concatenate([grad_query, grad_key, grad_value], axis=1).astype(BF16)
    gqkv_ref[0] = grad_qkv
    gb_ref[0] = jnp.sum(grad_qkv.astype(F32), axis=0, keepdims=True)
    part_ref[0] = dot(grad_qkv, w_ref[...], NT).astype(BF16)

    def use(rows, value):
        out_ref[rows, :] = resid_ref[rows, :] + value

    pl.when(step == 1)(gather.middle)
    pl.when(step == 3)(block.middle)
    pl.when(step == 6)(block.middle_two)

    @pl.when(step == TEAM - 1)
    def _():
        wo_grad_ref[...] = wo_grad[...].astype(BF16)
        block.finish(use)
        gather.sent()


def attend_back(block, w_out, w_qkv, qkv, tables, attn, down, resid, after, cid):
    seqs, rows, _ = qkv.shape
    width = LOCAL * HEAD_DIM
    return pl.pallas_call(
        attend_back_kernel,
        grid=(seqs,),
        in_specs=[
            ANY,
            whole(width, D),
            whole(D, 3 * width),
            per_seq(rows, 3 * width),
            per_seq(3, rows, 128),
            per_seq(rows, width),
            ANY,
            whole(rows, D),
            ANY,
        ],
        out_specs=[per_seq(rows, 3 * width), per_seq(rows, D), per_seq(1, 3 * width), whole(width, D), whole(rows, D)],
        out_shape=[
            jax.ShapeDtypeStruct((seqs, rows, 3 * width), BF16),
            jax.ShapeDtypeStruct((seqs, rows, D), BF16),
            jax.ShapeDtypeStruct((seqs, 1, 3 * width), F32),
            jax.ShapeDtypeStruct((width, D), BF16),
            jax.ShapeDtypeStruct((rows, D), F32),
        ],
        scratch_shapes=[pltpu.VMEM((seqs, rows, D), BF16), pltpu.VMEM((width, D), F32)]
        + Gather.sems
        + Sum.scratch(rows, D)
        + Sum.sems,
        cost_estimate=lasting(65),
        compiler_params=params(cid),
    )(block, w_out, w_qkv, qkv, tables, attn, down, resid, after)


def team_shards(
    inputs, positions, norm1_gain, norm1_bias, qkv_weight, qkv_bias, out_weight, norm2_gain, norm2_bias,
    gate_weight, up_weight, down_weight, out_grad,
):
    n = lax.axis_size("fsdp")
    planes = n // TEAM
    rows = inputs.shape[0]
    tokens = TEAM * rows
    depth = qkv_weight.shape[0]
    ff = down_weight.shape[0]
    width = LOCAL * HEAD_DIM
    lines = [[z * TEAM + i for z in range(planes)] for i in range(TEAM)]
    mine = lax.rem(lax.axis_index("fsdp"), TEAM)

    def line_sum(x):
        return lax.psum_scatter(x, "fsdp", scatter_dimension=0, tiled=True, axis_index_groups=lines)

    w_out = lax.all_gather(out_weight, "fsdp", axis=0, tiled=True, axis_index_groups=lines)
    pieces = opening(qkv_weight, planes, 0)
    pieces = pieces.reshape(TEAM * depth, 3 * width)
    small = jnp.stack([norm1_gain, norm1_bias, norm2_gain, norm2_bias])
    small = jnp.concatenate([small, qkv_bias.reshape(-1, depth)])
    small = jnp.pad(small, ((0, 16 - small.shape[0]), (0, 128 - depth)))
    places = jnp.pad(positions.reshape(-1, 128).astype(BF16), ((0, 16 - rows // 128), (0, 0)))
    half = ROT // 2
    rate = 10000.0 ** (-np.arange(half) / half)
    rate = np.tile(np.concatenate([rate, rate, np.zeros(HEAD_DIM - ROT)]), 128 // HEAD_DIM)[None].astype(np.float32)
    both, x_all, w_qkv, tables, norms, b_qkv = second(
        gate_weight, up_weight, inputs, small, places, pieces, jnp.asarray(rate), planes, 1
    )
    w_qkv = w_qkv.reshape(D, 3 * width)
    gain_one, bias_one, gain_two, bias_two = (norms[i : i + 1] for i in range(4))
    both = both.reshape(TEAM * depth, 2 * planes * ff)
    h_one, qkv, attn_low, resid, h_two, w_both = attend(
        x_all, gain_one, bias_one, w_qkv, b_qkv, w_out, tables, gain_two, bias_two, both, planes, 2
    )
    w_both = w_both.reshape(D, 2 * planes * ff)
    pre, hidden, grad_down, g_all, w_down = expand(h_two, w_both, out_grad, down_weight, planes, 3)
    hidden, w_down = hidden.reshape(tokens, planes * ff), w_down.reshape(planes * ff, D)
    grad_resid, sums_two, block, grad_w_both = mlp_back(
        pre, g_all, h_two.reshape(tokens, D), w_down, w_both, resid, out_grad, gain_two, grad_down, 5
    )
    grad_down = line_sum(grad_down)
    grad_w_both = line_sum(grad_w_both)
    down = dot(hidden, w_down).astype(BF16).reshape(TEAM, rows, D)
    grad_qkv, part, grad_bias, grad_out, block_out = attend_back(
        block, w_out, w_qkv, qkv, tables, attn_low, down, resid, grad_down, 6
    )
    grad_qkv = grad_qkv.reshape(tokens, 3 * width)
    grad_w_qkv = dot(h_one.reshape(tokens, D), grad_qkv, TN).astype(BF16)
    part, grad_w_qkv, grad_w_both = lax.optimization_barrier((part, grad_w_qkv, grad_w_both))
    blocks = grad_w_both.reshape(TEAM, depth, 2 * planes * ff)
    branch = grad_out.reshape(planes, depth, D)
    norm_part, blocks, branch, shared = last(
        part, inputs, gain_one, blocks, branch, sums_two, grad_bias, grad_w_qkv, 7
    )
    grad_w_qkv = line_sum(grad_w_qkv)
    block_out, input_grad = block_out.astype(BF16), grad_resid + norm_part
    grad_gate_w, grad_up_w = both_grads(blocks, planes)
    blocks = grad_w_qkv.reshape(TEAM, depth, 3 * width)
    blocks, sums = closing(blocks, shared, (input_grad, grad_up_w), 8)
    grad_w_qkv, grad_out = rest_grads(blocks, branch)

    return (
        block_out,
        input_grad,
        sums[0, :depth],
        sums[1, :depth],
        grad_w_qkv,
        sums[4 : 4 + qkv_bias.shape[0] // depth, :depth].reshape(-1),
        grad_out,
        sums[2, :depth],
        sums[3, :depth],
        grad_gate_w,
        grad_up_w,
        grad_down.astype(F32),
    )


def rotate_pairs(heads, places, sign):
    half_rot = ROT // 2
    frequency = 10000.0 ** (-jnp.arange(half_rot, dtype=jnp.float32) / half_rot)
    angles = places.astype(jnp.float32)[:, None] * frequency[None, :]
    cosine = jnp.cos(angles)[:, None, :]
    sine_part = sign * jnp.sin(angles)[:, None, :]
    front_part = heads[..., :half_rot]
    back_part = heads[..., half_rot:ROT]
    return jnp.concatenate(
        [
            front_part * cosine - back_part * sine_part,
            back_part * cosine + front_part * sine_part,
            heads[..., ROT:],
        ],
        axis=-1,
    )


def by_groups(heads):
    group_heads = min(8, HEADS)
    shaped = heads.reshape(heads.shape[0], HEADS // group_heads, group_heads, HEAD_DIM)
    return jnp.moveaxis(shaped, 1, 0)


def from_groups(grouped):
    return jnp.moveaxis(grouped, 0, 1).reshape(grouped.shape[1], HEADS, HEAD_DIM)


def plain_group(block_items, allowed):
    query_part, key_part, value_part = block_items
    scores = (
        jnp.einsum("qhd,khd->hqk", query_part, key_part, preferred_element_type=jnp.float32) * 0.125
    )
    masked = jnp.where(allowed[None], scores, -1e30)
    row_max = jnp.max(masked, axis=-1, keepdims=True)
    exponent = jnp.exp(masked - row_max)
    row_total = jnp.sum(exponent, axis=-1, keepdims=True)
    soft_probs = (exponent / row_total).astype(jnp.bfloat16)
    mixed_part = jnp.einsum(
        "hqk,khd->qhd", soft_probs, value_part, preferred_element_type=jnp.float32
    )
    return (mixed_part, (row_max + jnp.log(row_total))[..., 0])


def plain_back(block_items, allowed):
    query_part, key_part, value_part, grad_part, row_delta, log_total = block_items
    scores = (
        jnp.einsum("qhd,khd->hqk", query_part, key_part, preferred_element_type=jnp.float32) * 0.125
    )
    soft_probs = jnp.where(allowed[None], jnp.exp(scores - log_total[..., None]), 0.0)
    grad_probs = jnp.einsum(
        "qhd,khd->hqk", grad_part, value_part.astype(jnp.float32), precision=lax.Precision.HIGHEST
    )
    rounded_probs = soft_probs.astype(jnp.bfloat16).astype(jnp.float32)
    grad_value = jnp.einsum("hqk,qhd->khd", rounded_probs, grad_part, precision=lax.Precision.HIGHEST)
    grad_scores = (soft_probs * (grad_probs - row_delta[..., None])).astype(jnp.bfloat16)
    grad_query = 0.125 * jnp.einsum(
        "hqk,khd->qhd", grad_scores, key_part, preferred_element_type=jnp.float32
    )
    grad_key = 0.125 * jnp.einsum(
        "hqk,qhd->khd", grad_scores, query_part, preferred_element_type=jnp.float32
    )
    return (grad_query, grad_key, grad_value)


def shards(
    inputs,
    positions,
    norm1_gain,
    norm1_bias,
    qkv_weight,
    qkv_bias,
    out_weight,
    norm2_gain,
    norm2_bias,
    gate_weight,
    up_weight,
    down_weight,
    out_grad,
):
    tok_rows = inputs.shape[0]
    gain_one, bias_one, w_qkv, b_qkv, w_out = (
        lax.all_gather(norm1_gain, "fsdp", axis=0, tiled=True),
        lax.all_gather(norm1_bias, "fsdp", axis=0, tiled=True),
        lax.all_gather(qkv_weight, "fsdp", axis=0, tiled=True),
        lax.all_gather(qkv_bias, "fsdp", axis=0, tiled=True),
        lax.all_gather(out_weight, "fsdp", axis=0, tiled=True),
    )
    stream = inputs.astype(jnp.float32)
    normed_one, inverse_one = normalize(stream)
    h_one = (normed_one * gain_one.astype(jnp.float32) + bias_one.astype(jnp.float32)).astype(
        jnp.bfloat16
    )
    qkv_pre = jnp.dot(h_one, w_qkv, preferred_element_type=jnp.float32) + b_qkv.astype(jnp.float32)
    qkv_heads = qkv_pre.reshape(tok_rows, 3, HEADS, HEAD_DIM)
    query_low = rotate_pairs(qkv_heads[:, 0], positions, 1.0).astype(jnp.bfloat16)
    key_all = rotate_pairs(qkv_heads[:, 1], positions, 1.0).astype(jnp.bfloat16)
    value_all = qkv_heads[:, 2].astype(jnp.bfloat16)
    token_index = jnp.arange(tok_rows, dtype=jnp.int32)
    allowed = (token_index[None, :] <= token_index[:, None]) & (
        token_index[None, :] >= (token_index - positions)[:, None]
    )
    mixed_grouped, log_grouped = lax.map(
        lambda block_items: plain_group(block_items, allowed),
        (by_groups(query_low), by_groups(key_all), by_groups(value_all)),
    )
    mixed_heads = from_groups(mixed_grouped)
    attn_low = mixed_heads.reshape(tok_rows, D).astype(jnp.bfloat16)
    resid = stream + jnp.dot(attn_low, w_out, preferred_element_type=jnp.float32)
    gain_two, bias_two, w_gate, w_up, w_down = (
        lax.all_gather(norm2_gain, "fsdp", axis=0, tiled=True),
        lax.all_gather(norm2_bias, "fsdp", axis=0, tiled=True),
        lax.all_gather(gate_weight, "fsdp", axis=0, tiled=True),
        lax.all_gather(up_weight, "fsdp", axis=0, tiled=True),
        lax.all_gather(down_weight, "fsdp", axis=0, tiled=True),
    )
    normed_two, inverse_two = normalize(resid)
    h_two = (normed_two * gain_two.astype(jnp.float32) + bias_two.astype(jnp.float32)).astype(
        jnp.bfloat16
    )
    gate_pre = jnp.dot(h_two, w_gate, preferred_element_type=jnp.float32)
    up_pre = jnp.dot(h_two, w_up, preferred_element_type=jnp.float32)
    sigmoid_gate = jax.nn.sigmoid(gate_pre)
    silu_gate = gate_pre * sigmoid_gate
    hidden = (silu_gate * up_pre).astype(jnp.bfloat16)
    block_out = (resid + jnp.dot(hidden, w_down, preferred_element_type=jnp.float32)).astype(
        jnp.bfloat16
    )
    gain_two, w_gate, w_up, w_down = (
        lax.all_gather(norm2_gain, "fsdp", axis=0, tiled=True),
        lax.all_gather(gate_weight, "fsdp", axis=0, tiled=True),
        lax.all_gather(up_weight, "fsdp", axis=0, tiled=True),
        lax.all_gather(down_weight, "fsdp", axis=0, tiled=True),
    )
    grad_down_w = jnp.einsum("tf,td->fd", hidden, out_grad, preferred_element_type=jnp.float32)
    grad_hidden = jnp.einsum("td,fd->tf", out_grad, w_down, preferred_element_type=jnp.float32)
    grad_gate = (
        grad_hidden * up_pre * sigmoid_gate * (1.0 + gate_pre * (1.0 - sigmoid_gate))
    ).astype(jnp.bfloat16)
    grad_up = (grad_hidden * silu_gate).astype(jnp.bfloat16)
    grad_gate_w = jnp.einsum("td,tf->df", h_two, grad_gate, preferred_element_type=jnp.float32)
    grad_up_w = jnp.einsum("td,tf->df", h_two, grad_up, preferred_element_type=jnp.float32)
    grad_htwo = jnp.einsum(
        "tf,df->td", grad_gate, w_gate, preferred_element_type=jnp.float32
    ) + jnp.einsum("tf,df->td", grad_up, w_up, preferred_element_type=jnp.float32)
    grad_gain_two = jnp.sum(grad_htwo * normed_two, axis=0)
    grad_bias_two = jnp.sum(grad_htwo, axis=0)
    grad_resid = out_grad.astype(jnp.float32) + norm_back(
        grad_htwo * gain_two.astype(jnp.float32), normed_two, inverse_two
    )
    mlp_sums = (
        lax.psum_scatter(grad_gain_two, "fsdp", scatter_dimension=0, tiled=True),
        lax.psum_scatter(grad_bias_two, "fsdp", scatter_dimension=0, tiled=True),
        lax.psum_scatter(grad_gate_w, "fsdp", scatter_dimension=0, tiled=True),
        lax.psum_scatter(grad_up_w, "fsdp", scatter_dimension=0, tiled=True),
        lax.psum_scatter(grad_down_w, "fsdp", scatter_dimension=0, tiled=True),
    )
    gain_one, w_qkv, w_out = (
        lax.all_gather(norm1_gain, "fsdp", axis=0, tiled=True),
        lax.all_gather(qkv_weight, "fsdp", axis=0, tiled=True),
        lax.all_gather(out_weight, "fsdp", axis=0, tiled=True),
    )
    grad_branch = grad_resid.astype(jnp.bfloat16)
    grad_out_w = jnp.einsum("ti,td->id", attn_low, grad_branch, preferred_element_type=jnp.float32)
    grad_att = jnp.einsum(
        "td,id->ti", grad_branch, w_out, preferred_element_type=jnp.float32
    ).reshape(tok_rows, HEADS, HEAD_DIM)
    group_heads = min(8, HEADS)
    row_delta = jnp.sum(grad_att * mixed_heads, axis=-1)
    delta_grouped = row_delta.reshape(tok_rows, HEADS // group_heads, group_heads).transpose(
        1, 2, 0
    )
    query_grouped, key_grouped, value_grouped = lax.map(
        lambda block_items: plain_back(block_items, allowed),
        (
            by_groups(query_low),
            by_groups(key_all),
            by_groups(value_all),
            by_groups(grad_att),
            delta_grouped,
            log_grouped,
        ),
    )
    grad_query = from_groups(query_grouped)
    grad_key = from_groups(key_grouped)
    grad_value = from_groups(value_grouped)
    grad_qkv = (
        jnp.stack(
            [
                rotate_pairs(grad_query, positions, -1.0),
                rotate_pairs(grad_key, positions, -1.0),
                grad_value,
            ],
            axis=1,
        )
        .reshape(tok_rows, 3 * D)
        .astype(jnp.bfloat16)
    )
    grad_qkv_w = jnp.einsum("td,tk->dk", h_one, grad_qkv, preferred_element_type=jnp.float32)
    grad_qkv_b = jnp.sum(grad_qkv.astype(jnp.float32), axis=0)
    grad_hone = jnp.einsum("tk,dk->td", grad_qkv, w_qkv, preferred_element_type=jnp.float32)
    grad_gain_one = jnp.sum(grad_hone * normed_one, axis=0)
    grad_bias_one = jnp.sum(grad_hone, axis=0)
    input_grad = grad_resid + norm_back(
        grad_hone * gain_one.astype(jnp.float32), normed_one, inverse_one
    )
    attn_sums = (
        lax.psum_scatter(grad_gain_one, "fsdp", scatter_dimension=0, tiled=True),
        lax.psum_scatter(grad_bias_one, "fsdp", scatter_dimension=0, tiled=True),
        lax.psum_scatter(grad_qkv_w, "fsdp", scatter_dimension=0, tiled=True),
        lax.psum_scatter(grad_qkv_b, "fsdp", scatter_dimension=0, tiled=True),
        lax.psum_scatter(grad_out_w, "fsdp", scatter_dimension=0, tiled=True),
    )
    return (
        block_out,
        input_grad,
        attn_sums[0],
        attn_sums[1],
        attn_sums[2],
        attn_sums[3],
        attn_sums[4],
        mlp_sums[0],
        mlp_sums[1],
        mlp_sums[2],
        mlp_sums[3],
        mlp_sums[4],
    )


def solution(mesh):
    devices = mesh.shape["fsdp"]
    rows, columns = P("fsdp", None), P("fsdp")
    body = team_shards if devices % TEAM == 0 and D == devices * HEAD_DIM else shards
    return jax.shard_map(
        body,
        mesh=mesh,
        in_specs=(rows, columns, columns, columns, rows, columns, rows, columns, columns, rows, rows, rows, rows),
        out_specs=(rows, rows, columns, columns, rows, columns, rows, columns, columns, rows, rows, rows),
        check_vma=False,
    )
```

```python
import functools

import jax
import jax.numpy as jnp
import numpy as np
from jax import lax
from jax.experimental import pallas as pl
from jax.experimental.pallas import tpu as pltpu
from jax.sharding import PartitionSpec as P

D = 2048
HEADS = 32
HEAD_DIM = 64
ROT = 16
EPS = 1e-05
TEAM = 8
LOCAL = HEADS // TEAM
MESH = pl.DeviceIdType.MESH
BF16 = jnp.bfloat16
F32 = jnp.float32
ANY = pl.BlockSpec(memory_space=pl.ANY)
VMEM = pl.BlockSpec(memory_space=pltpu.VMEM)


def lasting(us):
    return pl.CostEstimate(flops=0, bytes_accessed=int(us * 3.6e6), transcendentals=0)


def params(cid=None, limit=56):
    extra = {} if cid is None else {"collective_id": cid, "has_side_effects": True}
    return pltpu.CompilerParams(vmem_limit_bytes=limit * 1024 * 1024, **extra)


def place():
    me = lax.axis_index("fsdp")
    mine = lax.rem(me, TEAM)
    return mine, me - mine, mine // 2, lax.rem(mine, 2)


def chip_at(chip, step):
    along_x, along_y = lax.rem(chip, 2), chip // 2
    if step & 1:
        along_x = 1 - along_x
    if step & 2:
        along_y = 1 - along_y
    return along_y * 2 + along_x


def relation(chip, core, r):
    return chip_at(chip, r // 2) * 2 + lax.rem(core + r, 2)


def greet(devices):
    barrier = pltpu.get_barrier_semaphore()
    for device in devices:
        pl.semaphore_signal(barrier, inc=1, device_id=(device,), device_id_type=MESH)
    pl.semaphore_wait(barrier, len(devices))


def remote(src, dst, send, recv, device):
    return pltpu.make_async_remote_copy(
        src_ref=src, dst_ref=dst, send_sem=send, recv_sem=recv, device_id=(device,), device_id_type=MESH
    )


class Swap:
    sems = [pltpu.SemaphoreType.DMA, pltpu.SemaphoreType.DMA((TEAM,)), pltpu.SemaphoreType.DMA((TEAM,))]

    def __init__(self, src, out, sems, same=False, near_first=False):
        own_sem, send, recv = sems
        mine, base, chip, core = place()
        others = [relation(chip, core, r) for r in range(1, TEAM)]
        self.near = [base + other for other in others]
        self.copies = [
            remote(
                src if same else src.at[other], out.at[r if near_first else mine], send.at[r], recv.at[r], base + other
            )
            for r, other in enumerate(others, 1)
        ]
        own = src if same else src.at[mine]
        self.copies.append(pltpu.make_async_copy(own, out.at[0 if near_first else mine], own_sem))

    def start(self):
        for copy in self.copies:
            copy.start()

    def finish(self):
        for copy in self.copies:
            copy.wait()


class Line:
    def sems(planes):
        return [pltpu.SemaphoreType.DMA, pltpu.SemaphoreType.DMA((planes,)), pltpu.SemaphoreType.DMA((planes,))]

    def __init__(self, planes, src, out, sems, same=False, within=False):
        own_sem, send, recv = sems
        mine, base, _, _ = place()
        plane = base // TEAM
        others = [lax.rem(plane + k, planes) for k in range(1, planes)]
        self.near = [other * TEAM + mine for other in others]
        self.copies = [
            remote(src if same else src.at[other], out.at[plane], send.at[k], recv.at[k], other * TEAM + mine)
            for k, other in enumerate(others)
        ]
        own = src if same else src.at[plane]
        self.own = None if within else pltpu.make_async_copy(own, out.at[plane], own_sem)

    def start(self):
        for copy in self.copies:
            copy.start()
        if self.own is not None:
            self.own.start()

    def finish(self):
        for copy in self.copies:
            copy.wait()
        if self.own is not None:
            self.own.wait()


class LineGather:
    def sems(planes):
        return [pltpu.SemaphoreType.DMA, pltpu.SemaphoreType.DMA((2, planes)), pltpu.SemaphoreType.DMA((2, planes))]

    def __init__(self, planes, src, out, sems):
        own_sem, self.send, self.recv = sems
        mine, base, _, _ = place()
        self.plane, self.planes, self.src, self.out = base // TEAM, planes, src, out
        self.me = base + mine
        self.near = [lax.rem(self.plane + k, planes) * TEAM + mine for k in (1, planes - 1)]
        self.own = pltpu.make_async_copy(src, out.at[self.plane], own_sem)

    def copy(self, way, stage):
        step = 1 - 2 * way
        block, to = self.plane - step * (stage - 1), self.plane + step
        is_there = (block >= 0) & (block < self.planes) & (to >= 0) & (to < self.planes)
        src = self.src if stage == 1 else self.out.at[block]
        sems = self.send.at[way, stage], self.recv.at[way, stage]
        return is_there, remote(src, self.out.at[block], *sems, self.me + step * TEAM)

    def arrived(self, way, stage):
        block = self.plane - (1 - 2 * way) * stage

        @pl.when((block >= 0) & (block < self.planes))
        def _():
            dst = self.out.at[block]
            remote(dst, dst, self.send.at[way, stage], self.recv.at[way, stage], self.me).wait_recv()

    def start(self):
        self.own.start()
        self.stage(1)

    def stage(self, stage):
        for way in (0, 1):
            if stage > 1:
                self.arrived(way, stage - 1)
            is_there, copy = self.copy(way, stage)
            pl.when(is_there)(copy.start)

    def finish(self):
        self.own.wait()
        for way in (0, 1):
            self.arrived(way, self.planes - 1)
            for stage in range(1, self.planes):
                is_there, copy = self.copy(way, stage)
                pl.when(is_there)(copy.wait_send)


def slices(ref, pieces, size):
    return jnp.concatenate([ref[:, i * size : (i + 1) * size] for i in pieces], axis=1)


def opening_kernel(
    planes, qkv_ref, gate_ref, up_ref, x_ref, out_weight_ref, small_ref, place_ref, rate_ref,
    pieces_ref, x_all_ref, w_qkv_ref, w_out_ref, tab_ref, norm_ref, b_ref, cut, landed, made, all_ref, places_ref, tables, *sems,
):
    mine, base, _, _ = place()
    plane = base // TEAM
    swap, gather = Swap(made, pieces_ref, sems[:3]), Gather(x_ref, x_all_ref, sems[3:10])
    vectors = Swap(small_ref, all_ref.at[plane], sems[10:13], same=True)
    places = Swap(place_ref, places_ref, sems[13:16], same=True, near_first=True)
    line = Line(planes, all_ref.at[plane], all_ref, sems[16:19], same=True, within=True)
    rows, heads = LineGather(planes, landed, w_qkv_ref, sems[19:22]), Swap(cut, landed, sems[22:25])
    outs = LineGather(planes, out_weight_ref, w_out_ref, sems[25:28])
    for i in range(TEAM):
        cut[i] = slices(qkv_ref, [s * HEADS + z * TEAM + i for s in range(3) for z in range(planes)], HEAD_DIM)
    greet(swap.near + line.near)
    outs.start()
    heads.start()
    vectors.start()
    places.start()
    size = gate_ref.shape[1] // (planes * TEAM)
    for i in range(TEAM):
        units = [z * TEAM + i for z in range(planes)]
        made[i] = jnp.concatenate([slices(gate_ref, units, size), slices(up_ref, units, size)], axis=1)
    outs.stage(2)
    heads.finish()
    rows.start()
    gather.start()
    swap.start()
    vectors.finish()
    line.start()
    for stage in range(3, planes):
        outs.stage(stage)
    places.finish()
    square = (128, 128)

    @pl.loop(0, TEAM)
    def _(i):
        known = places_ref[i].astype(F32)
        for part in range(tables.shape[2] // 128):
            at = jnp.transpose(jnp.broadcast_to(known[part : part + 1, :], square))
            here = pl.ds(part * 128, 128)
            angle = at * rate_ref[...]
            tables[i, 0, here, :] = jnp.cos(angle)
            tables[i, 1, here, :] = jnp.sin(angle)
            token = lax.broadcasted_iota(jnp.int32, square, 0) + part * 128
            tables[i, 2, here, :] = token.astype(F32) - at

    store = pltpu.make_async_copy(tables, tab_ref, sems[28])
    store.start()
    rows.stage(2)
    gather.middle()
    for stage in range(3, planes):
        rows.stage(stage)
    line.finish()
    depth = gate_ref.shape[0]
    each = [all_ref[z, i].astype(F32) for z in range(planes) for i in range(TEAM)]
    for i in range(4):
        norm_ref[i : i + 1, :] = jnp.concatenate([known[i : i + 1, :depth] for known in each], axis=1)
    per = qkv_ref.shape[1] // (planes * TEAM * depth)
    bias = []
    for part in range(3):
        for z in range(planes):
            head = part * HEADS + z * TEAM + mine
            known = all_ref[head // per // TEAM, lax.rem(head // per, TEAM)].astype(F32)
            row = lax.broadcasted_iota(jnp.int32, known.shape, 0) == 4 + lax.rem(head, per)
            bias.append(jnp.sum(jnp.where(row, known, 0.0), axis=0, keepdims=True)[:, :depth])
    b_ref[...] = jnp.concatenate(bias, axis=1)
    gather.finish()
    swap.finish()
    rows.finish()
    outs.finish()
    store.wait()


def opening(qkv, gate, up, inputs, out_weight, small, positions, rate, planes, cid):
    shape = (TEAM, gate.shape[0], 2 * gate.shape[1] // TEAM)
    heads = (TEAM, qkv.shape[0], qkv.shape[1] // TEAM)
    tables = (TEAM, 3, inputs.shape[0], 128)
    return pl.pallas_call(
        functools.partial(opening_kernel, planes),
        out_shape=[
            jax.ShapeDtypeStruct(shape, BF16),
            jax.ShapeDtypeStruct((TEAM,) + inputs.shape, BF16),
            jax.ShapeDtypeStruct((planes,) + heads, BF16),
            jax.ShapeDtypeStruct((planes,) + out_weight.shape, BF16),
            jax.ShapeDtypeStruct(tables, F32),
            jax.ShapeDtypeStruct((4, inputs.shape[1]), F32),
            jax.ShapeDtypeStruct((1, heads[2]), F32),
        ],
        in_specs=[VMEM] * 8,
        out_specs=[ANY] * 5 + [VMEM] * 2,
        scratch_shapes=[
            pltpu.VMEM(heads, BF16),
            pltpu.VMEM(heads, BF16),
            pltpu.VMEM(shape, BF16),
            pltpu.VMEM((planes, TEAM) + small.shape, BF16),
            pltpu.VMEM((TEAM,) + positions.shape, BF16),
            pltpu.VMEM(tables, F32),
        ]
        + Swap.sems
        + Gather.sems
        + Swap.sems * 2
        + Line.sems(planes)
        + LineGather.sems(planes)
        + Swap.sems
        + LineGather.sems(planes)
        + [pltpu.SemaphoreType.DMA],
        cost_estimate=lasting(80),
        compiler_params=params(cid),
    )(qkv, gate, up, inputs, out_weight, small, positions, rate)


def unslice(held, parts, planes, outs):
    size = held.shape[2] // (parts * planes)
    for at in range(parts * planes):
        row = jnp.concatenate([held[i, :, at * size : (at + 1) * size] for i in range(TEAM)], axis=1)
        out, first = (outs[at // planes], at % planes) if len(outs) > 1 else (outs[0], at)
        out[:, first * TEAM * size : (first + 1) * TEAM * size] = row.astype(F32)


def first_kernel(planes, held_ref, far_ref, gate_ref, up_ref, wo_ref):
    unslice(held_ref, 2, planes, [gate_ref, up_ref])
    wo_ref[...] = added(far_ref)


def first_grads(held, far):
    _, depth, width = held.shape
    return pl.pallas_call(
        functools.partial(first_kernel, far.shape[0]),
        out_shape=[jax.ShapeDtypeStruct((depth, width * TEAM // 2), F32)] * 2
        + [jax.ShapeDtypeStruct(far.shape[1:], F32)],
        in_specs=[VMEM] * 2,
        out_specs=[VMEM] * 3,
        cost_estimate=lasting(4),
        compiler_params=params(),
    )(held, far)


def rest_kernel(planes, held_ref, w_ref):
    unslice(held_ref, 3, planes, [w_ref])


def rest_grads(held, planes):
    _, depth, width = held.shape
    return pl.pallas_call(
        functools.partial(rest_kernel, planes),
        out_shape=jax.ShapeDtypeStruct((depth, width * TEAM), F32),
        in_specs=[VMEM],
        out_specs=VMEM,
        cost_estimate=lasting(3),
        compiler_params=params(),
    )(held)


def added(ref):
    total = ref[0].astype(F32)
    for i in range(1, ref.shape[0]):
        total = total + ref[i].astype(F32)
    return total


def close_kernel(w_ref, _, __, ___, held_ref, *sems):
    swap = Swap(w_ref, held_ref, sems)
    greet(swap.near)
    swap.start()
    swap.finish()


def closing(blocks, after, cid):
    return pl.pallas_call(
        close_kernel,
        out_shape=jax.ShapeDtypeStruct(blocks.shape, BF16),
        in_specs=[VMEM, ANY, ANY, ANY],
        out_specs=ANY,
        scratch_shapes=Swap.sems,
        cost_estimate=lasting(14),
        compiler_params=params(cid),
    )(blocks, *after)


class Gather:
    sems = [pltpu.SemaphoreType.DMA((5,)), pltpu.SemaphoreType.DMA((5,)), pltpu.SemaphoreType.DMA((2,)),
            pltpu.SemaphoreType.DMA((2,)), pltpu.SemaphoreType.DMA((6,)), pltpu.SemaphoreType.DMA((6,)),
            pltpu.SemaphoreType.DMA]

    def __init__(self, src, out, sems):
        send, recv, hop_send, hop_recv, pass_send, pass_recv, own_sem = sems
        _, base, chip, core = place()
        side, over = (chip_at(chip, k) * 2 + core for k in (1, 2))
        self.sibling = base + chip * 2 + 1 - core
        self.near = [base + side, base + over, self.sibling]
        half = src.shape[0] // 2
        top, low = pl.ds(0, half), pl.ds(half, half)
        self.first = [
            remote(src.at[part], out.at[at, part], send.at[i], recv.at[i], base + to)
            for i, (part, at, to) in enumerate(((top, 2, side), (low, 4, over), (low, 2, side), (top, 4, over)))
        ]
        self.first.append(remote(src, out.at[1], send.at[4], recv.at[4], self.sibling))
        self.own = pltpu.make_async_copy(src, out.at[0], own_sem)
        self.hops = [
            remote(out.at[at, part], out.at[6, part], hop_send.at[i], hop_recv.at[i], base + to)
            for i, (at, part, to) in enumerate(((2, top, over), (4, low, side)))
        ]
        self.passed = [
            remote(out.at[at, part], out.at[at + 1, part], pass_send.at[i], pass_recv.at[i], self.sibling)
            for i, (at, part) in enumerate(((2, top), (4, low), (2, low), (4, top), (6, top), (6, low)))
        ]

    def start(self):
        for copy in self.first:
            copy.start()
        self.own.start()

    def middle(self):
        for i in (0, 1):
            self.first[i].wait_recv()
            self.hops[i].start()
            self.passed[i].start()

    def finish(self):
        for i in range(2, TEAM):
            self.ready(i)
        self.first[4].wait_recv()
        self.own.wait()
        self.sent()

    def ready(self, i):
        if i == 0:
            self.own.wait()
        elif i == 1:
            self.first[4].wait_recv()
        elif i == 6:
            for j in (0, 1):
                self.hops[j].wait_recv()
                self.passed[4 + j].start()
        elif i % 2 == 0:
            self.first[1 + i // 2].wait_recv()
            self.passed[1 + i // 2].start()
        else:
            for j in {3: (0, 2), 5: (1, 3), 7: (4, 5)}[i]:
                self.passed[j].wait_recv()

    def sent(self):
        for copy in self.first + self.hops + self.passed:
            copy.wait_send()


class Sum:
    def scratch(rows, width):
        return [pltpu.VMEM((4, rows, width), BF16), pltpu.VMEM((4, rows, width), BF16),
                pltpu.VMEM((2, rows // 2, width), BF16), pltpu.VMEM((2, rows, width), BF16)]

    sems = [pltpu.SemaphoreType.DMA((4,))] * 3 + [pltpu.SemaphoreType.DMA((2,))] * 2 + [pltpu.SemaphoreType.DMA((4,))] * 2

    def __init__(self, blocks, scratch, sems, away=None):
        self.own, self.beside, self.via, self.far = scratch
        load_sem, near_send, near_recv, via_send, via_recv, far_send, far_recv = sems
        _, base, chip, core = place()
        sibling = base + chip * 2 + 1 - core
        side, over = (base + chip_at(chip, k) * 2 + core for k in (1, 2))
        self.near = [side, over, sibling]
        self.half = self.own.shape[1] // 2
        top, low = pl.ds(0, self.half), pl.ds(self.half, self.half)
        self.loads = [
            pltpu.make_async_copy(blocks.at[2 * k], self.own.at[k], load_sem.at[k])
            for k in range(4)
            if away is None
        ]

        def near_copy(k):
            src = blocks.at[2 * k + 1] if away is None else away.at[k]
            return remote(src, self.beside.at[k], near_send.at[k], near_recv.at[k], sibling)

        self.near_copy = near_copy
        self.nears = [near_copy(k) for k in range(4)]
        self.vias = [
            remote(self.own.at[3, part], self.via.at[i], via_send.at[i], via_recv.at[i], to)
            for i, (part, to) in enumerate(((top, side), (low, over)))
        ]
        self.fars = [
            remote(self.own.at[k, part], self.far.at[k - 1, part], far_send.at[i], far_recv.at[i], to)
            for i, (k, part, to) in enumerate(((2, low, over), (1, top, side), (2, top, over), (1, low, side)))
        ]

    def start(self):
        for k in (3, 2, 1, 0):
            self.loads[k].start()
            self.nears[k].start()

    def pair(self, k):
        if self.loads:
            self.loads[k].wait()
        self.nears[k].wait_recv()

        @pl.loop(0, self.own.shape[1] // 16)
        def _(i):
            part = pl.ds(pl.multiple_of(i * 16, 16), 16)
            self.own[k, part, :] = (self.own[k, part, :].astype(F32) + self.beside[k, part, :].astype(F32)).astype(BF16)

    def middle_a(self):
        self.pair(3)
        for copy in self.vias:
            copy.start()

    def middle_b(self):
        self.pair(2)
        self.fars[0].start()

    def middle_c(self):
        self.pair(1)
        self.fars[1].start()

    def middle(self):
        self.middle_a()
        self.middle_b()
        self.middle_c()

    def middle_two(self):
        for i, k in ((0, 2), (1, 1)):
            self.vias[i].wait_recv()

            @pl.loop(0, self.half // 16)
            def _(j, i=i, k=k):
                part = pl.ds(pl.multiple_of(j * 16, 16), 16)
                at = pl.ds(pl.multiple_of(j * 16 + i * self.half, 16), 16)
                self.own[k, at, :] = (self.own[k, at, :].astype(F32) + self.via[i, part, :].astype(F32)).astype(BF16)

            self.fars[2 + i].start()

    def finish(self, use):
        if self.loads:
            self.loads[0].wait()
        self.nears[0].wait_recv()
        for copy in self.fars:
            copy.wait_recv()

        @pl.loop(0, self.own.shape[1] // 16)
        def _(i):
            part = pl.ds(pl.multiple_of(i * 16, 16), 16)
            total = self.own[0, part, :].astype(F32) + self.beside[0, part, :].astype(F32)
            use(part, total + self.far[0, part, :].astype(F32) + self.far[1, part, :].astype(F32))

        for copy in self.nears + self.vias + self.fars:
            copy.wait_send()


def fold(x):
    return x[:8] + x[8:]


def expand_kernel(
    planes, h_ref, w_ref, g_ref, down_ref, pre_ref, hidden_ref, grad_ref, g_all_ref, wd_ref, held, g, total, w, *sems
):
    gather, line = Gather(g_ref, g_all_ref, sems[:7]), LineGather(planes, down_ref, wd_ref, sems[7:10])
    step = pl.program_id(0)

    @pl.when(step == 0)
    def _():
        greet(gather.near + line.near)
        line.start()
        gather.start()
        weights = pltpu.make_async_copy(w_ref, w, sems[11])
        weights.start()
        weights.wait()

    pre = dot(h_ref[0], w[...])
    pre_ref[0] = pre
    ff = hidden_ref.shape[2]
    gate_pre, up_pre = pre[:, :ff], pre[:, ff:]
    hidden = (gate_pre * jax.nn.sigmoid(gate_pre) * up_pre).astype(BF16)
    hidden_ref[0] = hidden
    held[step] = hidden
    pl.when(step == TEAM - 2)(functools.partial(line.stage, 2))

    @pl.when(step == TEAM - 1)
    def _():
        def load(i):
            return pltpu.make_async_copy(g_all_ref.at[i], g.at[i % 2], sems[10].at[i % 2])

        gather.middle()
        gather.ready(0)
        load(0).start()
        for i in range(TEAM):
            if i < TEAM - 1:
                gather.ready(i + 1)
                load(i + 1).start()
            load(i).wait()
            product = dot(held[i], g[i % 2], TN)
            total[...] = product if i == 0 else total[...] + product
            if i == 4:
                for stage in range(3, planes):
                    line.stage(stage)
        grad_ref[...] = total[...].astype(BF16)
        gather.sent()
        line.finish()


def expand(h_two, w_both, out_grad, down, planes, cid):
    seqs, rows, _ = h_two.shape
    width = w_both.shape[1]
    return pl.pallas_call(
        functools.partial(expand_kernel, planes),
        grid=(seqs,),
        in_specs=[per_seq(rows, D), ANY, VMEM, VMEM],
        out_specs=[per_seq(rows, width), per_seq(rows, width // 2), whole(width // 2, D), ANY, ANY],
        out_shape=[
            jax.ShapeDtypeStruct((seqs, rows, width), F32),
            jax.ShapeDtypeStruct((seqs, rows, width // 2), BF16),
            jax.ShapeDtypeStruct((width // 2, D), BF16),
            jax.ShapeDtypeStruct((seqs, rows, D), BF16),
            jax.ShapeDtypeStruct((planes,) + down.shape, BF16),
        ],
        scratch_shapes=[
            pltpu.VMEM((seqs, rows, width // 2), BF16),
            pltpu.VMEM((2, rows, D), BF16),
            pltpu.VMEM((width // 2, D), F32),
            pltpu.VMEM((D, width), BF16),
        ]
        + Gather.sems
        + LineGather.sems(planes)
        + [pltpu.SemaphoreType.DMA((2,)), pltpu.SemaphoreType.DMA],
        cost_estimate=lasting(55),
        compiler_params=params(cid),
    )(h_two, w_both, out_grad, down)


def mlp_back_kernel(
    pre_ref, g_all_ref, h_ref, wd_ref, w_ref, resid_ref, g_ref, norm_ref, _,
    out_ref, sums_ref, block_ref, grad_w_ref,
    pre, g_all, turned, made, grads, away, w, resid, own_grad, *scratch,
):
    pre_sem, g_sem, turned_sem, made_sem, late_sem = scratch[11:]
    total = Sum(None, scratch[:4], scratch[4:11], away)
    rows, ff = pre_ref.shape[1], wd_ref.shape[0]
    chunk = turned.shape[2]

    def loads(i):
        slot, at = lax.rem(i, 2), TEAM - 1 - i
        return (
            pltpu.make_async_copy(pre_ref.at[at], pre.at[slot], pre_sem.at[slot]),
            pltpu.make_async_copy(g_all_ref.at[at], g_all.at[slot], g_sem.at[slot]),
        )

    def load_chunk(i):
        slot = lax.rem(i, 2)
        columns = pl.ds(pl.multiple_of(i * chunk, chunk), chunk)
        return pltpu.make_async_copy(h_ref.at[:, columns], turned.at[slot], turned_sem.at[slot])

    def store_chunk(i):
        slot = lax.rem(i, 2)
        part = pl.ds(pl.multiple_of(i * chunk, chunk), chunk)
        return pltpu.make_async_copy(made.at[slot], grad_w_ref.at[part, :], made_sem.at[slot])

    for copy in loads(0):
        copy.start()
    late = [
        pltpu.make_async_copy(src, dst, late_sem.at[i])
        for i, (src, dst) in enumerate(((w_ref, w), (resid_ref, resid), (g_ref, own_grad)))
    ]
    for copy in late:
        copy.start()
    greet(total.near)

    @pl.loop(0, TEAM)
    def _(i):
        slot = lax.rem(i, 2)
        k, at = 3 - i // 2, TEAM - 1 - i

        @pl.when(i < TEAM - 1)
        def _():
            for copy in loads(i + 1):
                copy.start()

        for copy in loads(i):
            copy.wait()
        grad_hidden = dot(g_all[slot], wd_ref[...], NT)
        gate_pre, up_pre = pre[slot, :, :ff], pre[slot, :, ff:]
        sigmoid = jax.nn.sigmoid(gate_pre)
        grad_gate = grad_hidden * up_pre * sigmoid * (1.0 + gate_pre * (1.0 - sigmoid))
        grad_up = grad_hidden * (gate_pre * sigmoid)
        part = pl.ds(pl.multiple_of(at * rows, rows), rows)
        grads[part, :] = jnp.concatenate([grad_gate, grad_up], axis=1).astype(BF16)

        def make(to):
            to[k] = dot(grads[part, :], w[...], NT).astype(BF16)

        pl.when(i == 0)(late[0].wait)

        @pl.when(lax.rem(i, 2) == 0)
        def _():
            make(away)
            total.near_copy(k).start()

        @pl.when(lax.rem(i, 2) == 1)
        def _():
            make(total.own)

        for step, advance in ((1, total.middle_a), (3, total.middle_b), (5, total.middle_c)):
            pl.when(i == step)(advance)

    load_chunk(0).start()
    total.middle_two()
    chunks = h_ref.shape[1] // chunk

    @pl.loop(0, chunks)
    def _(i):
        slot = lax.rem(i, 2)

        @pl.when(i < chunks - 1)
        def _():
            load_chunk(i + 1).start()

        load_chunk(i).wait()

        @pl.when(i >= 2)
        def _():
            store_chunk(i - 2).wait()

        made[slot] = dot(turned[slot], grads[...], TN).astype(BF16)
        store_chunk(i).start()

    sums_ref[...] = jnp.zeros_like(sums_ref)
    for copy in late[1:]:
        copy.wait()

    def use(rows, value):
        normed, inverse = normalize(resid[rows, :])
        sums_ref[:8, :] += fold(value * normed)
        sums_ref[8:, :] += fold(value)
        grad = own_grad[rows, :].astype(F32) + norm_back(value * norm_ref[2:3, :], normed, inverse)
        out_ref[rows, :] = grad
        block_ref[rows, :] = grad.astype(BF16)

    total.finish(use)
    store_chunk(chunks - 2).wait()
    store_chunk(chunks - 1).wait()


def mlp_back(pre, g_all, h_two, w_down, w_both, resid, out_grad, gain, after, cid):
    seqs, rows, both = pre.shape
    width = resid.shape[1]
    chunk = 256
    two = pltpu.SemaphoreType.DMA((2,))
    return pl.pallas_call(
        mlp_back_kernel,
        out_shape=[
            jax.ShapeDtypeStruct((rows, width), F32),
            jax.ShapeDtypeStruct((16, width), F32),
            jax.ShapeDtypeStruct((rows, width), BF16),
            jax.ShapeDtypeStruct((width, both), BF16),
        ],
        in_specs=[ANY, ANY, ANY, VMEM, ANY, ANY, ANY, VMEM, ANY],
        out_specs=[VMEM, VMEM, VMEM, ANY],
        scratch_shapes=[
            pltpu.VMEM((2, rows, both), F32),
            pltpu.VMEM((2, rows, width), BF16),
            pltpu.VMEM((2, seqs * rows, chunk), BF16),
            pltpu.VMEM((2, chunk, both), BF16),
            pltpu.VMEM((seqs * rows, both), BF16),
            pltpu.VMEM((4, rows, width), BF16),
            pltpu.VMEM((width, both), BF16),
            pltpu.VMEM((rows, width), F32),
            pltpu.VMEM((rows, width), BF16),
        ]
        + Sum.scratch(rows, width)
        + Sum.sems
        + [two] * 4
        + [pltpu.SemaphoreType.DMA((3,))],
        cost_estimate=lasting(60),
        compiler_params=params(cid, 50),
    )(pre, g_all, h_two, w_down, w_both, resid, out_grad, gain, after)


def share(x, sums, bias, planes, per, depth):
    mine = place()[0]
    x[...] = jnp.zeros_like(x)
    sums = [jnp.sum(v, axis=0, keepdims=True) for v in sums]
    for z in range(planes):
        for i in range(TEAM):
            at = (z * TEAM + i) * depth
            for row, v in enumerate(sums):
                x[i, z, row : row + 1, :depth] = v[:, at : at + depth]
    for part in range(3):
        for z in range(planes):
            head = part * HEADS + z * TEAM + mine
            owner = head // per
            at = (part * planes + z) * HEAD_DIM
            x[lax.rem(owner, TEAM), owner // TEAM, pl.ds(4 + lax.rem(head, per), 1), :depth] = bias[:, at : at + HEAD_DIM]


def last_kernel(
    planes, part_ref, x_ref, norm_ref, both_ref, branch_ref, sums_two_ref, bias_ref, _,
    out_ref, held_ref, far_ref, vector_ref, sums, shared, got, block, beyond, *scratch,
):
    total, swap = Sum(part_ref, scratch[:4], scratch[4:11]), Swap(both_ref, held_ref, scratch[11:14])
    line, inner = Line(planes, branch_ref, far_ref, scratch[14:17]), Swap(shared, got, scratch[17:20])
    outer = Line(planes, block, beyond, scratch[20:])
    greet(swap.near + line.near)
    total.start()
    line.start()
    total.middle()
    total.middle_two()
    swap.start()
    sums[...] = jnp.zeros_like(sums)

    def use(rows, value):
        normed, inverse = normalize(x_ref[rows, :].astype(F32))
        sums[:8, :] += fold(value * normed)
        sums[8:, :] += fold(value)
        out_ref[rows, :] = norm_back(value * norm_ref[0:1, :], normed, inverse)

    total.finish(use)
    vectors = [sums[:8, :], sums[8:, :], sums_two_ref[:8, :], sums_two_ref[8:, :]]
    depth = part_ref.shape[2] // (planes * TEAM)
    share(shared, vectors, added(bias_ref), planes, bias_ref.shape[2] // (planes * depth), depth)
    inner.start()
    inner.finish()
    block[...] = added(got)
    outer.start()
    outer.finish()
    vector_ref[...] = added(beyond)
    swap.finish()
    line.finish()


def last(part, inputs, gain, both, branch, sums_two, bias, after, cid):
    rows, width = inputs.shape
    planes = branch.shape[0]
    vectors = (TEAM, planes, 8, 128)
    return pl.pallas_call(
        functools.partial(last_kernel, planes),
        out_shape=[
            jax.ShapeDtypeStruct((rows, width), F32),
            jax.ShapeDtypeStruct(both.shape, BF16),
            jax.ShapeDtypeStruct(branch.shape, BF16),
            jax.ShapeDtypeStruct(vectors[2:], F32),
        ],
        in_specs=[ANY, VMEM, VMEM, VMEM, VMEM, VMEM, VMEM, ANY],
        out_specs=[VMEM, ANY, ANY, VMEM],
        scratch_shapes=[pltpu.VMEM((16, width), F32)]
        + [pltpu.VMEM(vectors, F32)] * 2
        + [pltpu.VMEM(vectors[1:], F32)] * 2
        + Sum.scratch(rows, width)
        + Sum.sems
        + Swap.sems
        + Line.sems(planes)
        + Swap.sems
        + Line.sems(planes),
        cost_estimate=lasting(58),
        compiler_params=params(cid),
    )(part, inputs, gain, both, branch, sums_two, bias, after)


def dot(a, b, dims=((1,), (0,))):
    return lax.dot_general(a, b, (dims, ((), ())), preferred_element_type=F32)


NT = ((1,), (1,))
TN = ((0,), (0,))


def normalize(stream):
    average = jnp.mean(stream, axis=-1, keepdims=True)
    centered = stream - average
    variance = jnp.mean(centered * centered, axis=-1, keepdims=True)
    inverse = lax.rsqrt(variance + EPS)
    return centered * inverse, inverse


def norm_back(grad_norm, normed, inverse):
    return inverse * (
        grad_norm
        - jnp.mean(grad_norm, axis=-1, keepdims=True)
        - normed * jnp.mean(grad_norm * normed, axis=-1, keepdims=True)
    )


def turn(heads, cosine, sine):
    half, width = ROT // 2, heads.shape[-1]
    lanes = lax.broadcasted_iota(jnp.int32, heads.shape, 1) % HEAD_DIM
    moved = jnp.where(lanes < half, -pltpu.roll(heads, width - half, 1), pltpu.roll(heads, half, 1))
    return heads * cosine + moved * sine


def wide(table):
    return jnp.concatenate([table] * (LOCAL * HEAD_DIM // 128), axis=1)


def visible(start):
    size = start.shape[0]
    rows = lax.broadcasted_iota(jnp.int32, (size, size), 0)
    columns = lax.broadcasted_iota(jnp.int32, (size, size), 1)
    start = jnp.concatenate([start] * (size // start.shape[1]), axis=1)
    return (columns <= rows) & (columns.astype(F32) >= start)


def head_of(x, h):
    lanes = lax.broadcasted_iota(jnp.int32, x.shape, 1)
    return jnp.where((lanes >= h * HEAD_DIM) & (lanes < (h + 1) * HEAD_DIM), x, jnp.zeros_like(x))


def soft(query, key, allowed):
    scores = dot(query, key, NT) * 0.125
    masked = jnp.where(allowed, scores, -1e30)
    exponent = jnp.exp(masked - jnp.max(masked, axis=-1, keepdims=True))
    return exponent / jnp.sum(exponent, axis=-1, keepdims=True)


def attend_kernel(
    planes, x_ref, norm_ref, w_ref, b_ref, wo_ref, tab_ref, both_ref,
    h_ref, qkv_ref, attn_ref, resid_ref, h_two_ref, w_both_ref, block, away, w, *scratch,
):
    total, gather = Sum(None, scratch[:4], scratch[4:11], away), Gather(block, h_two_ref, scratch[11:18])
    line = LineGather(planes, both_ref, w_both_ref, scratch[18:21])
    step = pl.program_id(0)

    @pl.when(step == 0)
    def _():
        greet(total.near + line.near)
        line.start()
        weights = pltpu.make_async_copy(w_ref, w, scratch[21])
        weights.start()
        weights.wait()

    pl.when(step == TEAM - 2)(functools.partial(line.stage, 2))
    stream = x_ref[0].astype(F32)
    normed, _ = normalize(stream)
    h_one = (normed * norm_ref[0:1, :] + norm_ref[1:2, :]).astype(BF16)
    h_ref[0] = h_one
    qkv = dot(h_one, w[...]) + b_ref[...]
    width = LOCAL * HEAD_DIM
    cosine, sine = wide(tab_ref[0, 0]), wide(tab_ref[0, 1])
    query = turn(qkv[:, :width], cosine, sine).astype(BF16)
    key = turn(qkv[:, width : 2 * width], cosine, sine).astype(BF16)
    value = qkv[:, 2 * width :].astype(BF16)
    qkv_ref[0, :, :width] = query
    qkv_ref[0, :, width : 2 * width] = key
    qkv_ref[0, :, 2 * width :] = value
    allowed = visible(tab_ref[0, 2])
    mixed = jnp.zeros((query.shape[0], width), F32)
    for h in range(LOCAL):
        probs = soft(head_of(query, h), key, allowed).astype(BF16)
        mixed = mixed + dot(probs, head_of(value, h))
    attn_low = mixed.astype(BF16)
    attn_ref[0] = attn_low
    part = dot(attn_low, wo_ref[...]).astype(BF16)
    k = 3 - step // 2

    @pl.when(lax.rem(step, 2) == 0)
    def _():
        away[k] = part
        total.near_copy(k).start()

    @pl.when(lax.rem(step, 2) == 1)
    def _():
        total.own[k] = part

    for at, advance in ((1, total.middle_a), (3, total.middle_b), (5, total.middle_c), (6, total.middle_two)):
        pl.when(step == at)(advance)

    def use(rows, value):
        resid = x_ref[0, rows, :].astype(F32) + value
        resid_ref[rows, :] = resid
        normed, _ = normalize(resid)
        block[rows, :] = (normed * norm_ref[2:3, :] + norm_ref[3:4, :]).astype(BF16)

    @pl.when(step == TEAM - 1)
    def _():
        total.finish(use)
        gather.start()
        for stage in range(3, planes):
            line.stage(stage)
        gather.middle()
        gather.finish()
        line.finish()


def per_seq(*shape):
    return pl.BlockSpec((1,) + shape, lambda s: (s,) + (0,) * len(shape))


def whole(*shape):
    return pl.BlockSpec(shape, lambda s: (0,) * len(shape))


def attend(x_all, norms, w_qkv, b_qkv, w_out, tables, both, planes, cid):
    seqs, rows, _ = x_all.shape
    width = LOCAL * HEAD_DIM

    def far_first(*shape):
        return pl.BlockSpec((1,) + shape, lambda s: (seqs - 1 - s,) + (0,) * len(shape))

    return pl.pallas_call(
        functools.partial(attend_kernel, planes),
        grid=(seqs,),
        in_specs=[
            far_first(rows, D),
            whole(4, D),
            ANY,
            whole(1, 3 * width),
            whole(width, D),
            far_first(3, rows, 128),
            VMEM,
        ],
        out_specs=[far_first(rows, D), far_first(rows, 3 * width), far_first(rows, width), whole(rows, D), ANY, ANY],
        out_shape=[
            jax.ShapeDtypeStruct((seqs, rows, D), BF16),
            jax.ShapeDtypeStruct((seqs, rows, 3 * width), BF16),
            jax.ShapeDtypeStruct((seqs, rows, width), BF16),
            jax.ShapeDtypeStruct((rows, D), F32),
            jax.ShapeDtypeStruct((seqs, rows, D), BF16),
            jax.ShapeDtypeStruct((planes,) + both.shape, BF16),
        ],
        scratch_shapes=[
            pltpu.VMEM((rows, D), BF16),
            pltpu.VMEM((4, rows, D), BF16),
            pltpu.VMEM((D, 3 * width), BF16),
        ]
        + Sum.scratch(rows, D)
        + Sum.sems
        + Gather.sems
        + LineGather.sems(planes)
        + [pltpu.SemaphoreType.DMA],
        cost_estimate=lasting(100),
        compiler_params=params(cid),
    )(x_all, norms, w_qkv, b_qkv, w_out, tables, both)


def attend_back_kernel(
    block_ref, wo_ref, w_ref, qkv_ref, tab_ref, attn_ref, hidden_ref, wd_ref, resid_ref, _,
    gqkv_ref, part_ref, gb_ref, wo_grad_ref, out_ref, held, wo_grad, away, *scratch,
):
    gather, block = Gather(block_ref, held, scratch[:7]), Sum(None, scratch[7:11], scratch[11:], away)
    step = pl.program_id(0)

    @pl.when(step == 0)
    def _():
        greet(gather.near)
        gather.start()
        wo_grad[...] = jnp.zeros_like(wo_grad)

    part = dot(hidden_ref[0], wd_ref[...]).astype(BF16)
    k = 3 - step // 2

    @pl.when(lax.rem(step, 2) == 0)
    def _():
        away[k] = part
        block.near_copy(k).start()

    @pl.when(lax.rem(step, 2) == 1)
    def _():
        block.own[k] = part

    for i in range(TEAM):
        pl.when(step == i)(functools.partial(gather.ready, i))
    grad = held[step]
    width = LOCAL * HEAD_DIM
    wo_grad[...] += dot(attn_ref[0], grad, TN)
    grad_att = dot(grad, wo_ref[...], NT).astype(BF16)
    query, key, value = (qkv_ref[0, :, i * width : (i + 1) * width] for i in range(3))
    allowed = visible(tab_ref[0, 2])
    zero = jnp.zeros((query.shape[0], width), F32)
    grad_query, grad_key, grad_value = zero, zero, zero
    for h in range(LOCAL):
        query_h, key_h, grad_h = head_of(query, h), head_of(key, h), head_of(grad_att, h)
        probs = soft(query_h, key, allowed)
        low = probs.astype(BF16)
        grad_probs = dot(grad_h, value, NT)
        delta = jnp.sum(low.astype(F32) * grad_probs, axis=-1, keepdims=True)
        grad_scores = (probs * (grad_probs - delta)).astype(BF16)
        grad_value = grad_value + dot(low, grad_h, TN)
        grad_query = grad_query + dot(grad_scores, key_h)
        grad_key = grad_key + dot(grad_scores, query_h, TN)
    cosine, sine = wide(tab_ref[0, 0]), -wide(tab_ref[0, 1])
    grad_query = turn(grad_query * 0.125, cosine, sine)
    grad_key = turn(grad_key * 0.125, cosine, sine)
    grad_qkv = jnp.concatenate([grad_query, grad_key, grad_value], axis=1).astype(BF16)
    gqkv_ref[0] = grad_qkv
    gb_ref[0] = jnp.sum(grad_qkv.astype(F32), axis=0, keepdims=True)
    part_ref[0] = dot(grad_qkv, w_ref[...], NT).astype(BF16)

    def use(rows, value):
        out_ref[rows, :] = resid_ref[rows, :] + value

    pl.when(step == 1)(gather.middle)
    for at, advance in ((1, block.middle_a), (3, block.middle_b), (5, block.middle_c), (6, block.middle_two)):
        pl.when(step == at)(advance)

    @pl.when(step == TEAM - 1)
    def _():
        wo_grad_ref[...] = wo_grad[...].astype(BF16)
        block.finish(use)
        gather.sent()


def attend_back(block, w_out, w_qkv, qkv, tables, attn, hidden, w_down, resid, after, cid):
    seqs, rows, _ = qkv.shape
    width = LOCAL * HEAD_DIM

    def far_first(*shape):
        return pl.BlockSpec((1,) + shape, lambda s: (seqs - 1 - s,) + (0,) * len(shape))

    return pl.pallas_call(
        attend_back_kernel,
        grid=(seqs,),
        in_specs=[
            ANY,
            whole(width, D),
            whole(D, 3 * width),
            per_seq(rows, 3 * width),
            per_seq(3, rows, 128),
            per_seq(rows, width),
            far_first(rows, hidden.shape[2]),
            VMEM,
            VMEM,
            ANY,
        ],
        out_specs=[per_seq(rows, 3 * width), per_seq(rows, D), per_seq(1, 3 * width), whole(width, D), whole(rows, D)],
        out_shape=[
            jax.ShapeDtypeStruct((seqs, rows, 3 * width), BF16),
            jax.ShapeDtypeStruct((seqs, rows, D), BF16),
            jax.ShapeDtypeStruct((seqs, 1, 3 * width), F32),
            jax.ShapeDtypeStruct((width, D), BF16),
            jax.ShapeDtypeStruct((rows, D), F32),
        ],
        scratch_shapes=[
            pltpu.VMEM((seqs, rows, D), BF16),
            pltpu.VMEM((width, D), F32),
            pltpu.VMEM((4, rows, D), BF16),
        ]
        + Gather.sems
        + Sum.scratch(rows, D)
        + Sum.sems,
        cost_estimate=lasting(65),
        compiler_params=params(cid, 54),
    )(block, w_out, w_qkv, qkv, tables, attn, hidden, w_down, resid, after)


def team_shards(
    inputs, positions, norm1_gain, norm1_bias, qkv_weight, qkv_bias, out_weight, norm2_gain, norm2_bias,
    gate_weight, up_weight, down_weight, out_grad,
):
    n = lax.axis_size("fsdp")
    planes = n // TEAM
    rows = inputs.shape[0]
    tokens = TEAM * rows
    depth = qkv_weight.shape[0]
    ff = down_weight.shape[0]
    width = LOCAL * HEAD_DIM
    lines = [[z * TEAM + i for z in range(planes)] for i in range(TEAM)]
    mine = lax.rem(lax.axis_index("fsdp"), TEAM)

    def line_sum(x):
        return lax.psum_scatter(x, "fsdp", scatter_dimension=0, tiled=True, axis_index_groups=lines)

    small = jnp.stack([norm1_gain, norm1_bias, norm2_gain, norm2_bias])
    small = jnp.concatenate([small, qkv_bias.reshape(-1, depth)])
    small = jnp.pad(small, ((0, 16 - small.shape[0]), (0, 128 - depth)))
    places = jnp.pad(positions.reshape(-1, 128).astype(BF16), ((0, 16 - rows // 128), (0, 0)))
    half = ROT // 2
    rate = 10000.0 ** (-np.arange(half) / half)
    rate = np.tile(np.concatenate([rate, rate, np.zeros(HEAD_DIM - ROT)]), 128 // HEAD_DIM)[None].astype(np.float32)
    both, x_all, w_qkv, w_out, tables, norms, b_qkv = opening(
        qkv_weight, gate_weight, up_weight, inputs, out_weight, small, places, jnp.asarray(rate), planes, 1
    )
    w_out = w_out.reshape(width, D)
    w_qkv = w_qkv.reshape(D, 3 * width)
    both = both.reshape(TEAM * depth, 2 * planes * ff)
    h_one, qkv, attn_low, resid, h_two, w_both = attend(
        x_all, norms, w_qkv, b_qkv, w_out, tables, both, planes, 2
    )
    w_both = w_both.reshape(D, 2 * planes * ff)
    pre, hidden, grad_down, g_all, w_down = expand(h_two, w_both, out_grad, down_weight, planes, 3)
    w_down = w_down.reshape(planes * ff, D)
    grad_resid, sums_two, block, grad_w_both = mlp_back(
        pre, g_all, h_two.reshape(tokens, D), w_down, w_both, resid, out_grad, norms, grad_down, 5
    )
    grad_down = line_sum(grad_down)
    grad_w_both = line_sum(grad_w_both)
    grad_qkv, part, grad_bias, grad_out, block_out = attend_back(
        block, w_out, w_qkv, qkv, tables, attn_low, hidden, w_down, resid, grad_down, 6
    )
    grad_qkv = grad_qkv.reshape(tokens, 3 * width)
    grad_w_qkv = dot(h_one.reshape(tokens, D), grad_qkv, TN).astype(BF16)
    part, grad_w_qkv = lax.optimization_barrier((part, grad_w_qkv))
    blocks = grad_w_both.reshape(TEAM, depth, 2 * planes * ff)
    branch = grad_out.reshape(planes, depth, D)
    norm_part, blocks, branch, sums = last(
        part, inputs, norms, blocks, branch, sums_two, grad_bias, grad_w_qkv, 7
    )
    grad_w_qkv = line_sum(grad_w_qkv)
    block_out, input_grad = block_out.astype(BF16), grad_resid + norm_part
    grad_gate_w, grad_up_w, grad_out = first_grads(blocks, branch)
    blocks = closing(grad_w_qkv.reshape(TEAM, depth, 3 * width), (input_grad, grad_up_w, sums), 8)
    grad_w_qkv = rest_grads(blocks, planes)

    return (
        block_out,
        input_grad,
        sums[0, :depth],
        sums[1, :depth],
        grad_w_qkv,
        sums[4 : 4 + qkv_bias.shape[0] // depth, :depth].reshape(-1),
        grad_out,
        sums[2, :depth],
        sums[3, :depth],
        grad_gate_w,
        grad_up_w,
        grad_down.astype(F32),
    )


def rotate_pairs(heads, places, sign):
    half_rot = ROT // 2
    frequency = 10000.0 ** (-jnp.arange(half_rot, dtype=jnp.float32) / half_rot)
    angles = places.astype(jnp.float32)[:, None] * frequency[None, :]
    cosine = jnp.cos(angles)[:, None, :]
    sine_part = sign * jnp.sin(angles)[:, None, :]
    front_part = heads[..., :half_rot]
    back_part = heads[..., half_rot:ROT]
    return jnp.concatenate(
        [
            front_part * cosine - back_part * sine_part,
            back_part * cosine + front_part * sine_part,
            heads[..., ROT:],
        ],
        axis=-1,
    )


def by_groups(heads):
    group_heads = min(8, HEADS)
    shaped = heads.reshape(heads.shape[0], HEADS // group_heads, group_heads, HEAD_DIM)
    return jnp.moveaxis(shaped, 1, 0)


def from_groups(grouped):
    return jnp.moveaxis(grouped, 0, 1).reshape(grouped.shape[1], HEADS, HEAD_DIM)


def plain_group(block_items, allowed):
    query_part, key_part, value_part = block_items
    scores = (
        jnp.einsum("qhd,khd->hqk", query_part, key_part, preferred_element_type=jnp.float32) * 0.125
    )
    masked = jnp.where(allowed[None], scores, -1e30)
    row_max = jnp.max(masked, axis=-1, keepdims=True)
    exponent = jnp.exp(masked - row_max)
    row_total = jnp.sum(exponent, axis=-1, keepdims=True)
    soft_probs = (exponent / row_total).astype(jnp.bfloat16)
    mixed_part = jnp.einsum(
        "hqk,khd->qhd", soft_probs, value_part, preferred_element_type=jnp.float32
    )
    return (mixed_part, (row_max + jnp.log(row_total))[..., 0])


def plain_back(block_items, allowed):
    query_part, key_part, value_part, grad_part, row_delta, log_total = block_items
    scores = (
        jnp.einsum("qhd,khd->hqk", query_part, key_part, preferred_element_type=jnp.float32) * 0.125
    )
    soft_probs = jnp.where(allowed[None], jnp.exp(scores - log_total[..., None]), 0.0)
    grad_probs = jnp.einsum(
        "qhd,khd->hqk", grad_part, value_part.astype(jnp.float32), precision=lax.Precision.HIGHEST
    )
    rounded_probs = soft_probs.astype(jnp.bfloat16).astype(jnp.float32)
    grad_value = jnp.einsum("hqk,qhd->khd", rounded_probs, grad_part, precision=lax.Precision.HIGHEST)
    grad_scores = (soft_probs * (grad_probs - row_delta[..., None])).astype(jnp.bfloat16)
    grad_query = 0.125 * jnp.einsum(
        "hqk,khd->qhd", grad_scores, key_part, preferred_element_type=jnp.float32
    )
    grad_key = 0.125 * jnp.einsum(
        "hqk,qhd->khd", grad_scores, query_part, preferred_element_type=jnp.float32
    )
    return (grad_query, grad_key, grad_value)


def shards(
    inputs,
    positions,
    norm1_gain,
    norm1_bias,
    qkv_weight,
    qkv_bias,
    out_weight,
    norm2_gain,
    norm2_bias,
    gate_weight,
    up_weight,
    down_weight,
    out_grad,
):
    tok_rows = inputs.shape[0]
    gain_one, bias_one, w_qkv, b_qkv, w_out = (
        lax.all_gather(norm1_gain, "fsdp", axis=0, tiled=True),
        lax.all_gather(norm1_bias, "fsdp", axis=0, tiled=True),
        lax.all_gather(qkv_weight, "fsdp", axis=0, tiled=True),
        lax.all_gather(qkv_bias, "fsdp", axis=0, tiled=True),
        lax.all_gather(out_weight, "fsdp", axis=0, tiled=True),
    )
    stream = inputs.astype(jnp.float32)
    normed_one, inverse_one = normalize(stream)
    h_one = (normed_one * gain_one.astype(jnp.float32) + bias_one.astype(jnp.float32)).astype(
        jnp.bfloat16
    )
    qkv_pre = jnp.dot(h_one, w_qkv, preferred_element_type=jnp.float32) + b_qkv.astype(jnp.float32)
    qkv_heads = qkv_pre.reshape(tok_rows, 3, HEADS, HEAD_DIM)
    query_low = rotate_pairs(qkv_heads[:, 0], positions, 1.0).astype(jnp.bfloat16)
    key_all = rotate_pairs(qkv_heads[:, 1], positions, 1.0).astype(jnp.bfloat16)
    value_all = qkv_heads[:, 2].astype(jnp.bfloat16)
    token_index = jnp.arange(tok_rows, dtype=jnp.int32)
    allowed = (token_index[None, :] <= token_index[:, None]) & (
        token_index[None, :] >= (token_index - positions)[:, None]
    )
    mixed_grouped, log_grouped = lax.map(
        lambda block_items: plain_group(block_items, allowed),
        (by_groups(query_low), by_groups(key_all), by_groups(value_all)),
    )
    mixed_heads = from_groups(mixed_grouped)
    attn_low = mixed_heads.reshape(tok_rows, D).astype(jnp.bfloat16)
    resid = stream + jnp.dot(attn_low, w_out, preferred_element_type=jnp.float32)
    gain_two, bias_two, w_gate, w_up, w_down = (
        lax.all_gather(norm2_gain, "fsdp", axis=0, tiled=True),
        lax.all_gather(norm2_bias, "fsdp", axis=0, tiled=True),
        lax.all_gather(gate_weight, "fsdp", axis=0, tiled=True),
        lax.all_gather(up_weight, "fsdp", axis=0, tiled=True),
        lax.all_gather(down_weight, "fsdp", axis=0, tiled=True),
    )
    normed_two, inverse_two = normalize(resid)
    h_two = (normed_two * gain_two.astype(jnp.float32) + bias_two.astype(jnp.float32)).astype(
        jnp.bfloat16
    )
    gate_pre = jnp.dot(h_two, w_gate, preferred_element_type=jnp.float32)
    up_pre = jnp.dot(h_two, w_up, preferred_element_type=jnp.float32)
    sigmoid_gate = jax.nn.sigmoid(gate_pre)
    silu_gate = gate_pre * sigmoid_gate
    hidden = (silu_gate * up_pre).astype(jnp.bfloat16)
    block_out = (resid + jnp.dot(hidden, w_down, preferred_element_type=jnp.float32)).astype(
        jnp.bfloat16
    )
    gain_two, w_gate, w_up, w_down = (
        lax.all_gather(norm2_gain, "fsdp", axis=0, tiled=True),
        lax.all_gather(gate_weight, "fsdp", axis=0, tiled=True),
        lax.all_gather(up_weight, "fsdp", axis=0, tiled=True),
        lax.all_gather(down_weight, "fsdp", axis=0, tiled=True),
    )
    grad_down_w = jnp.einsum("tf,td->fd", hidden, out_grad, preferred_element_type=jnp.float32)
    grad_hidden = jnp.einsum("td,fd->tf", out_grad, w_down, preferred_element_type=jnp.float32)
    grad_gate = (
        grad_hidden * up_pre * sigmoid_gate * (1.0 + gate_pre * (1.0 - sigmoid_gate))
    ).astype(jnp.bfloat16)
    grad_up = (grad_hidden * silu_gate).astype(jnp.bfloat16)
    grad_gate_w = jnp.einsum("td,tf->df", h_two, grad_gate, preferred_element_type=jnp.float32)
    grad_up_w = jnp.einsum("td,tf->df", h_two, grad_up, preferred_element_type=jnp.float32)
    grad_htwo = jnp.einsum(
        "tf,df->td", grad_gate, w_gate, preferred_element_type=jnp.float32
    ) + jnp.einsum("tf,df->td", grad_up, w_up, preferred_element_type=jnp.float32)
    grad_gain_two = jnp.sum(grad_htwo * normed_two, axis=0)
    grad_bias_two = jnp.sum(grad_htwo, axis=0)
    grad_resid = out_grad.astype(jnp.float32) + norm_back(
        grad_htwo * gain_two.astype(jnp.float32), normed_two, inverse_two
    )
    mlp_sums = (
        lax.psum_scatter(grad_gain_two, "fsdp", scatter_dimension=0, tiled=True),
        lax.psum_scatter(grad_bias_two, "fsdp", scatter_dimension=0, tiled=True),
        lax.psum_scatter(grad_gate_w, "fsdp", scatter_dimension=0, tiled=True),
        lax.psum_scatter(grad_up_w, "fsdp", scatter_dimension=0, tiled=True),
        lax.psum_scatter(grad_down_w, "fsdp", scatter_dimension=0, tiled=True),
    )
    gain_one, w_qkv, w_out = (
        lax.all_gather(norm1_gain, "fsdp", axis=0, tiled=True),
        lax.all_gather(qkv_weight, "fsdp", axis=0, tiled=True),
        lax.all_gather(out_weight, "fsdp", axis=0, tiled=True),
    )
    grad_branch = grad_resid.astype(jnp.bfloat16)
    grad_out_w = jnp.einsum("ti,td->id", attn_low, grad_branch, preferred_element_type=jnp.float32)
    grad_att = jnp.einsum(
        "td,id->ti", grad_branch, w_out, preferred_element_type=jnp.float32
    ).reshape(tok_rows, HEADS, HEAD_DIM)
    group_heads = min(8, HEADS)
    row_delta = jnp.sum(grad_att * mixed_heads, axis=-1)
    delta_grouped = row_delta.reshape(tok_rows, HEADS // group_heads, group_heads).transpose(
        1, 2, 0
    )
    query_grouped, key_grouped, value_grouped = lax.map(
        lambda block_items: plain_back(block_items, allowed),
        (
            by_groups(query_low),
            by_groups(key_all),
            by_groups(value_all),
            by_groups(grad_att),
            delta_grouped,
            log_grouped,
        ),
    )
    grad_query = from_groups(query_grouped)
    grad_key = from_groups(key_grouped)
    grad_value = from_groups(value_grouped)
    grad_qkv = (
        jnp.stack(
            [
                rotate_pairs(grad_query, positions, -1.0),
                rotate_pairs(grad_key, positions, -1.0),
                grad_value,
            ],
            axis=1,
        )
        .reshape(tok_rows, 3 * D)
        .astype(jnp.bfloat16)
    )
    grad_qkv_w = jnp.einsum("td,tk->dk", h_one, grad_qkv, preferred_element_type=jnp.float32)
    grad_qkv_b = jnp.sum(grad_qkv.astype(jnp.float32), axis=0)
    grad_hone = jnp.einsum("tk,dk->td", grad_qkv, w_qkv, preferred_element_type=jnp.float32)
    grad_gain_one = jnp.sum(grad_hone * normed_one, axis=0)
    grad_bias_one = jnp.sum(grad_hone, axis=0)
    input_grad = grad_resid + norm_back(
        grad_hone * gain_one.astype(jnp.float32), normed_one, inverse_one
    )
    attn_sums = (
        lax.psum_scatter(grad_gain_one, "fsdp", scatter_dimension=0, tiled=True),
        lax.psum_scatter(grad_bias_one, "fsdp", scatter_dimension=0, tiled=True),
        lax.psum_scatter(grad_qkv_w, "fsdp", scatter_dimension=0, tiled=True),
        lax.psum_scatter(grad_qkv_b, "fsdp", scatter_dimension=0, tiled=True),
        lax.psum_scatter(grad_out_w, "fsdp", scatter_dimension=0, tiled=True),
    )
    return (
        block_out,
        input_grad,
        attn_sums[0],
        attn_sums[1],
        attn_sums[2],
        attn_sums[3],
        attn_sums[4],
        mlp_sums[0],
        mlp_sums[1],
        mlp_sums[2],
        mlp_sums[3],
        mlp_sums[4],
    )


def solution(mesh):
    devices = mesh.shape["fsdp"]
    rows, columns = P("fsdp", None), P("fsdp")
    body = team_shards if devices % TEAM == 0 and D == devices * HEAD_DIM else shards
    return jax.shard_map(
        body,
        mesh=mesh,
        in_specs=(rows, columns, columns, columns, rows, columns, rows, columns, columns, rows, rows, rows, rows),
        out_specs=(rows, rows, columns, columns, rows, columns, rows, columns, columns, rows, rows, rows),
        check_vma=False,
    )
```

```python
import functools

import jax
import jax.numpy as jnp
import numpy as np
from jax import lax
from jax.experimental import pallas as pl
from jax.experimental.pallas import tpu as pltpu
from jax.sharding import PartitionSpec as P

D = 2048
HEADS = 32
HEAD_DIM = 64
ROT = 16
EPS = 1e-05
TEAM = 8
LOCAL = HEADS // TEAM
MESH = pl.DeviceIdType.MESH
BF16 = jnp.bfloat16
F32 = jnp.float32
ANY = pl.BlockSpec(memory_space=pl.ANY)
VMEM = pl.BlockSpec(memory_space=pltpu.VMEM)


def lasting(us):
    return pl.CostEstimate(flops=0, bytes_accessed=int(us * 3.6e6), transcendentals=0)


def params(cid=None, limit=56):
    extra = {} if cid is None else {"collective_id": cid, "has_side_effects": True}
    return pltpu.CompilerParams(vmem_limit_bytes=limit * 1024 * 1024, **extra)


def place():
    me = lax.axis_index("fsdp")
    mine = lax.rem(me, TEAM)
    return mine, me - mine, mine // 2, lax.rem(mine, 2)


def chip_at(chip, step):
    along_x, along_y = lax.rem(chip, 2), chip // 2
    if step & 1:
        along_x = 1 - along_x
    if step & 2:
        along_y = 1 - along_y
    return along_y * 2 + along_x


def relation(chip, core, r):
    return chip_at(chip, r // 2) * 2 + lax.rem(core + r, 2)


def greet(devices):
    barrier = pltpu.get_barrier_semaphore()
    for device in devices:
        pl.semaphore_signal(barrier, inc=1, device_id=(device,), device_id_type=MESH)
    pl.semaphore_wait(barrier, len(devices))


def remote(src, dst, send, recv, device):
    return pltpu.make_async_remote_copy(
        src_ref=src, dst_ref=dst, send_sem=send, recv_sem=recv, device_id=(device,), device_id_type=MESH
    )


class Swap:
    sems = [pltpu.SemaphoreType.DMA, pltpu.SemaphoreType.DMA((TEAM,)), pltpu.SemaphoreType.DMA((TEAM,))]

    def __init__(self, src, out, sems, same=False, near_first=False):
        own_sem, send, recv = sems
        mine, base, chip, core = place()
        others = [relation(chip, core, r) for r in range(1, TEAM)]
        self.near = [base + other for other in others]
        self.copies = [
            remote(
                src if same else src.at[other], out.at[r if near_first else mine], send.at[r], recv.at[r], base + other
            )
            for r, other in enumerate(others, 1)
        ]
        own = src if same else src.at[mine]
        self.copies.append(pltpu.make_async_copy(own, out.at[0 if near_first else mine], own_sem))

    def start(self):
        for copy in self.copies:
            copy.start()

    def finish(self):
        for copy in self.copies:
            copy.wait()


class Line:
    def sems(planes):
        return [pltpu.SemaphoreType.DMA, pltpu.SemaphoreType.DMA((planes,)), pltpu.SemaphoreType.DMA((planes,))]

    def __init__(self, planes, src, out, sems, same=False, within=False):
        own_sem, send, recv = sems
        mine, base, _, _ = place()
        plane = base // TEAM
        others = [lax.rem(plane + k, planes) for k in range(1, planes)]
        self.near = [other * TEAM + mine for other in others]
        self.copies = [
            remote(src if same else src.at[other], out.at[plane], send.at[k], recv.at[k], other * TEAM + mine)
            for k, other in enumerate(others)
        ]
        own = src if same else src.at[plane]
        self.own = None if within else pltpu.make_async_copy(own, out.at[plane], own_sem)

    def start(self):
        for copy in self.copies:
            copy.start()
        if self.own is not None:
            self.own.start()

    def finish(self):
        for copy in self.copies:
            copy.wait()
        if self.own is not None:
            self.own.wait()


class LineGather:
    def sems(planes):
        return [pltpu.SemaphoreType.DMA, pltpu.SemaphoreType.DMA((2, planes)), pltpu.SemaphoreType.DMA((2, planes))]

    def __init__(self, planes, src, out, sems):
        own_sem, self.send, self.recv = sems
        mine, base, _, _ = place()
        self.plane, self.planes, self.src, self.out = base // TEAM, planes, src, out
        self.me = base + mine
        self.near = [lax.rem(self.plane + k, planes) * TEAM + mine for k in (1, planes - 1)]
        self.own = pltpu.make_async_copy(src, out.at[self.plane], own_sem)

    def copy(self, way, stage):
        step = 1 - 2 * way
        block, to = self.plane - step * (stage - 1), self.plane + step
        is_there = (block >= 0) & (block < self.planes) & (to >= 0) & (to < self.planes)
        src = self.src if stage == 1 else self.out.at[block]
        sems = self.send.at[way, stage], self.recv.at[way, stage]
        return is_there, remote(src, self.out.at[block], *sems, self.me + step * TEAM)

    def arrived(self, way, stage):
        block = self.plane - (1 - 2 * way) * stage

        @pl.when((block >= 0) & (block < self.planes))
        def _():
            dst = self.out.at[block]
            remote(dst, dst, self.send.at[way, stage], self.recv.at[way, stage], self.me).wait_recv()

    def start(self):
        self.own.start()
        self.stage(1)

    def stage(self, stage):
        for way in (0, 1):
            if stage > 1:
                self.arrived(way, stage - 1)
            is_there, copy = self.copy(way, stage)
            pl.when(is_there)(copy.start)

    def finish(self):
        self.own.wait()
        for way in (0, 1):
            self.arrived(way, self.planes - 1)
            for stage in range(1, self.planes):
                is_there, copy = self.copy(way, stage)
                pl.when(is_there)(copy.wait_send)


def slices(ref, pieces, size):
    return jnp.concatenate([ref[:, i * size : (i + 1) * size] for i in pieces], axis=1)


def opening_kernel(
    planes, qkv_ref, gate_ref, up_ref, x_ref, out_weight_ref, position_ref, bias_ref, *refs
):
    vector_refs, rate_ref = refs[:4], refs[4]
    pieces_ref, x_all_ref, w_qkv_ref, w_out_ref, tab_ref, norm_ref, b_ref = refs[5:12]
    cut, landed, made, small_ref, place_ref, all_ref, places_ref, tables = refs[12:20]
    sems = refs[20:]
    mine, base, _, _ = place()
    plane = base // TEAM
    swap, gather = Swap(made, pieces_ref, sems[:3]), Gather(x_ref, x_all_ref, sems[3:10])
    vectors = Swap(small_ref, all_ref.at[plane], sems[10:13], same=True)
    places = Swap(place_ref, places_ref, sems[13:16], same=True, near_first=True)
    line = Line(planes, all_ref.at[plane], all_ref, sems[16:19], same=True, within=True)
    rows, heads = LineGather(planes, landed, w_qkv_ref, sems[19:22]), Swap(cut, landed, sems[22:25])
    outs = LineGather(planes, out_weight_ref, w_out_ref, sems[25:28])
    depth = gate_ref.shape[0]
    for row, ref in enumerate(vector_refs):
        small_ref[row : row + 1, :depth] = ref[...].astype(F32).reshape(1, depth)
    bias = bias_ref[...].astype(F32).reshape(1, bias_ref.shape[0])
    for i in range(bias_ref.shape[0] // depth):
        small_ref[4 + i : 5 + i, :depth] = bias[:, i * depth : (i + 1) * depth]
    known = position_ref[...].astype(F32).reshape(1, position_ref.shape[0])
    for i in range(position_ref.shape[0] // 128):
        place_ref[i : i + 1, :] = known[:, i * 128 : (i + 1) * 128]
    for i in range(TEAM):
        cut[i] = slices(qkv_ref, [s * HEADS + z * TEAM + i for s in range(3) for z in range(planes)], HEAD_DIM)
    greet(swap.near + line.near)
    outs.start()
    heads.start()
    vectors.start()
    places.start()
    size = gate_ref.shape[1] // (planes * TEAM)
    for i in range(TEAM):
        units = [z * TEAM + i for z in range(planes)]
        made[i] = jnp.concatenate([slices(gate_ref, units, size), slices(up_ref, units, size)], axis=1)
    outs.stage(2)
    heads.finish()
    rows.start()
    gather.start()
    swap.start()
    vectors.finish()
    line.start()
    for stage in range(3, planes):
        outs.stage(stage)
    places.finish()
    square = (128, 128)

    @pl.loop(0, TEAM)
    def _(i):
        known = places_ref[i]
        for part in range(tables.shape[2] // 128):
            at = jnp.transpose(jnp.broadcast_to(known[part : part + 1, :], square))
            here = pl.ds(part * 128, 128)
            angle = at * rate_ref[...]
            tables[i, 0, here, :] = jnp.cos(angle)
            tables[i, 1, here, :] = jnp.sin(angle)
            token = lax.broadcasted_iota(jnp.int32, square, 0) + part * 128
            tables[i, 2, here, :] = token.astype(F32) - at

    store = pltpu.make_async_copy(tables, tab_ref, sems[28])
    store.start()
    rows.stage(2)
    gather.middle()
    for stage in range(3, planes):
        rows.stage(stage)
    line.finish()
    each = [all_ref[z, i] for z in range(planes) for i in range(TEAM)]
    for i in range(4):
        norm_ref[i : i + 1, :] = jnp.concatenate([known[i : i + 1, :depth] for known in each], axis=1)
    per = qkv_ref.shape[1] // (planes * TEAM * depth)
    bias = []
    for part in range(3):
        for z in range(planes):
            head = part * HEADS + z * TEAM + mine
            known = all_ref[head // per // TEAM, lax.rem(head // per, TEAM)]
            row = lax.broadcasted_iota(jnp.int32, known.shape, 0) == 4 + lax.rem(head, per)
            bias.append(jnp.sum(jnp.where(row, known, 0.0), axis=0, keepdims=True)[:, :depth])
    b_ref[...] = jnp.concatenate(bias, axis=1)
    gather.finish()
    swap.finish()
    rows.finish()
    outs.finish()
    store.wait()


def opening(qkv, gate, up, inputs, out_weight, positions, bias, vectors, rate, planes, cid):
    shape = (TEAM, gate.shape[0], 2 * gate.shape[1] // TEAM)
    heads = (TEAM, qkv.shape[0], qkv.shape[1] // TEAM)
    tables = (TEAM, 3, inputs.shape[0], 128)
    return pl.pallas_call(
        functools.partial(opening_kernel, planes),
        out_shape=[
            jax.ShapeDtypeStruct(shape, BF16),
            jax.ShapeDtypeStruct((TEAM,) + inputs.shape, BF16),
            jax.ShapeDtypeStruct((planes,) + heads, BF16),
            jax.ShapeDtypeStruct((planes,) + out_weight.shape, BF16),
            jax.ShapeDtypeStruct(tables, F32),
            jax.ShapeDtypeStruct((4, inputs.shape[1]), F32),
            jax.ShapeDtypeStruct((1, heads[2]), F32),
        ],
        in_specs=[VMEM] * 12,
        out_specs=[ANY] * 5 + [VMEM] * 2,
        scratch_shapes=[
            pltpu.VMEM(heads, BF16),
            pltpu.VMEM(heads, BF16),
            pltpu.VMEM(shape, BF16),
            pltpu.VMEM((8, 128), F32),
            pltpu.VMEM((8, 128), F32),
            pltpu.VMEM((planes, TEAM, 8, 128), F32),
            pltpu.VMEM((TEAM, 8, 128), F32),
            pltpu.VMEM(tables, F32),
        ]
        + Swap.sems
        + Gather.sems
        + Swap.sems * 2
        + Line.sems(planes)
        + LineGather.sems(planes)
        + Swap.sems
        + LineGather.sems(planes)
        + [pltpu.SemaphoreType.DMA],
        cost_estimate=lasting(80),
        compiler_params=params(cid),
    )(qkv, gate, up, inputs, out_weight, positions, bias, *vectors, rate)


def unslice(held, parts, planes, outs):
    size = held.shape[2] // (parts * planes)
    for at in range(parts * planes):
        row = jnp.concatenate([held[i, :, at * size : (at + 1) * size] for i in range(TEAM)], axis=1)
        out, first = (outs[at // planes], at % planes) if len(outs) > 1 else (outs[0], at)
        out[:, first * TEAM * size : (first + 1) * TEAM * size] = row.astype(F32)


def first_kernel(planes, held_ref, far_ref, gate_ref, up_ref, wo_ref):
    unslice(held_ref, 2, planes, [gate_ref, up_ref])
    wo_ref[...] = added(far_ref)


def first_grads(held, far):
    _, depth, width = held.shape
    return pl.pallas_call(
        functools.partial(first_kernel, far.shape[0]),
        out_shape=[jax.ShapeDtypeStruct((depth, width * TEAM // 2), F32)] * 2
        + [jax.ShapeDtypeStruct(far.shape[1:], F32)],
        in_specs=[VMEM] * 2,
        out_specs=[VMEM] * 3,
        cost_estimate=lasting(4),
        compiler_params=params(),
    )(held, far)


def rest_kernel(planes, held_ref, w_ref):
    unslice(held_ref, 3, planes, [w_ref])


def rest_grads(held, planes):
    _, depth, width = held.shape
    return pl.pallas_call(
        functools.partial(rest_kernel, planes),
        out_shape=jax.ShapeDtypeStruct((depth, width * TEAM), F32),
        in_specs=[VMEM],
        out_specs=VMEM,
        cost_estimate=lasting(3),
        compiler_params=params(),
    )(held)


def added(ref):
    total = ref[0].astype(F32)
    for i in range(1, ref.shape[0]):
        total = total + ref[i].astype(F32)
    return total


def close_kernel(w_ref, _, __, ___, held_ref, *sems):
    swap = Swap(w_ref, held_ref, sems)
    greet(swap.near)
    swap.start()
    swap.finish()


def both_close_kernel(planes, w_ref, shared_ref, _, __, held_ref, vector_ref, got, block, beyond, *sems):
    swap, inner = Swap(w_ref, held_ref, sems[:3]), Swap(shared_ref, got, sems[3:6])
    outer = Line(planes, block, beyond, sems[6:])
    greet(swap.near + outer.near)
    inner.start()
    swap.start()
    inner.finish()
    block[...] = added(got)
    outer.start()
    outer.finish()
    vector_ref[...] = added(beyond)
    swap.finish()


def both_closing(blocks, shared, after, cid):
    planes = shared.shape[1]
    return pl.pallas_call(
        functools.partial(both_close_kernel, planes),
        out_shape=[jax.ShapeDtypeStruct(blocks.shape, BF16), jax.ShapeDtypeStruct(shared.shape[2:], F32)],
        in_specs=[VMEM, VMEM, ANY, ANY],
        out_specs=[ANY, VMEM],
        scratch_shapes=[pltpu.VMEM(shared.shape, F32)]
        + [pltpu.VMEM(shared.shape[1:], F32)] * 2
        + Swap.sems * 2
        + Line.sems(planes),
        cost_estimate=lasting(22),
        compiler_params=params(cid),
    )(blocks, shared, *after)


def closing(blocks, after, cid):
    return pl.pallas_call(
        close_kernel,
        out_shape=jax.ShapeDtypeStruct(blocks.shape, BF16),
        in_specs=[VMEM, ANY, ANY, ANY],
        out_specs=ANY,
        scratch_shapes=Swap.sems,
        cost_estimate=lasting(14),
        compiler_params=params(cid),
    )(blocks, *after)


class Gather:
    sems = [pltpu.SemaphoreType.DMA((5,)), pltpu.SemaphoreType.DMA((5,)), pltpu.SemaphoreType.DMA((2,)),
            pltpu.SemaphoreType.DMA((2,)), pltpu.SemaphoreType.DMA((6,)), pltpu.SemaphoreType.DMA((6,)),
            pltpu.SemaphoreType.DMA]

    def __init__(self, src, out, sems):
        send, recv, hop_send, hop_recv, pass_send, pass_recv, own_sem = sems
        _, base, chip, core = place()
        side, over = (chip_at(chip, k) * 2 + core for k in (1, 2))
        self.sibling = base + chip * 2 + 1 - core
        self.near = [base + side, base + over, self.sibling]
        half = src.shape[0] // 2
        top, low = pl.ds(0, half), pl.ds(half, half)
        self.first = [
            remote(src.at[part], out.at[at, part], send.at[i], recv.at[i], base + to)
            for i, (part, at, to) in enumerate(((top, 2, side), (low, 4, over), (low, 2, side), (top, 4, over)))
        ]
        self.first.append(remote(src, out.at[1], send.at[4], recv.at[4], self.sibling))
        self.own = pltpu.make_async_copy(src, out.at[0], own_sem)
        self.hops = [
            remote(out.at[at, part], out.at[6, part], hop_send.at[i], hop_recv.at[i], base + to)
            for i, (at, part, to) in enumerate(((2, top, over), (4, low, side)))
        ]
        self.passed = [
            remote(out.at[at, part], out.at[at + 1, part], pass_send.at[i], pass_recv.at[i], self.sibling)
            for i, (at, part) in enumerate(((2, top), (4, low), (2, low), (4, top), (6, top), (6, low)))
        ]

    def start(self):
        for copy in self.first:
            copy.start()
        self.own.start()

    def middle(self):
        for i in (0, 1):
            self.first[i].wait_recv()
            self.hops[i].start()
            self.passed[i].start()

    def finish(self):
        for i in range(2, TEAM):
            self.ready(i)
        self.first[4].wait_recv()
        self.own.wait()
        self.sent()

    def ready(self, i):
        if i == 0:
            self.own.wait()
        elif i == 1:
            self.first[4].wait_recv()
        elif i == 6:
            for j in (0, 1):
                self.hops[j].wait_recv()
                self.passed[4 + j].start()
        elif i % 2 == 0:
            self.first[1 + i // 2].wait_recv()
            self.passed[1 + i // 2].start()
        else:
            for j in {3: (0, 2), 5: (1, 3), 7: (4, 5)}[i]:
                self.passed[j].wait_recv()

    def sent(self):
        for copy in self.first + self.hops + self.passed:
            copy.wait_send()


class Sum:
    def scratch(rows, width):
        return [pltpu.VMEM((4, rows, width), BF16), pltpu.VMEM((4, rows, width), BF16),
                pltpu.VMEM((2, rows // 2, width), BF16), pltpu.VMEM((2, rows, width), BF16)]

    sems = [pltpu.SemaphoreType.DMA((4,))] * 3 + [pltpu.SemaphoreType.DMA((2,))] * 2 + [pltpu.SemaphoreType.DMA((4,))] * 2

    def __init__(self, blocks, scratch, sems, away=None):
        self.own, self.beside, self.via, self.far = scratch
        load_sem, near_send, near_recv, via_send, via_recv, far_send, far_recv = sems
        _, base, chip, core = place()
        sibling = base + chip * 2 + 1 - core
        side, over = (base + chip_at(chip, k) * 2 + core for k in (1, 2))
        self.near = [side, over, sibling]
        self.half = self.own.shape[1] // 2
        top, low = pl.ds(0, self.half), pl.ds(self.half, self.half)
        self.loads = [
            pltpu.make_async_copy(blocks.at[2 * k], self.own.at[k], load_sem.at[k])
            for k in range(4)
            if away is None
        ]

        def near_copy(k):
            src = blocks.at[2 * k + 1] if away is None else away.at[k]
            return remote(src, self.beside.at[k], near_send.at[k], near_recv.at[k], sibling)

        self.near_copy = near_copy
        self.nears = [near_copy(k) for k in range(4)]
        self.vias = [
            remote(self.own.at[3, part], self.via.at[i], via_send.at[i], via_recv.at[i], to)
            for i, (part, to) in enumerate(((top, side), (low, over)))
        ]
        self.fars = [
            remote(self.own.at[k, part], self.far.at[k - 1, part], far_send.at[i], far_recv.at[i], to)
            for i, (k, part, to) in enumerate(((2, low, over), (1, top, side), (2, top, over), (1, low, side)))
        ]

    def start(self):
        for k in (3, 2, 1, 0):
            self.loads[k].start()
            self.nears[k].start()

    def pair(self, k):
        if self.loads:
            self.loads[k].wait()
        self.nears[k].wait_recv()

        @pl.loop(0, self.own.shape[1] // 16)
        def _(i):
            part = pl.ds(pl.multiple_of(i * 16, 16), 16)
            self.own[k, part, :] = (self.own[k, part, :].astype(F32) + self.beside[k, part, :].astype(F32)).astype(BF16)

    def middle_a(self):
        self.pair(3)
        for copy in self.vias:
            copy.start()

    def middle_b(self):
        self.pair(2)
        self.fars[0].start()

    def middle_c(self):
        self.pair(1)
        self.fars[1].start()

    def middle(self):
        self.middle_a()
        self.middle_b()
        self.middle_c()

    def middle_two(self):
        for i, k in ((0, 2), (1, 1)):
            self.vias[i].wait_recv()

            @pl.loop(0, self.half // 16)
            def _(j, i=i, k=k):
                part = pl.ds(pl.multiple_of(j * 16, 16), 16)
                at = pl.ds(pl.multiple_of(j * 16 + i * self.half, 16), 16)
                self.own[k, at, :] = (self.own[k, at, :].astype(F32) + self.via[i, part, :].astype(F32)).astype(BF16)

            self.fars[2 + i].start()

    def finish(self, use):
        if self.loads:
            self.loads[0].wait()
        self.nears[0].wait_recv()
        for copy in self.fars:
            copy.wait_recv()

        @pl.loop(0, self.own.shape[1] // 16)
        def _(i):
            part = pl.ds(pl.multiple_of(i * 16, 16), 16)
            total = self.own[0, part, :].astype(F32) + self.beside[0, part, :].astype(F32)
            use(part, total + self.far[0, part, :].astype(F32) + self.far[1, part, :].astype(F32))

        for copy in self.nears + self.vias + self.fars:
            copy.wait_send()


def fold(x):
    return x[:8] + x[8:]


def expand_kernel(
    planes, h_ref, w_ref, g_ref, down_ref, pre_ref, hidden_ref, grad_ref, g_all_ref, wd_ref, held, g, total, w, *sems
):
    gather, line = Gather(g_ref, g_all_ref, sems[:7]), LineGather(planes, down_ref, wd_ref, sems[7:10])
    step = pl.program_id(0)

    @pl.when(step == 0)
    def _():
        greet(gather.near + line.near)
        line.start()
        gather.start()
        weights = pltpu.make_async_copy(w_ref, w, sems[11])
        weights.start()
        weights.wait()

    pre = dot(h_ref[0], w[...])
    pre_ref[0] = pre
    ff = hidden_ref.shape[2]
    gate_pre, up_pre = pre[:, :ff], pre[:, ff:]
    hidden = (gate_pre * jax.nn.sigmoid(gate_pre) * up_pre).astype(BF16)
    hidden_ref[0] = hidden
    held[step] = hidden
    pl.when(step == TEAM - 3)(functools.partial(line.stage, 2))

    @pl.when(step == TEAM - 1)
    def _():
        def load(i):
            return pltpu.make_async_copy(g_all_ref.at[i], g.at[i % 2], sems[10].at[i % 2])

        gather.middle()
        gather.ready(0)
        load(0).start()
        for i in range(TEAM):
            if i < TEAM - 1:
                gather.ready(i + 1)
                load(i + 1).start()
            load(i).wait()
            product = dot(held[i], g[i % 2], TN)
            total[...] = product if i == 0 else total[...] + product
            if i == 4:
                for stage in range(3, planes):
                    line.stage(stage)
        grad_ref[...] = total[...].astype(BF16)
        gather.sent()
        line.finish()


def expand(h_two, w_both, out_grad, down, planes, cid):
    seqs, rows, _ = h_two.shape
    width = w_both.shape[1]
    return pl.pallas_call(
        functools.partial(expand_kernel, planes),
        grid=(seqs,),
        in_specs=[per_seq(rows, D), ANY, VMEM, VMEM],
        out_specs=[per_seq(rows, width), per_seq(rows, width // 2), whole(width // 2, D), ANY, ANY],
        out_shape=[
            jax.ShapeDtypeStruct((seqs, rows, width), F32),
            jax.ShapeDtypeStruct((seqs, rows, width // 2), BF16),
            jax.ShapeDtypeStruct((width // 2, D), BF16),
            jax.ShapeDtypeStruct((seqs, rows, D), BF16),
            jax.ShapeDtypeStruct((planes,) + down.shape, BF16),
        ],
        scratch_shapes=[
            pltpu.VMEM((seqs, rows, width // 2), BF16),
            pltpu.VMEM((2, rows, D), BF16),
            pltpu.VMEM((width // 2, D), F32),
            pltpu.VMEM((D, width), BF16),
        ]
        + Gather.sems
        + LineGather.sems(planes)
        + [pltpu.SemaphoreType.DMA((2,)), pltpu.SemaphoreType.DMA],
        cost_estimate=lasting(55),
        compiler_params=params(cid),
    )(h_two, w_both, out_grad, down)


def mlp_back_kernel(
    pre_ref, g_all_ref, h_ref, wd_ref, w_ref, resid_ref, g_ref, norm_ref, _,
    out_ref, sums_ref, block_ref, grad_w_ref,
    pre, g_all, turned, made, grads, away, w, resid, own_grad, wd, *scratch,
):
    pre_sem, g_sem, turned_sem, made_sem, late_sem = scratch[11:]
    total = Sum(None, scratch[:4], scratch[4:11], away)
    rows, ff = pre_ref.shape[1], wd_ref.shape[0]
    chunk = turned.shape[2]

    def loads(i):
        slot, at = lax.rem(i, 2), TEAM - 1 - i
        return (
            pltpu.make_async_copy(pre_ref.at[at], pre.at[slot], pre_sem.at[slot]),
            pltpu.make_async_copy(g_all_ref.at[at], g_all.at[slot], g_sem.at[slot]),
        )

    def load_chunk(i):
        slot = lax.rem(i, 2)
        columns = pl.ds(pl.multiple_of(i * chunk, chunk), chunk)
        return pltpu.make_async_copy(h_ref.at[:, columns], turned.at[slot], turned_sem.at[slot])

    def store_chunk(i):
        slot = lax.rem(i, 2)
        part = pl.ds(pl.multiple_of(i * chunk, chunk), chunk)
        return pltpu.make_async_copy(made.at[slot], grad_w_ref.at[part, :], made_sem.at[slot])

    for copy in loads(0):
        copy.start()
    late = [
        pltpu.make_async_copy(src, dst, late_sem.at[i])
        for i, (src, dst) in enumerate(((wd_ref, wd), (w_ref, w), (resid_ref, resid), (g_ref, own_grad)))
    ]
    for copy in late:
        copy.start()
    greet(total.near)

    @pl.loop(0, TEAM)
    def _(i):
        slot = lax.rem(i, 2)
        k, at = 3 - i // 2, TEAM - 1 - i

        @pl.when(i < TEAM - 1)
        def _():
            for copy in loads(i + 1):
                copy.start()

        for copy in loads(i):
            copy.wait()
        pl.when(i == 0)(late[0].wait)
        grad_hidden = dot(g_all[slot], wd[...], NT)
        gate_pre, up_pre = pre[slot, :, :ff], pre[slot, :, ff:]
        sigmoid = jax.nn.sigmoid(gate_pre)
        grad_gate = grad_hidden * up_pre * sigmoid * (1.0 + gate_pre * (1.0 - sigmoid))
        grad_up = grad_hidden * (gate_pre * sigmoid)
        part = pl.ds(pl.multiple_of(at * rows, rows), rows)
        grads[part, :] = jnp.concatenate([grad_gate, grad_up], axis=1).astype(BF16)

        def make(to):
            to[k] = dot(grads[part, :], w[...], NT).astype(BF16)

        pl.when(i == 0)(late[1].wait)

        @pl.when(lax.rem(i, 2) == 0)
        def _():
            make(away)
            total.near_copy(k).start()

        @pl.when(lax.rem(i, 2) == 1)
        def _():
            make(total.own)

        for step, advance in ((1, total.middle_a), (3, total.middle_b), (5, total.middle_c)):
            pl.when(i == step)(advance)

    load_chunk(0).start()
    total.middle_two()
    chunks = h_ref.shape[1] // chunk

    @pl.loop(0, chunks)
    def _(i):
        slot = lax.rem(i, 2)

        @pl.when(i < chunks - 1)
        def _():
            load_chunk(i + 1).start()

        load_chunk(i).wait()

        @pl.when(i >= 2)
        def _():
            store_chunk(i - 2).wait()

        made[slot] = dot(turned[slot], grads[...], TN).astype(BF16)
        store_chunk(i).start()

    sums_ref[...] = jnp.zeros_like(sums_ref)
    for copy in late[2:]:
        copy.wait()

    def use(rows, value):
        normed, inverse = normalize(resid[rows, :])
        sums_ref[:8, :] += fold(value * normed)
        sums_ref[8:, :] += fold(value)
        grad = own_grad[rows, :].astype(F32) + norm_back(value * norm_ref[2:3, :], normed, inverse)
        out_ref[rows, :] = grad
        block_ref[rows, :] = grad.astype(BF16)

    total.finish(use)
    store_chunk(chunks - 2).wait()
    store_chunk(chunks - 1).wait()


def mlp_back(pre, g_all, h_two, w_down, w_both, resid, out_grad, gain, after, cid):
    seqs, rows, both = pre.shape
    width = resid.shape[1]
    chunk = 256
    two = pltpu.SemaphoreType.DMA((2,))
    return pl.pallas_call(
        mlp_back_kernel,
        out_shape=[
            jax.ShapeDtypeStruct((rows, width), F32),
            jax.ShapeDtypeStruct((16, width), F32),
            jax.ShapeDtypeStruct((rows, width), BF16),
            jax.ShapeDtypeStruct((width, both), BF16),
        ],
        in_specs=[ANY, ANY, ANY, ANY, ANY, ANY, ANY, VMEM, ANY],
        out_specs=[VMEM, VMEM, VMEM, ANY],
        scratch_shapes=[
            pltpu.VMEM((2, rows, both), F32),
            pltpu.VMEM((2, rows, width), BF16),
            pltpu.VMEM((2, seqs * rows, chunk), BF16),
            pltpu.VMEM((2, chunk, both), BF16),
            pltpu.VMEM((seqs * rows, both), BF16),
            pltpu.VMEM((4, rows, width), BF16),
            pltpu.VMEM((width, both), BF16),
            pltpu.VMEM((rows, width), F32),
            pltpu.VMEM((rows, width), BF16),
            pltpu.VMEM((both // 2, width), BF16),
        ]
        + Sum.scratch(rows, width)
        + Sum.sems
        + [two] * 4
        + [pltpu.SemaphoreType.DMA((4,))],
        cost_estimate=lasting(60),
        compiler_params=params(cid, 50),
    )(pre, g_all, h_two, w_down, w_both, resid, out_grad, gain, after)


def share(x, sums, bias, planes, per, depth):
    mine = place()[0]
    x[...] = jnp.zeros_like(x)
    sums = [jnp.sum(v, axis=0, keepdims=True) for v in sums]
    for z in range(planes):
        for i in range(TEAM):
            at = (z * TEAM + i) * depth
            for row, v in enumerate(sums):
                x[i, z, row : row + 1, :depth] = v[:, at : at + depth]
    for part in range(3):
        for z in range(planes):
            head = part * HEADS + z * TEAM + mine
            owner = head // per
            at = (part * planes + z) * HEAD_DIM
            x[lax.rem(owner, TEAM), owner // TEAM, pl.ds(4 + lax.rem(head, per), 1), :depth] = bias[:, at : at + HEAD_DIM]


def last_kernel(
    planes, part_ref, x_ref, norm_ref, branch_ref, sums_two_ref, bias_ref, _,
    out_ref, far_ref, shared_ref, sums, *scratch,
):
    total, line = Sum(part_ref, scratch[:4], scratch[4:11]), Line(planes, branch_ref, far_ref, scratch[11:])
    greet(total.near + line.near)
    line.start()
    total.start()
    total.middle()
    total.middle_two()
    sums[...] = jnp.zeros_like(sums)

    def use(rows, value):
        normed, inverse = normalize(x_ref[rows, :].astype(F32))
        sums[:8, :] += fold(value * normed)
        sums[8:, :] += fold(value)
        out_ref[rows, :] = norm_back(value * norm_ref[0:1, :], normed, inverse)

    total.finish(use)
    vectors = [sums[:8, :], sums[8:, :], sums_two_ref[:8, :], sums_two_ref[8:, :]]
    depth = part_ref.shape[2] // (planes * TEAM)
    share(shared_ref, vectors, added(bias_ref), planes, bias_ref.shape[2] // (planes * depth), depth)
    line.finish()


def last(part, inputs, gain, branch, sums_two, bias, after, cid):
    rows, width = inputs.shape
    planes = branch.shape[0]
    vectors = (TEAM, planes, 8, 128)
    return pl.pallas_call(
        functools.partial(last_kernel, planes),
        out_shape=[
            jax.ShapeDtypeStruct((rows, width), F32),
            jax.ShapeDtypeStruct(branch.shape, BF16),
            jax.ShapeDtypeStruct(vectors, F32),
        ],
        in_specs=[ANY, VMEM, VMEM, VMEM, VMEM, VMEM, ANY],
        out_specs=[VMEM, ANY, VMEM],
        scratch_shapes=[pltpu.VMEM((16, width), F32)]
        + Sum.scratch(rows, width)
        + Sum.sems
        + Line.sems(planes),
        cost_estimate=lasting(58),
        compiler_params=params(cid),
    )(part, inputs, gain, branch, sums_two, bias, after)


def dot(a, b, dims=((1,), (0,))):
    return lax.dot_general(a, b, (dims, ((), ())), preferred_element_type=F32)


NT = ((1,), (1,))
TN = ((0,), (0,))


def normalize(stream):
    average = jnp.mean(stream, axis=-1, keepdims=True)
    centered = stream - average
    variance = jnp.mean(centered * centered, axis=-1, keepdims=True)
    inverse = lax.rsqrt(variance + EPS)
    return centered * inverse, inverse


def norm_back(grad_norm, normed, inverse):
    return inverse * (
        grad_norm
        - jnp.mean(grad_norm, axis=-1, keepdims=True)
        - normed * jnp.mean(grad_norm * normed, axis=-1, keepdims=True)
    )


def turn(heads, cosine, sine):
    half, width = ROT // 2, heads.shape[-1]
    lanes = lax.broadcasted_iota(jnp.int32, heads.shape, 1) % HEAD_DIM
    moved = jnp.where(lanes < half, -pltpu.roll(heads, width - half, 1), pltpu.roll(heads, half, 1))
    return heads * cosine + moved * sine


def wide(table):
    return jnp.concatenate([table] * (LOCAL * HEAD_DIM // 128), axis=1)


def visible(start):
    size = start.shape[0]
    rows = lax.broadcasted_iota(jnp.int32, (size, size), 0)
    columns = lax.broadcasted_iota(jnp.int32, (size, size), 1)
    start = jnp.concatenate([start] * (size // start.shape[1]), axis=1)
    return (columns <= rows) & (columns.astype(F32) >= start)


def head_of(x, h):
    lanes = lax.broadcasted_iota(jnp.int32, x.shape, 1)
    return jnp.where((lanes >= h * HEAD_DIM) & (lanes < (h + 1) * HEAD_DIM), x, jnp.zeros_like(x))


def soft(query, key, allowed):
    scores = dot(query, key, NT) * 0.125
    masked = jnp.where(allowed, scores, -1e30)
    exponent = jnp.exp(masked - jnp.max(masked, axis=-1, keepdims=True))
    return exponent / jnp.sum(exponent, axis=-1, keepdims=True)


def attend_kernel(
    planes, x_ref, norm_ref, w_ref, b_ref, wo_ref, tab_ref, both_ref,
    h_ref, qkv_ref, attn_ref, resid_ref, h_two_ref, w_both_ref, block, away, w, *scratch,
):
    total, gather = Sum(None, scratch[:4], scratch[4:11], away), Gather(block, h_two_ref, scratch[11:18])
    line = LineGather(planes, both_ref, w_both_ref, scratch[18:21])
    step = pl.program_id(0)

    @pl.when(step == 0)
    def _():
        greet(total.near + line.near)
        line.start()
        weights = pltpu.make_async_copy(w_ref, w, scratch[21])
        weights.start()
        weights.wait()

    pl.when(step == TEAM - 2)(functools.partial(line.stage, 2))
    stream = x_ref[0].astype(F32)
    normed, _ = normalize(stream)
    h_one = (normed * norm_ref[0:1, :] + norm_ref[1:2, :]).astype(BF16)
    h_ref[0] = h_one
    qkv = dot(h_one, w[...]) + b_ref[...]
    width = LOCAL * HEAD_DIM
    cosine, sine = wide(tab_ref[0, 0]), wide(tab_ref[0, 1])
    query = turn(qkv[:, :width], cosine, sine).astype(BF16)
    key = turn(qkv[:, width : 2 * width], cosine, sine).astype(BF16)
    value = qkv[:, 2 * width :].astype(BF16)
    qkv_ref[0, :, :width] = query
    qkv_ref[0, :, width : 2 * width] = key
    qkv_ref[0, :, 2 * width :] = value
    allowed = visible(tab_ref[0, 2])
    mixed = jnp.zeros((query.shape[0], width), F32)
    for h in range(LOCAL):
        probs = soft(head_of(query, h), key, allowed).astype(BF16)
        mixed = mixed + dot(probs, head_of(value, h))
    attn_low = mixed.astype(BF16)
    attn_ref[0] = attn_low
    part = dot(attn_low, wo_ref[...]).astype(BF16)
    k = 3 - step // 2

    @pl.when(lax.rem(step, 2) == 0)
    def _():
        away[k] = part
        total.near_copy(k).start()

    @pl.when(lax.rem(step, 2) == 1)
    def _():
        total.own[k] = part

    for at, advance in ((1, total.middle_a), (3, total.middle_b), (5, total.middle_c), (6, total.middle_two)):
        pl.when(step == at)(advance)

    def use(rows, value):
        resid = x_ref[0, rows, :].astype(F32) + value
        resid_ref[rows, :] = resid
        normed, _ = normalize(resid)
        block[rows, :] = (normed * norm_ref[2:3, :] + norm_ref[3:4, :]).astype(BF16)

    @pl.when(step == TEAM - 1)
    def _():
        total.finish(use)
        gather.start()
        for stage in range(3, planes):
            line.stage(stage)
        gather.middle()
        gather.finish()
        line.finish()


def per_seq(*shape):
    return pl.BlockSpec((1,) + shape, lambda s: (s,) + (0,) * len(shape))


def whole(*shape):
    return pl.BlockSpec(shape, lambda s: (0,) * len(shape))


def attend(x_all, norms, w_qkv, b_qkv, w_out, tables, both, planes, cid):
    seqs, rows, _ = x_all.shape
    width = LOCAL * HEAD_DIM

    def far_first(*shape):
        return pl.BlockSpec((1,) + shape, lambda s: (seqs - 1 - s,) + (0,) * len(shape))

    return pl.pallas_call(
        functools.partial(attend_kernel, planes),
        grid=(seqs,),
        in_specs=[
            far_first(rows, D),
            whole(4, D),
            ANY,
            whole(1, 3 * width),
            whole(width, D),
            far_first(3, rows, 128),
            VMEM,
        ],
        out_specs=[far_first(rows, D), far_first(rows, 3 * width), far_first(rows, width), whole(rows, D), ANY, ANY],
        out_shape=[
            jax.ShapeDtypeStruct((seqs, rows, D), BF16),
            jax.ShapeDtypeStruct((seqs, rows, 3 * width), BF16),
            jax.ShapeDtypeStruct((seqs, rows, width), BF16),
            jax.ShapeDtypeStruct((rows, D), F32),
            jax.ShapeDtypeStruct((seqs, rows, D), BF16),
            jax.ShapeDtypeStruct((planes,) + both.shape, BF16),
        ],
        scratch_shapes=[
            pltpu.VMEM((rows, D), BF16),
            pltpu.VMEM((4, rows, D), BF16),
            pltpu.VMEM((D, 3 * width), BF16),
        ]
        + Sum.scratch(rows, D)
        + Sum.sems
        + Gather.sems
        + LineGather.sems(planes)
        + [pltpu.SemaphoreType.DMA],
        cost_estimate=lasting(100),
        compiler_params=params(cid),
    )(x_all, norms, w_qkv, b_qkv, w_out, tables, both)


def attend_back_kernel(
    block_ref, wo_ref, w_ref, qkv_ref, tab_ref, attn_ref, hidden_ref, wd_ref, resid_ref, _,
    gqkv_ref, part_ref, gb_ref, wo_grad_ref, out_ref, held, wo_grad, away, *scratch,
):
    gather, block = Gather(block_ref, held, scratch[:7]), Sum(None, scratch[7:11], scratch[11:], away)
    step = pl.program_id(0)

    @pl.when(step == 0)
    def _():
        greet(gather.near)
        gather.start()
        wo_grad[...] = jnp.zeros_like(wo_grad)

    part = dot(hidden_ref[0], wd_ref[...]).astype(BF16)
    k = 3 - step // 2

    @pl.when(lax.rem(step, 2) == 0)
    def _():
        away[k] = part
        block.near_copy(k).start()

    @pl.when(lax.rem(step, 2) == 1)
    def _():
        block.own[k] = part

    for i in range(TEAM):
        pl.when(step == i)(functools.partial(gather.ready, i))
    grad = held[step]
    width = LOCAL * HEAD_DIM
    wo_grad[...] += dot(attn_ref[0], grad, TN)
    grad_att = dot(grad, wo_ref[...], NT).astype(BF16)
    query, key, value = (qkv_ref[0, :, i * width : (i + 1) * width] for i in range(3))
    allowed = visible(tab_ref[0, 2])
    zero = jnp.zeros((query.shape[0], width), F32)
    grad_query, grad_key, grad_value = zero, zero, zero
    for h in range(LOCAL):
        query_h, key_h, grad_h = head_of(query, h), head_of(key, h), head_of(grad_att, h)
        probs = soft(query_h, key, allowed)
        low = probs.astype(BF16)
        grad_probs = dot(grad_h, value, NT)
        delta = jnp.sum(low.astype(F32) * grad_probs, axis=-1, keepdims=True)
        grad_scores = (probs * (grad_probs - delta)).astype(BF16)
        grad_value = grad_value + dot(low, grad_h, TN)
        grad_query = grad_query + dot(grad_scores, key_h)
        grad_key = grad_key + dot(grad_scores, query_h, TN)
    cosine, sine = wide(tab_ref[0, 0]), -wide(tab_ref[0, 1])
    grad_query = turn(grad_query * 0.125, cosine, sine)
    grad_key = turn(grad_key * 0.125, cosine, sine)
    grad_qkv = jnp.concatenate([grad_query, grad_key, grad_value], axis=1).astype(BF16)
    gqkv_ref[0] = grad_qkv
    gb_ref[0] = jnp.sum(grad_qkv.astype(F32), axis=0, keepdims=True)
    part_ref[0] = dot(grad_qkv, w_ref[...], NT).astype(BF16)

    def use(rows, value):
        out_ref[rows, :] = resid_ref[rows, :] + value

    pl.when(step == 1)(gather.middle)
    for at, advance in ((1, block.middle_a), (3, block.middle_b), (5, block.middle_c), (6, block.middle_two)):
        pl.when(step == at)(advance)

    @pl.when(step == TEAM - 1)
    def _():
        wo_grad_ref[...] = wo_grad[...].astype(BF16)
        block.finish(use)
        gather.sent()


def attend_back(block, w_out, w_qkv, qkv, tables, attn, hidden, w_down, resid, after, cid):
    seqs, rows, _ = qkv.shape
    width = LOCAL * HEAD_DIM

    def far_first(*shape):
        return pl.BlockSpec((1,) + shape, lambda s: (seqs - 1 - s,) + (0,) * len(shape))

    return pl.pallas_call(
        attend_back_kernel,
        grid=(seqs,),
        in_specs=[
            ANY,
            whole(width, D),
            whole(D, 3 * width),
            per_seq(rows, 3 * width),
            per_seq(3, rows, 128),
            per_seq(rows, width),
            far_first(rows, hidden.shape[2]),
            VMEM,
            VMEM,
            ANY,
        ],
        out_specs=[per_seq(rows, 3 * width), per_seq(rows, D), per_seq(1, 3 * width), whole(width, D), whole(rows, D)],
        out_shape=[
            jax.ShapeDtypeStruct((seqs, rows, 3 * width), BF16),
            jax.ShapeDtypeStruct((seqs, rows, D), BF16),
            jax.ShapeDtypeStruct((seqs, 1, 3 * width), F32),
            jax.ShapeDtypeStruct((width, D), BF16),
            jax.ShapeDtypeStruct((rows, D), F32),
        ],
        scratch_shapes=[
            pltpu.VMEM((seqs, rows, D), BF16),
            pltpu.VMEM((width, D), F32),
            pltpu.VMEM((4, rows, D), BF16),
        ]
        + Gather.sems
        + Sum.scratch(rows, D)
        + Sum.sems,
        cost_estimate=lasting(65),
        compiler_params=params(cid, 54),
    )(block, w_out, w_qkv, qkv, tables, attn, hidden, w_down, resid, after)


def team_shards(
    inputs, positions, norm1_gain, norm1_bias, qkv_weight, qkv_bias, out_weight, norm2_gain, norm2_bias,
    gate_weight, up_weight, down_weight, out_grad,
):
    n = lax.axis_size("fsdp")
    planes = n // TEAM
    rows = inputs.shape[0]
    tokens = TEAM * rows
    depth = qkv_weight.shape[0]
    ff = down_weight.shape[0]
    width = LOCAL * HEAD_DIM
    lines = [[z * TEAM + i for z in range(planes)] for i in range(TEAM)]
    mine = lax.rem(lax.axis_index("fsdp"), TEAM)

    def line_sum(x):
        return lax.psum_scatter(x, "fsdp", scatter_dimension=0, tiled=True, axis_index_groups=lines)

    half = ROT // 2
    rate = 10000.0 ** (-np.arange(half) / half)
    rate = np.tile(np.concatenate([rate, rate, np.zeros(HEAD_DIM - ROT)]), 128 // HEAD_DIM)[None].astype(np.float32)
    both, x_all, w_qkv, w_out, tables, norms, b_qkv = opening(
        qkv_weight, gate_weight, up_weight, inputs, out_weight, positions, qkv_bias,
        (norm1_gain, norm1_bias, norm2_gain, norm2_bias), jnp.asarray(rate), planes, 1,
    )
    w_out = w_out.reshape(width, D)
    w_qkv = w_qkv.reshape(D, 3 * width)
    both = both.reshape(TEAM * depth, 2 * planes * ff)
    h_one, qkv, attn_low, resid, h_two, w_both = attend(
        x_all, norms, w_qkv, b_qkv, w_out, tables, both, planes, 2
    )
    w_both = w_both.reshape(D, 2 * planes * ff)
    pre, hidden, grad_down, g_all, w_down = expand(h_two, w_both, out_grad, down_weight, planes, 3)
    w_down = w_down.reshape(planes * ff, D)
    grad_resid, sums_two, block, grad_w_both = mlp_back(
        pre, g_all, h_two.reshape(tokens, D), w_down, w_both, resid, out_grad, norms, grad_down, 5
    )
    grad_down = line_sum(grad_down)
    grad_w_both = line_sum(grad_w_both)
    grad_qkv, part, grad_bias, grad_out, block_out = attend_back(
        block, w_out, w_qkv, qkv, tables, attn_low, hidden, w_down, resid, grad_down, 6
    )
    grad_qkv = grad_qkv.reshape(tokens, 3 * width)
    grad_w_qkv = dot(h_one.reshape(tokens, D), grad_qkv, TN).astype(BF16)
    part, grad_w_qkv = lax.optimization_barrier((part, grad_w_qkv))
    branch = grad_out.reshape(planes, depth, D)
    norm_part, branch, shared = last(part, inputs, norms, branch, sums_two, grad_bias, grad_w_qkv, 7)
    grad_w_qkv = line_sum(grad_w_qkv)
    blocks = grad_w_both.reshape(TEAM, depth, 2 * planes * ff)
    blocks, sums = both_closing(blocks, shared, (norm_part, branch), 9)
    block_out, input_grad = block_out.astype(BF16), grad_resid + norm_part
    grad_gate_w, grad_up_w, grad_out = first_grads(blocks, branch)
    blocks = closing(grad_w_qkv.reshape(TEAM, depth, 3 * width), (input_grad, grad_up_w, sums), 8)
    grad_w_qkv = rest_grads(blocks, planes)

    return (
        block_out,
        input_grad,
        sums[0, :depth],
        sums[1, :depth],
        grad_w_qkv,
        sums[4 : 4 + qkv_bias.shape[0] // depth, :depth].reshape(-1),
        grad_out,
        sums[2, :depth],
        sums[3, :depth],
        grad_gate_w,
        grad_up_w,
        grad_down.astype(F32),
    )


def rotate_pairs(heads, places, sign):
    half_rot = ROT // 2
    frequency = 10000.0 ** (-jnp.arange(half_rot, dtype=jnp.float32) / half_rot)
    angles = places.astype(jnp.float32)[:, None] * frequency[None, :]
    cosine = jnp.cos(angles)[:, None, :]
    sine_part = sign * jnp.sin(angles)[:, None, :]
    front_part = heads[..., :half_rot]
    back_part = heads[..., half_rot:ROT]
    return jnp.concatenate(
        [
            front_part * cosine - back_part * sine_part,
            back_part * cosine + front_part * sine_part,
            heads[..., ROT:],
        ],
        axis=-1,
    )


def by_groups(heads):
    group_heads = min(8, HEADS)
    shaped = heads.reshape(heads.shape[0], HEADS // group_heads, group_heads, HEAD_DIM)
    return jnp.moveaxis(shaped, 1, 0)


def from_groups(grouped):
    return jnp.moveaxis(grouped, 0, 1).reshape(grouped.shape[1], HEADS, HEAD_DIM)


def plain_group(block_items, allowed):
    query_part, key_part, value_part = block_items
    scores = (
        jnp.einsum("qhd,khd->hqk", query_part, key_part, preferred_element_type=jnp.float32) * 0.125
    )
    masked = jnp.where(allowed[None], scores, -1e30)
    row_max = jnp.max(masked, axis=-1, keepdims=True)
    exponent = jnp.exp(masked - row_max)
    row_total = jnp.sum(exponent, axis=-1, keepdims=True)
    soft_probs = (exponent / row_total).astype(jnp.bfloat16)
    mixed_part = jnp.einsum(
        "hqk,khd->qhd", soft_probs, value_part, preferred_element_type=jnp.float32
    )
    return (mixed_part, (row_max + jnp.log(row_total))[..., 0])


def plain_back(block_items, allowed):
    query_part, key_part, value_part, grad_part, row_delta, log_total = block_items
    scores = (
        jnp.einsum("qhd,khd->hqk", query_part, key_part, preferred_element_type=jnp.float32) * 0.125
    )
    soft_probs = jnp.where(allowed[None], jnp.exp(scores - log_total[..., None]), 0.0)
    grad_probs = jnp.einsum(
        "qhd,khd->hqk", grad_part, value_part.astype(jnp.float32), precision=lax.Precision.HIGHEST
    )
    rounded_probs = soft_probs.astype(jnp.bfloat16).astype(jnp.float32)
    grad_value = jnp.einsum("hqk,qhd->khd", rounded_probs, grad_part, precision=lax.Precision.HIGHEST)
    grad_scores = (soft_probs * (grad_probs - row_delta[..., None])).astype(jnp.bfloat16)
    grad_query = 0.125 * jnp.einsum(
        "hqk,khd->qhd", grad_scores, key_part, preferred_element_type=jnp.float32
    )
    grad_key = 0.125 * jnp.einsum(
        "hqk,qhd->khd", grad_scores, query_part, preferred_element_type=jnp.float32
    )
    return (grad_query, grad_key, grad_value)


def shards(
    inputs,
    positions,
    norm1_gain,
    norm1_bias,
    qkv_weight,
    qkv_bias,
    out_weight,
    norm2_gain,
    norm2_bias,
    gate_weight,
    up_weight,
    down_weight,
    out_grad,
):
    tok_rows = inputs.shape[0]
    gain_one, bias_one, w_qkv, b_qkv, w_out = (
        lax.all_gather(norm1_gain, "fsdp", axis=0, tiled=True),
        lax.all_gather(norm1_bias, "fsdp", axis=0, tiled=True),
        lax.all_gather(qkv_weight, "fsdp", axis=0, tiled=True),
        lax.all_gather(qkv_bias, "fsdp", axis=0, tiled=True),
        lax.all_gather(out_weight, "fsdp", axis=0, tiled=True),
    )
    stream = inputs.astype(jnp.float32)
    normed_one, inverse_one = normalize(stream)
    h_one = (normed_one * gain_one.astype(jnp.float32) + bias_one.astype(jnp.float32)).astype(
        jnp.bfloat16
    )
    qkv_pre = jnp.dot(h_one, w_qkv, preferred_element_type=jnp.float32) + b_qkv.astype(jnp.float32)
    qkv_heads = qkv_pre.reshape(tok_rows, 3, HEADS, HEAD_DIM)
    query_low = rotate_pairs(qkv_heads[:, 0], positions, 1.0).astype(jnp.bfloat16)
    key_all = rotate_pairs(qkv_heads[:, 1], positions, 1.0).astype(jnp.bfloat16)
    value_all = qkv_heads[:, 2].astype(jnp.bfloat16)
    token_index = jnp.arange(tok_rows, dtype=jnp.int32)
    allowed = (token_index[None, :] <= token_index[:, None]) & (
        token_index[None, :] >= (token_index - positions)[:, None]
    )
    mixed_grouped, log_grouped = lax.map(
        lambda block_items: plain_group(block_items, allowed),
        (by_groups(query_low), by_groups(key_all), by_groups(value_all)),
    )
    mixed_heads = from_groups(mixed_grouped)
    attn_low = mixed_heads.reshape(tok_rows, D).astype(jnp.bfloat16)
    resid = stream + jnp.dot(attn_low, w_out, preferred_element_type=jnp.float32)
    gain_two, bias_two, w_gate, w_up, w_down = (
        lax.all_gather(norm2_gain, "fsdp", axis=0, tiled=True),
        lax.all_gather(norm2_bias, "fsdp", axis=0, tiled=True),
        lax.all_gather(gate_weight, "fsdp", axis=0, tiled=True),
        lax.all_gather(up_weight, "fsdp", axis=0, tiled=True),
        lax.all_gather(down_weight, "fsdp", axis=0, tiled=True),
    )
    normed_two, inverse_two = normalize(resid)
    h_two = (normed_two * gain_two.astype(jnp.float32) + bias_two.astype(jnp.float32)).astype(
        jnp.bfloat16
    )
    gate_pre = jnp.dot(h_two, w_gate, preferred_element_type=jnp.float32)
    up_pre = jnp.dot(h_two, w_up, preferred_element_type=jnp.float32)
    sigmoid_gate = jax.nn.sigmoid(gate_pre)
    silu_gate = gate_pre * sigmoid_gate
    hidden = (silu_gate * up_pre).astype(jnp.bfloat16)
    block_out = (resid + jnp.dot(hidden, w_down, preferred_element_type=jnp.float32)).astype(
        jnp.bfloat16
    )
    gain_two, w_gate, w_up, w_down = (
        lax.all_gather(norm2_gain, "fsdp", axis=0, tiled=True),
        lax.all_gather(gate_weight, "fsdp", axis=0, tiled=True),
        lax.all_gather(up_weight, "fsdp", axis=0, tiled=True),
        lax.all_gather(down_weight, "fsdp", axis=0, tiled=True),
    )
    grad_down_w = jnp.einsum("tf,td->fd", hidden, out_grad, preferred_element_type=jnp.float32)
    grad_hidden = jnp.einsum("td,fd->tf", out_grad, w_down, preferred_element_type=jnp.float32)
    grad_gate = (
        grad_hidden * up_pre * sigmoid_gate * (1.0 + gate_pre * (1.0 - sigmoid_gate))
    ).astype(jnp.bfloat16)
    grad_up = (grad_hidden * silu_gate).astype(jnp.bfloat16)
    grad_gate_w = jnp.einsum("td,tf->df", h_two, grad_gate, preferred_element_type=jnp.float32)
    grad_up_w = jnp.einsum("td,tf->df", h_two, grad_up, preferred_element_type=jnp.float32)
    grad_htwo = jnp.einsum(
        "tf,df->td", grad_gate, w_gate, preferred_element_type=jnp.float32
    ) + jnp.einsum("tf,df->td", grad_up, w_up, preferred_element_type=jnp.float32)
    grad_gain_two = jnp.sum(grad_htwo * normed_two, axis=0)
    grad_bias_two = jnp.sum(grad_htwo, axis=0)
    grad_resid = out_grad.astype(jnp.float32) + norm_back(
        grad_htwo * gain_two.astype(jnp.float32), normed_two, inverse_two
    )
    mlp_sums = (
        lax.psum_scatter(grad_gain_two, "fsdp", scatter_dimension=0, tiled=True),
        lax.psum_scatter(grad_bias_two, "fsdp", scatter_dimension=0, tiled=True),
        lax.psum_scatter(grad_gate_w, "fsdp", scatter_dimension=0, tiled=True),
        lax.psum_scatter(grad_up_w, "fsdp", scatter_dimension=0, tiled=True),
        lax.psum_scatter(grad_down_w, "fsdp", scatter_dimension=0, tiled=True),
    )
    gain_one, w_qkv, w_out = (
        lax.all_gather(norm1_gain, "fsdp", axis=0, tiled=True),
        lax.all_gather(qkv_weight, "fsdp", axis=0, tiled=True),
        lax.all_gather(out_weight, "fsdp", axis=0, tiled=True),
    )
    grad_branch = grad_resid.astype(jnp.bfloat16)
    grad_out_w = jnp.einsum("ti,td->id", attn_low, grad_branch, preferred_element_type=jnp.float32)
    grad_att = jnp.einsum(
        "td,id->ti", grad_branch, w_out, preferred_element_type=jnp.float32
    ).reshape(tok_rows, HEADS, HEAD_DIM)
    group_heads = min(8, HEADS)
    row_delta = jnp.sum(grad_att * mixed_heads, axis=-1)
    delta_grouped = row_delta.reshape(tok_rows, HEADS // group_heads, group_heads).transpose(
        1, 2, 0
    )
    query_grouped, key_grouped, value_grouped = lax.map(
        lambda block_items: plain_back(block_items, allowed),
        (
            by_groups(query_low),
            by_groups(key_all),
            by_groups(value_all),
            by_groups(grad_att),
            delta_grouped,
            log_grouped,
        ),
    )
    grad_query = from_groups(query_grouped)
    grad_key = from_groups(key_grouped)
    grad_value = from_groups(value_grouped)
    grad_qkv = (
        jnp.stack(
            [
                rotate_pairs(grad_query, positions, -1.0),
                rotate_pairs(grad_key, positions, -1.0),
                grad_value,
            ],
            axis=1,
        )
        .reshape(tok_rows, 3 * D)
        .astype(jnp.bfloat16)
    )
    grad_qkv_w = jnp.einsum("td,tk->dk", h_one, grad_qkv, preferred_element_type=jnp.float32)
    grad_qkv_b = jnp.sum(grad_qkv.astype(jnp.float32), axis=0)
    grad_hone = jnp.einsum("tk,dk->td", grad_qkv, w_qkv, preferred_element_type=jnp.float32)
    grad_gain_one = jnp.sum(grad_hone * normed_one, axis=0)
    grad_bias_one = jnp.sum(grad_hone, axis=0)
    input_grad = grad_resid + norm_back(
        grad_hone * gain_one.astype(jnp.float32), normed_one, inverse_one
    )
    attn_sums = (
        lax.psum_scatter(grad_gain_one, "fsdp", scatter_dimension=0, tiled=True),
        lax.psum_scatter(grad_bias_one, "fsdp", scatter_dimension=0, tiled=True),
        lax.psum_scatter(grad_qkv_w, "fsdp", scatter_dimension=0, tiled=True),
        lax.psum_scatter(grad_qkv_b, "fsdp", scatter_dimension=0, tiled=True),
        lax.psum_scatter(grad_out_w, "fsdp", scatter_dimension=0, tiled=True),
    )
    return (
        block_out,
        input_grad,
        attn_sums[0],
        attn_sums[1],
        attn_sums[2],
        attn_sums[3],
        attn_sums[4],
        mlp_sums[0],
        mlp_sums[1],
        mlp_sums[2],
        mlp_sums[3],
        mlp_sums[4],
    )


def solution(mesh):
    devices = mesh.shape["fsdp"]
    rows, columns = P("fsdp", None), P("fsdp")
    body = team_shards if devices % TEAM == 0 and D == devices * HEAD_DIM else shards
    return jax.shard_map(
        body,
        mesh=mesh,
        in_specs=(rows, columns, columns, columns, rows, columns, rows, columns, columns, rows, rows, rows, rows),
        out_specs=(rows, rows, columns, columns, rows, columns, rows, columns, columns, rows, rows, rows),
        check_vma=False,
    )
```

```python
import functools

import jax
import jax.numpy as jnp
import numpy as np
from jax import lax
from jax.experimental import pallas as pl
from jax.experimental.pallas import tpu as pltpu
from jax.sharding import PartitionSpec as P

D = 2048
HEADS = 32
HEAD_DIM = 64
ROT = 16
EPS = 1e-05
TEAM = 8
LOCAL = HEADS // TEAM
MESH = pl.DeviceIdType.MESH
BF16 = jnp.bfloat16
F32 = jnp.float32
ANY = pl.BlockSpec(memory_space=pl.ANY)
VMEM = pl.BlockSpec(memory_space=pltpu.VMEM)


def lasting(us):
    return pl.CostEstimate(flops=0, bytes_accessed=int(us * 3.6e6), transcendentals=0)


def params(cid=None, limit=56):
    extra = {} if cid is None else {"collective_id": cid, "has_side_effects": True}
    return pltpu.CompilerParams(vmem_limit_bytes=limit * 1024 * 1024, **extra)


def place():
    me = lax.axis_index("fsdp")
    mine = lax.rem(me, TEAM)
    return mine, me - mine, mine // 2, lax.rem(mine, 2)


def chip_at(chip, step):
    along_x, along_y = lax.rem(chip, 2), chip // 2
    if step & 1:
        along_x = 1 - along_x
    if step & 2:
        along_y = 1 - along_y
    return along_y * 2 + along_x


def relation(chip, core, r):
    return chip_at(chip, r // 2) * 2 + lax.rem(core + r, 2)


def greet(devices):
    barrier = pltpu.get_barrier_semaphore()
    for device in devices:
        pl.semaphore_signal(barrier, inc=1, device_id=(device,), device_id_type=MESH)
    pl.semaphore_wait(barrier, len(devices))


def remote(src, dst, send, recv, device):
    return pltpu.make_async_remote_copy(
        src_ref=src, dst_ref=dst, send_sem=send, recv_sem=recv, device_id=(device,), device_id_type=MESH
    )


class Swap:
    sems = [pltpu.SemaphoreType.DMA, pltpu.SemaphoreType.DMA((TEAM,)), pltpu.SemaphoreType.DMA((TEAM,))]

    def __init__(self, src, out, sems, same=False, near_first=False):
        own_sem, send, recv = sems
        mine, base, chip, core = place()
        others = [relation(chip, core, r) for r in range(1, TEAM)]
        self.near = [base + other for other in others]
        self.copies = [
            remote(
                src if same else src.at[other], out.at[r if near_first else mine], send.at[r], recv.at[r], base + other
            )
            for r, other in enumerate(others, 1)
        ]
        own = src if same else src.at[mine]
        self.copies.append(pltpu.make_async_copy(own, out.at[0 if near_first else mine], own_sem))

    def start(self):
        for copy in self.copies:
            copy.start()

    def finish(self):
        for copy in self.copies:
            copy.wait()


class Line:
    def sems(planes):
        return [pltpu.SemaphoreType.DMA, pltpu.SemaphoreType.DMA((planes,)), pltpu.SemaphoreType.DMA((planes,))]

    def __init__(self, planes, src, out, sems, same=False, within=False):
        own_sem, send, recv = sems
        mine, base, _, _ = place()
        plane = base // TEAM
        others = [lax.rem(plane + k, planes) for k in range(1, planes)]
        self.near = [other * TEAM + mine for other in others]
        self.copies = [
            remote(src if same else src.at[other], out.at[plane], send.at[k], recv.at[k], other * TEAM + mine)
            for k, other in enumerate(others)
        ]
        own = src if same else src.at[plane]
        self.own = None if within else pltpu.make_async_copy(own, out.at[plane], own_sem)

    def start(self):
        for copy in self.copies:
            copy.start()
        if self.own is not None:
            self.own.start()

    def finish(self):
        for copy in self.copies:
            copy.wait()
        if self.own is not None:
            self.own.wait()


class LineGather:
    def sems(planes):
        return [pltpu.SemaphoreType.DMA, pltpu.SemaphoreType.DMA((2, planes)), pltpu.SemaphoreType.DMA((2, planes))]

    def __init__(self, planes, src, out, sems):
        own_sem, self.send, self.recv = sems
        mine, base, _, _ = place()
        self.plane, self.planes, self.src, self.out = base // TEAM, planes, src, out
        self.me = base + mine
        self.near = [lax.rem(self.plane + k, planes) * TEAM + mine for k in (1, planes - 1)]
        self.own = pltpu.make_async_copy(src, out.at[self.plane], own_sem)

    def copy(self, way, stage):
        step = 1 - 2 * way
        block, to = self.plane - step * (stage - 1), self.plane + step
        is_there = (block >= 0) & (block < self.planes) & (to >= 0) & (to < self.planes)
        src = self.src if stage == 1 else self.out.at[block]
        sems = self.send.at[way, stage], self.recv.at[way, stage]
        return is_there, remote(src, self.out.at[block], *sems, self.me + step * TEAM)

    def arrived(self, way, stage):
        block = self.plane - (1 - 2 * way) * stage

        @pl.when((block >= 0) & (block < self.planes))
        def _():
            dst = self.out.at[block]
            remote(dst, dst, self.send.at[way, stage], self.recv.at[way, stage], self.me).wait_recv()

    def start(self):
        self.own.start()
        self.stage(1)

    def stage(self, stage):
        for way in (0, 1):
            if stage > 1:
                self.arrived(way, stage - 1)
            is_there, copy = self.copy(way, stage)
            pl.when(is_there)(copy.start)

    def finish(self):
        self.own.wait()
        for way in (0, 1):
            self.arrived(way, self.planes - 1)
            for stage in range(1, self.planes):
                is_there, copy = self.copy(way, stage)
                pl.when(is_there)(copy.wait_send)


def slices(ref, pieces, size):
    return jnp.concatenate([ref[:, i * size : (i + 1) * size] for i in pieces], axis=1)


def unslice(held, parts, planes, outs):
    size = held.shape[2] // (parts * planes)
    for at in range(parts * planes):
        row = jnp.concatenate([held[i, :, at * size : (at + 1) * size] for i in range(TEAM)], axis=1)
        out, first = (outs[at // planes], at % planes) if len(outs) > 1 else (outs[0], at)
        out[:, first * TEAM * size : (first + 1) * TEAM * size] = row.astype(F32)


def first_kernel(planes, held_ref, far_ref, gate_ref, up_ref, wo_ref):
    unslice(held_ref, 2, planes, [gate_ref, up_ref])
    wo_ref[...] = added(far_ref)


def first_grads(held, far):
    _, depth, width = held.shape
    return pl.pallas_call(
        functools.partial(first_kernel, far.shape[0]),
        out_shape=[jax.ShapeDtypeStruct((depth, width * TEAM // 2), F32)] * 2
        + [jax.ShapeDtypeStruct(far.shape[1:], F32)],
        in_specs=[VMEM] * 2,
        out_specs=[VMEM] * 3,
        cost_estimate=lasting(4),
        compiler_params=params(),
    )(held, far)


def rest_kernel(planes, held_ref, w_ref):
    unslice(held_ref, 3, planes, [w_ref])


def rest_grads(held, planes):
    _, depth, width = held.shape
    return pl.pallas_call(
        functools.partial(rest_kernel, planes),
        out_shape=jax.ShapeDtypeStruct((depth, width * TEAM), F32),
        in_specs=[VMEM],
        out_specs=VMEM,
        cost_estimate=lasting(3),
        compiler_params=params(),
    )(held)


def added(ref):
    total = ref[0].astype(F32)
    for i in range(1, ref.shape[0]):
        total = total + ref[i].astype(F32)
    return total


def close_kernel(w_ref, _, __, ___, held_ref, *sems):
    swap = Swap(w_ref, held_ref, sems)
    greet(swap.near)
    swap.start()
    swap.finish()


def both_close_kernel(planes, w_ref, shared_ref, _, __, held_ref, vector_ref, got, block, beyond, *sems):
    swap, inner = Swap(w_ref, held_ref, sems[:3]), Swap(shared_ref, got, sems[3:6])
    outer = Line(planes, block, beyond, sems[6:])
    greet(swap.near + outer.near)
    inner.start()
    swap.start()
    inner.finish()
    block[...] = added(got)
    outer.start()
    outer.finish()
    vector_ref[...] = added(beyond)
    swap.finish()


def both_closing(blocks, shared, after, cid):
    planes = shared.shape[1]
    return pl.pallas_call(
        functools.partial(both_close_kernel, planes),
        out_shape=[jax.ShapeDtypeStruct(blocks.shape, BF16), jax.ShapeDtypeStruct(shared.shape[2:], F32)],
        in_specs=[VMEM, VMEM, ANY, ANY],
        out_specs=[ANY, VMEM],
        scratch_shapes=[pltpu.VMEM(shared.shape, F32)]
        + [pltpu.VMEM(shared.shape[1:], F32)] * 2
        + Swap.sems * 2
        + Line.sems(planes),
        cost_estimate=lasting(22),
        compiler_params=params(cid),
    )(blocks, shared, *after)


def closing(blocks, after, cid):
    return pl.pallas_call(
        close_kernel,
        out_shape=jax.ShapeDtypeStruct(blocks.shape, BF16),
        in_specs=[VMEM, ANY, ANY, ANY],
        out_specs=ANY,
        scratch_shapes=Swap.sems,
        cost_estimate=lasting(14),
        compiler_params=params(cid),
    )(blocks, *after)


class Gather:
    sems = [pltpu.SemaphoreType.DMA((5,)), pltpu.SemaphoreType.DMA((5,)), pltpu.SemaphoreType.DMA((2,)),
            pltpu.SemaphoreType.DMA((2,)), pltpu.SemaphoreType.DMA((6,)), pltpu.SemaphoreType.DMA((6,)),
            pltpu.SemaphoreType.DMA]

    def __init__(self, src, out, sems):
        send, recv, hop_send, hop_recv, pass_send, pass_recv, own_sem = sems
        _, base, chip, core = place()
        side, over = (chip_at(chip, k) * 2 + core for k in (1, 2))
        self.sibling = base + chip * 2 + 1 - core
        self.near = [base + side, base + over, self.sibling]
        half = src.shape[0] // 2
        top, low = pl.ds(0, half), pl.ds(half, half)
        self.first = [
            remote(src.at[part], out.at[at, part], send.at[i], recv.at[i], base + to)
            for i, (part, at, to) in enumerate(((top, 2, side), (low, 4, over), (low, 2, side), (top, 4, over)))
        ]
        self.first.append(remote(src, out.at[1], send.at[4], recv.at[4], self.sibling))
        self.own = pltpu.make_async_copy(src, out.at[0], own_sem)
        self.hops = [
            remote(out.at[at, part], out.at[6, part], hop_send.at[i], hop_recv.at[i], base + to)
            for i, (at, part, to) in enumerate(((2, top, over), (4, low, side)))
        ]
        self.passed = [
            remote(out.at[at, part], out.at[at + 1, part], pass_send.at[i], pass_recv.at[i], self.sibling)
            for i, (at, part) in enumerate(((2, top), (4, low), (2, low), (4, top), (6, top), (6, low)))
        ]

    def start(self):
        for copy in self.first:
            copy.start()
        self.own.start()

    def middle(self):
        for i in (0, 1):
            self.first[i].wait_recv()
            self.hops[i].start()
            self.passed[i].start()

    def finish(self):
        for i in range(2, TEAM):
            self.ready(i)
        self.first[4].wait_recv()
        self.own.wait()
        self.sent()

    def ready(self, i):
        if i == 0:
            self.own.wait()
        elif i == 1:
            self.first[4].wait_recv()
        elif i == 6:
            for j in (0, 1):
                self.hops[j].wait_recv()
                self.passed[4 + j].start()
        elif i % 2 == 0:
            self.first[1 + i // 2].wait_recv()
            self.passed[1 + i // 2].start()
        else:
            for j in {3: (0, 2), 5: (1, 3), 7: (4, 5)}[i]:
                self.passed[j].wait_recv()

    def sent(self):
        for copy in self.first + self.hops + self.passed:
            copy.wait_send()


class Sum:
    def scratch(rows, width):
        return [pltpu.VMEM((4, rows, width), BF16), pltpu.VMEM((4, rows, width), BF16),
                pltpu.VMEM((2, rows // 2, width), BF16), pltpu.VMEM((2, rows, width), BF16)]

    sems = [pltpu.SemaphoreType.DMA((4,))] * 3 + [pltpu.SemaphoreType.DMA((2,))] * 2 + [pltpu.SemaphoreType.DMA((4,))] * 2

    def __init__(self, blocks, scratch, sems, away=None):
        self.own, self.beside, self.via, self.far = scratch
        load_sem, near_send, near_recv, via_send, via_recv, far_send, far_recv = sems
        _, base, chip, core = place()
        sibling = base + chip * 2 + 1 - core
        side, over = (base + chip_at(chip, k) * 2 + core for k in (1, 2))
        self.near = [side, over, sibling]
        self.half = self.own.shape[1] // 2
        top, low = pl.ds(0, self.half), pl.ds(self.half, self.half)
        self.loads = [
            pltpu.make_async_copy(blocks.at[2 * k], self.own.at[k], load_sem.at[k])
            for k in range(4)
            if away is None
        ]

        def near_copy(k):
            src = blocks.at[2 * k + 1] if away is None else away.at[k]
            return remote(src, self.beside.at[k], near_send.at[k], near_recv.at[k], sibling)

        self.near_copy = near_copy
        self.nears = [near_copy(k) for k in range(4)]
        self.vias = [
            remote(self.own.at[3, part], self.via.at[i], via_send.at[i], via_recv.at[i], to)
            for i, (part, to) in enumerate(((top, side), (low, over)))
        ]
        self.fars = [
            remote(self.own.at[k, part], self.far.at[k - 1, part], far_send.at[i], far_recv.at[i], to)
            for i, (k, part, to) in enumerate(((2, low, over), (1, top, side), (2, top, over), (1, low, side)))
        ]

    def start(self):
        for k in (3, 2, 1, 0):
            self.loads[k].start()
            self.nears[k].start()

    def pair(self, k):
        if self.loads:
            self.loads[k].wait()
        self.nears[k].wait_recv()

        @pl.loop(0, self.own.shape[1] // 16)
        def _(i):
            part = pl.ds(pl.multiple_of(i * 16, 16), 16)
            self.own[k, part, :] = (self.own[k, part, :].astype(F32) + self.beside[k, part, :].astype(F32)).astype(BF16)

    def middle_a(self):
        self.pair(3)
        for copy in self.vias:
            copy.start()

    def middle_b(self):
        self.pair(2)
        self.fars[0].start()

    def middle_c(self):
        self.pair(1)
        self.fars[1].start()

    def middle(self):
        self.middle_a()
        self.middle_b()
        self.middle_c()

    def middle_two(self):
        for i, k in ((0, 2), (1, 1)):
            self.vias[i].wait_recv()

            @pl.loop(0, self.half // 16)
            def _(j, i=i, k=k):
                part = pl.ds(pl.multiple_of(j * 16, 16), 16)
                at = pl.ds(pl.multiple_of(j * 16 + i * self.half, 16), 16)
                self.own[k, at, :] = (self.own[k, at, :].astype(F32) + self.via[i, part, :].astype(F32)).astype(BF16)

            self.fars[2 + i].start()

    def finish(self, use):
        if self.loads:
            self.loads[0].wait()
        self.nears[0].wait_recv()
        for copy in self.fars:
            copy.wait_recv()

        @pl.loop(0, self.own.shape[1] // 16)
        def _(i):
            part = pl.ds(pl.multiple_of(i * 16, 16), 16)
            total = self.own[0, part, :].astype(F32) + self.beside[0, part, :].astype(F32)
            use(part, total + self.far[0, part, :].astype(F32) + self.far[1, part, :].astype(F32))

        for copy in self.nears + self.vias + self.fars:
            copy.wait_send()


def fold(x):
    return x[:8] + x[8:]


def expand_kernel(
    planes, h_ref, w_ref, g_ref, down_ref, pre_ref, hidden_ref, grad_ref, g_all_ref, wd_ref, held, g, total, w, *sems
):
    gather, line = Gather(g_ref, g_all_ref, sems[:7]), LineGather(planes, down_ref, wd_ref, sems[7:10])
    step = pl.program_id(0)

    @pl.when(step == 0)
    def _():
        greet(gather.near + line.near)
        line.start()
        gather.start()
        weights = pltpu.make_async_copy(w_ref, w, sems[11])
        weights.start()
        weights.wait()

    pre = dot(h_ref[0], w[...])
    pre_ref[0] = pre
    ff = hidden_ref.shape[2]
    gate_pre, up_pre = pre[:, :ff], pre[:, ff:]
    hidden = (gate_pre * jax.nn.sigmoid(gate_pre) * up_pre).astype(BF16)
    hidden_ref[0] = hidden
    held[step] = hidden
    pl.when(step == TEAM - 3)(functools.partial(line.stage, 2))

    @pl.when(step == TEAM - 1)
    def _():
        def load(i):
            return pltpu.make_async_copy(g_all_ref.at[i], g.at[i % 2], sems[10].at[i % 2])

        gather.middle()
        gather.ready(0)
        load(0).start()
        for i in range(TEAM):
            if i < TEAM - 1:
                gather.ready(i + 1)
                load(i + 1).start()
            load(i).wait()
            product = dot(held[i], g[i % 2], TN)
            total[...] = product if i == 0 else total[...] + product
            if i == 4:
                for stage in range(3, planes):
                    line.stage(stage)
        grad_ref[...] = total[...].astype(BF16)
        gather.sent()
        line.finish()


def expand(h_two, w_both, out_grad, down, planes, cid):
    seqs, rows, _ = h_two.shape
    width = w_both.shape[1]
    return pl.pallas_call(
        functools.partial(expand_kernel, planes),
        grid=(seqs,),
        in_specs=[per_seq(rows, D), ANY, VMEM, VMEM],
        out_specs=[per_seq(rows, width), per_seq(rows, width // 2), whole(width // 2, D), ANY, ANY],
        out_shape=[
            jax.ShapeDtypeStruct((seqs, rows, width), F32),
            jax.ShapeDtypeStruct((seqs, rows, width // 2), BF16),
            jax.ShapeDtypeStruct((width // 2, D), BF16),
            jax.ShapeDtypeStruct((seqs, rows, D), BF16),
            jax.ShapeDtypeStruct((planes,) + down.shape, BF16),
        ],
        scratch_shapes=[
            pltpu.VMEM((seqs, rows, width // 2), BF16),
            pltpu.VMEM((2, rows, D), BF16),
            pltpu.VMEM((width // 2, D), F32),
            pltpu.VMEM((D, width), BF16),
        ]
        + Gather.sems
        + LineGather.sems(planes)
        + [pltpu.SemaphoreType.DMA((2,)), pltpu.SemaphoreType.DMA],
        cost_estimate=lasting(55),
        compiler_params=params(cid),
    )(h_two, w_both, out_grad, down)


def mlp_back_kernel(
    pre_ref, g_all_ref, h_ref, wd_ref, w_ref, resid_ref, g_ref, norm_ref, _,
    out_ref, sums_ref, block_ref, grad_w_ref,
    pre, g_all, turned, made, grads, away, w, resid, own_grad, wd, *scratch,
):
    pre_sem, g_sem, turned_sem, made_sem, late_sem = scratch[11:]
    total = Sum(None, scratch[:4], scratch[4:11], away)
    rows, ff = pre_ref.shape[1], wd_ref.shape[0]
    chunk = turned.shape[2]

    def loads(i):
        slot, at = lax.rem(i, 2), TEAM - 1 - i
        return (
            pltpu.make_async_copy(pre_ref.at[at], pre.at[slot], pre_sem.at[slot]),
            pltpu.make_async_copy(g_all_ref.at[at], g_all.at[slot], g_sem.at[slot]),
        )

    def load_chunk(i):
        slot = lax.rem(i, 2)
        columns = pl.ds(pl.multiple_of(i * chunk, chunk), chunk)
        return pltpu.make_async_copy(h_ref.at[:, columns], turned.at[slot], turned_sem.at[slot])

    def store_chunk(i):
        slot = lax.rem(i, 2)
        part = pl.ds(pl.multiple_of(i * chunk, chunk), chunk)
        return pltpu.make_async_copy(made.at[slot], grad_w_ref.at[part, :], made_sem.at[slot])

    for copy in loads(0):
        copy.start()
    late = [
        pltpu.make_async_copy(src, dst, late_sem.at[i])
        for i, (src, dst) in enumerate(((wd_ref, wd), (w_ref, w), (resid_ref, resid), (g_ref, own_grad)))
    ]
    for copy in late:
        copy.start()
    greet(total.near)

    @pl.loop(0, TEAM)
    def _(i):
        slot = lax.rem(i, 2)
        k, at = 3 - i // 2, TEAM - 1 - i

        @pl.when(i < TEAM - 1)
        def _():
            for copy in loads(i + 1):
                copy.start()

        for copy in loads(i):
            copy.wait()
        pl.when(i == 0)(late[0].wait)
        grad_hidden = dot(g_all[slot], wd[...], NT)
        gate_pre, up_pre = pre[slot, :, :ff], pre[slot, :, ff:]
        sigmoid = jax.nn.sigmoid(gate_pre)
        grad_gate = grad_hidden * up_pre * sigmoid * (1.0 + gate_pre * (1.0 - sigmoid))
        grad_up = grad_hidden * (gate_pre * sigmoid)
        part = pl.ds(pl.multiple_of(at * rows, rows), rows)
        grads[part, :] = jnp.concatenate([grad_gate, grad_up], axis=1).astype(BF16)

        def make(to):
            to[k] = dot(grads[part, :], w[...], NT).astype(BF16)

        pl.when(i == 0)(late[1].wait)

        @pl.when(lax.rem(i, 2) == 0)
        def _():
            make(away)
            total.near_copy(k).start()

        @pl.when(lax.rem(i, 2) == 1)
        def _():
            make(total.own)

        for step, advance in ((1, total.middle_a), (3, total.middle_b), (5, total.middle_c)):
            pl.when(i == step)(advance)

    load_chunk(0).start()
    total.middle_two()
    chunks = h_ref.shape[1] // chunk

    @pl.loop(0, chunks)
    def _(i):
        slot = lax.rem(i, 2)

        @pl.when(i < chunks - 1)
        def _():
            load_chunk(i + 1).start()

        load_chunk(i).wait()

        @pl.when(i >= 2)
        def _():
            store_chunk(i - 2).wait()

        made[slot] = dot(turned[slot], grads[...], TN).astype(BF16)
        store_chunk(i).start()

    sums_ref[...] = jnp.zeros_like(sums_ref)
    for copy in late[2:]:
        copy.wait()

    def use(rows, value):
        normed, inverse = normalize(resid[rows, :])
        sums_ref[:8, :] += fold(value * normed)
        sums_ref[8:, :] += fold(value)
        grad = own_grad[rows, :].astype(F32) + norm_back(value * norm_ref[2:3, :], normed, inverse)
        out_ref[rows, :] = grad
        block_ref[rows, :] = grad.astype(BF16)

    total.finish(use)
    store_chunk(chunks - 2).wait()
    store_chunk(chunks - 1).wait()


def mlp_back(pre, g_all, h_two, w_down, w_both, resid, out_grad, gain, after, cid):
    seqs, rows, both = pre.shape
    width = resid.shape[1]
    chunk = 256
    two = pltpu.SemaphoreType.DMA((2,))
    return pl.pallas_call(
        mlp_back_kernel,
        out_shape=[
            jax.ShapeDtypeStruct((rows, width), F32),
            jax.ShapeDtypeStruct((16, width), F32),
            jax.ShapeDtypeStruct((rows, width), BF16),
            jax.ShapeDtypeStruct((width, both), BF16),
        ],
        in_specs=[ANY, ANY, ANY, ANY, ANY, ANY, ANY, VMEM, ANY],
        out_specs=[VMEM, VMEM, VMEM, ANY],
        scratch_shapes=[
            pltpu.VMEM((2, rows, both), F32),
            pltpu.VMEM((2, rows, width), BF16),
            pltpu.VMEM((2, seqs * rows, chunk), BF16),
            pltpu.VMEM((2, chunk, both), BF16),
            pltpu.VMEM((seqs * rows, both), BF16),
            pltpu.VMEM((4, rows, width), BF16),
            pltpu.VMEM((width, both), BF16),
            pltpu.VMEM((rows, width), F32),
            pltpu.VMEM((rows, width), BF16),
            pltpu.VMEM((both // 2, width), BF16),
        ]
        + Sum.scratch(rows, width)
        + Sum.sems
        + [two] * 4
        + [pltpu.SemaphoreType.DMA((4,))],
        cost_estimate=lasting(60),
        compiler_params=params(cid, 50),
    )(pre, g_all, h_two, w_down, w_both, resid, out_grad, gain, after)


def share(x, sums, bias, planes, per, depth):
    mine = place()[0]
    x[...] = jnp.zeros_like(x)
    sums = [jnp.sum(v, axis=0, keepdims=True) for v in sums]
    for z in range(planes):
        for i in range(TEAM):
            at = (z * TEAM + i) * depth
            for row, v in enumerate(sums):
                x[i, z, row : row + 1, :depth] = v[:, at : at + depth]
    for part in range(3):
        for z in range(planes):
            head = part * HEADS + z * TEAM + mine
            owner = head // per
            at = (part * planes + z) * HEAD_DIM
            x[lax.rem(owner, TEAM), owner // TEAM, pl.ds(4 + lax.rem(head, per), 1), :depth] = bias[:, at : at + HEAD_DIM]


def last_kernel(
    planes, part_ref, x_ref, norm_ref, branch_ref, sums_two_ref, bias_ref, _,
    out_ref, far_ref, shared_ref, sums, *scratch,
):
    total, line = Sum(part_ref, scratch[:4], scratch[4:11]), Line(planes, branch_ref, far_ref, scratch[11:])
    greet(total.near + line.near)
    line.start()
    total.start()
    total.middle()
    total.middle_two()
    sums[...] = jnp.zeros_like(sums)

    def use(rows, value):
        normed, inverse = normalize(x_ref[rows, :].astype(F32))
        sums[:8, :] += fold(value * normed)
        sums[8:, :] += fold(value)
        out_ref[rows, :] = norm_back(value * norm_ref[0:1, :], normed, inverse)

    total.finish(use)
    vectors = [sums[:8, :], sums[8:, :], sums_two_ref[:8, :], sums_two_ref[8:, :]]
    depth = part_ref.shape[2] // (planes * TEAM)
    share(shared_ref, vectors, added(bias_ref), planes, bias_ref.shape[2] // (planes * depth), depth)
    line.finish()


def last(part, inputs, gain, branch, sums_two, bias, after, cid):
    rows, width = inputs.shape
    planes = branch.shape[0]
    vectors = (TEAM, planes, 8, 128)
    return pl.pallas_call(
        functools.partial(last_kernel, planes),
        out_shape=[
            jax.ShapeDtypeStruct((rows, width), F32),
            jax.ShapeDtypeStruct(branch.shape, BF16),
            jax.ShapeDtypeStruct(vectors, F32),
        ],
        in_specs=[ANY, VMEM, VMEM, VMEM, VMEM, VMEM, ANY],
        out_specs=[VMEM, ANY, VMEM],
        scratch_shapes=[pltpu.VMEM((16, width), F32)]
        + Sum.scratch(rows, width)
        + Sum.sems
        + Line.sems(planes),
        cost_estimate=lasting(58),
        compiler_params=params(cid),
    )(part, inputs, gain, branch, sums_two, bias, after)


def dot(a, b, dims=((1,), (0,))):
    return lax.dot_general(a, b, (dims, ((), ())), preferred_element_type=F32)


NT = ((1,), (1,))
TN = ((0,), (0,))


def normalize(stream):
    average = jnp.mean(stream, axis=-1, keepdims=True)
    centered = stream - average
    variance = jnp.mean(centered * centered, axis=-1, keepdims=True)
    inverse = lax.rsqrt(variance + EPS)
    return centered * inverse, inverse


def norm_back(grad_norm, normed, inverse):
    return inverse * (
        grad_norm
        - jnp.mean(grad_norm, axis=-1, keepdims=True)
        - normed * jnp.mean(grad_norm * normed, axis=-1, keepdims=True)
    )


def turn(heads, cosine, sine):
    half, width = ROT // 2, heads.shape[-1]
    lanes = lax.broadcasted_iota(jnp.int32, heads.shape, 1) % HEAD_DIM
    moved = jnp.where(lanes < half, -pltpu.roll(heads, width - half, 1), pltpu.roll(heads, half, 1))
    return heads * cosine + moved * sine


def wide(table):
    return jnp.concatenate([table] * (LOCAL * HEAD_DIM // 128), axis=1)


def visible(start):
    size = start.shape[0]
    rows = lax.broadcasted_iota(jnp.int32, (size, size), 0)
    columns = lax.broadcasted_iota(jnp.int32, (size, size), 1)
    start = jnp.concatenate([start] * (size // start.shape[1]), axis=1)
    return (columns <= rows) & (columns.astype(F32) >= start)


def head_of(x, h):
    lanes = lax.broadcasted_iota(jnp.int32, x.shape, 1)
    return jnp.where((lanes >= h * HEAD_DIM) & (lanes < (h + 1) * HEAD_DIM), x, jnp.zeros_like(x))


def soft(query, key, allowed):
    scores = dot(query, key, NT) * 0.125
    masked = jnp.where(allowed, scores, -1e30)
    exponent = jnp.exp(masked - jnp.max(masked, axis=-1, keepdims=True))
    return exponent / jnp.sum(exponent, axis=-1, keepdims=True)


def attend_kernel(planes, qkv_w_ref, gate_ref, up_ref, x_ref, out_weight_ref, position_ref, bias_ref, *refs):
    vector_refs, rate_ref = refs[:4], refs[4]
    h_ref, qkv_ref, attn_ref, resid_ref, h_two_ref, w_both_ref, w_qkv_ref, w_out_ref, tab_ref, norm_ref = refs[5:15]
    cut, landed, made, both, small_ref, place_ref, all_ref, places_ref, tables = refs[15:24]
    x_all, w, wo, norms, b, block, away = refs[24:31]
    sems, scratch = refs[31:60], refs[60:]
    mine, base, _, _ = place()
    plane = base // TEAM
    swap, gather = Swap(made, both, sems[:3]), Gather(x_ref, x_all, sems[3:10])
    vectors = Swap(small_ref, all_ref.at[plane], sems[10:13], same=True)
    places = Swap(place_ref, places_ref, sems[13:16], same=True, near_first=True)
    line = Line(planes, all_ref.at[plane], all_ref, sems[16:19], same=True, within=True)
    rows, heads = LineGather(planes, landed, w, sems[19:22]), Swap(cut, landed, sems[22:25])
    outs = LineGather(planes, out_weight_ref, wo, sems[25:28])
    total, spread = Sum(None, scratch[:4], scratch[4:11], away), Gather(block, h_two_ref, scratch[11:18])
    wide_line = LineGather(planes, both, w_both_ref, scratch[18:21])
    stores = [
        pltpu.make_async_copy(src, dst, scratch[21].at[i])
        for i, (src, dst) in enumerate(((w, w_qkv_ref), (wo, w_out_ref), (tables, tab_ref)))
    ]
    step = pl.program_id(0)
    slot = TEAM - 1 - step

    @pl.when(step == 0)
    def _():
        depth = gate_ref.shape[0]
        for row, ref in enumerate(vector_refs):
            small_ref[row : row + 1, :depth] = ref[...].astype(F32).reshape(1, depth)
        bias = bias_ref[...].astype(F32).reshape(1, bias_ref.shape[0])
        for i in range(bias_ref.shape[0] // depth):
            small_ref[4 + i : 5 + i, :depth] = bias[:, i * depth : (i + 1) * depth]
        known = position_ref[...].astype(F32).reshape(1, position_ref.shape[0])
        for i in range(position_ref.shape[0] // 128):
            place_ref[i : i + 1, :] = known[:, i * 128 : (i + 1) * 128]
        for i in range(TEAM):
            cut[i] = slices(qkv_w_ref, [s * HEADS + z * TEAM + i for s in range(3) for z in range(planes)], HEAD_DIM)
        greet(swap.near + line.near)
        outs.start()
        heads.start()
        vectors.start()
        places.start()
        size = gate_ref.shape[1] // (planes * TEAM)
        for i in range(TEAM):
            units = [z * TEAM + i for z in range(planes)]
            made[i] = jnp.concatenate([slices(gate_ref, units, size), slices(up_ref, units, size)], axis=1)
        outs.stage(2)
        heads.finish()
        rows.start()
        gather.start()
        swap.start()
        vectors.finish()
        line.start()
        for stage in range(3, planes):
            outs.stage(stage)
        places.finish()
        square = (128, 128)

        @pl.loop(0, TEAM)
        def _(i):
            known = places_ref[i]
            for part in range(tables.shape[2] // 128):
                at = jnp.transpose(jnp.broadcast_to(known[part : part + 1, :], square))
                here = pl.ds(part * 128, 128)
                angle = at * rate_ref[...]
                tables[i, 0, here, :] = jnp.cos(angle)
                tables[i, 1, here, :] = jnp.sin(angle)
                token = lax.broadcasted_iota(jnp.int32, square, 0) + part * 128
                tables[i, 2, here, :] = token.astype(F32) - at

        rows.stage(2)
        gather.middle()
        for stage in range(3, planes):
            rows.stage(stage)
        line.finish()
        each = [all_ref[z, i] for z in range(planes) for i in range(TEAM)]
        for i in range(4):
            norms[i : i + 1, :] = jnp.concatenate([known[i : i + 1, :depth] for known in each], axis=1)
        per = qkv_w_ref.shape[1] // (planes * TEAM * depth)
        bias = []
        for part in range(3):
            for z in range(planes):
                head = part * HEADS + z * TEAM + mine
                known = all_ref[head // per // TEAM, lax.rem(head // per, TEAM)]
                row = lax.broadcasted_iota(jnp.int32, known.shape, 0) == 4 + lax.rem(head, per)
                bias.append(jnp.sum(jnp.where(row, known, 0.0), axis=0, keepdims=True)[:, :depth])
        b[...] = jnp.concatenate(bias, axis=1)
        gather.finish()
        swap.finish()
        rows.finish()
        outs.finish()
        wide_line.start()
        for copy in stores:
            copy.start()

    pl.when(step == TEAM - 2)(functools.partial(wide_line.stage, 2))
    stream = x_all[slot].astype(F32)
    normed, _ = normalize(stream)
    h_one = (normed * norms[0:1, :] + norms[1:2, :]).astype(BF16)
    h_ref[0] = h_one
    qkv = dot(h_one, w[...].reshape(-1, w.shape[-1])) + b[...]
    width = LOCAL * HEAD_DIM
    cosine, sine = wide(tables[slot, 0]), wide(tables[slot, 1])
    query = turn(qkv[:, :width], cosine, sine).astype(BF16)
    key = turn(qkv[:, width : 2 * width], cosine, sine).astype(BF16)
    value = qkv[:, 2 * width :].astype(BF16)
    qkv_ref[0, :, :width] = query
    qkv_ref[0, :, width : 2 * width] = key
    qkv_ref[0, :, 2 * width :] = value
    allowed = visible(tables[slot, 2])
    mixed = jnp.zeros((query.shape[0], width), F32)
    for h in range(LOCAL):
        probs = soft(head_of(query, h), key, allowed).astype(BF16)
        mixed = mixed + dot(probs, head_of(value, h))
    attn_low = mixed.astype(BF16)
    attn_ref[0] = attn_low
    part = dot(attn_low, wo[...].reshape(-1, D)).astype(BF16)
    k = 3 - step // 2

    @pl.when(lax.rem(step, 2) == 0)
    def _():
        away[k] = part
        total.near_copy(k).start()

    @pl.when(lax.rem(step, 2) == 1)
    def _():
        total.own[k] = part

    for at, advance in ((1, total.middle_a), (3, total.middle_b), (5, total.middle_c), (6, total.middle_two)):
        pl.when(step == at)(advance)

    def use(rows, value):
        resid = x_all[0, rows, :].astype(F32) + value
        resid_ref[rows, :] = resid
        normed, _ = normalize(resid)
        block[rows, :] = (normed * norms[2:3, :] + norms[3:4, :]).astype(BF16)

    @pl.when(step == TEAM - 1)
    def _():
        total.finish(use)
        spread.start()
        for stage in range(3, planes):
            wide_line.stage(stage)
        spread.middle()
        norm_ref[...] = norms[...]
        spread.finish()
        wide_line.finish()
        for copy in stores:
            copy.wait()


def per_seq(*shape):
    return pl.BlockSpec((1,) + shape, lambda s: (s,) + (0,) * len(shape))


def whole(*shape):
    return pl.BlockSpec(shape, lambda s: (0,) * len(shape))


def attend(qkv, gate, up, inputs, out_weight, positions, bias, vectors, rate, planes, cid):
    rows, _ = inputs.shape
    depth, width = qkv.shape[0], LOCAL * HEAD_DIM
    heads, units = (TEAM, depth, 3 * width), (TEAM, depth, 2 * gate.shape[1] // TEAM)
    tables = (TEAM, 3, rows, 128)
    known = [
        jax.ShapeDtypeStruct((planes,) + units, BF16),
        jax.ShapeDtypeStruct((planes,) + heads, BF16),
        jax.ShapeDtypeStruct((planes,) + out_weight.shape, BF16),
        jax.ShapeDtypeStruct(tables, F32),
    ]

    def far_first(*shape):
        return pl.BlockSpec((1,) + shape, lambda s: (TEAM - 1 - s,) + (0,) * len(shape))

    return pl.pallas_call(
        functools.partial(attend_kernel, planes),
        grid=(TEAM,),
        in_specs=[VMEM] * 12,
        out_specs=[far_first(rows, D), far_first(rows, 3 * width), far_first(rows, width), whole(rows, D)]
        + [ANY] * 5
        + [whole(4, D)],
        out_shape=[
            jax.ShapeDtypeStruct((TEAM, rows, D), BF16),
            jax.ShapeDtypeStruct((TEAM, rows, 3 * width), BF16),
            jax.ShapeDtypeStruct((TEAM, rows, width), BF16),
            jax.ShapeDtypeStruct((rows, D), F32),
            jax.ShapeDtypeStruct((TEAM, rows, D), BF16),
        ]
        + known
        + [jax.ShapeDtypeStruct((4, D), F32)],
        scratch_shapes=[
            pltpu.VMEM(heads, BF16),
            pltpu.VMEM(heads, BF16),
            pltpu.VMEM(units, BF16),
            pltpu.VMEM(units, BF16),
            pltpu.VMEM((8, 128), F32),
            pltpu.VMEM((8, 128), F32),
            pltpu.VMEM((planes, TEAM, 8, 128), F32),
            pltpu.VMEM((TEAM, 8, 128), F32),
            pltpu.VMEM(tables, F32),
            pltpu.VMEM((TEAM, rows, D), BF16),
            pltpu.VMEM((planes,) + heads, BF16),
            pltpu.VMEM((planes,) + out_weight.shape, BF16),
            pltpu.VMEM((4, D), F32),
            pltpu.VMEM((1, 3 * width), F32),
            pltpu.VMEM((rows, D), BF16),
            pltpu.VMEM((4, rows, D), BF16),
        ]
        + Swap.sems
        + Gather.sems
        + Swap.sems * 2
        + Line.sems(planes)
        + LineGather.sems(planes)
        + Swap.sems
        + LineGather.sems(planes)
        + [pltpu.SemaphoreType.DMA]
        + Sum.scratch(rows, D)
        + Sum.sems
        + Gather.sems
        + LineGather.sems(planes)
        + [pltpu.SemaphoreType.DMA((3,))],
        cost_estimate=lasting(180),
        compiler_params=params(cid),
    )(qkv, gate, up, inputs, out_weight, positions, bias, *vectors, rate)


def attend_back_kernel(
    block_ref, wo_ref, w_ref, qkv_ref, tab_ref, attn_ref, hidden_ref, wd_ref, resid_ref, _,
    gqkv_ref, part_ref, gb_ref, wo_grad_ref, out_ref, held, wo_grad, away, *scratch,
):
    gather, block = Gather(block_ref, held, scratch[:7]), Sum(None, scratch[7:11], scratch[11:], away)
    step = pl.program_id(0)

    @pl.when(step == 0)
    def _():
        greet(gather.near)
        gather.start()
        wo_grad[...] = jnp.zeros_like(wo_grad)

    part = dot(hidden_ref[0], wd_ref[...]).astype(BF16)
    k = 3 - step // 2

    @pl.when(lax.rem(step, 2) == 0)
    def _():
        away[k] = part
        block.near_copy(k).start()

    @pl.when(lax.rem(step, 2) == 1)
    def _():
        block.own[k] = part

    for i in range(TEAM):
        pl.when(step == i)(functools.partial(gather.ready, i))
    grad = held[step]
    width = LOCAL * HEAD_DIM
    wo_grad[...] += dot(attn_ref[0], grad, TN)
    grad_att = dot(grad, wo_ref[...], NT).astype(BF16)
    query, key, value = (qkv_ref[0, :, i * width : (i + 1) * width] for i in range(3))
    allowed = visible(tab_ref[0, 2])
    zero = jnp.zeros((query.shape[0], width), F32)
    grad_query, grad_key, grad_value = zero, zero, zero
    for h in range(LOCAL):
        query_h, key_h, grad_h = head_of(query, h), head_of(key, h), head_of(grad_att, h)
        probs = soft(query_h, key, allowed)
        low = probs.astype(BF16)
        grad_probs = dot(grad_h, value, NT)
        delta = jnp.sum(low.astype(F32) * grad_probs, axis=-1, keepdims=True)
        grad_scores = (probs * (grad_probs - delta)).astype(BF16)
        grad_value = grad_value + dot(low, grad_h, TN)
        grad_query = grad_query + dot(grad_scores, key_h)
        grad_key = grad_key + dot(grad_scores, query_h, TN)
    cosine, sine = wide(tab_ref[0, 0]), -wide(tab_ref[0, 1])
    grad_query = turn(grad_query * 0.125, cosine, sine)
    grad_key = turn(grad_key * 0.125, cosine, sine)
    grad_qkv = jnp.concatenate([grad_query, grad_key, grad_value], axis=1).astype(BF16)
    gqkv_ref[0] = grad_qkv
    gb_ref[0] = jnp.sum(grad_qkv.astype(F32), axis=0, keepdims=True)
    part_ref[0] = dot(grad_qkv, w_ref[...], NT).astype(BF16)

    def use(rows, value):
        out_ref[rows, :] = resid_ref[rows, :] + value

    pl.when(step == 1)(gather.middle)
    for at, advance in ((1, block.middle_a), (3, block.middle_b), (5, block.middle_c), (6, block.middle_two)):
        pl.when(step == at)(advance)

    @pl.when(step == TEAM - 1)
    def _():
        wo_grad_ref[...] = wo_grad[...].astype(BF16)
        block.finish(use)
        gather.sent()


def attend_back(block, w_out, w_qkv, qkv, tables, attn, hidden, w_down, resid, after, cid):
    seqs, rows, _ = qkv.shape
    width = LOCAL * HEAD_DIM

    def far_first(*shape):
        return pl.BlockSpec((1,) + shape, lambda s: (seqs - 1 - s,) + (0,) * len(shape))

    return pl.pallas_call(
        attend_back_kernel,
        grid=(seqs,),
        in_specs=[
            ANY,
            whole(width, D),
            whole(D, 3 * width),
            per_seq(rows, 3 * width),
            per_seq(3, rows, 128),
            per_seq(rows, width),
            far_first(rows, hidden.shape[2]),
            VMEM,
            VMEM,
            ANY,
        ],
        out_specs=[per_seq(rows, 3 * width), per_seq(rows, D), per_seq(1, 3 * width), whole(width, D), whole(rows, D)],
        out_shape=[
            jax.ShapeDtypeStruct((seqs, rows, 3 * width), BF16),
            jax.ShapeDtypeStruct((seqs, rows, D), BF16),
            jax.ShapeDtypeStruct((seqs, 1, 3 * width), F32),
            jax.ShapeDtypeStruct((width, D), BF16),
            jax.ShapeDtypeStruct((rows, D), F32),
        ],
        scratch_shapes=[
            pltpu.VMEM((seqs, rows, D), BF16),
            pltpu.VMEM((width, D), F32),
            pltpu.VMEM((4, rows, D), BF16),
        ]
        + Gather.sems
        + Sum.scratch(rows, D)
        + Sum.sems,
        cost_estimate=lasting(65),
        compiler_params=params(cid, 54),
    )(block, w_out, w_qkv, qkv, tables, attn, hidden, w_down, resid, after)


def team_shards(
    inputs, positions, norm1_gain, norm1_bias, qkv_weight, qkv_bias, out_weight, norm2_gain, norm2_bias,
    gate_weight, up_weight, down_weight, out_grad,
):
    n = lax.axis_size("fsdp")
    planes = n // TEAM
    rows = inputs.shape[0]
    tokens = TEAM * rows
    depth = qkv_weight.shape[0]
    ff = down_weight.shape[0]
    width = LOCAL * HEAD_DIM
    lines = [[z * TEAM + i for z in range(planes)] for i in range(TEAM)]
    mine = lax.rem(lax.axis_index("fsdp"), TEAM)

    def line_sum(x):
        return lax.psum_scatter(x, "fsdp", scatter_dimension=0, tiled=True, axis_index_groups=lines)

    half = ROT // 2
    rate = 10000.0 ** (-np.arange(half) / half)
    rate = np.tile(np.concatenate([rate, rate, np.zeros(HEAD_DIM - ROT)]), 128 // HEAD_DIM)[None].astype(np.float32)
    h_one, qkv, attn_low, resid, h_two, w_both, w_qkv, w_out, tables, norms = attend(
        qkv_weight, gate_weight, up_weight, inputs, out_weight, positions, qkv_bias,
        (norm1_gain, norm1_bias, norm2_gain, norm2_bias), jnp.asarray(rate), planes, 1,
    )
    w_both, w_qkv = w_both.reshape(D, 2 * planes * ff), w_qkv.reshape(D, 3 * width)
    w_out = w_out.reshape(width, D)
    pre, hidden, grad_down, g_all, w_down = expand(h_two, w_both, out_grad, down_weight, planes, 3)
    w_down = w_down.reshape(planes * ff, D)
    grad_resid, sums_two, block, grad_w_both = mlp_back(
        pre, g_all, h_two.reshape(tokens, D), w_down, w_both, resid, out_grad, norms, grad_down, 5
    )
    grad_down = line_sum(grad_down)
    grad_w_both = line_sum(grad_w_both)
    grad_qkv, part, grad_bias, grad_out, block_out = attend_back(
        block, w_out, w_qkv, qkv, tables, attn_low, hidden, w_down, resid, grad_down, 6
    )
    grad_qkv = grad_qkv.reshape(tokens, 3 * width)
    grad_w_qkv = dot(h_one.reshape(tokens, D), grad_qkv, TN).astype(BF16)
    part, grad_w_qkv = lax.optimization_barrier((part, grad_w_qkv))
    branch = grad_out.reshape(planes, depth, D)
    norm_part, branch, shared = last(part, inputs, norms, branch, sums_two, grad_bias, grad_w_qkv, 7)
    grad_w_qkv = line_sum(grad_w_qkv)
    blocks = grad_w_both.reshape(TEAM, depth, 2 * planes * ff)
    blocks, sums = both_closing(blocks, shared, (norm_part, branch), 9)
    block_out, input_grad = block_out.astype(BF16), grad_resid + norm_part
    grad_gate_w, grad_up_w, grad_out = first_grads(blocks, branch)
    blocks = closing(grad_w_qkv.reshape(TEAM, depth, 3 * width), (input_grad, grad_up_w, sums), 8)
    grad_w_qkv = rest_grads(blocks, planes)

    return (
        block_out,
        input_grad,
        sums[0, :depth],
        sums[1, :depth],
        grad_w_qkv,
        sums[4 : 4 + qkv_bias.shape[0] // depth, :depth].reshape(-1),
        grad_out,
        sums[2, :depth],
        sums[3, :depth],
        grad_gate_w,
        grad_up_w,
        grad_down.astype(F32),
    )


def rotate_pairs(heads, places, sign):
    half_rot = ROT // 2
    frequency = 10000.0 ** (-jnp.arange(half_rot, dtype=jnp.float32) / half_rot)
    angles = places.astype(jnp.float32)[:, None] * frequency[None, :]
    cosine = jnp.cos(angles)[:, None, :]
    sine_part = sign * jnp.sin(angles)[:, None, :]
    front_part = heads[..., :half_rot]
    back_part = heads[..., half_rot:ROT]
    return jnp.concatenate(
        [
            front_part * cosine - back_part * sine_part,
            back_part * cosine + front_part * sine_part,
            heads[..., ROT:],
        ],
        axis=-1,
    )


def by_groups(heads):
    group_heads = min(8, HEADS)
    shaped = heads.reshape(heads.shape[0], HEADS // group_heads, group_heads, HEAD_DIM)
    return jnp.moveaxis(shaped, 1, 0)


def from_groups(grouped):
    return jnp.moveaxis(grouped, 0, 1).reshape(grouped.shape[1], HEADS, HEAD_DIM)


def plain_group(block_items, allowed):
    query_part, key_part, value_part = block_items
    scores = (
        jnp.einsum("qhd,khd->hqk", query_part, key_part, preferred_element_type=jnp.float32) * 0.125
    )
    masked = jnp.where(allowed[None], scores, -1e30)
    row_max = jnp.max(masked, axis=-1, keepdims=True)
    exponent = jnp.exp(masked - row_max)
    row_total = jnp.sum(exponent, axis=-1, keepdims=True)
    soft_probs = (exponent / row_total).astype(jnp.bfloat16)
    mixed_part = jnp.einsum(
        "hqk,khd->qhd", soft_probs, value_part, preferred_element_type=jnp.float32
    )
    return (mixed_part, (row_max + jnp.log(row_total))[..., 0])


def plain_back(block_items, allowed):
    query_part, key_part, value_part, grad_part, row_delta, log_total = block_items
    scores = (
        jnp.einsum("qhd,khd->hqk", query_part, key_part, preferred_element_type=jnp.float32) * 0.125
    )
    soft_probs = jnp.where(allowed[None], jnp.exp(scores - log_total[..., None]), 0.0)
    grad_probs = jnp.einsum(
        "qhd,khd->hqk", grad_part, value_part.astype(jnp.float32), precision=lax.Precision.HIGHEST
    )
    rounded_probs = soft_probs.astype(jnp.bfloat16).astype(jnp.float32)
    grad_value = jnp.einsum("hqk,qhd->khd", rounded_probs, grad_part, precision=lax.Precision.HIGHEST)
    grad_scores = (soft_probs * (grad_probs - row_delta[..., None])).astype(jnp.bfloat16)
    grad_query = 0.125 * jnp.einsum(
        "hqk,khd->qhd", grad_scores, key_part, preferred_element_type=jnp.float32
    )
    grad_key = 0.125 * jnp.einsum(
        "hqk,qhd->khd", grad_scores, query_part, preferred_element_type=jnp.float32
    )
    return (grad_query, grad_key, grad_value)


def shards(
    inputs,
    positions,
    norm1_gain,
    norm1_bias,
    qkv_weight,
    qkv_bias,
    out_weight,
    norm2_gain,
    norm2_bias,
    gate_weight,
    up_weight,
    down_weight,
    out_grad,
):
    tok_rows = inputs.shape[0]
    gain_one, bias_one, w_qkv, b_qkv, w_out = (
        lax.all_gather(norm1_gain, "fsdp", axis=0, tiled=True),
        lax.all_gather(norm1_bias, "fsdp", axis=0, tiled=True),
        lax.all_gather(qkv_weight, "fsdp", axis=0, tiled=True),
        lax.all_gather(qkv_bias, "fsdp", axis=0, tiled=True),
        lax.all_gather(out_weight, "fsdp", axis=0, tiled=True),
    )
    stream = inputs.astype(jnp.float32)
    normed_one, inverse_one = normalize(stream)
    h_one = (normed_one * gain_one.astype(jnp.float32) + bias_one.astype(jnp.float32)).astype(
        jnp.bfloat16
    )
    qkv_pre = jnp.dot(h_one, w_qkv, preferred_element_type=jnp.float32) + b_qkv.astype(jnp.float32)
    qkv_heads = qkv_pre.reshape(tok_rows, 3, HEADS, HEAD_DIM)
    query_low = rotate_pairs(qkv_heads[:, 0], positions, 1.0).astype(jnp.bfloat16)
    key_all = rotate_pairs(qkv_heads[:, 1], positions, 1.0).astype(jnp.bfloat16)
    value_all = qkv_heads[:, 2].astype(jnp.bfloat16)
    token_index = jnp.arange(tok_rows, dtype=jnp.int32)
    allowed = (token_index[None, :] <= token_index[:, None]) & (
        token_index[None, :] >= (token_index - positions)[:, None]
    )
    mixed_grouped, log_grouped = lax.map(
        lambda block_items: plain_group(block_items, allowed),
        (by_groups(query_low), by_groups(key_all), by_groups(value_all)),
    )
    mixed_heads = from_groups(mixed_grouped)
    attn_low = mixed_heads.reshape(tok_rows, D).astype(jnp.bfloat16)
    resid = stream + jnp.dot(attn_low, w_out, preferred_element_type=jnp.float32)
    gain_two, bias_two, w_gate, w_up, w_down = (
        lax.all_gather(norm2_gain, "fsdp", axis=0, tiled=True),
        lax.all_gather(norm2_bias, "fsdp", axis=0, tiled=True),
        lax.all_gather(gate_weight, "fsdp", axis=0, tiled=True),
        lax.all_gather(up_weight, "fsdp", axis=0, tiled=True),
        lax.all_gather(down_weight, "fsdp", axis=0, tiled=True),
    )
    normed_two, inverse_two = normalize(resid)
    h_two = (normed_two * gain_two.astype(jnp.float32) + bias_two.astype(jnp.float32)).astype(
        jnp.bfloat16
    )
    gate_pre = jnp.dot(h_two, w_gate, preferred_element_type=jnp.float32)
    up_pre = jnp.dot(h_two, w_up, preferred_element_type=jnp.float32)
    sigmoid_gate = jax.nn.sigmoid(gate_pre)
    silu_gate = gate_pre * sigmoid_gate
    hidden = (silu_gate * up_pre).astype(jnp.bfloat16)
    block_out = (resid + jnp.dot(hidden, w_down, preferred_element_type=jnp.float32)).astype(
        jnp.bfloat16
    )
    gain_two, w_gate, w_up, w_down = (
        lax.all_gather(norm2_gain, "fsdp", axis=0, tiled=True),
        lax.all_gather(gate_weight, "fsdp", axis=0, tiled=True),
        lax.all_gather(up_weight, "fsdp", axis=0, tiled=True),
        lax.all_gather(down_weight, "fsdp", axis=0, tiled=True),
    )
    grad_down_w = jnp.einsum("tf,td->fd", hidden, out_grad, preferred_element_type=jnp.float32)
    grad_hidden = jnp.einsum("td,fd->tf", out_grad, w_down, preferred_element_type=jnp.float32)
    grad_gate = (
        grad_hidden * up_pre * sigmoid_gate * (1.0 + gate_pre * (1.0 - sigmoid_gate))
    ).astype(jnp.bfloat16)
    grad_up = (grad_hidden * silu_gate).astype(jnp.bfloat16)
    grad_gate_w = jnp.einsum("td,tf->df", h_two, grad_gate, preferred_element_type=jnp.float32)
    grad_up_w = jnp.einsum("td,tf->df", h_two, grad_up, preferred_element_type=jnp.float32)
    grad_htwo = jnp.einsum(
        "tf,df->td", grad_gate, w_gate, preferred_element_type=jnp.float32
    ) + jnp.einsum("tf,df->td", grad_up, w_up, preferred_element_type=jnp.float32)
    grad_gain_two = jnp.sum(grad_htwo * normed_two, axis=0)
    grad_bias_two = jnp.sum(grad_htwo, axis=0)
    grad_resid = out_grad.astype(jnp.float32) + norm_back(
        grad_htwo * gain_two.astype(jnp.float32), normed_two, inverse_two
    )
    mlp_sums = (
        lax.psum_scatter(grad_gain_two, "fsdp", scatter_dimension=0, tiled=True),
        lax.psum_scatter(grad_bias_two, "fsdp", scatter_dimension=0, tiled=True),
        lax.psum_scatter(grad_gate_w, "fsdp", scatter_dimension=0, tiled=True),
        lax.psum_scatter(grad_up_w, "fsdp", scatter_dimension=0, tiled=True),
        lax.psum_scatter(grad_down_w, "fsdp", scatter_dimension=0, tiled=True),
    )
    gain_one, w_qkv, w_out = (
        lax.all_gather(norm1_gain, "fsdp", axis=0, tiled=True),
        lax.all_gather(qkv_weight, "fsdp", axis=0, tiled=True),
        lax.all_gather(out_weight, "fsdp", axis=0, tiled=True),
    )
    grad_branch = grad_resid.astype(jnp.bfloat16)
    grad_out_w = jnp.einsum("ti,td->id", attn_low, grad_branch, preferred_element_type=jnp.float32)
    grad_att = jnp.einsum(
        "td,id->ti", grad_branch, w_out, preferred_element_type=jnp.float32
    ).reshape(tok_rows, HEADS, HEAD_DIM)
    group_heads = min(8, HEADS)
    row_delta = jnp.sum(grad_att * mixed_heads, axis=-1)
    delta_grouped = row_delta.reshape(tok_rows, HEADS // group_heads, group_heads).transpose(
        1, 2, 0
    )
    query_grouped, key_grouped, value_grouped = lax.map(
        lambda block_items: plain_back(block_items, allowed),
        (
            by_groups(query_low),
            by_groups(key_all),
            by_groups(value_all),
            by_groups(grad_att),
            delta_grouped,
            log_grouped,
        ),
    )
    grad_query = from_groups(query_grouped)
    grad_key = from_groups(key_grouped)
    grad_value = from_groups(value_grouped)
    grad_qkv = (
        jnp.stack(
            [
                rotate_pairs(grad_query, positions, -1.0),
                rotate_pairs(grad_key, positions, -1.0),
                grad_value,
            ],
            axis=1,
        )
        .reshape(tok_rows, 3 * D)
        .astype(jnp.bfloat16)
    )
    grad_qkv_w = jnp.einsum("td,tk->dk", h_one, grad_qkv, preferred_element_type=jnp.float32)
    grad_qkv_b = jnp.sum(grad_qkv.astype(jnp.float32), axis=0)
    grad_hone = jnp.einsum("tk,dk->td", grad_qkv, w_qkv, preferred_element_type=jnp.float32)
    grad_gain_one = jnp.sum(grad_hone * normed_one, axis=0)
    grad_bias_one = jnp.sum(grad_hone, axis=0)
    input_grad = grad_resid + norm_back(
        grad_hone * gain_one.astype(jnp.float32), normed_one, inverse_one
    )
    attn_sums = (
        lax.psum_scatter(grad_gain_one, "fsdp", scatter_dimension=0, tiled=True),
        lax.psum_scatter(grad_bias_one, "fsdp", scatter_dimension=0, tiled=True),
        lax.psum_scatter(grad_qkv_w, "fsdp", scatter_dimension=0, tiled=True),
        lax.psum_scatter(grad_qkv_b, "fsdp", scatter_dimension=0, tiled=True),
        lax.psum_scatter(grad_out_w, "fsdp", scatter_dimension=0, tiled=True),
    )
    return (
        block_out,
        input_grad,
        attn_sums[0],
        attn_sums[1],
        attn_sums[2],
        attn_sums[3],
        attn_sums[4],
        mlp_sums[0],
        mlp_sums[1],
        mlp_sums[2],
        mlp_sums[3],
        mlp_sums[4],
    )


def solution(mesh):
    devices = mesh.shape["fsdp"]
    rows, columns = P("fsdp", None), P("fsdp")
    body = team_shards if devices % TEAM == 0 and D == devices * HEAD_DIM else shards
    return jax.shard_map(
        body,
        mesh=mesh,
        in_specs=(rows, columns, columns, columns, rows, columns, rows, columns, columns, rows, rows, rows, rows),
        out_specs=(rows, rows, columns, columns, rows, columns, rows, columns, columns, rows, rows, rows),
        check_vma=False,
    )
```

```python
import functools

import jax
import jax.numpy as jnp
import numpy as np
from jax import lax
from jax.experimental import pallas as pl
from jax.experimental.pallas import tpu as pltpu
from jax.sharding import PartitionSpec as P

D = 2048
HEADS = 32
HEAD_DIM = 64
ROT = 16
EPS = 1e-05
TEAM = 8
LOCAL = HEADS // TEAM
MESH = pl.DeviceIdType.MESH
BF16 = jnp.bfloat16
F32 = jnp.float32
ANY = pl.BlockSpec(memory_space=pl.ANY)
VMEM = pl.BlockSpec(memory_space=pltpu.VMEM)


def lasting(us):
    return pl.CostEstimate(flops=0, bytes_accessed=int(us * 3.6e6), transcendentals=0)


def params(cid=None, limit=56):
    extra = {} if cid is None else {"collective_id": cid, "has_side_effects": True}
    return pltpu.CompilerParams(vmem_limit_bytes=limit * 1024 * 1024, **extra)


def place():
    me = lax.axis_index("fsdp")
    mine = lax.rem(me, TEAM)
    return mine, me - mine, mine // 2, lax.rem(mine, 2)


def chip_at(chip, step):
    along_x, along_y = lax.rem(chip, 2), chip // 2
    if step & 1:
        along_x = 1 - along_x
    if step & 2:
        along_y = 1 - along_y
    return along_y * 2 + along_x


def relation(chip, core, r):
    return chip_at(chip, r // 2) * 2 + lax.rem(core + r, 2)


def greet(devices):
    barrier = pltpu.get_barrier_semaphore()
    for device in devices:
        pl.semaphore_signal(barrier, inc=1, device_id=(device,), device_id_type=MESH)
    pl.semaphore_wait(barrier, len(devices))


def remote(src, dst, send, recv, device):
    return pltpu.make_async_remote_copy(
        src_ref=src, dst_ref=dst, send_sem=send, recv_sem=recv, device_id=(device,), device_id_type=MESH
    )


class Swap:
    sems = [pltpu.SemaphoreType.DMA, pltpu.SemaphoreType.DMA((TEAM,)), pltpu.SemaphoreType.DMA((TEAM,))]

    def __init__(self, src, out, sems, same=False, near_first=False):
        own_sem, send, recv = sems
        mine, base, chip, core = place()
        others = [relation(chip, core, r) for r in range(1, TEAM)]
        self.near = [base + other for other in others]
        self.copies = [
            remote(
                src if same else src.at[other], out.at[r if near_first else mine], send.at[r], recv.at[r], base + other
            )
            for r, other in enumerate(others, 1)
        ]
        own = src if same else src.at[mine]
        self.copies.append(pltpu.make_async_copy(own, out.at[0 if near_first else mine], own_sem))

    def start(self):
        for copy in self.copies:
            copy.start()

    def finish(self):
        for copy in self.copies:
            copy.wait()


class Line:
    def sems(planes):
        return [pltpu.SemaphoreType.DMA, pltpu.SemaphoreType.DMA((planes,)), pltpu.SemaphoreType.DMA((planes,))]

    def __init__(self, planes, src, out, sems, same=False, within=False):
        own_sem, send, recv = sems
        mine, base, _, _ = place()
        plane = base // TEAM
        others = [lax.rem(plane + k, planes) for k in range(1, planes)]
        self.near = [other * TEAM + mine for other in others]
        self.copies = [
            remote(src if same else src.at[other], out.at[plane], send.at[k], recv.at[k], other * TEAM + mine)
            for k, other in enumerate(others)
        ]
        own = src if same else src.at[plane]
        self.own = None if within else pltpu.make_async_copy(own, out.at[plane], own_sem)

    def start(self):
        for copy in self.copies:
            copy.start()
        if self.own is not None:
            self.own.start()

    def finish(self):
        for copy in self.copies:
            copy.wait()
        if self.own is not None:
            self.own.wait()


class LineGather:
    def sems(planes):
        return [pltpu.SemaphoreType.DMA, pltpu.SemaphoreType.DMA((2, planes)), pltpu.SemaphoreType.DMA((2, planes))]

    def __init__(self, planes, src, out, sems):
        own_sem, self.send, self.recv = sems
        mine, base, _, _ = place()
        self.plane, self.planes, self.src, self.out = base // TEAM, planes, src, out
        self.me = base + mine
        self.near = [lax.rem(self.plane + k, planes) * TEAM + mine for k in (1, planes - 1)]
        self.own = pltpu.make_async_copy(src, out.at[self.plane], own_sem)

    def copy(self, way, stage):
        step = 1 - 2 * way
        block, to = self.plane - step * (stage - 1), self.plane + step
        is_there = (block >= 0) & (block < self.planes) & (to >= 0) & (to < self.planes)
        src = self.src if stage == 1 else self.out.at[block]
        sems = self.send.at[way, stage], self.recv.at[way, stage]
        return is_there, remote(src, self.out.at[block], *sems, self.me + step * TEAM)

    def arrived(self, way, stage):
        block = self.plane - (1 - 2 * way) * stage

        @pl.when((block >= 0) & (block < self.planes))
        def _():
            dst = self.out.at[block]
            remote(dst, dst, self.send.at[way, stage], self.recv.at[way, stage], self.me).wait_recv()

    def start(self):
        self.own.start()
        self.stage(1)

    def stage(self, stage):
        for way in (0, 1):
            if stage > 1:
                self.arrived(way, stage - 1)
            is_there, copy = self.copy(way, stage)
            pl.when(is_there)(copy.start)

    def finish(self):
        self.own.wait()
        for way in (0, 1):
            self.arrived(way, self.planes - 1)
            for stage in range(1, self.planes):
                is_there, copy = self.copy(way, stage)
                pl.when(is_there)(copy.wait_send)


def slices(ref, pieces, size):
    return jnp.concatenate([ref[:, i * size : (i + 1) * size] for i in pieces], axis=1)


def unslice(held, parts, planes, outs):
    size = held.shape[2] // (parts * planes)
    for at in range(parts * planes):
        row = jnp.concatenate([held[i, :, at * size : (at + 1) * size] for i in range(TEAM)], axis=1)
        out, first = (outs[at // planes], at % planes) if len(outs) > 1 else (outs[0], at)
        out[:, first * TEAM * size : (first + 1) * TEAM * size] = row.astype(F32)


def first_kernel(planes, held_ref, far_ref, gate_ref, up_ref, wo_ref):
    unslice(held_ref, 2, planes, [gate_ref, up_ref])
    wo_ref[...] = added(far_ref)


def first_grads(held, far):
    _, depth, width = held.shape
    return pl.pallas_call(
        functools.partial(first_kernel, far.shape[0]),
        out_shape=[jax.ShapeDtypeStruct((depth, width * TEAM // 2), F32)] * 2
        + [jax.ShapeDtypeStruct(far.shape[1:], F32)],
        in_specs=[VMEM] * 2,
        out_specs=[VMEM] * 3,
        cost_estimate=lasting(4),
        compiler_params=params(),
    )(held, far)


def rest_kernel(planes, held_ref, w_ref):
    unslice(held_ref, 3, planes, [w_ref])


def rest_grads(held, planes):
    _, depth, width = held.shape
    return pl.pallas_call(
        functools.partial(rest_kernel, planes),
        out_shape=jax.ShapeDtypeStruct((depth, width * TEAM), F32),
        in_specs=[VMEM],
        out_specs=VMEM,
        cost_estimate=lasting(3),
        compiler_params=params(),
    )(held)


def added(ref):
    total = ref[0].astype(F32)
    for i in range(1, ref.shape[0]):
        total = total + ref[i].astype(F32)
    return total


def close_kernel(w_ref, _, __, ___, held_ref, *sems):
    swap = Swap(w_ref, held_ref, sems)
    greet(swap.near)
    swap.start()
    swap.finish()


def both_close_kernel(planes, w_ref, shared_ref, _, __, held_ref, vector_ref, got, block, beyond, *sems):
    swap, inner = Swap(w_ref, held_ref, sems[:3]), Swap(shared_ref, got, sems[3:6])
    outer = Line(planes, block, beyond, sems[6:])
    greet(swap.near + outer.near)
    inner.start()
    swap.start()
    inner.finish()
    block[...] = added(got)
    outer.start()
    outer.finish()
    vector_ref[...] = added(beyond)
    swap.finish()


def both_closing(blocks, shared, after, cid):
    planes = shared.shape[1]
    return pl.pallas_call(
        functools.partial(both_close_kernel, planes),
        out_shape=[jax.ShapeDtypeStruct(blocks.shape, BF16), jax.ShapeDtypeStruct(shared.shape[2:], F32)],
        in_specs=[VMEM, VMEM, ANY, ANY],
        out_specs=[ANY, VMEM],
        scratch_shapes=[pltpu.VMEM(shared.shape, F32)]
        + [pltpu.VMEM(shared.shape[1:], F32)] * 2
        + Swap.sems * 2
        + Line.sems(planes),
        cost_estimate=lasting(22),
        compiler_params=params(cid),
    )(blocks, shared, *after)


def closing(blocks, after, cid):
    return pl.pallas_call(
        close_kernel,
        out_shape=jax.ShapeDtypeStruct(blocks.shape, BF16),
        in_specs=[VMEM, ANY, ANY, ANY],
        out_specs=ANY,
        scratch_shapes=Swap.sems,
        cost_estimate=lasting(14),
        compiler_params=params(cid),
    )(blocks, *after)


class Gather:
    sems = [pltpu.SemaphoreType.DMA((5,)), pltpu.SemaphoreType.DMA((5,)), pltpu.SemaphoreType.DMA((2,)),
            pltpu.SemaphoreType.DMA((2,)), pltpu.SemaphoreType.DMA((6,)), pltpu.SemaphoreType.DMA((6,)),
            pltpu.SemaphoreType.DMA]

    def __init__(self, src, out, sems):
        send, recv, hop_send, hop_recv, pass_send, pass_recv, own_sem = sems
        _, base, chip, core = place()
        side, over = (chip_at(chip, k) * 2 + core for k in (1, 2))
        self.sibling = base + chip * 2 + 1 - core
        self.near = [base + side, base + over, self.sibling]
        half = src.shape[0] // 2
        top, low = pl.ds(0, half), pl.ds(half, half)
        self.first = [
            remote(src.at[part], out.at[at, part], send.at[i], recv.at[i], base + to)
            for i, (part, at, to) in enumerate(((top, 2, side), (low, 4, over), (low, 2, side), (top, 4, over)))
        ]
        self.first.append(remote(src, out.at[1], send.at[4], recv.at[4], self.sibling))
        self.own = pltpu.make_async_copy(src, out.at[0], own_sem)
        self.hops = [
            remote(out.at[at, part], out.at[6, part], hop_send.at[i], hop_recv.at[i], base + to)
            for i, (at, part, to) in enumerate(((2, top, over), (4, low, side)))
        ]
        self.passed = [
            remote(out.at[at, part], out.at[at + 1, part], pass_send.at[i], pass_recv.at[i], self.sibling)
            for i, (at, part) in enumerate(((2, top), (4, low), (2, low), (4, top), (6, top), (6, low)))
        ]

    def start(self):
        for copy in self.first:
            copy.start()
        self.own.start()

    def middle(self):
        for i in (0, 1):
            self.first[i].wait_recv()
            self.hops[i].start()
            self.passed[i].start()

    def finish(self):
        for i in range(2, TEAM):
            self.ready(i)
        self.first[4].wait_recv()
        self.own.wait()
        self.sent()

    def ready(self, i):
        if i == 0:
            self.own.wait()
        elif i == 1:
            self.first[4].wait_recv()
        elif i == 6:
            for j in (0, 1):
                self.hops[j].wait_recv()
                self.passed[4 + j].start()
        elif i % 2 == 0:
            self.first[1 + i // 2].wait_recv()
            self.passed[1 + i // 2].start()
        else:
            for j in {3: (0, 2), 5: (1, 3), 7: (4, 5)}[i]:
                self.passed[j].wait_recv()

    def sent(self):
        for copy in self.first + self.hops + self.passed:
            copy.wait_send()


class Sum:
    def scratch(rows, width):
        return [pltpu.VMEM((4, rows, width), BF16), pltpu.VMEM((4, rows, width), BF16),
                pltpu.VMEM((2, rows // 2, width), BF16), pltpu.VMEM((2, rows, width), BF16)]

    sems = [pltpu.SemaphoreType.DMA((4,))] * 3 + [pltpu.SemaphoreType.DMA((2,))] * 2 + [pltpu.SemaphoreType.DMA((4,))] * 2

    def __init__(self, blocks, scratch, sems, away=None):
        self.own, self.beside, self.via, self.far = scratch
        load_sem, near_send, near_recv, via_send, via_recv, far_send, far_recv = sems
        _, base, chip, core = place()
        sibling = base + chip * 2 + 1 - core
        side, over = (base + chip_at(chip, k) * 2 + core for k in (1, 2))
        self.near = [side, over, sibling]
        self.half = self.own.shape[1] // 2
        top, low = pl.ds(0, self.half), pl.ds(self.half, self.half)
        self.loads = [
            pltpu.make_async_copy(blocks.at[2 * k], self.own.at[k], load_sem.at[k])
            for k in range(4)
            if away is None
        ]

        def near_copy(k):
            src = blocks.at[2 * k + 1] if away is None else away.at[k]
            return remote(src, self.beside.at[k], near_send.at[k], near_recv.at[k], sibling)

        self.near_copy = near_copy
        self.nears = [near_copy(k) for k in range(4)]
        self.vias = [
            remote(self.own.at[3, part], self.via.at[i], via_send.at[i], via_recv.at[i], to)
            for i, (part, to) in enumerate(((top, side), (low, over)))
        ]
        self.fars = [
            remote(self.own.at[k, part], self.far.at[k - 1, part], far_send.at[i], far_recv.at[i], to)
            for i, (k, part, to) in enumerate(((2, low, over), (1, top, side), (2, top, over), (1, low, side)))
        ]

    def start(self):
        for k in (3, 2, 1, 0):
            self.loads[k].start()
            self.nears[k].start()

    def pair(self, k):
        if self.loads:
            self.loads[k].wait()
        self.nears[k].wait_recv()

        @pl.loop(0, self.own.shape[1] // 16)
        def _(i):
            part = pl.ds(pl.multiple_of(i * 16, 16), 16)
            self.own[k, part, :] = (self.own[k, part, :].astype(F32) + self.beside[k, part, :].astype(F32)).astype(BF16)

    def middle_a(self):
        self.pair(3)
        for copy in self.vias:
            copy.start()

    def middle_b(self):
        self.pair(2)
        self.fars[0].start()

    def middle_c(self):
        self.pair(1)
        self.fars[1].start()

    def middle(self):
        self.middle_a()
        self.middle_b()
        self.middle_c()

    def middle_two(self):
        for i, k in ((0, 2), (1, 1)):
            self.vias[i].wait_recv()

            @pl.loop(0, self.half // 16)
            def _(j, i=i, k=k):
                part = pl.ds(pl.multiple_of(j * 16, 16), 16)
                at = pl.ds(pl.multiple_of(j * 16 + i * self.half, 16), 16)
                self.own[k, at, :] = (self.own[k, at, :].astype(F32) + self.via[i, part, :].astype(F32)).astype(BF16)

            self.fars[2 + i].start()

    def finish(self, use):
        if self.loads:
            self.loads[0].wait()
        self.nears[0].wait_recv()
        for copy in self.fars:
            copy.wait_recv()

        @pl.loop(0, self.own.shape[1] // 16)
        def _(i):
            part = pl.ds(pl.multiple_of(i * 16, 16), 16)
            total = self.own[0, part, :].astype(F32) + self.beside[0, part, :].astype(F32)
            use(part, total + self.far[0, part, :].astype(F32) + self.far[1, part, :].astype(F32))

        for copy in self.nears + self.vias + self.fars:
            copy.wait_send()


def fold(x):
    return x[:8] + x[8:]


def expand_kernel(
    planes, h_ref, w_ref, g_ref, down_ref, pre_ref, hidden_ref, grad_ref, g_all_ref, wd_ref, held, g, total, w, *sems
):
    gather, line = Gather(g_ref, g_all_ref, sems[:7]), LineGather(planes, down_ref, wd_ref, sems[7:10])
    step = pl.program_id(0)

    @pl.when(step == 0)
    def _():
        greet(gather.near + line.near)
        line.start()
        gather.start()
        weights = pltpu.make_async_copy(w_ref, w, sems[11])
        weights.start()
        weights.wait()

    pre = dot(h_ref[0], w[...])
    pre_ref[0] = pre
    ff = hidden_ref.shape[2]
    gate_pre, up_pre = pre[:, :ff], pre[:, ff:]
    hidden = (gate_pre * jax.nn.sigmoid(gate_pre) * up_pre).astype(BF16)
    hidden_ref[0] = hidden
    held[step] = hidden
    pl.when(step == TEAM - 3)(functools.partial(line.stage, 2))

    @pl.when(step == TEAM - 1)
    def _():
        def load(i):
            return pltpu.make_async_copy(g_all_ref.at[i], g.at[i % 2], sems[10].at[i % 2])

        gather.middle()
        gather.ready(0)
        load(0).start()
        for i in range(TEAM):
            if i < TEAM - 1:
                gather.ready(i + 1)
                load(i + 1).start()
            load(i).wait()
            product = dot(held[i], g[i % 2], TN)
            total[...] = product if i == 0 else total[...] + product
            if i == 4:
                for stage in range(3, planes):
                    line.stage(stage)
        grad_ref[...] = total[...].astype(BF16)
        gather.sent()
        line.finish()


def expand(h_two, w_both, out_grad, down, planes, cid):
    seqs, rows, _ = h_two.shape
    width = w_both.shape[1]
    return pl.pallas_call(
        functools.partial(expand_kernel, planes),
        grid=(seqs,),
        in_specs=[per_seq(rows, D), ANY, VMEM, VMEM],
        out_specs=[per_seq(rows, width), per_seq(rows, width // 2), whole(width // 2, D), ANY, ANY],
        out_shape=[
            jax.ShapeDtypeStruct((seqs, rows, width), F32),
            jax.ShapeDtypeStruct((seqs, rows, width // 2), BF16),
            jax.ShapeDtypeStruct((width // 2, D), BF16),
            jax.ShapeDtypeStruct((seqs, rows, D), BF16),
            jax.ShapeDtypeStruct((planes,) + down.shape, BF16),
        ],
        scratch_shapes=[
            pltpu.VMEM((seqs, rows, width // 2), BF16),
            pltpu.VMEM((2, rows, D), BF16),
            pltpu.VMEM((width // 2, D), F32),
            pltpu.VMEM((D, width), BF16),
        ]
        + Gather.sems
        + LineGather.sems(planes)
        + [pltpu.SemaphoreType.DMA((2,)), pltpu.SemaphoreType.DMA],
        cost_estimate=lasting(55),
        compiler_params=params(cid),
    )(h_two, w_both, out_grad, down)


def mlp_back_kernel(
    pre_ref, g_all_ref, h_ref, wd_ref, w_ref, resid_ref, g_ref, norm_ref, _,
    out_ref, sums_ref, block_ref, grad_w_ref,
    pre, g_all, turned, made, grads, away, w, resid, own_grad, wd, *scratch,
):
    pre_sem, g_sem, turned_sem, made_sem, late_sem = scratch[11:]
    total = Sum(None, scratch[:4], scratch[4:11], away)
    rows, ff = pre_ref.shape[1], wd_ref.shape[0]
    chunk = turned.shape[2]

    def loads(i):
        slot, at = lax.rem(i, 2), TEAM - 1 - i
        return (
            pltpu.make_async_copy(pre_ref.at[at], pre.at[slot], pre_sem.at[slot]),
            pltpu.make_async_copy(g_all_ref.at[at], g_all.at[slot], g_sem.at[slot]),
        )

    def load_chunk(i):
        slot = lax.rem(i, 2)
        columns = pl.ds(pl.multiple_of(i * chunk, chunk), chunk)
        return pltpu.make_async_copy(h_ref.at[:, columns], turned.at[slot], turned_sem.at[slot])

    def store_chunk(i):
        slot = lax.rem(i, 2)
        part = pl.ds(pl.multiple_of(i * chunk, chunk), chunk)
        return pltpu.make_async_copy(made.at[slot], grad_w_ref.at[part, :], made_sem.at[slot])

    for copy in loads(0):
        copy.start()
    late = [
        pltpu.make_async_copy(src, dst, late_sem.at[i])
        for i, (src, dst) in enumerate(((wd_ref, wd), (w_ref, w), (resid_ref, resid), (g_ref, own_grad)))
    ]
    for copy in late:
        copy.start()
    greet(total.near)

    @pl.loop(0, TEAM)
    def _(i):
        slot = lax.rem(i, 2)
        k, at = 3 - i // 2, TEAM - 1 - i

        @pl.when(i < TEAM - 1)
        def _():
            for copy in loads(i + 1):
                copy.start()

        for copy in loads(i):
            copy.wait()
        pl.when(i == 0)(late[0].wait)
        grad_hidden = dot(g_all[slot], wd[...], NT)
        gate_pre, up_pre = pre[slot, :, :ff], pre[slot, :, ff:]
        sigmoid = jax.nn.sigmoid(gate_pre)
        grad_gate = grad_hidden * up_pre * sigmoid * (1.0 + gate_pre * (1.0 - sigmoid))
        grad_up = grad_hidden * (gate_pre * sigmoid)
        part = pl.ds(pl.multiple_of(at * rows, rows), rows)
        grads[part, :] = jnp.concatenate([grad_gate, grad_up], axis=1).astype(BF16)

        def make(to):
            to[k] = dot(grads[part, :], w[...], NT).astype(BF16)

        pl.when(i == 0)(late[1].wait)

        @pl.when(lax.rem(i, 2) == 0)
        def _():
            make(away)
            total.near_copy(k).start()

        @pl.when(lax.rem(i, 2) == 1)
        def _():
            make(total.own)

        for step, advance in ((1, total.middle_a), (3, total.middle_b), (5, total.middle_c)):
            pl.when(i == step)(advance)

    load_chunk(0).start()
    total.middle_two()
    chunks = h_ref.shape[1] // chunk

    @pl.loop(0, chunks)
    def _(i):
        slot = lax.rem(i, 2)

        @pl.when(i < chunks - 1)
        def _():
            load_chunk(i + 1).start()

        load_chunk(i).wait()

        @pl.when(i >= 2)
        def _():
            store_chunk(i - 2).wait()

        made[slot] = dot(turned[slot], grads[...], TN).astype(BF16)
        store_chunk(i).start()

    sums_ref[...] = jnp.zeros_like(sums_ref)
    for copy in late[2:]:
        copy.wait()

    def use(rows, value):
        normed, inverse = normalize(resid[rows, :])
        sums_ref[:8, :] += fold(value * normed)
        sums_ref[8:, :] += fold(value)
        grad = own_grad[rows, :].astype(F32) + norm_back(value * norm_ref[2:3, :], normed, inverse)
        out_ref[rows, :] = grad
        block_ref[rows, :] = grad.astype(BF16)

    total.finish(use)
    store_chunk(chunks - 2).wait()
    store_chunk(chunks - 1).wait()


def mlp_back(pre, g_all, h_two, w_down, w_both, resid, out_grad, gain, after, cid):
    seqs, rows, both = pre.shape
    width = resid.shape[1]
    chunk = 256
    two = pltpu.SemaphoreType.DMA((2,))
    return pl.pallas_call(
        mlp_back_kernel,
        out_shape=[
            jax.ShapeDtypeStruct((rows, width), F32),
            jax.ShapeDtypeStruct((16, width), F32),
            jax.ShapeDtypeStruct((rows, width), BF16),
            jax.ShapeDtypeStruct((width, both), BF16),
        ],
        in_specs=[ANY, ANY, ANY, ANY, ANY, ANY, ANY, VMEM, ANY],
        out_specs=[VMEM, VMEM, VMEM, ANY],
        scratch_shapes=[
            pltpu.VMEM((2, rows, both), F32),
            pltpu.VMEM((2, rows, width), BF16),
            pltpu.VMEM((2, seqs * rows, chunk), BF16),
            pltpu.VMEM((2, chunk, both), BF16),
            pltpu.VMEM((seqs * rows, both), BF16),
            pltpu.VMEM((4, rows, width), BF16),
            pltpu.VMEM((width, both), BF16),
            pltpu.VMEM((rows, width), F32),
            pltpu.VMEM((rows, width), BF16),
            pltpu.VMEM((both // 2, width), BF16),
        ]
        + Sum.scratch(rows, width)
        + Sum.sems
        + [two] * 4
        + [pltpu.SemaphoreType.DMA((4,))],
        cost_estimate=lasting(60),
        compiler_params=params(cid, 50),
    )(pre, g_all, h_two, w_down, w_both, resid, out_grad, gain, after)


def share(x, sums, bias, planes, per, depth):
    mine = place()[0]
    x[...] = jnp.zeros_like(x)
    sums = [jnp.sum(v, axis=0, keepdims=True) for v in sums]
    for z in range(planes):
        for i in range(TEAM):
            at = (z * TEAM + i) * depth
            for row, v in enumerate(sums):
                x[i, z, row : row + 1, :depth] = v[:, at : at + depth]
    for part in range(3):
        for z in range(planes):
            head = part * HEADS + z * TEAM + mine
            owner = head // per
            at = (part * planes + z) * HEAD_DIM
            x[lax.rem(owner, TEAM), owner // TEAM, pl.ds(4 + lax.rem(head, per), 1), :depth] = bias[:, at : at + HEAD_DIM]


def last_kernel(
    planes, part_ref, x_ref, norm_ref, branch_ref, sums_two_ref, bias_ref, _,
    out_ref, far_ref, shared_ref, sums, *scratch,
):
    total, line = Sum(part_ref, scratch[:4], scratch[4:11]), Line(planes, branch_ref, far_ref, scratch[11:])
    greet(total.near + line.near)
    line.start()
    total.start()
    total.middle()
    total.middle_two()
    sums[...] = jnp.zeros_like(sums)

    def use(rows, value):
        normed, inverse = normalize(x_ref[rows, :].astype(F32))
        sums[:8, :] += fold(value * normed)
        sums[8:, :] += fold(value)
        out_ref[rows, :] = norm_back(value * norm_ref[0:1, :], normed, inverse)

    total.finish(use)
    vectors = [sums[:8, :], sums[8:, :], sums_two_ref[:8, :], sums_two_ref[8:, :]]
    depth = part_ref.shape[2] // (planes * TEAM)
    share(shared_ref, vectors, added(bias_ref), planes, bias_ref.shape[2] // (planes * depth), depth)
    line.finish()


def last(part, inputs, gain, branch, sums_two, bias, after, cid):
    rows, width = inputs.shape
    planes = branch.shape[0]
    vectors = (TEAM, planes, 8, 128)
    return pl.pallas_call(
        functools.partial(last_kernel, planes),
        out_shape=[
            jax.ShapeDtypeStruct((rows, width), F32),
            jax.ShapeDtypeStruct(branch.shape, BF16),
            jax.ShapeDtypeStruct(vectors, F32),
        ],
        in_specs=[ANY, VMEM, VMEM, VMEM, VMEM, VMEM, ANY],
        out_specs=[VMEM, ANY, VMEM],
        scratch_shapes=[pltpu.VMEM((16, width), F32)]
        + Sum.scratch(rows, width)
        + Sum.sems
        + Line.sems(planes),
        cost_estimate=lasting(58),
        compiler_params=params(cid),
    )(part, inputs, gain, branch, sums_two, bias, after)


def dot(a, b, dims=((1,), (0,))):
    return lax.dot_general(a, b, (dims, ((), ())), preferred_element_type=F32)


NT = ((1,), (1,))
TN = ((0,), (0,))


def normalize(stream):
    average = jnp.mean(stream, axis=-1, keepdims=True)
    centered = stream - average
    variance = jnp.mean(centered * centered, axis=-1, keepdims=True)
    inverse = lax.rsqrt(variance + EPS)
    return centered * inverse, inverse


def norm_back(grad_norm, normed, inverse):
    return inverse * (
        grad_norm
        - jnp.mean(grad_norm, axis=-1, keepdims=True)
        - normed * jnp.mean(grad_norm * normed, axis=-1, keepdims=True)
    )


def turn(heads, cosine, sine):
    half, width = ROT // 2, heads.shape[-1]
    lanes = lax.broadcasted_iota(jnp.int32, heads.shape, 1) % HEAD_DIM
    moved = jnp.where(lanes < half, -pltpu.roll(heads, width - half, 1), pltpu.roll(heads, half, 1))
    return heads * cosine + moved * sine


def wide(table):
    return jnp.concatenate([table] * (LOCAL * HEAD_DIM // 128), axis=1)


def visible(start):
    size = start.shape[0]
    rows = lax.broadcasted_iota(jnp.int32, (size, size), 0)
    columns = lax.broadcasted_iota(jnp.int32, (size, size), 1)
    start = jnp.concatenate([start] * (size // start.shape[1]), axis=1)
    return (columns <= rows) & (columns.astype(F32) >= start)


def head_of(x, h):
    lanes = lax.broadcasted_iota(jnp.int32, x.shape, 1)
    return jnp.where((lanes >= h * HEAD_DIM) & (lanes < (h + 1) * HEAD_DIM), x, jnp.zeros_like(x))


def soft(query, key, allowed):
    scores = dot(query, key, NT) * 0.125
    masked = jnp.where(allowed, scores, -1e30)
    exponent = jnp.exp(masked - jnp.max(masked, axis=-1, keepdims=True))
    return exponent / jnp.sum(exponent, axis=-1, keepdims=True)


def attend_kernel(planes, qkv_w_ref, gate_ref, up_ref, x_ref, out_weight_ref, position_ref, bias_ref, *refs):
    vector_refs, rate_ref = refs[:4], refs[4]
    h_ref, qkv_ref, attn_ref, resid_ref, h_two_ref, w_both_ref, w_qkv_ref, w_out_ref, tab_ref, norm_ref = refs[5:15]
    cut, landed, made, both, small_ref, place_ref, all_ref, places_ref, tables = refs[15:24]
    x_all, w, wo, norms, b, block, away = refs[24:31]
    sems, scratch = refs[31:60], refs[60:]
    mine, base, _, _ = place()
    plane = base // TEAM
    swap, gather = Swap(made, both, sems[:3]), Gather(x_ref, x_all, sems[3:10])
    vectors = Swap(small_ref, all_ref.at[plane], sems[10:13], same=True)
    places = Swap(place_ref, places_ref, sems[13:16], same=True, near_first=True)
    line = Line(planes, all_ref.at[plane], all_ref, sems[16:19], same=True, within=True)
    rows, heads = LineGather(planes, landed, w, sems[19:22]), Swap(cut, landed, sems[22:25])
    outs = LineGather(planes, out_weight_ref, wo, sems[25:28])
    total, spread = Sum(None, scratch[:4], scratch[4:11], away), Gather(block, h_two_ref, scratch[11:18])
    wide_line = LineGather(planes, both, w_both_ref, scratch[18:21])
    stores = [
        pltpu.make_async_copy(src, dst, scratch[21].at[i])
        for i, (src, dst) in enumerate(((w, w_qkv_ref), (wo, w_out_ref), (tables, tab_ref)))
    ]
    step = pl.program_id(0)
    slot = TEAM - 1 - step

    @pl.when(step == 0)
    def _():
        depth = gate_ref.shape[0]
        for row, ref in enumerate(vector_refs):
            small_ref[row : row + 1, :depth] = ref[...].astype(F32).reshape(1, depth)
        bias = bias_ref[...].astype(F32).reshape(1, bias_ref.shape[0])
        for i in range(bias_ref.shape[0] // depth):
            small_ref[4 + i : 5 + i, :depth] = bias[:, i * depth : (i + 1) * depth]
        known = position_ref[...].astype(F32).reshape(1, position_ref.shape[0])
        for i in range(position_ref.shape[0] // 128):
            place_ref[i : i + 1, :] = known[:, i * 128 : (i + 1) * 128]
        for i in range(TEAM):
            cut[i] = slices(qkv_w_ref, [s * HEADS + z * TEAM + i for s in range(3) for z in range(planes)], HEAD_DIM)
        greet(swap.near + line.near)
        outs.start()
        heads.start()
        vectors.start()
        places.start()
        size = gate_ref.shape[1] // (planes * TEAM)
        for i in range(TEAM):
            units = [z * TEAM + i for z in range(planes)]
            made[i] = jnp.concatenate([slices(gate_ref, units, size), slices(up_ref, units, size)], axis=1)
        outs.stage(2)
        heads.finish()
        rows.start()
        gather.start()
        swap.start()
        vectors.finish()
        line.start()
        for stage in range(3, planes):
            outs.stage(stage)
        places.finish()
        square = (128, 128)

        @pl.loop(0, TEAM)
        def _(i):
            known = places_ref[i]
            for part in range(tables.shape[2] // 128):
                at = jnp.transpose(jnp.broadcast_to(known[part : part + 1, :], square))
                here = pl.ds(part * 128, 128)
                angle = at * rate_ref[...]
                tables[i, 0, here, :] = jnp.cos(angle)
                tables[i, 1, here, :] = jnp.sin(angle)
                token = lax.broadcasted_iota(jnp.int32, square, 0) + part * 128
                tables[i, 2, here, :] = token.astype(F32) - at

        rows.stage(2)
        gather.middle()
        for stage in range(3, planes):
            rows.stage(stage)
        line.finish()
        each = [all_ref[z, i] for z in range(planes) for i in range(TEAM)]
        for i in range(4):
            norms[i : i + 1, :] = jnp.concatenate([known[i : i + 1, :depth] for known in each], axis=1)
        per = qkv_w_ref.shape[1] // (planes * TEAM * depth)
        bias = []
        for part in range(3):
            for z in range(planes):
                head = part * HEADS + z * TEAM + mine
                known = all_ref[head // per // TEAM, lax.rem(head // per, TEAM)]
                row = lax.broadcasted_iota(jnp.int32, known.shape, 0) == 4 + lax.rem(head, per)
                bias.append(jnp.sum(jnp.where(row, known, 0.0), axis=0, keepdims=True)[:, :depth])
        b[...] = jnp.concatenate(bias, axis=1)
        gather.finish()
        swap.finish()
        wide_line.start()
        rows.finish()
        outs.finish()
        for copy in stores:
            copy.start()

    pl.when(step == TEAM - 2)(functools.partial(wide_line.stage, 2))
    stream = x_all[slot].astype(F32)
    normed, _ = normalize(stream)
    h_one = (normed * norms[0:1, :] + norms[1:2, :]).astype(BF16)
    h_ref[0] = h_one
    qkv = dot(h_one, w[...].reshape(-1, w.shape[-1])) + b[...]
    width = LOCAL * HEAD_DIM
    cosine, sine = wide(tables[slot, 0]), wide(tables[slot, 1])
    query = turn(qkv[:, :width], cosine, sine).astype(BF16)
    key = turn(qkv[:, width : 2 * width], cosine, sine).astype(BF16)
    value = qkv[:, 2 * width :].astype(BF16)
    qkv_ref[0, :, :width] = query
    qkv_ref[0, :, width : 2 * width] = key
    qkv_ref[0, :, 2 * width :] = value
    allowed = visible(tables[slot, 2])
    mixed = jnp.zeros((query.shape[0], width), F32)
    for h in range(LOCAL):
        probs = soft(head_of(query, h), key, allowed).astype(BF16)
        mixed = mixed + dot(probs, head_of(value, h))
    attn_low = mixed.astype(BF16)
    attn_ref[0] = attn_low
    part = dot(attn_low, wo[...].reshape(-1, D)).astype(BF16)
    k = 3 - step // 2

    @pl.when(lax.rem(step, 2) == 0)
    def _():
        away[k] = part
        total.near_copy(k).start()

    @pl.when(lax.rem(step, 2) == 1)
    def _():
        total.own[k] = part

    for at, advance in ((1, total.middle_a), (3, total.middle_b), (5, total.middle_c), (6, total.middle_two)):
        pl.when(step == at)(advance)

    def use(rows, value):
        resid = x_all[0, rows, :].astype(F32) + value
        resid_ref[rows, :] = resid
        normed, _ = normalize(resid)
        block[rows, :] = (normed * norms[2:3, :] + norms[3:4, :]).astype(BF16)

    @pl.when(step == TEAM - 1)
    def _():
        total.finish(use)
        spread.start()
        for stage in range(3, planes):
            wide_line.stage(stage)
        spread.middle()
        norm_ref[...] = norms[...]
        spread.finish()
        wide_line.finish()
        for copy in stores:
            copy.wait()


def per_seq(*shape):
    return pl.BlockSpec((1,) + shape, lambda s: (s,) + (0,) * len(shape))


def whole(*shape):
    return pl.BlockSpec(shape, lambda s: (0,) * len(shape))


def attend(qkv, gate, up, inputs, out_weight, positions, bias, vectors, rate, planes, cid):
    rows, _ = inputs.shape
    depth, width = qkv.shape[0], LOCAL * HEAD_DIM
    heads, units = (TEAM, depth, 3 * width), (TEAM, depth, 2 * gate.shape[1] // TEAM)
    tables = (TEAM, 3, rows, 128)
    known = [
        jax.ShapeDtypeStruct((planes,) + units, BF16),
        jax.ShapeDtypeStruct((planes,) + heads, BF16),
        jax.ShapeDtypeStruct((planes,) + out_weight.shape, BF16),
        jax.ShapeDtypeStruct(tables, F32),
    ]

    def far_first(*shape):
        return pl.BlockSpec((1,) + shape, lambda s: (TEAM - 1 - s,) + (0,) * len(shape))

    return pl.pallas_call(
        functools.partial(attend_kernel, planes),
        grid=(TEAM,),
        in_specs=[VMEM] * 12,
        out_specs=[far_first(rows, D), far_first(rows, 3 * width), far_first(rows, width), whole(rows, D)]
        + [ANY] * 5
        + [whole(4, D)],
        out_shape=[
            jax.ShapeDtypeStruct((TEAM, rows, D), BF16),
            jax.ShapeDtypeStruct((TEAM, rows, 3 * width), BF16),
            jax.ShapeDtypeStruct((TEAM, rows, width), BF16),
            jax.ShapeDtypeStruct((rows, D), F32),
            jax.ShapeDtypeStruct((TEAM, rows, D), BF16),
        ]
        + known
        + [jax.ShapeDtypeStruct((4, D), F32)],
        scratch_shapes=[
            pltpu.VMEM(heads, BF16),
            pltpu.VMEM(heads, BF16),
            pltpu.VMEM(units, BF16),
            pltpu.VMEM(units, BF16),
            pltpu.VMEM((8, 128), F32),
            pltpu.VMEM((8, 128), F32),
            pltpu.VMEM((planes, TEAM, 8, 128), F32),
            pltpu.VMEM((TEAM, 8, 128), F32),
            pltpu.VMEM(tables, F32),
            pltpu.VMEM((TEAM, rows, D), BF16),
            pltpu.VMEM((planes,) + heads, BF16),
            pltpu.VMEM((planes,) + out_weight.shape, BF16),
            pltpu.VMEM((4, D), F32),
            pltpu.VMEM((1, 3 * width), F32),
            pltpu.VMEM((rows, D), BF16),
            pltpu.VMEM((4, rows, D), BF16),
        ]
        + Swap.sems
        + Gather.sems
        + Swap.sems * 2
        + Line.sems(planes)
        + LineGather.sems(planes)
        + Swap.sems
        + LineGather.sems(planes)
        + [pltpu.SemaphoreType.DMA]
        + Sum.scratch(rows, D)
        + Sum.sems
        + Gather.sems
        + LineGather.sems(planes)
        + [pltpu.SemaphoreType.DMA((3,))],
        cost_estimate=lasting(180),
        compiler_params=params(cid),
    )(qkv, gate, up, inputs, out_weight, positions, bias, *vectors, rate)


def attend_back_kernel(
    block_ref, wo_ref, w_ref, qkv_ref, tab_ref, attn_ref, hidden_ref, wd_ref, resid_ref, _,
    gqkv_ref, part_ref, gb_ref, wo_grad_ref, out_ref, held, wo_grad, away, *scratch,
):
    gather, block = Gather(block_ref, held, scratch[:7]), Sum(None, scratch[7:11], scratch[11:], away)
    step = pl.program_id(0)

    @pl.when(step == 0)
    def _():
        greet(gather.near)
        gather.start()
        wo_grad[...] = jnp.zeros_like(wo_grad)

    part = dot(hidden_ref[0], wd_ref[...]).astype(BF16)
    k = 3 - step // 2

    @pl.when(lax.rem(step, 2) == 0)
    def _():
        away[k] = part
        block.near_copy(k).start()

    @pl.when(lax.rem(step, 2) == 1)
    def _():
        block.own[k] = part

    for i in range(TEAM):
        pl.when(step == i)(functools.partial(gather.ready, i))
    grad = held[step]
    width = LOCAL * HEAD_DIM
    wo_grad[...] += dot(attn_ref[0], grad, TN)
    grad_att = dot(grad, wo_ref[...], NT).astype(BF16)
    query, key, value = (qkv_ref[0, :, i * width : (i + 1) * width] for i in range(3))
    allowed = visible(tab_ref[0, 2])
    zero = jnp.zeros((query.shape[0], width), F32)
    grad_query, grad_key, grad_value = zero, zero, zero
    for h in range(LOCAL):
        query_h, key_h, grad_h = head_of(query, h), head_of(key, h), head_of(grad_att, h)
        probs = soft(query_h, key, allowed)
        low = probs.astype(BF16)
        grad_probs = dot(grad_h, value, NT)
        delta = jnp.sum(low.astype(F32) * grad_probs, axis=-1, keepdims=True)
        grad_scores = (probs * (grad_probs - delta)).astype(BF16)
        grad_value = grad_value + dot(low, grad_h, TN)
        grad_query = grad_query + dot(grad_scores, key_h)
        grad_key = grad_key + dot(grad_scores, query_h, TN)
    cosine, sine = wide(tab_ref[0, 0]), -wide(tab_ref[0, 1])
    grad_query = turn(grad_query * 0.125, cosine, sine)
    grad_key = turn(grad_key * 0.125, cosine, sine)
    grad_qkv = jnp.concatenate([grad_query, grad_key, grad_value], axis=1).astype(BF16)
    gqkv_ref[0] = grad_qkv
    gb_ref[0] = jnp.sum(grad_qkv.astype(F32), axis=0, keepdims=True)
    part_ref[0] = dot(grad_qkv, w_ref[...], NT).astype(BF16)

    def use(rows, value):
        out_ref[rows, :] = resid_ref[rows, :] + value

    pl.when(step == 1)(gather.middle)
    for at, advance in ((1, block.middle_a), (3, block.middle_b), (5, block.middle_c), (6, block.middle_two)):
        pl.when(step == at)(advance)

    @pl.when(step == TEAM - 1)
    def _():
        wo_grad_ref[...] = wo_grad[...].astype(BF16)
        block.finish(use)
        gather.sent()


def attend_back(block, w_out, w_qkv, qkv, tables, attn, hidden, w_down, resid, after, cid):
    seqs, rows, _ = qkv.shape
    width = LOCAL * HEAD_DIM

    def far_first(*shape):
        return pl.BlockSpec((1,) + shape, lambda s: (seqs - 1 - s,) + (0,) * len(shape))

    return pl.pallas_call(
        attend_back_kernel,
        grid=(seqs,),
        in_specs=[
            ANY,
            whole(width, D),
            whole(D, 3 * width),
            per_seq(rows, 3 * width),
            per_seq(3, rows, 128),
            per_seq(rows, width),
            far_first(rows, hidden.shape[2]),
            VMEM,
            VMEM,
            ANY,
        ],
        out_specs=[per_seq(rows, 3 * width), per_seq(rows, D), per_seq(1, 3 * width), whole(width, D), whole(rows, D)],
        out_shape=[
            jax.ShapeDtypeStruct((seqs, rows, 3 * width), BF16),
            jax.ShapeDtypeStruct((seqs, rows, D), BF16),
            jax.ShapeDtypeStruct((seqs, 1, 3 * width), F32),
            jax.ShapeDtypeStruct((width, D), BF16),
            jax.ShapeDtypeStruct((rows, D), F32),
        ],
        scratch_shapes=[
            pltpu.VMEM((seqs, rows, D), BF16),
            pltpu.VMEM((width, D), F32),
            pltpu.VMEM((4, rows, D), BF16),
        ]
        + Gather.sems
        + Sum.scratch(rows, D)
        + Sum.sems,
        cost_estimate=lasting(65),
        compiler_params=params(cid, 54),
    )(block, w_out, w_qkv, qkv, tables, attn, hidden, w_down, resid, after)


def team_shards(
    inputs, positions, norm1_gain, norm1_bias, qkv_weight, qkv_bias, out_weight, norm2_gain, norm2_bias,
    gate_weight, up_weight, down_weight, out_grad,
):
    n = lax.axis_size("fsdp")
    planes = n // TEAM
    rows = inputs.shape[0]
    tokens = TEAM * rows
    depth = qkv_weight.shape[0]
    ff = down_weight.shape[0]
    width = LOCAL * HEAD_DIM
    lines = [[z * TEAM + i for z in range(planes)] for i in range(TEAM)]
    mine = lax.rem(lax.axis_index("fsdp"), TEAM)

    def line_sum(x):
        return lax.psum_scatter(x, "fsdp", scatter_dimension=0, tiled=True, axis_index_groups=lines)

    half = ROT // 2
    rate = 10000.0 ** (-np.arange(half) / half)
    rate = np.tile(np.concatenate([rate, rate, np.zeros(HEAD_DIM - ROT)]), 128 // HEAD_DIM)[None].astype(np.float32)
    h_one, qkv, attn_low, resid, h_two, w_both, w_qkv, w_out, tables, norms = attend(
        qkv_weight, gate_weight, up_weight, inputs, out_weight, positions, qkv_bias,
        (norm1_gain, norm1_bias, norm2_gain, norm2_bias), jnp.asarray(rate), planes, 1,
    )
    w_both, w_qkv = w_both.reshape(D, 2 * planes * ff), w_qkv.reshape(D, 3 * width)
    w_out = w_out.reshape(width, D)
    pre, hidden, grad_down, g_all, w_down = expand(h_two, w_both, out_grad, down_weight, planes, 3)
    w_down = w_down.reshape(planes * ff, D)
    grad_resid, sums_two, block, grad_w_both = mlp_back(
        pre, g_all, h_two.reshape(tokens, D), w_down, w_both, resid, out_grad, norms, grad_down, 5
    )
    grad_down = line_sum(grad_down)
    grad_w_both = line_sum(grad_w_both)
    grad_qkv, part, grad_bias, grad_out, block_out = attend_back(
        block, w_out, w_qkv, qkv, tables, attn_low, hidden, w_down, resid, grad_down, 6
    )
    grad_qkv = grad_qkv.reshape(tokens, 3 * width)
    grad_w_qkv = dot(h_one.reshape(tokens, D), grad_qkv, TN).astype(BF16)
    part, grad_w_qkv = lax.optimization_barrier((part, grad_w_qkv))
    branch = grad_out.reshape(planes, depth, D)
    norm_part, branch, shared = last(part, inputs, norms, branch, sums_two, grad_bias, grad_w_qkv, 7)
    grad_w_qkv = line_sum(grad_w_qkv)
    blocks = grad_w_both.reshape(TEAM, depth, 2 * planes * ff)
    blocks, sums = both_closing(blocks, shared, (norm_part, branch), 9)
    block_out, input_grad = block_out.astype(BF16), grad_resid + norm_part
    grad_gate_w, grad_up_w, grad_out = first_grads(blocks, branch)
    blocks = closing(grad_w_qkv.reshape(TEAM, depth, 3 * width), (input_grad, grad_up_w, sums), 8)
    grad_w_qkv = rest_grads(blocks, planes)

    return (
        block_out,
        input_grad,
        sums[0, :depth],
        sums[1, :depth],
        grad_w_qkv,
        sums[4 : 4 + qkv_bias.shape[0] // depth, :depth].reshape(-1),
        grad_out,
        sums[2, :depth],
        sums[3, :depth],
        grad_gate_w,
        grad_up_w,
        grad_down.astype(F32),
    )


def rotate_pairs(heads, places, sign):
    half_rot = ROT // 2
    frequency = 10000.0 ** (-jnp.arange(half_rot, dtype=jnp.float32) / half_rot)
    angles = places.astype(jnp.float32)[:, None] * frequency[None, :]
    cosine = jnp.cos(angles)[:, None, :]
    sine_part = sign * jnp.sin(angles)[:, None, :]
    front_part = heads[..., :half_rot]
    back_part = heads[..., half_rot:ROT]
    return jnp.concatenate(
        [
            front_part * cosine - back_part * sine_part,
            back_part * cosine + front_part * sine_part,
            heads[..., ROT:],
        ],
        axis=-1,
    )


def by_groups(heads):
    group_heads = min(8, HEADS)
    shaped = heads.reshape(heads.shape[0], HEADS // group_heads, group_heads, HEAD_DIM)
    return jnp.moveaxis(shaped, 1, 0)


def from_groups(grouped):
    return jnp.moveaxis(grouped, 0, 1).reshape(grouped.shape[1], HEADS, HEAD_DIM)


def plain_group(block_items, allowed):
    query_part, key_part, value_part = block_items
    scores = (
        jnp.einsum("qhd,khd->hqk", query_part, key_part, preferred_element_type=jnp.float32) * 0.125
    )
    masked = jnp.where(allowed[None], scores, -1e30)
    row_max = jnp.max(masked, axis=-1, keepdims=True)
    exponent = jnp.exp(masked - row_max)
    row_total = jnp.sum(exponent, axis=-1, keepdims=True)
    soft_probs = (exponent / row_total).astype(jnp.bfloat16)
    mixed_part = jnp.einsum(
        "hqk,khd->qhd", soft_probs, value_part, preferred_element_type=jnp.float32
    )
    return (mixed_part, (row_max + jnp.log(row_total))[..., 0])


def plain_back(block_items, allowed):
    query_part, key_part, value_part, grad_part, row_delta, log_total = block_items
    scores = (
        jnp.einsum("qhd,khd->hqk", query_part, key_part, preferred_element_type=jnp.float32) * 0.125
    )
    soft_probs = jnp.where(allowed[None], jnp.exp(scores - log_total[..., None]), 0.0)
    grad_probs = jnp.einsum(
        "qhd,khd->hqk", grad_part, value_part.astype(jnp.float32), precision=lax.Precision.HIGHEST
    )
    rounded_probs = soft_probs.astype(jnp.bfloat16).astype(jnp.float32)
    grad_value = jnp.einsum("hqk,qhd->khd", rounded_probs, grad_part, precision=lax.Precision.HIGHEST)
    grad_scores = (soft_probs * (grad_probs - row_delta[..., None])).astype(jnp.bfloat16)
    grad_query = 0.125 * jnp.einsum(
        "hqk,khd->qhd", grad_scores, key_part, preferred_element_type=jnp.float32
    )
    grad_key = 0.125 * jnp.einsum(
        "hqk,qhd->khd", grad_scores, query_part, preferred_element_type=jnp.float32
    )
    return (grad_query, grad_key, grad_value)


def shards(
    inputs,
    positions,
    norm1_gain,
    norm1_bias,
    qkv_weight,
    qkv_bias,
    out_weight,
    norm2_gain,
    norm2_bias,
    gate_weight,
    up_weight,
    down_weight,
    out_grad,
):
    tok_rows = inputs.shape[0]
    gain_one, bias_one, w_qkv, b_qkv, w_out = (
        lax.all_gather(norm1_gain, "fsdp", axis=0, tiled=True),
        lax.all_gather(norm1_bias, "fsdp", axis=0, tiled=True),
        lax.all_gather(qkv_weight, "fsdp", axis=0, tiled=True),
        lax.all_gather(qkv_bias, "fsdp", axis=0, tiled=True),
        lax.all_gather(out_weight, "fsdp", axis=0, tiled=True),
    )
    stream = inputs.astype(jnp.float32)
    normed_one, inverse_one = normalize(stream)
    h_one = (normed_one * gain_one.astype(jnp.float32) + bias_one.astype(jnp.float32)).astype(
        jnp.bfloat16
    )
    qkv_pre = jnp.dot(h_one, w_qkv, preferred_element_type=jnp.float32) + b_qkv.astype(jnp.float32)
    qkv_heads = qkv_pre.reshape(tok_rows, 3, HEADS, HEAD_DIM)
    query_low = rotate_pairs(qkv_heads[:, 0], positions, 1.0).astype(jnp.bfloat16)
    key_all = rotate_pairs(qkv_heads[:, 1], positions, 1.0).astype(jnp.bfloat16)
    value_all = qkv_heads[:, 2].astype(jnp.bfloat16)
    token_index = jnp.arange(tok_rows, dtype=jnp.int32)
    allowed = (token_index[None, :] <= token_index[:, None]) & (
        token_index[None, :] >= (token_index - positions)[:, None]
    )
    mixed_grouped, log_grouped = lax.map(
        lambda block_items: plain_group(block_items, allowed),
        (by_groups(query_low), by_groups(key_all), by_groups(value_all)),
    )
    mixed_heads = from_groups(mixed_grouped)
    attn_low = mixed_heads.reshape(tok_rows, D).astype(jnp.bfloat16)
    resid = stream + jnp.dot(attn_low, w_out, preferred_element_type=jnp.float32)
    gain_two, bias_two, w_gate, w_up, w_down = (
        lax.all_gather(norm2_gain, "fsdp", axis=0, tiled=True),
        lax.all_gather(norm2_bias, "fsdp", axis=0, tiled=True),
        lax.all_gather(gate_weight, "fsdp", axis=0, tiled=True),
        lax.all_gather(up_weight, "fsdp", axis=0, tiled=True),
        lax.all_gather(down_weight, "fsdp", axis=0, tiled=True),
    )
    normed_two, inverse_two = normalize(resid)
    h_two = (normed_two * gain_two.astype(jnp.float32) + bias_two.astype(jnp.float32)).astype(
        jnp.bfloat16
    )
    gate_pre = jnp.dot(h_two, w_gate, preferred_element_type=jnp.float32)
    up_pre = jnp.dot(h_two, w_up, preferred_element_type=jnp.float32)
    sigmoid_gate = jax.nn.sigmoid(gate_pre)
    silu_gate = gate_pre * sigmoid_gate
    hidden = (silu_gate * up_pre).astype(jnp.bfloat16)
    block_out = (resid + jnp.dot(hidden, w_down, preferred_element_type=jnp.float32)).astype(
        jnp.bfloat16
    )
    gain_two, w_gate, w_up, w_down = (
        lax.all_gather(norm2_gain, "fsdp", axis=0, tiled=True),
        lax.all_gather(gate_weight, "fsdp", axis=0, tiled=True),
        lax.all_gather(up_weight, "fsdp", axis=0, tiled=True),
        lax.all_gather(down_weight, "fsdp", axis=0, tiled=True),
    )
    grad_down_w = jnp.einsum("tf,td->fd", hidden, out_grad, preferred_element_type=jnp.float32)
    grad_hidden = jnp.einsum("td,fd->tf", out_grad, w_down, preferred_element_type=jnp.float32)
    grad_gate = (
        grad_hidden * up_pre * sigmoid_gate * (1.0 + gate_pre * (1.0 - sigmoid_gate))
    ).astype(jnp.bfloat16)
    grad_up = (grad_hidden * silu_gate).astype(jnp.bfloat16)
    grad_gate_w = jnp.einsum("td,tf->df", h_two, grad_gate, preferred_element_type=jnp.float32)
    grad_up_w = jnp.einsum("td,tf->df", h_two, grad_up, preferred_element_type=jnp.float32)
    grad_htwo = jnp.einsum(
        "tf,df->td", grad_gate, w_gate, preferred_element_type=jnp.float32
    ) + jnp.einsum("tf,df->td", grad_up, w_up, preferred_element_type=jnp.float32)
    grad_gain_two = jnp.sum(grad_htwo * normed_two, axis=0)
    grad_bias_two = jnp.sum(grad_htwo, axis=0)
    grad_resid = out_grad.astype(jnp.float32) + norm_back(
        grad_htwo * gain_two.astype(jnp.float32), normed_two, inverse_two
    )
    mlp_sums = (
        lax.psum_scatter(grad_gain_two, "fsdp", scatter_dimension=0, tiled=True),
        lax.psum_scatter(grad_bias_two, "fsdp", scatter_dimension=0, tiled=True),
        lax.psum_scatter(grad_gate_w, "fsdp", scatter_dimension=0, tiled=True),
        lax.psum_scatter(grad_up_w, "fsdp", scatter_dimension=0, tiled=True),
        lax.psum_scatter(grad_down_w, "fsdp", scatter_dimension=0, tiled=True),
    )
    gain_one, w_qkv, w_out = (
        lax.all_gather(norm1_gain, "fsdp", axis=0, tiled=True),
        lax.all_gather(qkv_weight, "fsdp", axis=0, tiled=True),
        lax.all_gather(out_weight, "fsdp", axis=0, tiled=True),
    )
    grad_branch = grad_resid.astype(jnp.bfloat16)
    grad_out_w = jnp.einsum("ti,td->id", attn_low, grad_branch, preferred_element_type=jnp.float32)
    grad_att = jnp.einsum(
        "td,id->ti", grad_branch, w_out, preferred_element_type=jnp.float32
    ).reshape(tok_rows, HEADS, HEAD_DIM)
    group_heads = min(8, HEADS)
    row_delta = jnp.sum(grad_att * mixed_heads, axis=-1)
    delta_grouped = row_delta.reshape(tok_rows, HEADS // group_heads, group_heads).transpose(
        1, 2, 0
    )
    query_grouped, key_grouped, value_grouped = lax.map(
        lambda block_items: plain_back(block_items, allowed),
        (
            by_groups(query_low),
            by_groups(key_all),
            by_groups(value_all),
            by_groups(grad_att),
            delta_grouped,
            log_grouped,
        ),
    )
    grad_query = from_groups(query_grouped)
    grad_key = from_groups(key_grouped)
    grad_value = from_groups(value_grouped)
    grad_qkv = (
        jnp.stack(
            [
                rotate_pairs(grad_query, positions, -1.0),
                rotate_pairs(grad_key, positions, -1.0),
                grad_value,
            ],
            axis=1,
        )
        .reshape(tok_rows, 3 * D)
        .astype(jnp.bfloat16)
    )
    grad_qkv_w = jnp.einsum("td,tk->dk", h_one, grad_qkv, preferred_element_type=jnp.float32)
    grad_qkv_b = jnp.sum(grad_qkv.astype(jnp.float32), axis=0)
    grad_hone = jnp.einsum("tk,dk->td", grad_qkv, w_qkv, preferred_element_type=jnp.float32)
    grad_gain_one = jnp.sum(grad_hone * normed_one, axis=0)
    grad_bias_one = jnp.sum(grad_hone, axis=0)
    input_grad = grad_resid + norm_back(
        grad_hone * gain_one.astype(jnp.float32), normed_one, inverse_one
    )
    attn_sums = (
        lax.psum_scatter(grad_gain_one, "fsdp", scatter_dimension=0, tiled=True),
        lax.psum_scatter(grad_bias_one, "fsdp", scatter_dimension=0, tiled=True),
        lax.psum_scatter(grad_qkv_w, "fsdp", scatter_dimension=0, tiled=True),
        lax.psum_scatter(grad_qkv_b, "fsdp", scatter_dimension=0, tiled=True),
        lax.psum_scatter(grad_out_w, "fsdp", scatter_dimension=0, tiled=True),
    )
    return (
        block_out,
        input_grad,
        attn_sums[0],
        attn_sums[1],
        attn_sums[2],
        attn_sums[3],
        attn_sums[4],
        mlp_sums[0],
        mlp_sums[1],
        mlp_sums[2],
        mlp_sums[3],
        mlp_sums[4],
    )


def solution(mesh):
    devices = mesh.shape["fsdp"]
    rows, columns = P("fsdp", None), P("fsdp")
    body = team_shards if devices % TEAM == 0 and D == devices * HEAD_DIM else shards
    return jax.shard_map(
        body,
        mesh=mesh,
        in_specs=(rows, columns, columns, columns, rows, columns, rows, columns, columns, rows, rows, rows, rows),
        out_specs=(rows, rows, columns, columns, rows, columns, rows, columns, columns, rows, rows, rows),
        check_vma=False,
    )
```

```python
import functools

import jax
import jax.numpy as jnp
import numpy as np
from jax import lax
from jax.experimental import pallas as pl
from jax.experimental.pallas import tpu as pltpu
from jax.sharding import PartitionSpec as P

D = 2048
HEADS = 32
HEAD_DIM = 64
ROT = 16
EPS = 1e-05
TEAM = 8
LOCAL = HEADS // TEAM
MESH = pl.DeviceIdType.MESH
BF16 = jnp.bfloat16
F32 = jnp.float32
ANY = pl.BlockSpec(memory_space=pl.ANY)
VMEM = pl.BlockSpec(memory_space=pltpu.VMEM)


def lasting(us):
    return pl.CostEstimate(flops=0, bytes_accessed=int(us * 3.6e6), transcendentals=0)


def params(cid=None, limit=56):
    extra = {} if cid is None else {"collective_id": cid, "has_side_effects": True}
    return pltpu.CompilerParams(vmem_limit_bytes=limit * 1024 * 1024, **extra)


def place():
    me = lax.axis_index("fsdp")
    mine = lax.rem(me, TEAM)
    return mine, me - mine, mine // 2, lax.rem(mine, 2)


def chip_at(chip, step):
    along_x, along_y = lax.rem(chip, 2), chip // 2
    if step & 1:
        along_x = 1 - along_x
    if step & 2:
        along_y = 1 - along_y
    return along_y * 2 + along_x


def relation(chip, core, r):
    return chip_at(chip, r // 2) * 2 + lax.rem(core + r, 2)


def greet(devices):
    barrier = pltpu.get_barrier_semaphore()
    for device in devices:
        pl.semaphore_signal(barrier, inc=1, device_id=(device,), device_id_type=MESH)
    pl.semaphore_wait(barrier, len(devices))


def remote(src, dst, send, recv, device):
    return pltpu.make_async_remote_copy(
        src_ref=src, dst_ref=dst, send_sem=send, recv_sem=recv, device_id=(device,), device_id_type=MESH
    )


class Swap:
    sems = [pltpu.SemaphoreType.DMA, pltpu.SemaphoreType.DMA((TEAM,)), pltpu.SemaphoreType.DMA((TEAM,))]

    def __init__(self, src, out, sems, same=False, near_first=False):
        own_sem, send, recv = sems
        mine, base, chip, core = place()
        others = [relation(chip, core, r) for r in range(1, TEAM)]
        self.near = [base + other for other in others]
        self.copies = [
            remote(
                src if same else src.at[other], out.at[r if near_first else mine], send.at[r], recv.at[r], base + other
            )
            for r, other in enumerate(others, 1)
        ]
        own = src if same else src.at[mine]
        self.copies.append(pltpu.make_async_copy(own, out.at[0 if near_first else mine], own_sem))

    def start(self):
        for copy in self.copies:
            copy.start()

    def finish(self):
        for copy in self.copies:
            copy.wait()


class Line:
    def sems(planes):
        return [pltpu.SemaphoreType.DMA, pltpu.SemaphoreType.DMA((planes,)), pltpu.SemaphoreType.DMA((planes,))]

    def __init__(self, planes, src, out, sems, same=False, within=False):
        own_sem, send, recv = sems
        mine, base, _, _ = place()
        plane = base // TEAM
        others = [lax.rem(plane + k, planes) for k in range(1, planes)]
        self.near = [other * TEAM + mine for other in others]
        self.copies = [
            remote(src if same else src.at[other], out.at[plane], send.at[k], recv.at[k], other * TEAM + mine)
            for k, other in enumerate(others)
        ]
        own = src if same else src.at[plane]
        self.own = None if within else pltpu.make_async_copy(own, out.at[plane], own_sem)

    def start(self):
        for copy in self.copies:
            copy.start()
        if self.own is not None:
            self.own.start()

    def finish(self):
        for copy in self.copies:
            copy.wait()
        if self.own is not None:
            self.own.wait()


class LineGather:
    def sems(planes):
        return [pltpu.SemaphoreType.DMA, pltpu.SemaphoreType.DMA((2, planes)), pltpu.SemaphoreType.DMA((2, planes))]

    def __init__(self, planes, src, out, sems):
        own_sem, self.send, self.recv = sems
        mine, base, _, _ = place()
        self.plane, self.planes, self.src, self.out = base // TEAM, planes, src, out
        self.me = base + mine
        self.near = [lax.rem(self.plane + k, planes) * TEAM + mine for k in (1, planes - 1)]
        self.own = pltpu.make_async_copy(src, out.at[self.plane], own_sem)

    def copy(self, way, stage):
        step = 1 - 2 * way
        block, to = self.plane - step * (stage - 1), self.plane + step
        is_there = (block >= 0) & (block < self.planes) & (to >= 0) & (to < self.planes)
        src = self.src if stage == 1 else self.out.at[block]
        sems = self.send.at[way, stage], self.recv.at[way, stage]
        return is_there, remote(src, self.out.at[block], *sems, self.me + step * TEAM)

    def arrived(self, way, stage):
        block = self.plane - (1 - 2 * way) * stage

        @pl.when((block >= 0) & (block < self.planes))
        def _():
            dst = self.out.at[block]
            remote(dst, dst, self.send.at[way, stage], self.recv.at[way, stage], self.me).wait_recv()

    def start(self):
        self.own.start()
        self.stage(1)

    def stage(self, stage):
        for way in (0, 1):
            if stage > 1:
                self.arrived(way, stage - 1)
            is_there, copy = self.copy(way, stage)
            pl.when(is_there)(copy.start)

    def finish(self):
        self.own.wait()
        for way in (0, 1):
            self.arrived(way, self.planes - 1)
            for stage in range(1, self.planes):
                is_there, copy = self.copy(way, stage)
                pl.when(is_there)(copy.wait_send)


def slices(ref, pieces, size):
    return jnp.concatenate([ref[:, i * size : (i + 1) * size] for i in pieces], axis=1)


def unslice(held, parts, planes, outs):
    size = held.shape[2] // (parts * planes)
    for at in range(parts * planes):
        row = jnp.concatenate([held[i, :, at * size : (at + 1) * size] for i in range(TEAM)], axis=1)
        out, first = (outs[at // planes], at % planes) if len(outs) > 1 else (outs[0], at)
        out[:, first * TEAM * size : (first + 1) * TEAM * size] = row.astype(F32)


def first_kernel(planes, held_ref, far_ref, gate_ref, up_ref, wo_ref):
    unslice(held_ref, 2, planes, [gate_ref, up_ref])
    wo_ref[...] = added(far_ref)


def first_grads(held, far):
    _, depth, width = held.shape
    return pl.pallas_call(
        functools.partial(first_kernel, far.shape[0]),
        out_shape=[jax.ShapeDtypeStruct((depth, width * TEAM // 2), F32)] * 2
        + [jax.ShapeDtypeStruct(far.shape[1:], F32)],
        in_specs=[VMEM] * 2,
        out_specs=[VMEM] * 3,
        cost_estimate=lasting(4),
        compiler_params=params(),
    )(held, far)


def rest_kernel(planes, held_ref, w_ref):
    unslice(held_ref, 3, planes, [w_ref])


def rest_grads(held, planes):
    _, depth, width = held.shape
    return pl.pallas_call(
        functools.partial(rest_kernel, planes),
        out_shape=jax.ShapeDtypeStruct((depth, width * TEAM), F32),
        in_specs=[VMEM],
        out_specs=VMEM,
        cost_estimate=lasting(3),
        compiler_params=params(),
    )(held)


def added(ref):
    total = ref[0].astype(F32)
    for i in range(1, ref.shape[0]):
        total = total + ref[i].astype(F32)
    return total


def close_kernel(w_ref, _, __, ___, held_ref, *sems):
    swap = Swap(w_ref, held_ref, sems)
    greet(swap.near)
    swap.start()
    swap.finish()


def both_close_kernel(planes, w_ref, shared_ref, _, __, held_ref, vector_ref, got, block, beyond, *sems):
    swap, inner = Swap(w_ref, held_ref, sems[:3]), Swap(shared_ref, got, sems[3:6])
    outer = Line(planes, block, beyond, sems[6:])
    greet(swap.near + outer.near)
    inner.start()
    swap.start()
    inner.finish()
    block[...] = added(got)
    outer.start()
    outer.finish()
    vector_ref[...] = added(beyond)
    swap.finish()


def both_closing(blocks, shared, after, cid):
    planes = shared.shape[1]
    return pl.pallas_call(
        functools.partial(both_close_kernel, planes),
        out_shape=[jax.ShapeDtypeStruct(blocks.shape, BF16), jax.ShapeDtypeStruct(shared.shape[2:], F32)],
        in_specs=[VMEM, VMEM, ANY, ANY],
        out_specs=[ANY, VMEM],
        scratch_shapes=[pltpu.VMEM(shared.shape, F32)]
        + [pltpu.VMEM(shared.shape[1:], F32)] * 2
        + Swap.sems * 2
        + Line.sems(planes),
        cost_estimate=lasting(22),
        compiler_params=params(cid),
    )(blocks, shared, *after)


def closing(blocks, after, cid):
    return pl.pallas_call(
        close_kernel,
        out_shape=jax.ShapeDtypeStruct(blocks.shape, BF16),
        in_specs=[VMEM, ANY, ANY, ANY],
        out_specs=ANY,
        scratch_shapes=Swap.sems,
        cost_estimate=lasting(14),
        compiler_params=params(cid),
    )(blocks, *after)


class Gather:
    sems = [pltpu.SemaphoreType.DMA((5,)), pltpu.SemaphoreType.DMA((5,)), pltpu.SemaphoreType.DMA((2,)),
            pltpu.SemaphoreType.DMA((2,)), pltpu.SemaphoreType.DMA((6,)), pltpu.SemaphoreType.DMA((6,)),
            pltpu.SemaphoreType.DMA]

    def __init__(self, src, out, sems):
        send, recv, hop_send, hop_recv, pass_send, pass_recv, own_sem = sems
        _, base, chip, core = place()
        side, over = (chip_at(chip, k) * 2 + core for k in (1, 2))
        self.sibling = base + chip * 2 + 1 - core
        self.near = [base + side, base + over, self.sibling]
        half = src.shape[0] // 2
        top, low = pl.ds(0, half), pl.ds(half, half)
        self.first = [
            remote(src.at[part], out.at[at, part], send.at[i], recv.at[i], base + to)
            for i, (part, at, to) in enumerate(((top, 2, side), (low, 4, over), (low, 2, side), (top, 4, over)))
        ]
        self.first.append(remote(src, out.at[1], send.at[4], recv.at[4], self.sibling))
        self.own = pltpu.make_async_copy(src, out.at[0], own_sem)
        self.hops = [
            remote(out.at[at, part], out.at[6, part], hop_send.at[i], hop_recv.at[i], base + to)
            for i, (at, part, to) in enumerate(((2, top, over), (4, low, side)))
        ]
        self.passed = [
            remote(out.at[at, part], out.at[at + 1, part], pass_send.at[i], pass_recv.at[i], self.sibling)
            for i, (at, part) in enumerate(((2, top), (4, low), (2, low), (4, top), (6, top), (6, low)))
        ]

    def start(self):
        for copy in self.first:
            copy.start()
        self.own.start()

    def middle(self):
        for i in (0, 1):
            self.first[i].wait_recv()
            self.hops[i].start()
            self.passed[i].start()

    def finish(self):
        for i in range(2, TEAM):
            self.ready(i)
        self.first[4].wait_recv()
        self.own.wait()
        self.sent()

    def ready(self, i):
        if i == 0:
            self.own.wait()
        elif i == 1:
            self.first[4].wait_recv()
        elif i == 6:
            for j in (0, 1):
                self.hops[j].wait_recv()
                self.passed[4 + j].start()
        elif i % 2 == 0:
            self.first[1 + i // 2].wait_recv()
            self.passed[1 + i // 2].start()
        else:
            for j in {3: (0, 2), 5: (1, 3), 7: (4, 5)}[i]:
                self.passed[j].wait_recv()

    def sent(self):
        for copy in self.first + self.hops + self.passed:
            copy.wait_send()


class Sum:
    def scratch(rows, width):
        return [pltpu.VMEM((4, rows, width), BF16), pltpu.VMEM((4, rows, width), BF16),
                pltpu.VMEM((2, rows // 2, width), BF16), pltpu.VMEM((2, rows, width), BF16)]

    sems = [pltpu.SemaphoreType.DMA((4,))] * 3 + [pltpu.SemaphoreType.DMA((2,))] * 2 + [pltpu.SemaphoreType.DMA((4,))] * 2

    def __init__(self, blocks, scratch, sems, away=None):
        self.own, self.beside, self.via, self.far = scratch
        load_sem, near_send, near_recv, via_send, via_recv, far_send, far_recv = sems
        _, base, chip, core = place()
        sibling = base + chip * 2 + 1 - core
        side, over = (base + chip_at(chip, k) * 2 + core for k in (1, 2))
        self.near = [side, over, sibling]
        self.half = self.own.shape[1] // 2
        top, low = pl.ds(0, self.half), pl.ds(self.half, self.half)
        self.loads = [
            pltpu.make_async_copy(blocks.at[2 * k], self.own.at[k], load_sem.at[k])
            for k in range(4)
            if away is None
        ]

        def near_copy(k):
            src = blocks.at[2 * k + 1] if away is None else away.at[k]
            return remote(src, self.beside.at[k], near_send.at[k], near_recv.at[k], sibling)

        self.near_copy = near_copy
        self.nears = [near_copy(k) for k in range(4)]
        self.vias = [
            remote(self.own.at[3, part], self.via.at[i], via_send.at[i], via_recv.at[i], to)
            for i, (part, to) in enumerate(((top, side), (low, over)))
        ]
        self.fars = [
            remote(self.own.at[k, part], self.far.at[k - 1, part], far_send.at[i], far_recv.at[i], to)
            for i, (k, part, to) in enumerate(((2, low, over), (1, top, side), (2, top, over), (1, low, side)))
        ]

    def start(self):
        for k in (3, 2, 1, 0):
            self.loads[k].start()
            self.nears[k].start()

    def pair(self, k):
        if self.loads:
            self.loads[k].wait()
        self.nears[k].wait_recv()

        @pl.loop(0, self.own.shape[1] // 16)
        def _(i):
            part = pl.ds(pl.multiple_of(i * 16, 16), 16)
            self.own[k, part, :] = (self.own[k, part, :].astype(F32) + self.beside[k, part, :].astype(F32)).astype(BF16)

    def middle_a(self):
        self.pair(3)
        for copy in self.vias:
            copy.start()

    def middle_b(self):
        self.pair(2)
        self.fars[0].start()

    def middle_c(self):
        self.pair(1)
        self.fars[1].start()

    def middle(self):
        self.middle_a()
        self.middle_b()
        self.middle_c()

    def middle_two(self):
        for i, k in ((0, 2), (1, 1)):
            self.vias[i].wait_recv()

            @pl.loop(0, self.half // 16)
            def _(j, i=i, k=k):
                part = pl.ds(pl.multiple_of(j * 16, 16), 16)
                at = pl.ds(pl.multiple_of(j * 16 + i * self.half, 16), 16)
                self.own[k, at, :] = (self.own[k, at, :].astype(F32) + self.via[i, part, :].astype(F32)).astype(BF16)

            self.fars[2 + i].start()

    def finish(self, use):
        if self.loads:
            self.loads[0].wait()
        self.nears[0].wait_recv()
        for copy in self.fars:
            copy.wait_recv()

        @pl.loop(0, self.own.shape[1] // 16)
        def _(i):
            part = pl.ds(pl.multiple_of(i * 16, 16), 16)
            total = self.own[0, part, :].astype(F32) + self.beside[0, part, :].astype(F32)
            use(part, total + self.far[0, part, :].astype(F32) + self.far[1, part, :].astype(F32))

        for copy in self.nears + self.vias + self.fars:
            copy.wait_send()


def fold(x):
    return x[:8] + x[8:]


def expand_kernel(
    planes, h_ref, w_ref, g_ref, down_ref, pre_ref, hidden_ref, grad_ref, g_all_ref, wd_ref, held, g, total, w, *sems
):
    gather, line = Gather(g_ref, g_all_ref, sems[:7]), LineGather(planes, down_ref, wd_ref, sems[7:10])
    step = pl.program_id(0)

    @pl.when(step == 0)
    def _():
        greet(gather.near + line.near)
        line.start()
        gather.start()
        weights = pltpu.make_async_copy(w_ref, w, sems[11])
        weights.start()
        weights.wait()

    pre = dot(h_ref[0], w[...])
    pre_ref[0] = pre
    ff = hidden_ref.shape[2]
    gate_pre, up_pre = pre[:, :ff], pre[:, ff:]
    hidden = (gate_pre * jax.nn.sigmoid(gate_pre) * up_pre).astype(BF16)
    hidden_ref[0] = hidden
    held[step] = hidden
    pl.when(step == TEAM - 3)(functools.partial(line.stage, 2))

    @pl.when(step == TEAM - 1)
    def _():
        def load(i):
            return pltpu.make_async_copy(g_all_ref.at[i], g.at[i % 2], sems[10].at[i % 2])

        gather.middle()
        gather.ready(0)
        load(0).start()
        for i in range(TEAM):
            if i < TEAM - 1:
                gather.ready(i + 1)
                load(i + 1).start()
            load(i).wait()
            product = dot(held[i], g[i % 2], TN)
            total[...] = product if i == 0 else total[...] + product
            if i == 4:
                for stage in range(3, planes):
                    line.stage(stage)
        grad_ref[...] = total[...].astype(BF16)
        gather.sent()
        line.finish()


def expand(h_two, w_both, out_grad, down, planes, cid):
    seqs, rows, _ = h_two.shape
    width = w_both.shape[1]
    return pl.pallas_call(
        functools.partial(expand_kernel, planes),
        grid=(seqs,),
        in_specs=[per_seq(rows, D), ANY, VMEM, VMEM],
        out_specs=[per_seq(rows, width), per_seq(rows, width // 2), whole(width // 2, D), ANY, ANY],
        out_shape=[
            jax.ShapeDtypeStruct((seqs, rows, width), F32),
            jax.ShapeDtypeStruct((seqs, rows, width // 2), BF16),
            jax.ShapeDtypeStruct((width // 2, D), BF16),
            jax.ShapeDtypeStruct((seqs, rows, D), BF16),
            jax.ShapeDtypeStruct((planes,) + down.shape, BF16),
        ],
        scratch_shapes=[
            pltpu.VMEM((seqs, rows, width // 2), BF16),
            pltpu.VMEM((2, rows, D), BF16),
            pltpu.VMEM((width // 2, D), F32),
            pltpu.VMEM((D, width), BF16),
        ]
        + Gather.sems
        + LineGather.sems(planes)
        + [pltpu.SemaphoreType.DMA((2,)), pltpu.SemaphoreType.DMA],
        cost_estimate=lasting(55),
        compiler_params=params(cid),
    )(h_two, w_both, out_grad, down)


def mlp_back_kernel(
    pre_ref, g_all_ref, h_ref, wd_ref, w_ref, resid_ref, g_ref, norm_ref, _,
    out_ref, sums_ref, block_ref, grad_w_ref,
    pre, g_all, turned, made, grads, away, w, resid, own_grad, wd, *scratch,
):
    pre_sem, g_sem, turned_sem, made_sem, late_sem = scratch[11:]
    total = Sum(None, scratch[:4], scratch[4:11], away)
    rows, ff = pre_ref.shape[1], wd_ref.shape[0]
    chunk = turned.shape[2]

    def loads(i):
        slot, at = lax.rem(i, 2), TEAM - 1 - i
        return (
            pltpu.make_async_copy(pre_ref.at[at], pre.at[slot], pre_sem.at[slot]),
            pltpu.make_async_copy(g_all_ref.at[at], g_all.at[slot], g_sem.at[slot]),
        )

    def load_chunk(i):
        slot = lax.rem(i, 2)
        columns = pl.ds(pl.multiple_of(i * chunk, chunk), chunk)
        return pltpu.make_async_copy(h_ref.at[:, columns], turned.at[slot], turned_sem.at[slot])

    def store_chunk(i):
        slot = lax.rem(i, 2)
        part = pl.ds(pl.multiple_of(i * chunk, chunk), chunk)
        return pltpu.make_async_copy(made.at[slot], grad_w_ref.at[part, :], made_sem.at[slot])

    for copy in loads(0):
        copy.start()
    late = [
        pltpu.make_async_copy(src, dst, late_sem.at[i])
        for i, (src, dst) in enumerate(((wd_ref, wd), (w_ref, w), (resid_ref, resid), (g_ref, own_grad)))
    ]
    for copy in late:
        copy.start()
    greet(total.near)

    @pl.loop(0, TEAM)
    def _(i):
        slot = lax.rem(i, 2)
        k, at = 3 - i // 2, TEAM - 1 - i

        @pl.when(i < TEAM - 1)
        def _():
            for copy in loads(i + 1):
                copy.start()

        for copy in loads(i):
            copy.wait()
        pl.when(i == 0)(late[0].wait)
        grad_hidden = dot(g_all[slot], wd[...], NT)
        gate_pre, up_pre = pre[slot, :, :ff], pre[slot, :, ff:]
        sigmoid = jax.nn.sigmoid(gate_pre)
        grad_gate = grad_hidden * up_pre * sigmoid * (1.0 + gate_pre * (1.0 - sigmoid))
        grad_up = grad_hidden * (gate_pre * sigmoid)
        part = pl.ds(pl.multiple_of(at * rows, rows), rows)
        grads[part, :] = jnp.concatenate([grad_gate, grad_up], axis=1).astype(BF16)

        def make(to):
            to[k] = dot(grads[part, :], w[...], NT).astype(BF16)

        pl.when(i == 0)(late[1].wait)

        @pl.when(lax.rem(i, 2) == 0)
        def _():
            make(away)
            total.near_copy(k).start()

        @pl.when(lax.rem(i, 2) == 1)
        def _():
            make(total.own)

        for step, advance in ((1, total.middle_a), (3, total.middle_b), (5, total.middle_c)):
            pl.when(i == step)(advance)

    load_chunk(0).start()
    total.middle_two()
    chunks = h_ref.shape[1] // chunk

    @pl.loop(0, chunks)
    def _(i):
        slot = lax.rem(i, 2)

        @pl.when(i < chunks - 1)
        def _():
            load_chunk(i + 1).start()

        load_chunk(i).wait()

        @pl.when(i >= 2)
        def _():
            store_chunk(i - 2).wait()

        made[slot] = dot(turned[slot], grads[...], TN).astype(BF16)
        store_chunk(i).start()

    sums_ref[...] = jnp.zeros_like(sums_ref)
    for copy in late[2:]:
        copy.wait()

    def use(rows, value):
        normed, inverse = normalize(resid[rows, :])
        sums_ref[:8, :] += fold(value * normed)
        sums_ref[8:, :] += fold(value)
        grad = own_grad[rows, :].astype(F32) + norm_back(value * norm_ref[2:3, :], normed, inverse)
        out_ref[rows, :] = grad
        block_ref[rows, :] = grad.astype(BF16)

    total.finish(use)
    store_chunk(chunks - 2).wait()
    store_chunk(chunks - 1).wait()


def mlp_back(pre, g_all, h_two, w_down, w_both, resid, out_grad, gain, after, cid):
    seqs, rows, both = pre.shape
    width = resid.shape[1]
    chunk = 256
    two = pltpu.SemaphoreType.DMA((2,))
    return pl.pallas_call(
        mlp_back_kernel,
        out_shape=[
            jax.ShapeDtypeStruct((rows, width), F32),
            jax.ShapeDtypeStruct((16, width), F32),
            jax.ShapeDtypeStruct((rows, width), BF16),
            jax.ShapeDtypeStruct((width, both), BF16),
        ],
        in_specs=[ANY, ANY, ANY, ANY, ANY, ANY, ANY, VMEM, ANY],
        out_specs=[VMEM, VMEM, VMEM, ANY],
        scratch_shapes=[
            pltpu.VMEM((2, rows, both), F32),
            pltpu.VMEM((2, rows, width), BF16),
            pltpu.VMEM((2, seqs * rows, chunk), BF16),
            pltpu.VMEM((2, chunk, both), BF16),
            pltpu.VMEM((seqs * rows, both), BF16),
            pltpu.VMEM((4, rows, width), BF16),
            pltpu.VMEM((width, both), BF16),
            pltpu.VMEM((rows, width), F32),
            pltpu.VMEM((rows, width), BF16),
            pltpu.VMEM((both // 2, width), BF16),
        ]
        + Sum.scratch(rows, width)
        + Sum.sems
        + [two] * 4
        + [pltpu.SemaphoreType.DMA((4,))],
        cost_estimate=lasting(60),
        compiler_params=params(cid, 50),
    )(pre, g_all, h_two, w_down, w_both, resid, out_grad, gain, after)


def share(x, sums, bias, planes, per, depth):
    mine = place()[0]
    x[...] = jnp.zeros_like(x)
    sums = [jnp.sum(v, axis=0, keepdims=True) for v in sums]
    for z in range(planes):
        for i in range(TEAM):
            at = (z * TEAM + i) * depth
            for row, v in enumerate(sums):
                x[i, z, row : row + 1, :depth] = v[:, at : at + depth]
    for part in range(3):
        for z in range(planes):
            head = part * HEADS + z * TEAM + mine
            owner = head // per
            at = (part * planes + z) * HEAD_DIM
            x[lax.rem(owner, TEAM), owner // TEAM, pl.ds(4 + lax.rem(head, per), 1), :depth] = bias[:, at : at + HEAD_DIM]


def last_kernel(
    planes, part_ref, x_ref, norm_ref, branch_ref, sums_two_ref, bias_ref, _,
    out_ref, far_ref, shared_ref, sums, *scratch,
):
    total, line = Sum(part_ref, scratch[:4], scratch[4:11]), Line(planes, branch_ref, far_ref, scratch[11:])
    greet(total.near + line.near)
    line.start()
    total.start()
    total.middle()
    total.middle_two()
    sums[...] = jnp.zeros_like(sums)

    def use(rows, value):
        normed, inverse = normalize(x_ref[rows, :].astype(F32))
        sums[:8, :] += fold(value * normed)
        sums[8:, :] += fold(value)
        out_ref[rows, :] = norm_back(value * norm_ref[0:1, :], normed, inverse)

    total.finish(use)
    vectors = [sums[:8, :], sums[8:, :], sums_two_ref[:8, :], sums_two_ref[8:, :]]
    depth = part_ref.shape[2] // (planes * TEAM)
    share(shared_ref, vectors, added(bias_ref), planes, bias_ref.shape[2] // (planes * depth), depth)
    line.finish()


def last(part, inputs, gain, branch, sums_two, bias, after, cid):
    rows, width = inputs.shape
    planes = branch.shape[0]
    vectors = (TEAM, planes, 8, 128)
    return pl.pallas_call(
        functools.partial(last_kernel, planes),
        out_shape=[
            jax.ShapeDtypeStruct((rows, width), F32),
            jax.ShapeDtypeStruct(branch.shape, BF16),
            jax.ShapeDtypeStruct(vectors, F32),
        ],
        in_specs=[ANY, VMEM, VMEM, VMEM, VMEM, VMEM, ANY],
        out_specs=[VMEM, ANY, VMEM],
        scratch_shapes=[pltpu.VMEM((16, width), F32)]
        + Sum.scratch(rows, width)
        + Sum.sems
        + Line.sems(planes),
        cost_estimate=lasting(58),
        compiler_params=params(cid),
    )(part, inputs, gain, branch, sums_two, bias, after)


def dot(a, b, dims=((1,), (0,))):
    return lax.dot_general(a, b, (dims, ((), ())), preferred_element_type=F32)


NT = ((1,), (1,))
TN = ((0,), (0,))


def normalize(stream):
    average = jnp.mean(stream, axis=-1, keepdims=True)
    centered = stream - average
    variance = jnp.mean(centered * centered, axis=-1, keepdims=True)
    inverse = lax.rsqrt(variance + EPS)
    return centered * inverse, inverse


def norm_back(grad_norm, normed, inverse):
    return inverse * (
        grad_norm
        - jnp.mean(grad_norm, axis=-1, keepdims=True)
        - normed * jnp.mean(grad_norm * normed, axis=-1, keepdims=True)
    )


def turn(heads, cosine, sine):
    half, width = ROT // 2, heads.shape[-1]
    lanes = lax.broadcasted_iota(jnp.int32, heads.shape, 1) % HEAD_DIM
    moved = jnp.where(lanes < half, -pltpu.roll(heads, width - half, 1), pltpu.roll(heads, half, 1))
    return heads * cosine + moved * sine


def wide(table):
    return jnp.concatenate([table] * (LOCAL * HEAD_DIM // 128), axis=1)


def visible(start):
    size = start.shape[0]
    rows = lax.broadcasted_iota(jnp.int32, (size, size), 0)
    columns = lax.broadcasted_iota(jnp.int32, (size, size), 1)
    start = jnp.concatenate([start] * (size // start.shape[1]), axis=1)
    return (columns <= rows) & (columns.astype(F32) >= start)


def head_of(x, h):
    lanes = lax.broadcasted_iota(jnp.int32, x.shape, 1)
    return jnp.where((lanes >= h * HEAD_DIM) & (lanes < (h + 1) * HEAD_DIM), x, jnp.zeros_like(x))


def soft(query, key, allowed):
    scores = dot(query, key, NT) * 0.125
    masked = jnp.where(allowed, scores, -1e30)
    exponent = jnp.exp(masked - jnp.max(masked, axis=-1, keepdims=True))
    return exponent / jnp.sum(exponent, axis=-1, keepdims=True)


def attend_kernel(planes, qkv_w_ref, gate_ref, up_ref, x_ref, out_weight_ref, position_ref, bias_ref, *refs):
    vector_refs, rate_ref = refs[:4], refs[4]
    h_ref, qkv_ref, attn_ref, resid_ref, h_two_ref, w_both_ref, w_qkv_ref, w_out_ref, tab_ref, norm_ref = refs[5:15]
    cut, landed, made, both, small_ref, place_ref, all_ref, places_ref, tables = refs[15:24]
    x_all, w, wo, norms, b, block, away = refs[24:31]
    sems, scratch = refs[31:60], refs[60:]
    mine, base, _, _ = place()
    plane = base // TEAM
    swap, gather = Swap(made, both, sems[:3]), Gather(x_ref, x_all, sems[3:10])
    vectors = Swap(small_ref, all_ref.at[plane], sems[10:13], same=True)
    places = Swap(place_ref, places_ref, sems[13:16], same=True, near_first=True)
    line = Line(planes, all_ref.at[plane], all_ref, sems[16:19], same=True, within=True)
    rows, heads = LineGather(planes, landed, w, sems[19:22]), Swap(cut, landed, sems[22:25])
    outs = LineGather(planes, out_weight_ref, wo, sems[25:28])
    total, spread = Sum(None, scratch[:4], scratch[4:11], away), Gather(block, h_two_ref, scratch[11:18])
    wide_line = LineGather(planes, both, w_both_ref, scratch[18:21])
    stores = [
        pltpu.make_async_copy(src, dst, scratch[21].at[i])
        for i, (src, dst) in enumerate(((w, w_qkv_ref), (wo, w_out_ref), (tables, tab_ref)))
    ]
    step = pl.program_id(0)
    slot = TEAM - 1 - step

    @pl.when(step == 0)
    def _():
        depth = gate_ref.shape[0]
        for row, ref in enumerate(vector_refs):
            small_ref[row : row + 1, :depth] = ref[...].astype(F32).reshape(1, depth)
        bias = bias_ref[...].astype(F32).reshape(1, bias_ref.shape[0])
        for i in range(bias_ref.shape[0] // depth):
            small_ref[4 + i : 5 + i, :depth] = bias[:, i * depth : (i + 1) * depth]
        known = position_ref[...].astype(F32).reshape(1, position_ref.shape[0])
        for i in range(position_ref.shape[0] // 128):
            place_ref[i : i + 1, :] = known[:, i * 128 : (i + 1) * 128]
        for i in range(TEAM):
            cut[i] = slices(qkv_w_ref, [s * HEADS + z * TEAM + i for s in range(3) for z in range(planes)], HEAD_DIM)
        greet(swap.near + line.near)
        outs.start()
        heads.start()
        vectors.start()
        places.start()
        size = gate_ref.shape[1] // (planes * TEAM)
        for i in range(TEAM):
            units = [z * TEAM + i for z in range(planes)]
            made[i] = jnp.concatenate([slices(gate_ref, units, size), slices(up_ref, units, size)], axis=1)
        outs.stage(2)
        heads.finish()
        rows.start()
        gather.start()
        swap.start()
        vectors.finish()
        line.start()
        for stage in range(3, planes):
            outs.stage(stage)
        places.finish()
        square = (128, 128)

        @pl.loop(0, TEAM)
        def _(i):
            known = places_ref[i]
            for part in range(tables.shape[2] // 128):
                at = jnp.transpose(jnp.broadcast_to(known[part : part + 1, :], square))
                here = pl.ds(part * 128, 128)
                angle = at * rate_ref[...]
                tables[i, 0, here, :] = jnp.cos(angle)
                tables[i, 1, here, :] = jnp.sin(angle)
                token = lax.broadcasted_iota(jnp.int32, square, 0) + part * 128
                tables[i, 2, here, :] = token.astype(F32) - at

        rows.stage(2)
        gather.middle()
        for stage in range(3, planes):
            rows.stage(stage)
        line.finish()
        each = [all_ref[z, i] for z in range(planes) for i in range(TEAM)]
        for i in range(4):
            norms[i : i + 1, :] = jnp.concatenate([known[i : i + 1, :depth] for known in each], axis=1)
        per = qkv_w_ref.shape[1] // (planes * TEAM * depth)
        bias = []
        for part in range(3):
            for z in range(planes):
                head = part * HEADS + z * TEAM + mine
                known = all_ref[head // per // TEAM, lax.rem(head // per, TEAM)]
                row = lax.broadcasted_iota(jnp.int32, known.shape, 0) == 4 + lax.rem(head, per)
                bias.append(jnp.sum(jnp.where(row, known, 0.0), axis=0, keepdims=True)[:, :depth])
        b[...] = jnp.concatenate(bias, axis=1)
        swap.finish()
        wide_line.start()
        gather.finish()
        rows.finish()
        outs.finish()
        for copy in stores:
            copy.start()

    pl.when(step == TEAM - 2)(functools.partial(wide_line.stage, 2))
    stream = x_all[slot].astype(F32)
    normed, _ = normalize(stream)
    h_one = (normed * norms[0:1, :] + norms[1:2, :]).astype(BF16)
    h_ref[0] = h_one
    qkv = dot(h_one, w[...].reshape(-1, w.shape[-1])) + b[...]
    width = LOCAL * HEAD_DIM
    cosine, sine = wide(tables[slot, 0]), wide(tables[slot, 1])
    query = turn(qkv[:, :width], cosine, sine).astype(BF16)
    key = turn(qkv[:, width : 2 * width], cosine, sine).astype(BF16)
    value = qkv[:, 2 * width :].astype(BF16)
    qkv_ref[0, :, :width] = query
    qkv_ref[0, :, width : 2 * width] = key
    qkv_ref[0, :, 2 * width :] = value
    allowed = visible(tables[slot, 2])
    mixed = jnp.zeros((query.shape[0], width), F32)
    for h in range(LOCAL):
        probs = soft(head_of(query, h), key, allowed).astype(BF16)
        mixed = mixed + dot(probs, head_of(value, h))
    attn_low = mixed.astype(BF16)
    attn_ref[0] = attn_low
    part = dot(attn_low, wo[...].reshape(-1, D)).astype(BF16)
    k = 3 - step // 2

    @pl.when(lax.rem(step, 2) == 0)
    def _():
        away[k] = part
        total.near_copy(k).start()

    @pl.when(lax.rem(step, 2) == 1)
    def _():
        total.own[k] = part

    for at, advance in ((1, total.middle_a), (3, total.middle_b), (5, total.middle_c), (6, total.middle_two)):
        pl.when(step == at)(advance)

    def use(rows, value):
        resid = x_all[0, rows, :].astype(F32) + value
        resid_ref[rows, :] = resid
        normed, _ = normalize(resid)
        block[rows, :] = (normed * norms[2:3, :] + norms[3:4, :]).astype(BF16)

    @pl.when(step == TEAM - 1)
    def _():
        total.finish(use)
        spread.start()
        for stage in range(3, planes):
            wide_line.stage(stage)
        spread.middle()
        norm_ref[...] = norms[...]
        spread.finish()
        wide_line.finish()
        for copy in stores:
            copy.wait()


def per_seq(*shape):
    return pl.BlockSpec((1,) + shape, lambda s: (s,) + (0,) * len(shape))


def whole(*shape):
    return pl.BlockSpec(shape, lambda s: (0,) * len(shape))


def attend(qkv, gate, up, inputs, out_weight, positions, bias, vectors, rate, planes, cid):
    rows, _ = inputs.shape
    depth, width = qkv.shape[0], LOCAL * HEAD_DIM
    heads, units = (TEAM, depth, 3 * width), (TEAM, depth, 2 * gate.shape[1] // TEAM)
    tables = (TEAM, 3, rows, 128)
    known = [
        jax.ShapeDtypeStruct((planes,) + units, BF16),
        jax.ShapeDtypeStruct((planes,) + heads, BF16),
        jax.ShapeDtypeStruct((planes,) + out_weight.shape, BF16),
        jax.ShapeDtypeStruct(tables, F32),
    ]

    def far_first(*shape):
        return pl.BlockSpec((1,) + shape, lambda s: (TEAM - 1 - s,) + (0,) * len(shape))

    return pl.pallas_call(
        functools.partial(attend_kernel, planes),
        grid=(TEAM,),
        in_specs=[VMEM] * 12,
        out_specs=[far_first(rows, D), far_first(rows, 3 * width), far_first(rows, width), whole(rows, D)]
        + [ANY] * 5
        + [whole(4, D)],
        out_shape=[
            jax.ShapeDtypeStruct((TEAM, rows, D), BF16),
            jax.ShapeDtypeStruct((TEAM, rows, 3 * width), BF16),
            jax.ShapeDtypeStruct((TEAM, rows, width), BF16),
            jax.ShapeDtypeStruct((rows, D), F32),
            jax.ShapeDtypeStruct((TEAM, rows, D), BF16),
        ]
        + known
        + [jax.ShapeDtypeStruct((4, D), F32)],
        scratch_shapes=[
            pltpu.VMEM(heads, BF16),
            pltpu.VMEM(heads, BF16),
            pltpu.VMEM(units, BF16),
            pltpu.VMEM(units, BF16),
            pltpu.VMEM((8, 128), F32),
            pltpu.VMEM((8, 128), F32),
            pltpu.VMEM((planes, TEAM, 8, 128), F32),
            pltpu.VMEM((TEAM, 8, 128), F32),
            pltpu.VMEM(tables, F32),
            pltpu.VMEM((TEAM, rows, D), BF16),
            pltpu.VMEM((planes,) + heads, BF16),
            pltpu.VMEM((planes,) + out_weight.shape, BF16),
            pltpu.VMEM((4, D), F32),
            pltpu.VMEM((1, 3 * width), F32),
            pltpu.VMEM((rows, D), BF16),
            pltpu.VMEM((4, rows, D), BF16),
        ]
        + Swap.sems
        + Gather.sems
        + Swap.sems * 2
        + Line.sems(planes)
        + LineGather.sems(planes)
        + Swap.sems
        + LineGather.sems(planes)
        + [pltpu.SemaphoreType.DMA]
        + Sum.scratch(rows, D)
        + Sum.sems
        + Gather.sems
        + LineGather.sems(planes)
        + [pltpu.SemaphoreType.DMA((3,))],
        cost_estimate=lasting(180),
        compiler_params=params(cid),
    )(qkv, gate, up, inputs, out_weight, positions, bias, *vectors, rate)


def attend_back_kernel(
    block_ref, wo_ref, w_ref, qkv_ref, tab_ref, attn_ref, hidden_ref, wd_ref, resid_ref, _,
    gqkv_ref, part_ref, gb_ref, wo_grad_ref, out_ref, held, wo_grad, away, *scratch,
):
    gather, block = Gather(block_ref, held, scratch[:7]), Sum(None, scratch[7:11], scratch[11:], away)
    step = pl.program_id(0)

    @pl.when(step == 0)
    def _():
        greet(gather.near)
        gather.start()
        wo_grad[...] = jnp.zeros_like(wo_grad)

    part = dot(hidden_ref[0], wd_ref[...]).astype(BF16)
    k = 3 - step // 2

    @pl.when(lax.rem(step, 2) == 0)
    def _():
        away[k] = part
        block.near_copy(k).start()

    @pl.when(lax.rem(step, 2) == 1)
    def _():
        block.own[k] = part

    for i in range(TEAM):
        pl.when(step == i)(functools.partial(gather.ready, i))
    grad = held[step]
    width = LOCAL * HEAD_DIM
    wo_grad[...] += dot(attn_ref[0], grad, TN)
    grad_att = dot(grad, wo_ref[...], NT).astype(BF16)
    query, key, value = (qkv_ref[0, :, i * width : (i + 1) * width] for i in range(3))
    allowed = visible(tab_ref[0, 2])
    zero = jnp.zeros((query.shape[0], width), F32)
    grad_query, grad_key, grad_value = zero, zero, zero
    for h in range(LOCAL):
        query_h, key_h, grad_h = head_of(query, h), head_of(key, h), head_of(grad_att, h)
        probs = soft(query_h, key, allowed)
        low = probs.astype(BF16)
        grad_probs = dot(grad_h, value, NT)
        delta = jnp.sum(low.astype(F32) * grad_probs, axis=-1, keepdims=True)
        grad_scores = (probs * (grad_probs - delta)).astype(BF16)
        grad_value = grad_value + dot(low, grad_h, TN)
        grad_query = grad_query + dot(grad_scores, key_h)
        grad_key = grad_key + dot(grad_scores, query_h, TN)
    cosine, sine = wide(tab_ref[0, 0]), -wide(tab_ref[0, 1])
    grad_query = turn(grad_query * 0.125, cosine, sine)
    grad_key = turn(grad_key * 0.125, cosine, sine)
    grad_qkv = jnp.concatenate([grad_query, grad_key, grad_value], axis=1).astype(BF16)
    gqkv_ref[0] = grad_qkv
    gb_ref[0] = jnp.sum(grad_qkv.astype(F32), axis=0, keepdims=True)
    part_ref[0] = dot(grad_qkv, w_ref[...], NT).astype(BF16)

    def use(rows, value):
        out_ref[rows, :] = resid_ref[rows, :] + value

    pl.when(step == 1)(gather.middle)
    for at, advance in ((1, block.middle_a), (3, block.middle_b), (5, block.middle_c), (6, block.middle_two)):
        pl.when(step == at)(advance)

    @pl.when(step == TEAM - 1)
    def _():
        wo_grad_ref[...] = wo_grad[...].astype(BF16)
        block.finish(use)
        gather.sent()


def attend_back(block, w_out, w_qkv, qkv, tables, attn, hidden, w_down, resid, after, cid):
    seqs, rows, _ = qkv.shape
    width = LOCAL * HEAD_DIM

    def far_first(*shape):
        return pl.BlockSpec((1,) + shape, lambda s: (seqs - 1 - s,) + (0,) * len(shape))

    return pl.pallas_call(
        attend_back_kernel,
        grid=(seqs,),
        in_specs=[
            ANY,
            whole(width, D),
            whole(D, 3 * width),
            per_seq(rows, 3 * width),
            per_seq(3, rows, 128),
            per_seq(rows, width),
            far_first(rows, hidden.shape[2]),
            VMEM,
            VMEM,
            ANY,
        ],
        out_specs=[per_seq(rows, 3 * width), per_seq(rows, D), per_seq(1, 3 * width), whole(width, D), whole(rows, D)],
        out_shape=[
            jax.ShapeDtypeStruct((seqs, rows, 3 * width), BF16),
            jax.ShapeDtypeStruct((seqs, rows, D), BF16),
            jax.ShapeDtypeStruct((seqs, 1, 3 * width), F32),
            jax.ShapeDtypeStruct((width, D), BF16),
            jax.ShapeDtypeStruct((rows, D), F32),
        ],
        scratch_shapes=[
            pltpu.VMEM((seqs, rows, D), BF16),
            pltpu.VMEM((width, D), F32),
            pltpu.VMEM((4, rows, D), BF16),
        ]
        + Gather.sems
        + Sum.scratch(rows, D)
        + Sum.sems,
        cost_estimate=lasting(65),
        compiler_params=params(cid, 54),
    )(block, w_out, w_qkv, qkv, tables, attn, hidden, w_down, resid, after)


def team_shards(
    inputs, positions, norm1_gain, norm1_bias, qkv_weight, qkv_bias, out_weight, norm2_gain, norm2_bias,
    gate_weight, up_weight, down_weight, out_grad,
):
    n = lax.axis_size("fsdp")
    planes = n // TEAM
    rows = inputs.shape[0]
    tokens = TEAM * rows
    depth = qkv_weight.shape[0]
    ff = down_weight.shape[0]
    width = LOCAL * HEAD_DIM
    lines = [[z * TEAM + i for z in range(planes)] for i in range(TEAM)]
    mine = lax.rem(lax.axis_index("fsdp"), TEAM)

    def line_sum(x):
        return lax.psum_scatter(x, "fsdp", scatter_dimension=0, tiled=True, axis_index_groups=lines)

    half = ROT // 2
    rate = 10000.0 ** (-np.arange(half) / half)
    rate = np.tile(np.concatenate([rate, rate, np.zeros(HEAD_DIM - ROT)]), 128 // HEAD_DIM)[None].astype(np.float32)
    h_one, qkv, attn_low, resid, h_two, w_both, w_qkv, w_out, tables, norms = attend(
        qkv_weight, gate_weight, up_weight, inputs, out_weight, positions, qkv_bias,
        (norm1_gain, norm1_bias, norm2_gain, norm2_bias), jnp.asarray(rate), planes, 1,
    )
    w_both, w_qkv = w_both.reshape(D, 2 * planes * ff), w_qkv.reshape(D, 3 * width)
    w_out = w_out.reshape(width, D)
    pre, hidden, grad_down, g_all, w_down = expand(h_two, w_both, out_grad, down_weight, planes, 3)
    w_down = w_down.reshape(planes * ff, D)
    grad_resid, sums_two, block, grad_w_both = mlp_back(
        pre, g_all, h_two.reshape(tokens, D), w_down, w_both, resid, out_grad, norms, grad_down, 5
    )
    grad_down = line_sum(grad_down)
    grad_w_both = line_sum(grad_w_both)
    grad_qkv, part, grad_bias, grad_out, block_out = attend_back(
        block, w_out, w_qkv, qkv, tables, attn_low, hidden, w_down, resid, grad_down, 6
    )
    grad_qkv = grad_qkv.reshape(tokens, 3 * width)
    grad_w_qkv = dot(h_one.reshape(tokens, D), grad_qkv, TN).astype(BF16)
    part, grad_w_qkv = lax.optimization_barrier((part, grad_w_qkv))
    branch = grad_out.reshape(planes, depth, D)
    norm_part, branch, shared = last(part, inputs, norms, branch, sums_two, grad_bias, grad_w_qkv, 7)
    grad_w_qkv = line_sum(grad_w_qkv)
    blocks = grad_w_both.reshape(TEAM, depth, 2 * planes * ff)
    blocks, sums = both_closing(blocks, shared, (norm_part, branch), 9)
    block_out, input_grad = block_out.astype(BF16), grad_resid + norm_part
    grad_gate_w, grad_up_w, grad_out = first_grads(blocks, branch)
    blocks = closing(grad_w_qkv.reshape(TEAM, depth, 3 * width), (input_grad, grad_up_w, sums), 8)
    grad_w_qkv = rest_grads(blocks, planes)

    return (
        block_out,
        input_grad,
        sums[0, :depth],
        sums[1, :depth],
        grad_w_qkv,
        sums[4 : 4 + qkv_bias.shape[0] // depth, :depth].reshape(-1),
        grad_out,
        sums[2, :depth],
        sums[3, :depth],
        grad_gate_w,
        grad_up_w,
        grad_down.astype(F32),
    )


def rotate_pairs(heads, places, sign):
    half_rot = ROT // 2
    frequency = 10000.0 ** (-jnp.arange(half_rot, dtype=jnp.float32) / half_rot)
    angles = places.astype(jnp.float32)[:, None] * frequency[None, :]
    cosine = jnp.cos(angles)[:, None, :]
    sine_part = sign * jnp.sin(angles)[:, None, :]
    front_part = heads[..., :half_rot]
    back_part = heads[..., half_rot:ROT]
    return jnp.concatenate(
        [
            front_part * cosine - back_part * sine_part,
            back_part * cosine + front_part * sine_part,
            heads[..., ROT:],
        ],
        axis=-1,
    )


def by_groups(heads):
    group_heads = min(8, HEADS)
    shaped = heads.reshape(heads.shape[0], HEADS // group_heads, group_heads, HEAD_DIM)
    return jnp.moveaxis(shaped, 1, 0)


def from_groups(grouped):
    return jnp.moveaxis(grouped, 0, 1).reshape(grouped.shape[1], HEADS, HEAD_DIM)


def plain_group(block_items, allowed):
    query_part, key_part, value_part = block_items
    scores = (
        jnp.einsum("qhd,khd->hqk", query_part, key_part, preferred_element_type=jnp.float32) * 0.125
    )
    masked = jnp.where(allowed[None], scores, -1e30)
    row_max = jnp.max(masked, axis=-1, keepdims=True)
    exponent = jnp.exp(masked - row_max)
    row_total = jnp.sum(exponent, axis=-1, keepdims=True)
    soft_probs = (exponent / row_total).astype(jnp.bfloat16)
    mixed_part = jnp.einsum(
        "hqk,khd->qhd", soft_probs, value_part, preferred_element_type=jnp.float32
    )
    return (mixed_part, (row_max + jnp.log(row_total))[..., 0])


def plain_back(block_items, allowed):
    query_part, key_part, value_part, grad_part, row_delta, log_total = block_items
    scores = (
        jnp.einsum("qhd,khd->hqk", query_part, key_part, preferred_element_type=jnp.float32) * 0.125
    )
    soft_probs = jnp.where(allowed[None], jnp.exp(scores - log_total[..., None]), 0.0)
    grad_probs = jnp.einsum(
        "qhd,khd->hqk", grad_part, value_part.astype(jnp.float32), precision=lax.Precision.HIGHEST
    )
    rounded_probs = soft_probs.astype(jnp.bfloat16).astype(jnp.float32)
    grad_value = jnp.einsum("hqk,qhd->khd", rounded_probs, grad_part, precision=lax.Precision.HIGHEST)
    grad_scores = (soft_probs * (grad_probs - row_delta[..., None])).astype(jnp.bfloat16)
    grad_query = 0.125 * jnp.einsum(
        "hqk,khd->qhd", grad_scores, key_part, preferred_element_type=jnp.float32
    )
    grad_key = 0.125 * jnp.einsum(
        "hqk,qhd->khd", grad_scores, query_part, preferred_element_type=jnp.float32
    )
    return (grad_query, grad_key, grad_value)


def shards(
    inputs,
    positions,
    norm1_gain,
    norm1_bias,
    qkv_weight,
    qkv_bias,
    out_weight,
    norm2_gain,
    norm2_bias,
    gate_weight,
    up_weight,
    down_weight,
    out_grad,
):
    tok_rows = inputs.shape[0]
    gain_one, bias_one, w_qkv, b_qkv, w_out = (
        lax.all_gather(norm1_gain, "fsdp", axis=0, tiled=True),
        lax.all_gather(norm1_bias, "fsdp", axis=0, tiled=True),
        lax.all_gather(qkv_weight, "fsdp", axis=0, tiled=True),
        lax.all_gather(qkv_bias, "fsdp", axis=0, tiled=True),
        lax.all_gather(out_weight, "fsdp", axis=0, tiled=True),
    )
    stream = inputs.astype(jnp.float32)
    normed_one, inverse_one = normalize(stream)
    h_one = (normed_one * gain_one.astype(jnp.float32) + bias_one.astype(jnp.float32)).astype(
        jnp.bfloat16
    )
    qkv_pre = jnp.dot(h_one, w_qkv, preferred_element_type=jnp.float32) + b_qkv.astype(jnp.float32)
    qkv_heads = qkv_pre.reshape(tok_rows, 3, HEADS, HEAD_DIM)
    query_low = rotate_pairs(qkv_heads[:, 0], positions, 1.0).astype(jnp.bfloat16)
    key_all = rotate_pairs(qkv_heads[:, 1], positions, 1.0).astype(jnp.bfloat16)
    value_all = qkv_heads[:, 2].astype(jnp.bfloat16)
    token_index = jnp.arange(tok_rows, dtype=jnp.int32)
    allowed = (token_index[None, :] <= token_index[:, None]) & (
        token_index[None, :] >= (token_index - positions)[:, None]
    )
    mixed_grouped, log_grouped = lax.map(
        lambda block_items: plain_group(block_items, allowed),
        (by_groups(query_low), by_groups(key_all), by_groups(value_all)),
    )
    mixed_heads = from_groups(mixed_grouped)
    attn_low = mixed_heads.reshape(tok_rows, D).astype(jnp.bfloat16)
    resid = stream + jnp.dot(attn_low, w_out, preferred_element_type=jnp.float32)
    gain_two, bias_two, w_gate, w_up, w_down = (
        lax.all_gather(norm2_gain, "fsdp", axis=0, tiled=True),
        lax.all_gather(norm2_bias, "fsdp", axis=0, tiled=True),
        lax.all_gather(gate_weight, "fsdp", axis=0, tiled=True),
        lax.all_gather(up_weight, "fsdp", axis=0, tiled=True),
        lax.all_gather(down_weight, "fsdp", axis=0, tiled=True),
    )
    normed_two, inverse_two = normalize(resid)
    h_two = (normed_two * gain_two.astype(jnp.float32) + bias_two.astype(jnp.float32)).astype(
        jnp.bfloat16
    )
    gate_pre = jnp.dot(h_two, w_gate, preferred_element_type=jnp.float32)
    up_pre = jnp.dot(h_two, w_up, preferred_element_type=jnp.float32)
    sigmoid_gate = jax.nn.sigmoid(gate_pre)
    silu_gate = gate_pre * sigmoid_gate
    hidden = (silu_gate * up_pre).astype(jnp.bfloat16)
    block_out = (resid + jnp.dot(hidden, w_down, preferred_element_type=jnp.float32)).astype(
        jnp.bfloat16
    )
    gain_two, w_gate, w_up, w_down = (
        lax.all_gather(norm2_gain, "fsdp", axis=0, tiled=True),
        lax.all_gather(gate_weight, "fsdp", axis=0, tiled=True),
        lax.all_gather(up_weight, "fsdp", axis=0, tiled=True),
        lax.all_gather(down_weight, "fsdp", axis=0, tiled=True),
    )
    grad_down_w = jnp.einsum("tf,td->fd", hidden, out_grad, preferred_element_type=jnp.float32)
    grad_hidden = jnp.einsum("td,fd->tf", out_grad, w_down, preferred_element_type=jnp.float32)
    grad_gate = (
        grad_hidden * up_pre * sigmoid_gate * (1.0 + gate_pre * (1.0 - sigmoid_gate))
    ).astype(jnp.bfloat16)
    grad_up = (grad_hidden * silu_gate).astype(jnp.bfloat16)
    grad_gate_w = jnp.einsum("td,tf->df", h_two, grad_gate, preferred_element_type=jnp.float32)
    grad_up_w = jnp.einsum("td,tf->df", h_two, grad_up, preferred_element_type=jnp.float32)
    grad_htwo = jnp.einsum(
        "tf,df->td", grad_gate, w_gate, preferred_element_type=jnp.float32
    ) + jnp.einsum("tf,df->td", grad_up, w_up, preferred_element_type=jnp.float32)
    grad_gain_two = jnp.sum(grad_htwo * normed_two, axis=0)
    grad_bias_two = jnp.sum(grad_htwo, axis=0)
    grad_resid = out_grad.astype(jnp.float32) + norm_back(
        grad_htwo * gain_two.astype(jnp.float32), normed_two, inverse_two
    )
    mlp_sums = (
        lax.psum_scatter(grad_gain_two, "fsdp", scatter_dimension=0, tiled=True),
        lax.psum_scatter(grad_bias_two, "fsdp", scatter_dimension=0, tiled=True),
        lax.psum_scatter(grad_gate_w, "fsdp", scatter_dimension=0, tiled=True),
        lax.psum_scatter(grad_up_w, "fsdp", scatter_dimension=0, tiled=True),
        lax.psum_scatter(grad_down_w, "fsdp", scatter_dimension=0, tiled=True),
    )
    gain_one, w_qkv, w_out = (
        lax.all_gather(norm1_gain, "fsdp", axis=0, tiled=True),
        lax.all_gather(qkv_weight, "fsdp", axis=0, tiled=True),
        lax.all_gather(out_weight, "fsdp", axis=0, tiled=True),
    )
    grad_branch = grad_resid.astype(jnp.bfloat16)
    grad_out_w = jnp.einsum("ti,td->id", attn_low, grad_branch, preferred_element_type=jnp.float32)
    grad_att = jnp.einsum(
        "td,id->ti", grad_branch, w_out, preferred_element_type=jnp.float32
    ).reshape(tok_rows, HEADS, HEAD_DIM)
    group_heads = min(8, HEADS)
    row_delta = jnp.sum(grad_att * mixed_heads, axis=-1)
    delta_grouped = row_delta.reshape(tok_rows, HEADS // group_heads, group_heads).transpose(
        1, 2, 0
    )
    query_grouped, key_grouped, value_grouped = lax.map(
        lambda block_items: plain_back(block_items, allowed),
        (
            by_groups(query_low),
            by_groups(key_all),
            by_groups(value_all),
            by_groups(grad_att),
            delta_grouped,
            log_grouped,
        ),
    )
    grad_query = from_groups(query_grouped)
    grad_key = from_groups(key_grouped)
    grad_value = from_groups(value_grouped)
    grad_qkv = (
        jnp.stack(
            [
                rotate_pairs(grad_query, positions, -1.0),
                rotate_pairs(grad_key, positions, -1.0),
                grad_value,
            ],
            axis=1,
        )
        .reshape(tok_rows, 3 * D)
        .astype(jnp.bfloat16)
    )
    grad_qkv_w = jnp.einsum("td,tk->dk", h_one, grad_qkv, preferred_element_type=jnp.float32)
    grad_qkv_b = jnp.sum(grad_qkv.astype(jnp.float32), axis=0)
    grad_hone = jnp.einsum("tk,dk->td", grad_qkv, w_qkv, preferred_element_type=jnp.float32)
    grad_gain_one = jnp.sum(grad_hone * normed_one, axis=0)
    grad_bias_one = jnp.sum(grad_hone, axis=0)
    input_grad = grad_resid + norm_back(
        grad_hone * gain_one.astype(jnp.float32), normed_one, inverse_one
    )
    attn_sums = (
        lax.psum_scatter(grad_gain_one, "fsdp", scatter_dimension=0, tiled=True),
        lax.psum_scatter(grad_bias_one, "fsdp", scatter_dimension=0, tiled=True),
        lax.psum_scatter(grad_qkv_w, "fsdp", scatter_dimension=0, tiled=True),
        lax.psum_scatter(grad_qkv_b, "fsdp", scatter_dimension=0, tiled=True),
        lax.psum_scatter(grad_out_w, "fsdp", scatter_dimension=0, tiled=True),
    )
    return (
        block_out,
        input_grad,
        attn_sums[0],
        attn_sums[1],
        attn_sums[2],
        attn_sums[3],
        attn_sums[4],
        mlp_sums[0],
        mlp_sums[1],
        mlp_sums[2],
        mlp_sums[3],
        mlp_sums[4],
    )


def solution(mesh):
    devices = mesh.shape["fsdp"]
    rows, columns = P("fsdp", None), P("fsdp")
    body = team_shards if devices % TEAM == 0 and D == devices * HEAD_DIM else shards
    return jax.shard_map(
        body,
        mesh=mesh,
        in_specs=(rows, columns, columns, columns, rows, columns, rows, columns, columns, rows, rows, rows, rows),
        out_specs=(rows, rows, columns, columns, rows, columns, rows, columns, columns, rows, rows, rows),
        check_vma=False,
    )
```
